128 devices in a mesh: dp: 2 (over core), ctx: 64 (over x, y, z).
Axes of the slice: x: 4, y: 4, z: 4, core: 2. Of those that a mesh axis runs over, the one named last changes fastest.
Arguments:
- tokens: bfloat16 [2, 8192, 640], P('dp', 'ctx'), may hold values from -16 to 16
- doc_lengths: int32 [2, 8], P('dp'), may hold values from 1 to 4160, as said below
- block_order: int32 [128], replicated, may hold values from 0 to 127, as said below
- attn_norm: bfloat16 [640], P(('dp', 'ctx')), may hold values from 0.25 to 1.75
- query_weight: bfloat16 [640, 1024], P(('dp', 'ctx')), may hold values from -0.25 to 0.25
- key_weight: bfloat16 [640, 256], P(('dp', 'ctx')), may hold values from -0.25 to 0.25
- value_weight: bfloat16 [640, 256], P(('dp', 'ctx')), may hold values from -0.25 to 0.25
- query_gain: bfloat16 [256], P(('dp', 'ctx')), may hold values from 0.25 to 1.75
- key_gain: bfloat16 [256], P(('dp', 'ctx')), may hold values from 0.25 to 1.75
- output_weight: bfloat16 [1024, 640], P(('dp', 'ctx')), may hold values from -0.1875 to 0.1875
- attn_post_norm: bfloat16 [640], P(('dp', 'ctx')), may hold values from 0.25 to 1.75
- ffn_norm: bfloat16 [640], P(('dp', 'ctx')), may hold values from 0.25 to 1.75
- gate_weight: bfloat16 [640, 2048], P(('dp', 'ctx')), may hold values from -0.25 to 0.25
- up_weight: bfloat16 [640, 2048], P(('dp', 'ctx')), may hold values from -0.25 to 0.25
- down_weight: bfloat16 [2048, 640], P(('dp', 'ctx')), may hold values from -0.125 to 0.125
- ffn_post_norm: bfloat16 [640], P(('dp', 'ctx')), may hold values from 0.25 to 1.75
- out_cot: bfloat16 [2, 8192, 640], P('dp', 'ctx'), may hold values from -6 to 6
Outputs:
- block_out: bfloat16 [2, 8192, 640], P('dp', 'ctx')
- tokens_grad: bfloat16 [2, 8192, 640], P('dp', 'ctx')
- attn_norm_grad: float32 [640], P(('dp', 'ctx'))
- query_grad: float32 [640, 1024], P(('dp', 'ctx'))
- key_grad: float32 [640, 256], P(('dp', 'ctx'))
- value_grad: float32 [640, 256], P(('dp', 'ctx'))
- query_gain_grad: float32 [256], P(('dp', 'ctx'))
- key_gain_grad: float32 [256], P(('dp', 'ctx'))
- output_grad: float32 [1024, 640], P(('dp', 'ctx'))
- attn_post_norm_grad: float32 [640], P(('dp', 'ctx'))
- ffn_norm_grad: float32 [640], P(('dp', 'ctx'))
- gate_grad: float32 [640, 2048], P(('dp', 'ctx'))
- up_grad: float32 [640, 2048], P(('dp', 'ctx'))
- down_grad: float32 [2048, 640], P(('dp', 'ctx'))
- ffn_post_norm_grad: float32 [640], P(('dp', 'ctx'))
The draws below stay inside these ranges and needn't reach their ends.
Inputs may be any that keep to these rules, and one draw needn't show every extreme that they name: `doc_lengths`: in each row the lengths are positive and sum to 8192; the longest, 4160, is the row's first or last document. `block_order`: A permutation of the 128 block numbers; entries 2c and 2c + 1, the blocks that index c of ctx holds, sum to 127.
All inputs are finite; a program needn't handle non-finite values.
Results may differ from the reference program's by a relative error of at most 0.029.
Values may be sent and summed in bfloat16 or wider, within the bound.
A program may use at most 128 MiB of HBM per device.

```python
import math
import jax
import jax.numpy as jnp
from jax import lax

D = 640
HEADS = 4
HEAD = 256
FF = 2048
NDOC = 8
QW = 1024
BATCH = 2
SEQ = 8192
BLOCK = 64
BLOCKS = 128
LONGEST = 4160


def draw_tokens(key, part):
    key = jax.random.fold_in(key, 13)
    drawn_key, row_key, column_key = jax.random.split(key, 3)
    drawn_draw = jnp.clip(jax.random.normal(drawn_key, (BATCH, SEQ, D), jnp.float32), -4.0, 4.0)
    row_scale = jnp.exp(jax.random.uniform(row_key, (BATCH, SEQ, 1), jnp.float32, math.log(0.4), math.log(2.5)))
    column_scale = jnp.exp(jax.random.uniform(column_key, (1, 1, D), jnp.float32, math.log(0.6), math.log(1.6)))
    return (drawn_draw * row_scale * column_scale).astype(jnp.bfloat16)


def one_row_lengths(row_key):
    rest_tokens = SEQ - LONGEST
    pick_key, side_key = jax.random.split(row_key)
    cut_points = jnp.sort(jax.random.permutation(pick_key, rest_tokens - 1)[:NDOC - 2] + 1).astype(jnp.int32)
    edges = jnp.concatenate([jnp.zeros((1,), jnp.int32), cut_points, jnp.full((1,), rest_tokens, jnp.int32)])
    pieces = edges[1:] - edges[:-1]
    longest = jnp.full((1,), LONGEST, jnp.int32)
    at_front = jnp.concatenate([longest, pieces])
    at_back = jnp.concatenate([pieces, longest])
    flipped = jax.random.randint(side_key, (), 0, 2)
    return jnp.where(flipped == 0, at_front, at_back).astype(jnp.int32)


def draw_doc_lengths(key, part):
    key = jax.random.fold_in(key, 11)
    return jax.vmap(one_row_lengths)(jax.random.split(key, BATCH))


def draw_block_order(key, part):
    key = jax.random.fold_in(key, 12)
    pairs = BLOCKS // 2
    lower = jax.random.permutation(key, pairs).astype(jnp.int32)
    return jnp.stack([lower, BLOCKS - 1 - lower], axis=1).reshape(BLOCKS).astype(jnp.int32)


def shard_levels(key, extent, cuts, low, largest):
    def one(dim, blocks):
        steps = jax.random.uniform(jax.random.fold_in(jax.random.fold_in(key, 6), dim), (blocks,), jnp.float32, low / len(cuts), largest / len(cuts))
        return jnp.repeat(jnp.exp(steps), extent[dim] // blocks).reshape((-1,) + (1,) * (len(extent) - dim - 1))

    loudness = one(*cuts[0])
    for cut in cuts[1:]:
        loudness = loudness * one(*cut)
    return loudness


def normal_values(own_key, dims, deviation, most, cuts=(), kind=jnp.bfloat16):
    entries = deviation * jax.random.normal(own_key, dims, jnp.float32)
    if cuts:
        entries = entries * shard_levels(own_key, dims, cuts, -0.22, 0.18)
    return jnp.clip(entries, -most, most).astype(kind)


def setup_inputs(seed: int = 0) -> dict:
    splits = jax.random.split(jax.random.key(seed), 18)
    return {
        "tokens": draw_tokens(jax.random.fold_in(splits[17], 71), 0),
        "doc_lengths": draw_doc_lengths(jax.random.fold_in(splits[17], 71), 0),
        "block_order": draw_block_order(jax.random.fold_in(splits[17], 71), 0),
        "attn_norm": jnp.clip(1.0 + 0.15 * jax.random.normal(splits[3], (D,), jnp.float32), 0.25, 1.75).astype(jnp.bfloat16),
        "query_weight": normal_values(splits[4], (D, QW), D ** -0.5, 0.25, ((0, 128),)),
        "key_weight": normal_values(splits[5], (D, HEAD), D ** -0.5, 0.25, ((0, 128),)),
        "value_weight": normal_values(splits[6], (D, HEAD), D ** -0.5, 0.25, ((0, 128),)),
        "query_gain": jnp.clip(1.0 + 0.15 * jax.random.normal(splits[7], (HEAD,), jnp.float32), 0.25, 1.75).astype(jnp.bfloat16),
        "key_gain": jnp.clip(1.0 + 0.15 * jax.random.normal(splits[8], (HEAD,), jnp.float32), 0.25, 1.75).astype(jnp.bfloat16),
        "output_weight": normal_values(splits[9], (QW, D), QW ** -0.5, 0.1875, ((0, 128),)),
        "attn_post_norm": jnp.clip(1.0 + 0.15 * jax.random.normal(splits[10], (D,), jnp.float32), 0.25, 1.75).astype(jnp.bfloat16),
        "ffn_norm": jnp.clip(1.0 + 0.15 * jax.random.normal(splits[11], (D,), jnp.float32), 0.25, 1.75).astype(jnp.bfloat16),
        "gate_weight": normal_values(splits[12], (D, FF), D ** -0.5, 0.25, ((0, 128),)),
        "up_weight": normal_values(splits[13], (D, FF), D ** -0.5, 0.25, ((0, 128),)),
        "down_weight": normal_values(splits[14], (FF, D), FF ** -0.5, 0.125, ((0, 128),)),
        "ffn_post_norm": jnp.clip(1.0 + 0.15 * jax.random.normal(splits[15], (D,), jnp.float32), 0.25, 1.75).astype(jnp.bfloat16),
        "out_cot": normal_values(splits[16], (BATCH, SEQ, D), 1.0, 6.0, ((0, 2), (1, 64))),
    }


@jax.custom_vjp
def low(v):
    return lax.optimization_barrier(v.astype(jnp.bfloat16)).astype(jnp.float32)

@jax.custom_vjp
def low_back(v):
    return v

def low_keep(v):
    return (low(v), None)

def low_pass(kept, grad):
    return (grad,)

def back_keep(v):
    return (v, None)

def back_low(kept, grad):
    return (low(grad),)
low.defvjp(low_keep, low_pass)
low_back.defvjp(back_keep, back_low)
EPSILON = 1e-06
ROPE_BASE = 1000000.0
MASKED = -1e+30

def highest(left, right):
    return jnp.dot(left, right, precision=lax.Precision.HIGHEST)

def rms_scale(values, weights):
    return values * lax.rsqrt(lax.optimization_barrier(jnp.mean(values * values, axis=-1, keepdims=True)) + EPSILON) * weights

def rope_turn(vectors, places):
    halfway = vectors.shape[-1] // 2
    steps_up = jnp.arange(halfway, dtype=jnp.float32)
    frequency = ROPE_BASE ** (-2.0 * steps_up / vectors.shape[-1])
    angles = places.astype(jnp.float32)[:, None] * frequency[None, :]
    angles = jnp.concatenate([angles, angles], axis=-1)
    if vectors.ndim == 3:
        angles = angles[:, None, :]
    turned = jnp.concatenate([-vectors[..., halfway:], vectors[..., :halfway]], axis=-1)
    return vectors * jnp.cos(angles) + turned * jnp.sin(angles)

def place_tables(lengths, block_order):
    rows_all = jnp.arange(SEQ, dtype=jnp.int32)
    seq_place = block_order[rows_all // BLOCK] * BLOCK + rows_all % BLOCK
    starts = jnp.cumsum(lengths) - lengths
    segment = lax.optimization_barrier(jnp.sum((starts[None, 1:] <= seq_place[:, None]).astype(jnp.int32), axis=1))
    return (seq_place, segment, seq_place - starts[segment])

def attend(query_rot, key_rot, value_rot, seq_place, segment):
    span_rows = min(512, SEQ)
    score_scale = float(query_rot.shape[-1]) ** (-0.5)

    def one_block(inputs):
        query_block, place_block, segment_block = inputs
        scores = jnp.einsum('ihd,jd->hij', query_block, key_rot, precision=lax.Precision.HIGHEST) * score_scale
        scores = low_back(scores)
        allowed = (segment[None, :] == segment_block[:, None]) & (seq_place[None, :] <= place_block[:, None])
        scores = jnp.where(allowed[None], scores, MASKED)
        attn_probs = jnp.exp(scores - jax.nn.logsumexp(scores, axis=-1, keepdims=True))
        return jnp.einsum('hij,jd->ihd', low(attn_probs), value_rot, precision=lax.Precision.HIGHEST)
    blocks_in = (query_rot.reshape(SEQ // span_rows, span_rows, HEADS, HEAD), seq_place.reshape(SEQ // span_rows, span_rows), segment.reshape(SEQ // span_rows, span_rows))
    result = lax.map(jax.checkpoint(one_block), blocks_in)
    return result.reshape(SEQ, HEADS, HEAD)

def layer(inputs, params, seq_place, segment, position):
    gain_attn, w_query, w_key, w_value, gain_query, gain_key, w_output, gain_post_attn, gain_ffn, w_gate, w_up, w_down, gain_post_ffn = params
    normed = low(rms_scale(inputs, gain_attn))
    query_raw = low_back(highest(normed, w_query)).reshape(SEQ, HEADS, HEAD)
    key_raw = low_back(highest(normed, w_key))
    value_raw = low_back(highest(normed, w_value))
    query_rot = low(rope_turn(rms_scale(query_raw, gain_query), position))
    key_rot = low(rope_turn(rms_scale(key_raw, gain_key), position))
    value_rot = low(value_raw)
    attn_sum = attend(query_rot, key_rot, value_rot, seq_place, segment)
    attn_low = low(low_back(attn_sum.reshape(SEQ, HEADS * HEAD)))
    proj_out = low_back(highest(attn_low, w_output))
    middle = inputs + rms_scale(proj_out, gain_post_attn)
    ffn_in = low(rms_scale(middle, gain_ffn))
    gate = low_back(highest(ffn_in, w_gate))
    upper = low_back(highest(ffn_in, w_up))
    hidden = low(jax.nn.gelu(gate, approximate=True) * upper)
    ffn_out = low_back(highest(hidden, w_down))
    return middle + rms_scale(ffn_out, gain_post_ffn)

def reference(tokens, doc_lengths, block_order, attn_norm, query_weight, key_weight, value_weight, query_gain, key_gain, output_weight, attn_post_norm, ffn_norm, gate_weight, up_weight, down_weight, ffn_post_norm, out_cot):
    weights_all = (attn_norm, query_weight, key_weight, value_weight, query_gain, key_gain, output_weight, attn_post_norm, ffn_norm, gate_weight, up_weight, down_weight, ffn_post_norm)
    params = tuple((item.astype(jnp.float32) for item in weights_all))
    outs_list = []
    grads_in = []
    totals = None
    for row_index in range(BATCH):
        seq_place, segment, position = place_tables(doc_lengths[row_index], block_order)

        def forward(row_in, weights_in):
            return layer(row_in, weights_in, seq_place, segment, position)
        result, pull = jax.vjp(forward, tokens[row_index].astype(jnp.float32), params)
        grad_row, grad_params = pull(out_cot[row_index].astype(jnp.float32))
        outs_list.append(result)
        grads_in.append(grad_row)
        if totals is None:
            totals = grad_params
        else:
            totals = tuple((first + second for first, second in zip(totals, grad_params)))
    return (jnp.stack(outs_list).astype(jnp.bfloat16), jnp.stack(grads_in).astype(jnp.bfloat16), totals[0], totals[1], totals[2], totals[3], totals[4], totals[5], totals[6], totals[7], totals[8], totals[9], totals[10], totals[11], totals[12])
```

```python
import functools

import jax
import jax.numpy as jnp
from jax import lax
from jax.experimental import pallas as pl
from jax.experimental.pallas import tpu as pltpu
from jax.sharding import PartitionSpec as P

EPSILON = 1e-06
ROPE_BASE = 1000000.0
MESH = pl.DeviceIdType.MESH
F32 = jnp.float32
BF16 = jnp.bfloat16
MIB = 2**20

X, Y, Z = 0, 1, 2
ORDERS = ((Z, Y, X), (X, Z, Y), (Y, X, Z))
KV_ROWS = ((0, 80), (80, 80), (160, 96))
HEADS = 4
HEAD = 256
SCALE = HEAD**-0.5
LOG2E = 1.4426950408889634


def place():
    chip = lax.axis_index("ctx")
    return (chip // 16, (chip // 4) % 4, chip % 4)


def shifted(value, step):
    return lax.rem(value + step + 4, 4)


def peer(axis, step):
    spot = list(place())
    spot[axis] = shifted(spot[axis], step)
    return (lax.axis_index("dp"), spot[0] * 16 + spot[1] * 4 + spot[2])


def other_core():
    return (1 - lax.axis_index("dp"), lax.axis_index("ctx"))


def greet():
    barrier = pltpu.get_barrier_semaphore()
    for axis in (X, Y, Z):
        for step in (1, 2, 3):
            pl.semaphore_signal(barrier, inc=1, device_id=peer(axis, step), device_id_type=MESH)
    pl.semaphore_signal(barrier, inc=1, device_id=other_core(), device_id_type=MESH)
    pl.semaphore_wait(barrier, 10)


class Links:
    def __init__(self, send, recv):
        self.send, self.recv, self.used, self.sent = send, recv, 0, []

    def copy(self, number, src, dst, device):
        return pltpu.make_async_remote_copy(
            src_ref=src,
            dst_ref=dst,
            send_sem=self.send.at[number],
            recv_sem=self.recv.at[number],
            device_id=device,
            device_id_type=MESH,
        )

    def start(self, src, dst, device):
        number = self.used
        self.used += 1
        copy = self.copy(number, src, dst, device)
        copy.start()
        self.sent.append(copy)
        return number

    def ring(self, axis, src_of, dst_of):
        mine = place()[axis]
        numbers = [
            self.start(src_of(step), dst_of(step, mine), peer(axis, step)) for step in (1, 2, 3)
        ]

        def wait(step):
            self.copy(
                numbers[step - 1],
                src_of(step),
                dst_of(step, shifted(mine, -step)),
                peer(axis, step),
            ).wait_recv()

        return wait

    def across(self, src, dst_of):
        mine = lax.axis_index("dp")
        number = self.start(src, dst_of(mine), other_core())

        def wait():
            self.copy(number, src, dst_of(1 - mine), other_core()).wait_recv()

        return wait

    def close(self):
        for copy in self.sent:
            copy.wait_send()


def all_steps(wait):
    for step in (1, 2, 3):
        wait(step)


VMEM = pl.BlockSpec(memory_space=pltpu.VMEM)
SMEM = pl.BlockSpec(memory_space=pltpu.SMEM)
ANY = pl.BlockSpec(memory_space=pl.ANY)


def link_call(kernel, number, semaphores, outs, ins, in_specs, out_specs, scratch=(), local=0):
    return pl.pallas_call(
        kernel,
        out_shape=[jax.ShapeDtypeStruct(shape, kind) for shape, kind in outs],
        in_specs=in_specs,
        out_specs=out_specs,
        scratch_shapes=[pltpu.VMEM(shape, kind) for shape, kind in scratch]
        + [pltpu.SemaphoreType.DMA((semaphores,)), pltpu.SemaphoreType.DMA((semaphores,))]
        + ([pltpu.SemaphoreType.DMA((local,))] if local else []),
        compiler_params=pltpu.CompilerParams(
            collective_id=number, has_side_effects=True, vmem_limit_bytes=60 * MIB
        ),
    )(*ins)


def early_kernel(a_ref, b_ref, c_ref, kvg_ref, pa_ref, pb_ref, pc_ref, u0_ref, u1_ref, send, recv):
    links = Links(send, recv)
    core = lax.axis_index("dp")
    spot = place()
    planes = (pa_ref, pb_ref, pc_ref)
    for part, own in enumerate((a_ref, b_ref, c_ref)):
        first, second, _ = ORDERS[part]
        planes[part][spot[second], spot[first]] = own[...]
    x, y, z = spot
    u0_ref[core, x, y, z] = kvg_ref[0:16]
    u1_ref[core, y, z, x] = kvg_ref[16:32]
    greet()

    def small(axis, unit, index_of):
        ref = (u0_ref, u1_ref)[unit]
        return links.ring(
            axis, lambda step: ref.at[index_of(spot[axis])], lambda step, at: ref.at[index_of(at)]
        )

    w0 = small(Z, 0, lambda at: (core, x, y, at))
    w1 = small(X, 1, lambda at: (core, y, z, at))
    waits = []
    for part in range(3):
        first, second, _ = ORDERS[part]
        ref, row = planes[part], spot[second]
        waits.append(
            links.ring(
                first,
                lambda step, ref=ref, row=row, first=first: ref.at[row, spot[first]],
                lambda step, at, ref=ref, row=row: ref.at[row, at],
            )
        )
    all_steps(w0)
    w0 = small(Y, 0, lambda at: (core, x, at))
    all_steps(w1)
    w1 = small(Z, 1, lambda at: (core, y, at))
    seconds = []
    for part in range(3):
        all_steps(waits[part])
        second = ORDERS[part][1]
        ref = planes[part]
        seconds.append(
            links.ring(
                second,
                lambda step, ref=ref, second=second: ref.at[spot[second]],
                lambda step, at, ref=ref: ref.at[at],
            )
        )
    all_steps(w0)
    w0 = small(X, 0, lambda at: (core, at))
    all_steps(w1)
    w1 = small(Y, 1, lambda at: (core, at))
    all_steps(w0)
    c0 = links.across(u0_ref.at[core], lambda at: u0_ref.at[at])
    all_steps(w1)
    c1 = links.across(u1_ref.at[core], lambda at: u1_ref.at[at])
    for wait in seconds:
        all_steps(wait)
    c0()
    c1()
    links.close()


def early(a, b, c, kvg):
    outs = [
        ((4, 4) + a.shape, BF16),
        ((4, 4) + b.shape, BF16),
        ((4, 4) + c.shape, BF16),
        ((2, 4, 4, 4, 16, 128), BF16),
        ((2, 4, 4, 4, 16, 128), BF16),
    ]
    return link_call(early_kernel, 1, 40, outs, (a, b, c, kvg), [VMEM] * 4, [VMEM] * 5)


def of_plane(ref, axis, at, *rest):
    index = [slice(None)] * 3
    index[axis] = at
    return ref.at[(*index, *rest)]


def chip_of(spot, axis, step):
    spot = list(spot)
    spot[axis] = shifted(spot[axis], step)
    return spot[0] * 16 + spot[1] * 4 + spot[2]


WEIGHTS = ((0, False), (0, False), (1, False), (1, False), (2, True))


def weight_plane(ref, part, by_chip, core, at):
    if by_chip:
        return of_plane(ref.at[core], ORDERS[part][2], at)
    return ref.at[core, at]


def plane_loop(part, body):
    first, second, last = ORDERS[part]

    def step(number, unused):
        spot = [None] * 3
        spot[first], spot[second], spot[last] = number % 4, number // 4, place()[last]
        body(spot, number // 4, number % 4)
        return unused

    lax.fori_loop(0, 16, step, 0)


def gather_kernel(*refs):
    b_ref, kv_ref, gp, op, up, qp, dp = refs[:7]
    s_ref, extra_ref, gw, ow, uw, qw, dw = refs[7:14]
    f1, g, sel, special, rsp = (refs[14 + 3 * i : 17 + 3 * i] for i in range(5))
    send, recv, local = refs[29:]
    links = Links(send, recv)
    core = lax.axis_index("dp")
    spot = place()
    me = lax.axis_index("ctx")
    weights = tuple(zip((gp, op, up, qp, dp), (gw, ow, uw, qw, dw), WEIGHTS))
    greet()
    waits = []
    for part, (row, rows) in enumerate(KV_ROWS):
        first = ORDERS[part][0]
        own = kv_ref.at[:, pl.ds(row, rows)]
        waits.append(
            links.ring(
                first,
                lambda step, own=own: own,
                lambda step, at, ref=f1[part]: ref.at[at],
            )
        )
    own_copies = []
    weight_waits = []
    for number, (plane, whole, (part, by_chip)) in enumerate(weights):
        last = ORDERS[part][2]

        def landing(core, at, whole=whole, part=part, by_chip=by_chip):
            return weight_plane(whole, part, by_chip, core, at)

        copy = pltpu.make_async_copy(plane, landing(core, spot[last]), local.at[number])
        copy.start()
        own_copies.append(copy)
        wait = links.ring(
            last,
            lambda step, plane=plane: plane,
            lambda step, at, landing=landing: landing(core, at),
        )
        over = links.across(plane, lambda at, landing=landing, last=last: landing(at, spot[last]))
        weight_waits.append((wait, landing, last, over))

    seconds = []
    for part, (row, rows) in enumerate(KV_ROWS):
        first, second, _ = ORDERS[part]
        f1[part][spot[first]] = kv_ref[:, row : row + rows]
        all_steps(waits[part])
        mine = spot[second]
        total = f1[part][0, 2].astype(F32)
        for at in range(4):
            g[part][mine, 2 * at] = f1[part][at, 0]
            g[part][mine, 2 * at + 1] = f1[part][at, 1]
            if at:
                total += f1[part][at, 2].astype(F32)
        g[part][mine, 8] = total.astype(BF16)
        seconds.append(
            links.ring(
                second,
                lambda step, ref=g[part], mine=mine: ref.at[mine],
                lambda step, at, ref=g[part]: ref.at[at],
            )
        )
    thirds = []
    for part, (row, rows) in enumerate(KV_ROWS):
        first, second, last = ORDERS[part]
        all_steps(seconds[part])

        def choose(at, i2, i1, part=part, row=row, rows=rows, last=last):
            low = g[part][i2, 2 * i1]
            high = g[part][i2, 2 * i1 + 1]
            source = b_ref[chip_of(at, last, 0)]
            plane = [at[axis] for axis in (X, Y, Z) if axis != last]
            s_ref[at[0], at[1], at[2], pl.ds(row, rows)] = jnp.where(
                source <= b_ref[me], low, high
            )
            for step in (1, 2, 3):
                target = b_ref[chip_of(spot, last, step)]
                sel[part][step - 1, plane[0], plane[1]] = jnp.where(source < target, low, high)

        plane_loop(part, choose)
        total = g[part][0, 8].astype(F32)
        for at in range(1, 4):
            total += g[part][at, 8].astype(F32)
        special[part][...] = total.astype(BF16)
        wait = links.ring(
            last,
            lambda step, part=part: sel[part].at[step - 1],
            lambda step, at, row=row, rows=rows, last=last: of_plane(
                s_ref, last, at, pl.ds(row, rows)
            ),
        )
        wait_special = links.ring(
            last,
            lambda step, part=part: special[part],
            lambda step, at, part=part: rsp[part].at[at],
        )
        thirds.append((wait, wait_special))
    overs = []
    for wait, landing, last, over in weight_waits:
        for step in (1, 3, 2):
            wait(step)
            at = shifted(spot[last], -step)
            overs.append(
                links.across(
                    landing(core, at), lambda at_core, landing=landing, at=at: landing(at_core, at)
                )
            )
        overs.append(over)
    extra_ref[0] = kv_ref[1]
    for part, (row, rows) in enumerate(KV_ROWS):
        last = ORDERS[part][2]
        wait, wait_special = thirds[part]
        all_steps(wait_special)
        rsp[part][spot[last]] = special[part][...]
        total = rsp[part][0].astype(F32)
        for at in range(1, 4):
            total += rsp[part][at].astype(F32)
        extra_ref[1, row : row + rows] = total.astype(BF16)
        all_steps(wait)
    for wait in overs:
        wait()
    for copy in own_copies:
        copy.wait()
    links.close()


def gather(b_all, kv3, planes):
    outs = [((4, 4, 4, 256, 128), BF16), ((2, 256, 128), BF16)]
    for plane, (part, by_chip) in zip(planes, WEIGHTS):
        shape = (2, 4, 4, 4, plane.shape[2], plane.shape[3]) if by_chip else (2, 4) + plane.shape
        outs.append((shape, BF16))
    scratch = []
    for shape in ((4, 3), (4, 9), (3, 4, 4), (), (4,)):
        for _, rows in KV_ROWS:
            scratch.append((shape + (rows, 128), BF16))
    return link_call(
        gather_kernel,
        2,
        80,
        outs,
        (b_all, kv3, *planes),
        [SMEM, VMEM] + [ANY] * 5,
        [VMEM, VMEM] + [ANY] * 5,
        scratch,
        local=5,
    )


def slots_kv(block):
    count = block.shape[0] * 64
    quarters = [block[:, 64 * i : 64 * i + 64].reshape(count, 128) for i in range(4)]
    return (
        jnp.concatenate(quarters[:2], axis=1),
        jnp.concatenate(quarters[2:], axis=1),
    )


CHUNK = 8
EXTRA = 64 * 64
KEYS = 66 * 64


def dot_nt(left, right):
    return lax.dot_general(left, right, (((1,), (1,)), ((), ())), preferred_element_type=F32)


def dot_tn(left, right):
    return lax.dot_general(left, right, (((0,), (0,)), ((), ())), preferred_element_type=F32)


def attend_kernel(q_ref, s_ref, x_ref, place_ref, start_ref, kplace_ref, o_ref, lse_ref):
    q = q_ref[...]
    latest = place_ref[...]
    earliest = start_ref[...]
    o_ref[...] = jnp.zeros_like(o_ref)
    lse_ref[...] = jnp.zeros_like(lse_ref)

    def chunk(block, key_place):
        keys, values = slots_kv(block)
        scores = dot_nt(q, keys)
        allowed = (key_place <= latest) & (key_place >= earliest)
        weights = jnp.where(allowed, jnp.exp2(scores * (SCALE * LOG2E)), 0.0)
        lse_ref[...] += jnp.sum(weights, axis=1, keepdims=True)
        o_ref[...] += jnp.dot(weights.astype(BF16), values, preferred_element_type=F32)

    def step(number, unused):
        at = pl.multiple_of(number * CHUNK * 64, CHUNK * 64)
        chunk(s_ref[pl.ds(number * CHUNK, CHUNK)], kplace_ref[:, pl.ds(at, CHUNK * 64)])
        return unused

    lax.fori_loop(0, 64 // CHUNK, step, 0)
    chunk(x_ref[...], kplace_ref[:, EXTRA:KEYS])
    total = lse_ref[...]
    o_ref[...] = o_ref[...] / total
    lse_ref[...] = jnp.log2(total)


def attend(query, slots, extra, latest, earliest, key_place):
    rows = query.shape[0]
    return pl.pallas_call(
        attend_kernel,
        out_shape=[
            jax.ShapeDtypeStruct((rows, HEAD), F32),
            jax.ShapeDtypeStruct((rows, 1), F32),
        ],
        compiler_params=pltpu.CompilerParams(vmem_limit_bytes=60 * MIB),
    )(query, slots, extra, latest[:, None], earliest[:, None], key_place[None, :])


def attend_back_kernel(
    q_ref, go_ref, s_ref, x_ref, place_ref, start_ref, kplace_ref, lse_ref, dot_ref, gq_ref, gs_ref, gx_ref
):
    q = q_ref[...]
    grad_out = go_ref[...]
    latest = place_ref[...]
    earliest = start_ref[...]
    lse = lse_ref[...]
    row_dot = dot_ref[...]
    gq_ref[...] = jnp.zeros_like(gq_ref)

    def chunk(block, key_place):
        keys, values = slots_kv(block)
        scores = dot_nt(keys, q)
        allowed = (key_place <= latest) & (key_place >= earliest)
        probs = jnp.where(allowed, jnp.exp2(scores * (SCALE * LOG2E) - lse), 0.0)
        grad_probs = dot_nt(values, grad_out)
        grad_scores = (probs * (grad_probs - row_dot)).astype(BF16)
        grad_values = jnp.dot(probs.astype(BF16), grad_out, preferred_element_type=F32).astype(BF16)
        grad_keys = (jnp.dot(grad_scores, q, preferred_element_type=F32) * SCALE).astype(BF16)
        gq_ref[...] += dot_tn(grad_scores, keys) * SCALE
        shape = (block.shape[0], 64, 128)
        return [
            grad[:, at : at + 128].reshape(shape)
            for grad in (grad_keys, grad_values)
            for at in (0, 128)
        ]

    def step(number, unused):
        at = pl.multiple_of(number * CHUNK * 64, CHUNK * 64)
        slots = pl.ds(number * CHUNK, CHUNK)
        parts = chunk(s_ref[slots], kplace_ref[pl.ds(at, CHUNK * 64)])
        for quarter, part in enumerate(parts):
            gs_ref[slots, 64 * quarter : 64 * quarter + 64] = part
        return unused

    lax.fori_loop(0, 64 // CHUNK, step, 0)
    for quarter, part in enumerate(chunk(x_ref[...], kplace_ref[EXTRA:KEYS])):
        gx_ref[:, 64 * quarter : 64 * quarter + 64] = part


def attend_back(query, grad_out, slots, extra, latest, earliest, key_place, lse, row_dot):
    return pl.pallas_call(
        attend_back_kernel,
        out_shape=[
            jax.ShapeDtypeStruct(query.shape, F32),
            jax.ShapeDtypeStruct(slots.shape, BF16),
            jax.ShapeDtypeStruct(extra.shape, BF16),
        ],
        compiler_params=pltpu.CompilerParams(vmem_limit_bytes=60 * MIB),
    )(
        query,
        grad_out,
        slots,
        extra,
        latest[None, :],
        earliest[None, :],
        key_place[:, None],
        lse[None, :],
        row_dot[None, :],
    )


def add_all(refs_values):
    total = refs_values[0].astype(F32)
    for value in refs_values[1:]:
        total += value.astype(F32)
    return total


def by_rows(rows, size, body):
    def step(number, unused):
        body(pl.ds(pl.multiple_of(number * size, size), size))
        return unused

    lax.fori_loop(0, rows // size, step, 0)


def scatter_kernel(*refs):
    b_ref, gs_ref, gx_ref = refs[:3]
    grads = refs[3:8]
    kv_out = refs[8]
    outs = refs[9:14]
    halves = refs[14:19]
    sums = refs[19:24]
    landed = refs[24:29]
    rb, rsp, acc, r2, h, r1 = (refs[29 + 3 * i : 32 + 3 * i] for i in range(6))
    send, recv, local = refs[47:]
    links = Links(send, recv)
    core = lax.axis_index("dp")
    spot = place()
    me = lax.axis_index("ctx")
    greet()

    overs = []
    for number, (grad, half, total) in enumerate(zip(grads, halves, sums)):
        overs.append(links.across(grad.at[1 - core], lambda at, half=half: half))
        copy = pltpu.make_async_copy(grad.at[core], total, local.at[number])
        copy.start()

    thirds = []
    for part, (row, rows) in enumerate(KV_ROWS):
        last = ORDERS[part][2]
        wait = links.ring(
            last,
            lambda step, row=row, rows=rows, last=last: of_plane(
                gs_ref, last, shifted(spot[last], step), pl.ds(row, rows)
            ),
            lambda step, at, part=part: rb[part].at[step - 1],
        )
        wait_special = links.ring(
            last,
            lambda step, row=row, rows=rows: gx_ref.at[1, pl.ds(row, rows)],
            lambda step, at, part=part: rsp[part].at[step - 1],
        )
        thirds.append((wait, wait_special))

    weight_waits = []
    for number, (total, half, over, land) in enumerate(zip(sums, halves, overs, landed)):
        part, by_chip = WEIGHTS[number]
        last = ORDERS[part][2]
        pltpu.make_async_copy(grads[number].at[core], total, local.at[number]).wait()
        over()
        if by_chip:

            def add(at, total=total, half=half):
                for z in range(4):
                    index = (at // 4, at % 4, z)
                    total[index] = (total[index].astype(F32) + half[index].astype(F32)).astype(BF16)

            def step16(at, unused, add=add):
                add(at)
                return unused

            lax.fori_loop(0, 16, step16, 0)
        else:
            for at in range(4):

                def add(rows, at=at, total=total, half=half):
                    total[at, rows] = (
                        total[at, rows].astype(F32) + half[at, rows].astype(F32)
                    ).astype(BF16)

                by_rows(total.shape[1], 16, add)
        weight_waits.append(
            links.ring(
                last,
                lambda step, total=total, last=last, by_chip=by_chip: (
                    of_plane(total, last, shifted(spot[last], step))
                    if by_chip
                    else total.at[shifted(spot[last], step)]
                ),
                lambda step, at, land=land: land.at[step - 1],
            )
        )

    seconds = []
    for part, (row, rows) in enumerate(KV_ROWS):
        first, second, last = ORDERS[part]
        wait, wait_special = thirds[part]
        all_steps(wait)
        all_steps(wait_special)
        special = add_all(
            [gx_ref[1, row : row + rows]] + [rsp[part][step] for step in range(3)]
        ).astype(BF16)
        for at in range(4):
            acc[part][at, 8] = special

        def collect(at, i2, i1, part=part, row=row, rows=rows, last=last):
            chip = chip_of(at, last, 0)
            source = b_ref[chip]
            plane = [at[axis] for axis in (X, Y, Z) if axis != last]
            own = gs_ref[at[0], at[1], at[2], pl.ds(row, rows)].astype(F32)
            none = jnp.zeros_like(own)
            take_low = source <= b_ref[me]
            low = jnp.where(take_low, own, none)
            high = jnp.where(take_low, none, own)
            high += jnp.where(chip == me, gx_ref[0, pl.ds(row, rows)].astype(F32), none)
            for step in (1, 2, 3):
                sender = b_ref[chip_of(spot, last, -step)]
                came = rb[part][step - 1, plane[0], plane[1]].astype(F32)
                low += jnp.where(source < sender, came, none)
                high += jnp.where(source < sender, none, came)
            acc[part][i2, 2 * i1] = low.astype(BF16)
            acc[part][i2, 2 * i1 + 1] = high.astype(BF16)

        plane_loop(part, collect)
        seconds.append(
            links.ring(
                second,
                lambda step, part=part, second=second: acc[part].at[shifted(spot[second], step)],
                lambda step, at, part=part: r2[part].at[step - 1],
            )
        )
    firsts = []
    for part, (row, rows) in enumerate(KV_ROWS):
        first, second, last = ORDERS[part]
        all_steps(seconds[part])

        def pick(index, part=part, second=second):
            return add_all(
                [acc[part][spot[second], index]] + [r2[part][step, index] for step in range(3)]
            ).astype(BF16)

        special = pick(8)
        for at in range(4):
            h[part][at, 0] = pick(2 * at)
            h[part][at, 1] = pick(2 * at + 1)
            h[part][at, 2] = special
        firsts.append(
            links.ring(
                first,
                lambda step, part=part, first=first: h[part].at[shifted(spot[first], step)],
                lambda step, at, part=part: r1[part].at[step - 1],
            )
        )
    for number, (total, land, out) in enumerate(zip(sums, landed, outs)):
        part, by_chip = WEIGHTS[number]
        last = ORDERS[part][2]
        all_steps(weight_waits[number])
        if by_chip:

            def add(at, unused, total=total, land=land, out=out, last=last):
                i, j = at // 4, at % 4
                out[i, j] = add_all(
                    [total[i, j, spot[last]]] + [land[step, i, j] for step in range(3)]
                ).astype(BF16)
                return unused

            lax.fori_loop(0, 16, add, 0)
        else:

            def add(rows, total=total, land=land, out=out, last=last):
                out[rows] = add_all(
                    [total[spot[last], rows]] + [land[step, rows] for step in range(3)]
                ).astype(BF16)

            by_rows(out.shape[0], 16, add)
    for part, (row, rows) in enumerate(KV_ROWS):
        first = ORDERS[part][0]
        all_steps(firsts[part])
        for index in range(3):
            kv_out[index, row : row + rows] = add_all(
                [h[part][spot[first], index]] + [r1[part][step, index] for step in range(3)]
            )
    links.close()


def scatter(b_all, grad_slots, grad_extra, grads):
    outs = [((3, 256, 128), F32)]
    halves, landed = [], []
    for grad, (part, by_chip) in zip(grads, WEIGHTS):
        plane = grad.shape[3:] if by_chip else grad.shape[2:]
        if by_chip:
            plane = grad.shape[2:4] + grad.shape[4:]
        outs.append((plane, BF16))
        halves.append((grad.shape[1:], BF16))
        landed.append(((3,) + plane, BF16))
    scratch = halves + halves + landed
    for shape in ((3, 4, 4), (3,), (4, 9), (3, 9), (4, 3), (3, 3)):
        for _, rows in KV_ROWS:
            scratch.append((shape + (rows, 128), BF16))
    return link_call(
        scatter_kernel,
        3,
        80,
        outs,
        (b_all, grad_slots, grad_extra, *grads),
        [SMEM, VMEM, VMEM] + [ANY] * 5,
        [VMEM] * 6,
        scratch,
        local=5,
    )


def late_kernel(*refs):
    flats = refs[:3]
    kvg_ref = refs[3]
    outs = refs[4:7]
    kvg_out = refs[7]
    r2, h, r1 = (refs[8 + 3 * i : 11 + 3 * i] for i in range(3))
    half, k3, k2, k1 = refs[17:21]
    l3, l2, l1 = refs[21:24]
    send, recv = refs[24:]
    links = Links(send, recv)
    core = lax.axis_index("dp")
    spot = place()
    greet()
    over = links.across(kvg_ref.at[1 - core], lambda at: half)
    seconds = []
    for part in range(3):
        second = ORDERS[part][1]
        seconds.append(
            links.ring(
                second,
                lambda step, part=part, second=second: flats[part].at[shifted(spot[second], step)],
                lambda step, at, part=part: r2[part].at[step - 1],
            )
        )
    over()

    def add(at, unused):
        i, j = at // 4, at % 4
        for k in range(4):
            k3[i, j, k] = (
                kvg_ref[core, i, j, k].astype(F32) + half[i, j, k].astype(F32)
            ).astype(BF16)
        return unused

    lax.fori_loop(0, 16, add, 0)
    w3 = links.ring(
        X, lambda step: k3.at[shifted(spot[X], step)], lambda step, at: l3.at[step - 1]
    )
    firsts = []

    def weights(part):
        first, second, _ = ORDERS[part]
        all_steps(seconds[part])
        for at in range(4):
            h[part][at] = add_all(
                [flats[part][spot[second], at]] + [r2[part][step, at] for step in range(3)]
            ).astype(BF16)
        firsts.append(
            links.ring(
                first,
                lambda step, part=part, first=first: h[part].at[shifted(spot[first], step)],
                lambda step, at, part=part: r1[part].at[step - 1],
            )
        )

    weights(0)
    all_steps(w3)
    for i in range(4):
        for j in range(4):
            k2[i, j] = add_all([k3[spot[X], i, j]] + [l3[step, i, j] for step in range(3)]).astype(
                BF16
            )
    w2 = links.ring(
        Y, lambda step: k2.at[shifted(spot[Y], step)], lambda step, at: l2.at[step - 1]
    )
    weights(1)
    weights(2)
    all_steps(w2)
    for i in range(4):
        k1[i] = add_all([k2[spot[Y], i]] + [l2[step, i] for step in range(3)]).astype(BF16)
    w1 = links.ring(
        Z, lambda step: k1.at[shifted(spot[Z], step)], lambda step, at: l1.at[step - 1]
    )
    for part in range(3):
        first = ORDERS[part][0]
        all_steps(firsts[part])
        outs[part][...] = add_all(
            [h[part][spot[first]]] + [r1[part][step] for step in range(3)]
        )
    all_steps(w1)
    kvg_out[...] = add_all([k1[spot[Z]]] + [l1[step] for step in range(3)])
    links.close()


def late(flats, kvg):
    outs = [(flat.shape[2:], F32) for flat in flats] + [((32, 128), F32)]
    scratch = []
    for shape in ((3, 4), (4,), (3,)):
        for flat in flats:
            scratch.append((shape + flat.shape[2:], BF16))
    for shape in ((4, 4, 4), (4, 4, 4), (4, 4), (4,), (3, 4, 4), (3, 4), (3,)):
        scratch.append((shape + (32, 128), BF16))
    return link_call(
        late_kernel, 4, 40, outs, (*flats, kvg), [VMEM] * 4, [VMEM] * 4, scratch
    )


def rms_scale(values, weights):
    return values * lax.rsqrt(jnp.mean(values * values, axis=-1, keepdims=True) + EPSILON) * weights


def rope_turn(vectors, cos, sin):
    halfway = vectors.shape[-1] // 2
    if vectors.ndim == 3:
        cos, sin = cos[:, None, :], sin[:, None, :]
    turned = jnp.concatenate([-vectors[..., halfway:], vectors[..., :halfway]], axis=-1)
    return vectors * cos + turned * sin


def norm_back(values, weights, incoming):
    unused, pull = jax.vjp(rms_scale, values, weights)
    return pull(incoming)


def dot32(left, right):
    return jnp.dot(left, right, preferred_element_type=F32)


def pack_rows(rows, to):
    return jnp.concatenate([rows, jnp.zeros((to - rows.shape[0], 128), rows.dtype)], axis=0)


def on_device(
    tokens,
    doc_lengths,
    block_order,
    attn_norm,
    query_weight,
    key_weight,
    value_weight,
    query_gain,
    key_gain,
    output_weight,
    attn_post_norm,
    ffn_norm,
    gate_weight,
    up_weight,
    down_weight,
    ffn_post_norm,
    out_cot,
):
    me = lax.axis_index("ctx")
    flat = lambda weight: weight.reshape(-1, 128)
    gains = jnp.concatenate(
        [attn_norm, attn_post_norm, ffn_norm, ffn_post_norm, query_gain, key_gain]
    )
    gains = jnp.concatenate([gains, jnp.zeros((104,), BF16)])[None]
    kvg = pack_rows(
        jnp.concatenate([flat(jnp.concatenate([key_weight, value_weight], axis=1)), gains]), 32
    )
    part_a = pack_rows(jnp.concatenate([flat(gate_weight), flat(output_weight)]), 128)
    part_b = pack_rows(jnp.concatenate([flat(up_weight), flat(query_weight)]), 128)
    part_c = flat(down_weight)
    pa, pb, pc, u0, u1 = early(part_a, part_b, part_c, kvg)
    whole = jnp.concatenate([u0, jnp.transpose(u1, (0, 3, 1, 2, 4, 5))], axis=4)
    whole = whole.reshape(128, 32, 128)
    w_kv = whole[:, :20].reshape(640, 512)
    gains = whole[:, 20].astype(F32)
    gain_attn, gain_post_attn, gain_ffn, gain_post_ffn = (
        gains[:, 5 * i : 5 * i + 5].reshape(640) for i in range(4)
    )
    gain_query, gain_key = (gains[:, 20 + 2 * i : 22 + 2 * i].reshape(256) for i in range(2))

    pairs = block_order.reshape(64, 2)
    b_all = jnp.min(pairs, axis=1)
    b_me = lax.dynamic_index_in_dim(b_all, me, keepdims=False)
    flip = lax.dynamic_index_in_dim(pairs, me, keepdims=False)[0] != b_me

    def low_first(rows):
        return jnp.where(flip, jnp.concatenate([rows[64:], rows[:64]]), rows)

    ramp = jnp.arange(64, dtype=jnp.int32)
    my_place = jnp.concatenate([b_me * 64 + ramp, (127 - b_me) * 64 + ramp])
    lengths = doc_lengths[0]
    starts = jnp.cumsum(lengths) - lengths
    my_start = jnp.max(
        jnp.where(starts[None, :] <= my_place[:, None], starts[None, :], 0), axis=1
    )
    my_position = my_place - my_start
    slot_block = jnp.where(b_all <= b_me, b_all, 127 - b_all)
    slot_block = jnp.concatenate([slot_block, jnp.stack([127 - b_me, jnp.where(b_me == 63, 1000, 63)])])
    key_place = (slot_block[:, None] * 64 + ramp[None, :]).reshape(KEYS)

    frequency = ROPE_BASE ** (-2.0 * jnp.arange(128, dtype=F32) / 256)
    angles = my_position.astype(F32)[:, None] * frequency[None, :]
    angles = jnp.concatenate([angles, angles], axis=-1)
    cos, sin = jnp.cos(angles), jnp.sin(angles)

    def head_side(raw_values, gain_values):
        return rope_turn(rms_scale(raw_values, gain_values), cos, sin)

    inputs = low_first(tokens[0]).astype(F32)
    normed = rms_scale(inputs, gain_attn).astype(BF16)
    kv_raw = dot32(normed, w_kv)
    key_raw, value_raw = kv_raw[:, :HEAD], kv_raw[:, HEAD:]
    key_rot = head_side(key_raw, gain_key).astype(BF16)
    kv = jnp.concatenate([key_rot, value_raw.astype(BF16)], axis=1)
    kv = jnp.transpose(kv.reshape(2, 64, 4, 128), (0, 2, 1, 3)).reshape(2, 256, 128)
    kv3 = jnp.concatenate([kv, jnp.where(b_me == 63, kv[:1], jnp.zeros_like(kv[:1]))])

    pa = pa.reshape(16, 128, 128)
    pb = pb.reshape(16, 128, 128)
    planes = (
        pa[:, :80].reshape(80, 2048),
        pa[:, 80:120].reshape(128, 640),
        pb[:, :80].reshape(80, 2048),
        pb[:, 80:120].reshape(80, 1024),
        pc.reshape(4, 4, 16, 640),
    )
    slots, extra, w_gate, w_output, w_up, w_query, w_down = gather(b_all, kv3, planes)
    slots = slots.reshape(64, 256, 128)
    w_gate = w_gate.reshape(640, 2048)
    w_output = w_output.reshape(1024, 640)
    w_up = w_up.reshape(640, 2048)
    w_query = w_query.reshape(640, 1024)
    w_down = w_down.reshape(2048, 640)

    k = jnp.arange(640, dtype=jnp.int32)
    at_core, at_y, at_z, at_x, at_row = k // 320, (k // 80) % 4, (k // 20) % 4, (k // 5) % 4, k % 5
    turn = (((at_core * 4 + at_x) * 4 + at_y) * 4 + at_z) * 5 + at_row
    turning = (k[:, None] == turn[None, :]).astype(BF16)

    def turned(values):
        return dot32(values, turning).astype(BF16)

    def unturned(values):
        return dot_nt(values.astype(BF16), turning)

    normed_b = turned(normed)
    query_raw = dot32(normed_b, w_query).reshape(128, HEADS, HEAD)
    query_rot = head_side(query_raw, gain_query).astype(BF16)

    def to_rows(values):
        return jnp.transpose(values.reshape(2, 64, HEADS, HEAD), (0, 2, 1, 3)).reshape(512, HEAD)

    def from_rows(rows):
        return jnp.transpose(rows.reshape(2, HEADS, 64, HEAD), (0, 2, 1, 3)).reshape(
            128, HEADS, HEAD
        )

    def row_numbers(numbers):
        return jnp.broadcast_to(numbers.reshape(2, 1, 64), (2, HEADS, 64)).reshape(512)

    query_rows = to_rows(query_rot)
    latest, earliest = row_numbers(my_place), row_numbers(my_start)
    attn_rows, lse = attend(query_rows, slots, extra, latest, earliest, key_place)
    attn_low = from_rows(attn_rows).reshape(128, HEADS * HEAD).astype(BF16)
    proj_out = dot32(attn_low, w_output)
    middle = inputs + rms_scale(proj_out, gain_post_attn)
    ffn_in = rms_scale(middle, gain_ffn).astype(BF16)
    ffn_in_b = turned(ffn_in)
    gate = dot32(ffn_in, w_gate)
    upper = dot32(ffn_in_b, w_up)

    def geglu(gate_in, upper_in):
        return jax.nn.gelu(gate_in, approximate=True) * upper_in

    hidden = geglu(gate, upper).astype(BF16)
    ffn_out = dot32(hidden, w_down)
    block_out = (middle + rms_scale(ffn_out, gain_post_ffn)).astype(BF16)
    grad_out = low_first(out_cot[0]).astype(F32)
    grad_ffn_out, post_ffn_term = norm_back(ffn_out, gain_post_ffn, grad_out)
    ffn_out_low = grad_ffn_out.astype(BF16)
    down_term = dot_tn(hidden, ffn_out_low).astype(BF16)
    grad_hidden = dot_nt(ffn_out_low, w_down)
    unused, pull_geglu = jax.vjp(geglu, gate, upper)
    grad_gate, grad_upper = pull_geglu(grad_hidden)
    grad_gate = grad_gate.astype(BF16)
    grad_upper = grad_upper.astype(BF16)
    gate_term = dot_tn(ffn_in, grad_gate).astype(BF16)
    upper_term = dot_tn(ffn_in_b, grad_upper).astype(BF16)
    grad_ffn_in = dot_nt(grad_gate, w_gate) + unturned(dot_nt(grad_upper, w_up))
    grad_middle_norm, ffn_norm_term = norm_back(middle, gain_ffn, grad_ffn_in)
    grad_middle = grad_out + grad_middle_norm
    grad_proj, post_attn_term = norm_back(proj_out, gain_post_attn, grad_middle)
    proj_low = grad_proj.astype(BF16)
    out_term = dot_tn(attn_low, proj_low).astype(BF16)
    grad_attn = to_rows(dot_nt(proj_low, w_output).astype(BF16))
    row_dot = jnp.sum(grad_attn.astype(F32) * attn_rows, axis=1)

    grad_query_rows, grad_slots, grad_extra = attend_back(
        query_rows, grad_attn, slots, extra, latest, earliest, key_place, lse[:, 0], row_dot
    )
    unused, pull_query = jax.vjp(head_side, query_raw, gain_query)
    grad_query_raw, query_gain_term = pull_query(from_rows(grad_query_rows))
    query_low = grad_query_raw.reshape(128, HEADS * HEAD).astype(BF16)
    query_term = dot_tn(normed_b, query_low).astype(BF16)

    grads = (
        gate_term.reshape(2, 4, 80, 2048),
        out_term.reshape(2, 4, 128, 640),
        upper_term.reshape(2, 4, 80, 2048),
        query_term.reshape(2, 4, 80, 1024),
        down_term.reshape(2, 4, 4, 4, 16, 640),
    )
    kv_sum, *planes = scatter(b_all, grad_slots.reshape(4, 4, 4, 256, 128), grad_extra, grads)
    low_sum = kv_sum[0] + jnp.where(b_me == 63, kv_sum[2], jnp.zeros_like(kv_sum[2]))
    kv_grad = jnp.stack([low_sum, kv_sum[1]]).reshape(2, 4, 64, 128)
    kv_grad = jnp.transpose(kv_grad, (0, 2, 1, 3)).reshape(128, 512)
    unused, pull_key = jax.vjp(head_side, key_raw, gain_key)
    grad_key_raw, key_gain_term = pull_key(kv_grad[:, :HEAD])
    kv_low = jnp.concatenate([grad_key_raw, kv_grad[:, HEAD:]], axis=1).astype(BF16)
    kv_term = dot_tn(normed, kv_low).astype(BF16)
    grad_normed = unturned(dot_nt(query_low, w_query)) + dot_nt(kv_low, w_kv)
    grad_inputs, attn_norm_term = norm_back(inputs, gain_attn, grad_normed)
    tokens_grad = (grad_middle + grad_inputs).astype(BF16)

    terms = [
        term.reshape(128, -1)
        for term in (
            attn_norm_term,
            post_attn_term,
            ffn_norm_term,
            post_ffn_term,
            query_gain_term,
            key_gain_term,
        )
    ]
    terms = jnp.concatenate(terms + [jnp.zeros((128, 104), F32)], axis=1).astype(BF16)
    kvg_term = jnp.concatenate(
        [kv_term.reshape(128, 20, 128), terms[:, None], jnp.zeros((128, 11, 128), BF16)], axis=1
    ).reshape(2, 4, 4, 4, 32, 128)
    gate_sum, out_sum, up_sum, query_sum, down_sum = planes
    blank = jnp.zeros((16, 8, 128), BF16)
    flats = (
        jnp.concatenate(
            [gate_sum.reshape(16, 80, 128), out_sum.reshape(16, 40, 128), blank], axis=1
        ).reshape(4, 4, 128, 128),
        jnp.concatenate(
            [up_sum.reshape(16, 80, 128), query_sum.reshape(16, 40, 128), blank], axis=1
        ).reshape(4, 4, 128, 128),
        down_sum.reshape(4, 4, 80, 128),
    )
    fa, fb, fc, fk = late(flats, kvg_term)
    kv_final = fk[:20].reshape(5, 512)
    gain_sums = fk[20]
    fives = [gain_sums[5 * i : 5 * i + 5] for i in range(4)]
    return (
        low_first(block_out)[None],
        low_first(tokens_grad)[None],
        fives[0],
        fb[80:120].reshape(5, 1024),
        kv_final[:, :HEAD],
        kv_final[:, HEAD:],
        gain_sums[20:22],
        gain_sums[22:24],
        fa[80:120].reshape(8, 640),
        fives[1],
        fives[2],
        fa[:80].reshape(5, 2048),
        fb[:80].reshape(5, 2048),
        fc.reshape(16, 640),
        fives[3],
    )


def solution(mesh):
    rows = P(("dp", "ctx"), None)
    vector = P(("dp", "ctx"))
    stream = P("dp", "ctx", None)
    return jax.shard_map(
        on_device,
        mesh=mesh,
        in_specs=(
            stream,
            P("dp", None),
            P(),
            vector,
            rows,
            rows,
            rows,
            vector,
            vector,
            rows,
            vector,
            vector,
            rows,
            rows,
            rows,
            vector,
            stream,
        ),
        out_specs=(
            stream,
            stream,
            vector,
            rows,
            rows,
            rows,
            vector,
            vector,
            rows,
            vector,
            vector,
            rows,
            rows,
            rows,
            vector,
        ),
        check_vma=False,
    )
```

```python
from types import SimpleNamespace

import jax
import jax.numpy as jnp
import numpy as np
from jax import lax
from jax.experimental import pallas as pl
from jax.experimental.pallas import tpu as pltpu
from jax.sharding import PartitionSpec as P

EPSILON = 1e-06
ROPE_BASE = 1000000.0
MESH = pl.DeviceIdType.MESH
F32 = jnp.float32
BF16 = jnp.bfloat16
MIB = 2**20

X, Y, Z = 0, 1, 2
ORDERS = ((Z, Y, X), (X, Z, Y), (Y, X, Z))
UNITS = (
    ((0, 0), (0, 1), (0, 2), (0, 3), (3, 0))
    + ((1, 0), (1, 1), (1, 2), (1, 3), (3, 1))
    + ((2, 0), (2, 1), (2, 2), (2, 3), (3, 2), (3, 3))
)
KV_ROWS = ((0, 80), (80, 80), (160, 96))
HEADS = 4
HEAD = 256
SCALE = HEAD**-0.5
LOG2E = 1.4426950408889634


def place():
    chip = lax.axis_index("ctx")
    return (chip // 16, (chip // 4) % 4, chip % 4)


def shifted(value, step):
    return lax.rem(value + step + 4, 4)


def peer(axis, step):
    spot = list(place())
    spot[axis] = shifted(spot[axis], step)
    return (lax.axis_index("dp"), spot[0] * 16 + spot[1] * 4 + spot[2])


def other_core():
    return (1 - lax.axis_index("dp"), lax.axis_index("ctx"))


def greet():
    barrier = pltpu.get_barrier_semaphore()
    for axis in (X, Y, Z):
        for step in (1, 2, 3):
            pl.semaphore_signal(barrier, inc=1, device_id=peer(axis, step), device_id_type=MESH)
    pl.semaphore_signal(barrier, inc=1, device_id=other_core(), device_id_type=MESH)


def greeted():
    pl.semaphore_wait(pltpu.get_barrier_semaphore(), 10)


class Ring:
    def __init__(self, links, axis, source, landing):
        self.links, self.axis, self.source, self.landing = links, axis, source, landing
        self.numbers = [links.number() for _ in range(3)]

    def copy(self, step, sender):
        return self.links.copy(
            self.numbers[step - 1],
            self.source(step),
            self.landing(step, sender),
            peer(self.axis, step),
        )

    def start(self, step):
        self.links.start(self.copy(step, place()[self.axis]))

    def wait(self, step):
        self.copy(step, shifted(place()[self.axis], -step)).wait_recv()

    def wait_all(self):
        for step in (1, 2, 3):
            self.wait(step)

    def sent(self):
        for step in (1, 2, 3):
            self.links.sent(self.numbers[step - 1])


class Across:
    def __init__(self, links, source, landing):
        mine = lax.axis_index("dp")
        self.links, self.number = links, links.number()
        links.start(links.copy(self.number, source, landing(mine), other_core()))
        self.came = links.copy(self.number, source, landing(1 - mine), other_core())

    def wait(self):
        self.came.wait_recv()

    def sent(self):
        self.links.sent(self.number)


class Links:
    def __init__(self, send, recv):
        self.send, self.recv, self.used, self.open = send, recv, 0, {}

    def number(self):
        self.used += 1
        return self.used - 1

    def copy(self, number, source, landing, device):
        copy = pltpu.make_async_remote_copy(
            src_ref=source,
            dst_ref=landing,
            send_sem=self.send.at[number],
            recv_sem=self.recv.at[number],
            device_id=device,
            device_id_type=MESH,
        )
        self.latest = (number, copy)
        return copy

    def start(self, copy):
        copy.start()
        self.open[self.latest[0]] = copy

    def sent(self, number):
        self.open.pop(number).wait_send()

    def ring(self, axis, source, landing, begin=True):
        ring = Ring(self, axis, source, landing)
        if begin:
            for step in (1, 2, 3):
                ring.start(step)
        return ring

    def across(self, source, landing):
        return Across(self, source, landing)

    def close(self):
        for number in tuple(self.open):
            self.sent(number)


VMEM = pl.BlockSpec(memory_space=pltpu.VMEM)
SMEM = pl.BlockSpec(memory_space=pltpu.SMEM)


def hold(kind, *shape):
    return pltpu.VMEM(shape, kind)


def run(stage, numbers, ins, outs, scratch, number=None, copies=0):
    flat, shape = jax.tree.flatten(scratch, is_leaf=lambda leaf: not isinstance(leaf, (dict, list)))

    def kernel(*refs):
        count = len(numbers) + len(ins) + len(outs)
        named = dict(zip((*numbers, *ins, *outs), refs))
        named.update(jax.tree.unflatten(shape, refs[count : count + len(flat)]))
        r = SimpleNamespace(**named)
        if copies:
            r.links = Links(*refs[count + len(flat) :])
        stage(r)

    remote = dict(collective_id=number, has_side_effects=True) if copies else {}
    results = pl.pallas_call(
        kernel,
        out_shape=[jax.ShapeDtypeStruct(out.shape, out.dtype) for out in outs.values()],
        in_specs=[SMEM] * len(numbers) + [VMEM] * len(ins),
        out_specs=[VMEM] * len(outs),
        scratch_shapes=flat + [pltpu.SemaphoreType.DMA((copies,))] * (2 if copies else 0),
        compiler_params=pltpu.CompilerParams(vmem_limit_bytes=60 * MIB, **remote),
    )(*numbers.values(), *ins.values())
    return dict(zip(outs, results))


def dot32(left, right):
    return jnp.dot(left, right, preferred_element_type=F32)


def dot_nt(left, right):
    return lax.dot_general(left, right, (((1,), (1,)), ((), ())), preferred_element_type=F32)


def dot_tn(left, right):
    return lax.dot_general(left, right, (((0,), (0,)), ((), ())), preferred_element_type=F32)


def add_all(values):
    total = values[0].astype(F32)
    for value in values[1:]:
        total += value.astype(F32)
    return total


def loop(count, body):
    def step(number, unused):
        body(number)
        return unused

    lax.fori_loop(0, count, step, 0)


def my_low(r):
    chip = lax.axis_index("ctx")
    return jnp.minimum(r.block_order[2 * chip], r.block_order[2 * chip + 1])


def low_of(r, chip):
    return jnp.minimum(r.block_order[2 * chip], r.block_order[2 * chip + 1])


def low_first(r, rows):
    chip = lax.axis_index("ctx")
    flip = r.block_order[2 * chip] > r.block_order[2 * chip + 1]
    return jnp.where(flip, jnp.concatenate([rows[64:], rows[:64]], axis=0), rows)


def document_starts(r, places):
    start = jnp.zeros_like(places)
    at = 0
    for number in range(1, 8):
        at = at + r.doc_lengths[0, number - 1]
        start = jnp.where(places >= at, at, start)
    return start


def places_of(r, within, high):
    low = my_low(r)
    return jnp.where(high, 127 - low, low) * 64 + within


def number_table():
    table = np.zeros((8, 768), np.int32)
    k = np.arange(640)
    table[0, :640], table[1, :640] = k % 5, k // 5
    core, y, z, x, row = k // 320, (k // 80) % 4, (k // 20) % 4, (k // 5) % 4, k % 5
    table[2, :640] = (((core * 4 + x) * 4 + y) * 4 + z) * 5 + row
    k = np.arange(768)
    table[3] = np.where(k % 6 < 5, 5 * (k // 6) + k % 6, -1)
    table[4, :256], table[5, :256] = np.arange(256) % 2, np.arange(256) // 2
    return table


def one_hot(rows, numbers):
    shape = (rows, numbers.shape[1])
    return jnp.where(lax.broadcasted_iota(jnp.int32, shape, 0) == numbers, 1.0, 0.0).astype(BF16)


GAINS = ((0, 640, 5, 0), (640, 640, 5, 5), (1280, 640, 5, 10), (1920, 640, 5, 15))
GAINS += ((2560, 256, 2, 20), (2816, 256, 2, 22))
G_ATTN, G_POST_ATTN, G_FFN, G_POST_FFN, G_QUERY, G_KEY = range(6)


def gain_maps(r, number):
    _, columns, held, lane = GAINS[number]
    row = 0 if held == 5 else 4
    rest, owner = r.table[row : row + 1, :columns], r.table[row + 1 : row + 2, :columns]
    lanes = one_hot(128, rest + lane)
    owners = lax.broadcasted_iota(jnp.int32, (128, columns), 0) == owner
    return lanes, owners


def gain(r, number):
    at, columns, _, _ = GAINS[number]
    return r.gains[0:1, at : at + columns]


def rows_of(r, base, weight, count):
    tiles = weight.shape[1] // 128
    for tile in range(tiles):
        r.stage[pl.ds(base + tile, count, stride=tiles)] = weight[
            :, 128 * tile : 128 * tile + 128
        ].astype(F32)


def columns_of(r, base, count, tiles, tile):
    return r.stage[pl.ds(base + tile, count, stride=tiles)]


def pack(r):
    rows_of(r, 0, r.gate_weight, 5)
    rows_of(r, 80, r.output_weight, 8)
    rows_of(r, 128, r.up_weight, 5)
    rows_of(r, 208, r.query_weight, 5)
    rows_of(r, 256, r.down_weight, 16)
    for tile in range(4):
        weight = (r.key_weight, r.value_weight)[tile // 2]
        half = 128 * (tile % 2)
        r.stage[pl.ds(336 + tile, 5, stride=4)] = weight[:, half : half + 128].astype(F32)
    r.stage[356:357] = r.gain_row[...].astype(F32)
    spot = place()
    for part, ref in enumerate(r.p):
        first, second, _ = ORDERS[part]
        rows = ref.shape[2]
        ref[spot[second], spot[first]] = r.stage[128 * part : 128 * part + rows].astype(BF16)
    core = lax.axis_index("dp")
    x, y, z = spot
    r.u[0][core, x, y, z] = r.stage[336:352].astype(BF16)
    r.u[1][core, y, z, x] = r.stage[352:368].astype(BF16)


def tables(r):
    r.x[...] = low_first(r, r.tokens[0].astype(F32))
    rows = lax.broadcasted_iota(jnp.int32, (128, 1), 0)
    places = places_of(r, rows % 64, rows >= 64)
    position = (places - document_starts(r, places)).astype(F32)
    angles = position * r.frequency[...]
    r.cos[...] = jnp.cos(angles)
    r.sin[...] = jnp.sin(angles)
    r.turning[...] = one_hot(640, r.table[2:3, :640])
    r.sixes[...] = one_hot(640, r.table[3:4, :])


NEVER = -(1 << 20)


def key_tables(r):
    mine = my_low(r)

    def chunk(number, token):
        plane = number % 4
        row = 4 * token + number
        for slot in range(16):
            spot = [slot // 4, slot % 4]
            spot.insert(chunk_axis(token), plane)
            low = low_of(r, spot[0] * 16 + spot[1] * 4 + spot[2])
            chosen = jnp.where(low < mine, low, 127 - low) * 64
            for_low = jnp.where(low < mine, chosen, NEVER)
            for_high = jnp.where(low == mine, NEVER, chosen)
            r.key_base[row, slot : slot + 1] = jnp.full((1, 128), for_low, jnp.int32)
            r.key_base[16 + row, slot : slot + 1] = jnp.full((1, 128), for_high, jnp.int32)

    for token in range(4):
        loop(4, lambda number, token=token: chunk(number, token))

    def turn(row):
        r.key_rows[pl.ds(row, 1)] = jnp.transpose(key_column(r, row, (row // 4) % 4))[0:1]

    loop(32, turn)


def key_column(r, row, token):
    base = jnp.broadcast_to(r.key_base[row][:, None, :], (16, 16, 128)).reshape(256, 128)
    return base + (lax.broadcasted_iota(jnp.int32, (256, 128), 0) % 16 + 16 * token)


def early(r):
    links = r.links
    core = lax.axis_index("dp")
    spot = place()
    x, y, z = spot

    def small(axis, unit, index_of):
        ref = r.u[unit]
        ring = links.ring(
            axis, lambda step: ref.at[index_of(spot[axis])], lambda step, at: ref.at[index_of(at)]
        )
        held.append(ring)
        return ring

    held = []

    one = small(Z, 0, lambda at: (core, x, y, at))
    two = small(X, 1, lambda at: (core, y, z, at))
    rings = []
    for part, ref in enumerate(r.p):
        first, second, _ = ORDERS[part]
        row = spot[second]
        rings.append(
            links.ring(
                first,
                lambda step, ref=ref, row=row, first=first: ref.at[row, spot[first]],
                lambda step, at, ref=ref, row=row: ref.at[row, at],
            )
        )
    tables(r)
    one.wait_all()
    one = small(Y, 0, lambda at: (core, x, at))
    two.wait_all()
    two = small(Z, 1, lambda at: (core, y, at))
    for part, ref in enumerate(r.p):
        rings[part].wait_all()
        second = ORDERS[part][1]
        rings.append(
            links.ring(
                second,
                lambda step, ref=ref, second=second: ref.at[spot[second]],
                lambda step, at, ref=ref: ref.at[at],
            )
        )
    key_tables(r)
    one.wait_all()
    one = small(X, 0, lambda at: (core, at))
    two.wait_all()
    two = small(Y, 1, lambda at: (core, at))
    spreads = {}
    for part, weights in ((2, (DOWN,)), (0, (GATE, OUTPUT)), (1, (QUERY, UP))):
        rings[3 + part].wait_all()
        for number in weights:
            unpack(r, number)
            if number not in (GATE, UP):
                spreads[number] = Spread(r, number)
    one.wait_all()
    three = links.across(r.u[0].at[core], lambda at: r.u[0].at[at])
    two.wait_all()
    four = links.across(r.u[1].at[core], lambda at: r.u[1].at[at])
    three.wait()
    four.wait()
    return rings, held + [three, four], spreads


def device_loop(body):
    def one(number):
        core, x, y, z = number // 64, (number // 16) % 4, (number // 4) % 4, number % 4
        body(pl.multiple_of(number * 24, 8), (core, x, y, z), (core, y, z, x))

    loop(128, one)


def unpack_small(r):
    def one(row, i0, i1):
        r.stage[pl.ds(row, 16)] = r.u[0][i0].astype(F32)
        r.stage[pl.ds(row + 16, 8)] = r.u[1][i1].astype(F32)[:8]

    device_loop(one)
    for tile in range(4):
        r.w_kv[:, 128 * tile : 128 * tile + 128] = columns_of(r, 0, 768, 4, tile).astype(BF16)
    held = r.stage[pl.ds(20, 128, stride=24)].astype(BF16)
    for number, (at, columns, _, _) in enumerate(GAINS):
        lanes, owners = gain_maps(r, number)
        spread = jnp.where(owners, dot32(held, lanes), 0.0)
        r.gains[0:1, at : at + columns] = jnp.sum(spread, axis=0, keepdims=True)


WEIGHTS = ((0, 0, 80, False), (0, 80, 40, False), (1, 0, 80, False), (1, 80, 40, False), (2, 0, 80, True))
GATE, OUTPUT, UP, QUERY, DOWN = range(5)


def own_plane(r, number):
    part = WEIGHTS[number][0]
    return weight_plane(r.w[number], number, lax.axis_index("dp"), place()[ORDERS[part][2]])


def weight_plane(ref, number, core, at):
    part, _, _, by_chip = WEIGHTS[number]
    if by_chip:
        return of_plane(ref.at[core], ORDERS[part][2], at)
    return ref.at[core, at]


def plane_tiles(number):
    return ((80, 16), (128, 5), (80, 16), (80, 8), (256, 5))[number]


def unpack(r, number):
    part, first, rows, by_chip = WEIGHTS[number]
    count, tiles = plane_tiles(number)
    plane = own_plane(r, number)

    def one(chip):
        r.stage[pl.ds(pl.multiple_of(chip * rows, 8), rows)] = r.p[part][
            chip // 4, chip % 4, first : first + rows
        ].astype(F32)

    loop(16, one)
    for tile in range(tiles):
        piece = columns_of(r, 0, count, tiles, tile).astype(BF16)
        lanes = slice(128 * tile, 128 * tile + 128)
        if by_chip:
            plane[:, :, :, lanes] = piece.reshape(4, 4, 16, 128)
        else:
            plane[:, lanes] = piece


def inverse_rms(values):
    return lax.rsqrt(jnp.mean(values * values, axis=-1, keepdims=True) + EPSILON)


def rms_scale(values, weights):
    return values * inverse_rms(values) * weights


def norm_back(values, weights, incoming):
    inverse = inverse_rms(values)
    normal = values * inverse
    scaled = incoming * weights
    back = (scaled - normal * jnp.mean(scaled * normal, axis=-1, keepdims=True)) * inverse
    return back, jnp.sum(incoming * normal, axis=0, keepdims=True)


def rope(r, u):
    cos, sin = r.cos[...], r.sin[...]
    one, two = u[:, :128], u[:, 128:]
    return jnp.concatenate([one * cos - two * sin, two * cos + one * sin], axis=1)


def rope_back(r, e):
    cos, sin = r.cos[...], r.sin[...]
    one, two = e[:, :128], e[:, 128:]
    return jnp.concatenate([one * cos + two * sin, two * cos - one * sin], axis=1)


def turned(r, values):
    return dot32(values, r.turning[...]).astype(BF16)


def unturned(r, values):
    return dot_nt(values.astype(BF16), r.turning[...])


def keys_values(r):
    x = r.x[...]
    normed = rms_scale(x, gain(r, G_ATTN)).astype(BF16)
    r.normed[...] = normed
    r.normed_six[...] = dot32(normed, r.sixes[...]).astype(BF16)
    raw = dot32(r.normed_six[...], r.w_kv[...])
    r.key_raw[...] = raw[:, :HEAD]
    keys = rope(r, rms_scale(raw[:, :HEAD], gain(r, G_KEY)))
    both = jnp.concatenate([keys, raw[:, HEAD:]], axis=1).astype(BF16)
    for block in range(2):
        for unit, (token, lane) in enumerate(UNITS):
            row = 64 * block + 16 * token
            r.kv3[block, 16 * unit : 16 * unit + 16] = both[
                row : row + 16, 128 * lane : 128 * lane + 128
            ]
    own = r.kv3[0]
    r.kv3[2] = jnp.where(my_low(r) == 63, own, jnp.zeros_like(own))


def of_plane(ref, axis, at, *rest):
    index = [slice(None)] * 3
    index[axis] = at
    return ref.at[(*index, *rest)]


def chip_of(spot, axis, step):
    spot = list(spot)
    spot[axis] = shifted(spot[axis], step)
    return spot[0] * 16 + spot[1] * 4 + spot[2]


def plane_loop(part, body):
    first, second, last = ORDERS[part]

    def one(number):
        spot = [None] * 3
        spot[first], spot[second], spot[last] = number % 4, number // 4, place()[last]
        body(spot, number // 4, number % 4)

    loop(16, one)


class Spread:
    def __init__(self, r, number):
        self.links, self.axis = r.links, ORDERS[WEIGHTS[number][0]][2]
        self.at = lambda core, at: weight_plane(r.w[number], number, core, at)
        self.core, self.mine = lax.axis_index("dp"), place()[self.axis]
        self.ring = r.links.ring(
            self.axis,
            lambda step: self.at(self.core, self.mine),
            lambda step, at: self.at(self.core, at),
        )
        self.overs = []
        self.over(self.mine)

    def over(self, at):
        self.overs.append(
            self.links.across(self.at(self.core, at), lambda core: self.at(core, at))
        )

    def pass_on(self):
        for step in (1, 3, 2):
            self.ring.wait(step)
            self.over(shifted(self.mine, -step))

    def finish(self):
        for over in self.overs:
            over.wait()

    def free(self):
        self.ring.sent()
        for over in self.overs:
            over.sent()


def gather_first(r):
    rings = []
    for part, (row, rows) in enumerate(KV_ROWS):
        own = r.kv3.at[:, pl.ds(row, rows)]
        rings.append(
            r.links.ring(
                ORDERS[part][0],
                lambda step, own=own: own,
                lambda step, at, ref=r.f1[part]: ref.at[at],
            )
        )
    return rings


def gather_second(r, firsts):
    spot = place()
    rings = []
    for part, (row, rows) in enumerate(KV_ROWS):
        first, second, _ = ORDERS[part]
        f1, g2, mine = r.f1[part], r.g2[part], spot[second]
        f1[spot[first]] = r.kv3[:, row : row + rows]
        firsts[part].wait_all()
        for at in range(4):
            g2[mine, 2 * at] = f1[at, 0]
            g2[mine, 2 * at + 1] = f1[at, 1]
        g2[mine, 8] = add_all([f1[at, 2] for at in range(4)]).astype(BF16)
        rings.append(
            r.links.ring(
                second,
                lambda step, g2=g2, mine=mine: g2.at[mine],
                lambda step, at, g2=g2: g2.at[at],
            )
        )
    return rings


def gather_third(r, seconds):
    spot = place()
    low_me = my_low(r)
    rings, specials = [], []
    for part, (row, rows) in enumerate(KV_ROWS):
        first, second, last = ORDERS[part]
        g2, sel, sp, rsp = r.g2[part], r.sel[part], r.sp[part], r.rsp[part]
        seconds[part].wait_all()
        targets = [low_of(r, chip_of(spot, last, step)) for step in (1, 2, 3)]

        def choose(at, i2, i1, g2=g2, sel=sel, row=row, rows=rows, last=last, targets=targets):
            low = g2[i2, 2 * i1]
            high = g2[i2, 2 * i1 + 1]
            source = low_of(r, chip_of(at, last, 0))
            plane = [at[axis] for axis in (X, Y, Z) if axis != last]
            r.slots[at[0], at[1], at[2], pl.ds(row, rows)] = jnp.where(source < low_me, low, high)
            for step in (1, 2, 3):
                sel[step - 1, plane[0], plane[1]] = jnp.where(
                    source < targets[step - 1], low, high
                )

        plane_loop(part, choose)
        sp[...] = add_all([g2[at, 8] for at in range(4)]).astype(BF16)
        rings.append(
            r.links.ring(
                last,
                lambda step, sel=sel: sel.at[step - 1],
                lambda step, at, row=row, rows=rows, last=last: of_plane(
                    r.slots, last, at, pl.ds(row, rows)
                ),
            )
        )
        specials.append(
            r.links.ring(
                last, lambda step, sp=sp: sp, lambda step, at, rsp=rsp: rsp.at[at]
            )
        )
    r.extra[0:2] = r.kv3[0:2]
    return rings, specials


def gather_special(r, specials):
    spot = place()
    for part, (row, rows) in enumerate(KV_ROWS):
        rsp = r.rsp[part]
        specials[part].wait_all()
        rsp[spot[ORDERS[part][2]]] = r.sp[part][...]
        r.extra[2, row : row + rows] = add_all([rsp[at] for at in range(4)]).astype(BF16)


QUARTER = 1.0 / 16
POWER = QUARTER * 1.4426950408889634


def chunk_axis(token):
    return ORDERS[token][2] if token < 3 else X


def chunk_index(token, plane):
    index = [slice(None)] * 3
    index[chunk_axis(token)] = plane
    return tuple(index)


def unit_rows(token, lane):
    return pl.ds(16 * UNITS.index((token, lane)), 16)


def chunk_kv(r, token, plane):
    index = chunk_index(token, plane)
    quarters = [
        r.slots[(*index, unit_rows(token, lane))].reshape(256, 128) for lane in range(4)
    ]
    return jnp.concatenate(quarters[:2], axis=1), jnp.concatenate(quarters[2:], axis=1)


def extra_kv(r):
    quarters = [
        jnp.concatenate(
            [r.extra[block, unit_rows(token, lane)] for block in range(3) for token in range(4)],
            axis=0,
        )
        for lane in range(4)
    ]
    return jnp.concatenate(quarters[:2], axis=1), jnp.concatenate(quarters[2:], axis=1)


def extra_places(r, numbers):
    low = my_low(r)
    block = jnp.where(numbers < 64, low, jnp.where(numbers < 128, 127 - low, 63))
    gone = (numbers >= 128) & (low == 63)
    return jnp.where(gone, 1 << 20, block * 64 + numbers % 64)


def query_places(r, numbers):
    return places_of(r, numbers % 64, numbers >= 256)


def attention(r, thirds, specials, between):
    spot = place()
    numbers = lax.broadcasted_iota(jnp.int32, (512, 1), 0)
    latest = query_places(r, numbers)
    earliest = document_starts(r, latest)
    query = r.query[...]
    r.attn[...] = jnp.zeros_like(r.attn)
    r.total[...] = jnp.zeros_like(r.total)

    def add(weights, values):
        total = weights[:, :128]
        if weights.shape[1] == 256:
            total = total + weights[:, 128:]
            r.total[...] += total
        else:
            r.total[...] += total
            r.total[:, :64] += weights[:, 128:]
        r.attn[...] += dot32(weights.astype(BF16), values)

    def chunk(token, plane):
        keys, values = chunk_kv(r, token, plane)
        scores = dot_nt(query, keys)
        row = 4 * token + plane
        allowed = jnp.concatenate(
            [
                r.key_rows[pl.ds(row, 1)] >= earliest[:256],
                r.key_rows[pl.ds(16 + row, 1)] >= earliest[256:],
            ],
            axis=0,
        )
        add(jnp.where(allowed, jnp.exp2(scores * POWER), 0.0), values)

    for token in range(3):
        chunk(token, spot[chunk_axis(token)])
    between(0)
    for number, step in enumerate((1, 3, 2)):
        for token in range(3):
            thirds[token].wait(step)
            chunk(token, shifted(spot[chunk_axis(token)], -step))
        between(number + 1)
    for plane in range(4):
        chunk(3, plane)
    gather_special(r, specials)
    keys, values = extra_kv(r)
    scores = dot_nt(query, keys)
    places = extra_places(r, lax.broadcasted_iota(jnp.int32, (1, 192), 1))
    allowed = (places >= earliest) & (places <= latest)
    add(jnp.where(allowed, jnp.exp2(scores * POWER), 0.0), values)
    total = jnp.sum(r.total[...], axis=1, keepdims=True)
    r.attn[...] = r.attn[...] / total
    r.total[...] = jnp.broadcast_to(jnp.log2(total), (512, 128))


def attention_back(r, between):
    spot = place()
    numbers = lax.broadcasted_iota(jnp.int32, (1, 512), 1)
    latest = query_places(r, numbers)
    earliest = document_starts(r, latest)
    query, grad_out = r.query[...], r.grad_attn[...]
    log_total = jnp.transpose(r.total[...])[0:1]
    row_dot = jnp.transpose(r.dots[...])[0:1]
    r.grad_query[...] = jnp.zeros_like(r.grad_query)

    def grads_of(keys, values, allowed):
        scores = dot_nt(keys, query)
        probs = jnp.where(allowed, jnp.exp2(scores * POWER - log_total), 0.0)
        grad_probs = dot_nt(values, grad_out)
        grad_scores = (probs * (grad_probs - row_dot)).astype(BF16)
        grad_values = dot32(probs.astype(BF16), grad_out)
        grad_keys = dot32(grad_scores, query) * QUARTER
        r.grad_query[...] += dot_tn(grad_scores, keys)
        return jnp.concatenate([grad_keys, grad_values], axis=1).astype(BF16)

    def chunk(token, plane):
        keys, values = chunk_kv(r, token, plane)
        row = 4 * token + plane
        low, high = key_column(r, row, token), key_column(r, 16 + row, token)
        allowed = jnp.concatenate([low, low, high, high], axis=1) >= earliest
        grads = grads_of(keys, values, allowed)
        index = chunk_index(token, plane)
        for lane in range(4):
            r.slots[(*index, unit_rows(token, lane))] = grads[
                :, 128 * lane : 128 * lane + 128
            ].reshape(4, 4, 16, 128)

    for plane in range(4):
        chunk(3, plane)
    between(0)
    rings, specials = scatter_third(r)
    for number, step in enumerate((1, 3, 2)):
        for token in range(3):
            chunk(token, shifted(spot[chunk_axis(token)], step))
            rings[token].start(step)
        between(number + 1)
    keys, values = extra_kv(r)
    places = extra_places(r, lax.broadcasted_iota(jnp.int32, (192, 1), 0))
    grads = grads_of(keys, values, (places >= earliest) & (places <= latest))
    for block in range(3):
        for unit, (token, lane) in enumerate(UNITS):
            row = 64 * block + 16 * token
            r.grad_extra[block, 16 * unit : 16 * unit + 16] = grads[
                row : row + 16, 128 * lane : 128 * lane + 128
            ]
    for ring in specials:
        for step in (1, 2, 3):
            ring.start(step)
    for token in range(3):
        chunk(token, spot[chunk_axis(token)])
    return rings, specials


GELU = 0.7978845608028654


def head_rows(block, head):
    start = 256 * block + 64 * head
    return slice(start, start + 64)


def queries(r):
    r.normed_b[...] = turned(r, r.normed[...])
    r.query_raw[...] = dot32(r.normed_b[...], r.w[QUERY][...].reshape(640, 1024))
    for head in range(HEADS):
        raw = r.query_raw[:, HEAD * head : HEAD * head + HEAD]
        rotated = rope(r, rms_scale(raw, gain(r, G_QUERY))).astype(BF16)
        for block in range(2):
            r.query[head_rows(block, head)] = rotated[64 * block : 64 * block + 64]


def gelu_parts(gate):
    inner = jnp.tanh(GELU * (gate + 0.044715 * gate * gate * gate))
    return 0.5 * gate * (1.0 + inner), inner


def columns(weight, at, width):
    rows = 8 * weight.shape[2]
    return weight[:, :, :, at : at + width].reshape(rows, width)


def down_rows(ref, number):
    return ref.at[number // 2, pl.ds(2 * (number % 2), 2)]


def feed_forward(r, spreads):
    spreads[OUTPUT].finish()
    for block in range(2):
        for head in range(HEADS):
            r.attn_low[64 * block : 64 * block + 64, HEAD * head : HEAD * head + HEAD] = r.attn[
                head_rows(block, head)
            ].astype(BF16)
    r.proj[...] = dot32(r.attn_low[...], r.w[OUTPUT][...].reshape(1024, 640))
    r.mid[...] = r.x[...] + rms_scale(r.proj[...], gain(r, G_POST_ATTN))
    r.ffn_in[...] = rms_scale(r.mid[...], gain(r, G_FFN)).astype(BF16)
    r.ffn_in_b[...] = turned(r, r.ffn_in[...])
    spreads[GATE].finish()
    spreads[UP].finish()
    for number in range(4):
        at = slice(512 * number, 512 * number + 512)
        gate = dot32(r.ffn_in[...], columns(r.w[GATE], 512 * number, 512))
        up = dot32(r.ffn_in_b[...], columns(r.w[UP], 512 * number, 512))
        r.gate[:, at] = gate
        r.up[:, at] = up
        r.hidden[:, at] = (gelu_parts(gate)[0] * up).astype(BF16)
    spreads[DOWN].finish()
    r.ffn_out[...] = dot32(r.hidden[...], r.w[DOWN][...].reshape(2048, 640))
    out = r.mid[...] + rms_scale(r.ffn_out[...], gain(r, G_POST_FFN))
    r.block_out[...] = low_first(r, out.astype(BF16))


def note_gain(r, number, term):
    at, count, _, _ = GAINS[number]
    r.gain_sums[0:1, at : at + count] = term


def feed_forward_back(r, spreads):
    for number in (GATE, OUTPUT, UP, DOWN):
        spreads[number].free()
    grad_out = low_first(r, r.out_cot[0].astype(F32))
    grad_ffn_out, term = norm_back(r.ffn_out[...], gain(r, G_POST_FFN), grad_out)
    note_gain(r, G_POST_FFN, term)
    low_grad = grad_ffn_out.astype(BF16)
    r.low_grad[...] = low_grad
    grad_in = jnp.zeros((128, 640), F32)
    grad_in_b = jnp.zeros((128, 640), F32)
    for number in range(4):
        at = slice(512 * number, 512 * number + 512)
        down = down_rows(r.w[DOWN], number)
        grad_hidden = dot_nt(low_grad, down[...].reshape(512, 640))
        down[...] = (
            dot_tn(r.hidden[:, at], low_grad).astype(BF16).reshape(2, 4, 4, 16, 640)
        )
        gate, up = r.gate[:, at], r.up[:, at]
        activated, inner = gelu_parts(gate)
        slope = 0.5 * (1.0 + inner) + 0.5 * gate * (1.0 - inner * inner) * GELU * (
            1.0 + 3 * 0.044715 * gate * gate
        )
        grad_gate = (grad_hidden * up * slope).astype(BF16)
        grad_up = (grad_hidden * activated).astype(BF16)
        grad_in += dot_nt(grad_gate, columns(r.w[GATE], 512 * number, 512))
        grad_in_b += dot_nt(grad_up, columns(r.w[UP], 512 * number, 512))
        term = dot_tn(r.ffn_in[...], grad_gate).astype(BF16)
        r.w[GATE][:, :, :, at] = term.reshape(2, 4, 80, 512)
        term = dot_tn(r.ffn_in_b[...], grad_up).astype(BF16)
        r.w[UP][:, :, :, at] = term.reshape(2, 4, 80, 512)
    halves = {number: send_half(r, number) for number in (DOWN, GATE, UP)}
    grad_in = grad_in + unturned(r, grad_in_b)
    back, term = norm_back(r.mid[...], gain(r, G_FFN), grad_in)
    note_gain(r, G_FFN, term)
    grad_mid = grad_out + back
    r.grad_mid[...] = grad_mid
    back, term = norm_back(r.proj[...], gain(r, G_POST_ATTN), grad_mid)
    note_gain(r, G_POST_ATTN, term)
    proj_low = back.astype(BF16)
    grad_attn = dot_nt(proj_low, r.w[OUTPUT][...].reshape(1024, 640)).astype(BF16)
    term = dot_tn(r.attn_low[...], proj_low).astype(BF16)
    r.w[OUTPUT][...] = term.reshape(2, 4, 128, 640)
    halves[OUTPUT] = send_half(r, OUTPUT)
    for block in range(2):
        for head in range(HEADS):
            r.grad_attn[head_rows(block, head)] = grad_attn[
                64 * block : 64 * block + 64, HEAD * head : HEAD * head + HEAD
            ]
    dots = jnp.sum(r.grad_attn[...].astype(F32) * r.attn[...], axis=1, keepdims=True)
    r.dots[...] = jnp.broadcast_to(dots, (512, 128))
    return halves


def queries_back(r, spreads):
    total = jnp.zeros((1, HEAD), F32)
    for head in range(HEADS):
        at = slice(HEAD * head, HEAD * head + HEAD)
        grad = jnp.concatenate([r.grad_query[head_rows(block, head)] for block in range(2)], axis=0)
        back, term = norm_back(
            r.query_raw[:, at], gain(r, G_QUERY), rope_back(r, grad * QUARTER)
        )
        total += term
        r.query_low[:, at] = back.astype(BF16)
    note_gain(r, G_QUERY, total)
    r.grad_normed[...] = unturned(r, dot_nt(r.query_low[...], r.w[QUERY][...].reshape(640, 1024)))
    spreads[QUERY].free()
    term = dot_tn(r.normed_b[...], r.query_low[...]).astype(BF16)
    r.w[QUERY][...] = term.reshape(2, 4, 80, 1024)
    return send_half(r, QUERY)


def send_half(r, number):
    grad, half = r.w[number], r.half[number]
    return r.links.across(grad.at[1 - lax.axis_index("dp")], lambda at: half)


def sum_halves(r, number, over):
    part, _, _, by_chip = WEIGHTS[number]
    last = ORDERS[part][2]
    core, mine = lax.axis_index("dp"), place()[last]
    grad, half, land = r.w[number], r.half[number], r.landed[number]
    over.wait()

    def join(*at):
        index = (core, *at)
        grad[index] = (grad[index].astype(F32) + half[at].astype(F32)).astype(BF16)

    if by_chip:
        loop(16, lambda at: join(at // 4, at % 4))
    else:
        rows = half.shape[1] // 16
        loop(
            4 * rows,
            lambda at: join(at // rows, pl.ds(pl.multiple_of((at % rows) * 16, 16), 16)),
        )
    return r.links.ring(
        last,
        lambda step: weight_plane(grad, number, core, shifted(mine, step)),
        lambda step, at: land.at[step - 1],
    )


def repack(r, number, ring):
    part, first, rows, by_chip = WEIGHTS[number]
    count, tiles = plane_tiles(number)
    own, land = own_plane(r, number), r.landed[number]
    ring.wait_all()
    for tile in range(tiles):
        lanes = slice(128 * tile, 128 * tile + 128)
        index = (slice(None),) * (3 if by_chip else 1) + (lanes,)
        total = add_all([own[index]] + [land[(step, *index)] for step in range(3)])
        r.stage[pl.ds(tile, count, stride=tiles)] = total.reshape(count, 128)

    def one(chip):
        r.p[part][chip // 4, chip % 4, first : first + rows] = r.stage[
            pl.ds(pl.multiple_of(chip * rows, 8), rows)
        ].astype(BF16)

    loop(16, one)


def late_second(r, part):
    second = ORDERS[part][1]
    mine = place()[second]
    return r.links.ring(
        second,
        lambda step: r.p[part].at[shifted(mine, step)],
        lambda step, at: r.second[part].at[step - 1],
    )


def late_first(r, part, ring):
    first, second, _ = ORDERS[part]
    mine, own = place()[first], place()[second]
    ring.wait_all()
    for at in range(4):
        r.line[part][at] = add_all(
            [r.p[part][own, at]] + [r.second[part][step, at] for step in range(3)]
        ).astype(BF16)
    return r.links.ring(
        first,
        lambda step: r.line[part].at[shifted(mine, step)],
        lambda step, at: r.first[part].at[step - 1],
    )


def late_end(r, part, ring, out):
    mine = place()[ORDERS[part][0]]
    ring.wait_all()
    out[...] = add_all([r.line[part][mine]] + [r.first[part][step] for step in range(3)])


def scatter_third(r):
    spot = place()
    rings, specials = [], []
    for part, (row, rows) in enumerate(KV_ROWS):
        last = ORDERS[part][2]
        rings.append(
            r.links.ring(
                last,
                lambda step, row=row, rows=rows, last=last: of_plane(
                    r.slots, last, shifted(spot[last], step), pl.ds(row, rows)
                ),
                lambda step, at, rb=r.rb[part]: rb.at[step - 1],
                begin=False,
            )
        )
        specials.append(
            r.links.ring(
                last,
                lambda step, row=row, rows=rows: r.grad_extra.at[2, pl.ds(row, rows)],
                lambda step, at, rs=r.rs[part]: rs.at[step - 1],
                begin=False,
            )
        )
    return rings, specials


def scatter_second(r, thirds, specials):
    spot = place()
    me = lax.axis_index("ctx")
    low_me = my_low(r)
    rings = []
    for part, (row, rows) in enumerate(KV_ROWS):
        first, second, last = ORDERS[part]
        rb, rs, total, land = r.rb[part], r.rs[part], r.g2[part], r.r2[part]
        thirds[part].wait_all()
        specials[part].wait_all()
        special = add_all([r.grad_extra[2, row : row + rows]] + [rs[step] for step in range(3)])
        for at in range(4):
            total[at, 8] = special.astype(BF16)
        senders = [low_of(r, chip_of(spot, last, -step)) for step in (1, 2, 3)]

        def collect(at, i2, i1, rb=rb, total=total, row=row, rows=rows, last=last, senders=senders):
            chip = chip_of(at, last, 0)
            source = low_of(r, chip)
            plane = [at[axis] for axis in (X, Y, Z) if axis != last]
            own = r.slots[at[0], at[1], at[2], pl.ds(row, rows)].astype(F32)
            none = jnp.zeros_like(own)
            low = jnp.where(source < low_me, own, none)
            high = jnp.where(source < low_me, none, own)
            low += jnp.where(chip == me, r.grad_extra[0, pl.ds(row, rows)].astype(F32), none)
            high += jnp.where(chip == me, r.grad_extra[1, pl.ds(row, rows)].astype(F32), none)
            for step in (1, 2, 3):
                came = rb[step - 1, plane[0], plane[1]].astype(F32)
                low += jnp.where(source < senders[step - 1], came, none)
                high += jnp.where(source < senders[step - 1], none, came)
            total[i2, 2 * i1] = low.astype(BF16)
            total[i2, 2 * i1 + 1] = high.astype(BF16)

        plane_loop(part, collect)
        rings.append(
            r.links.ring(
                second,
                lambda step, total=total, second=second: total.at[shifted(spot[second], step)],
                lambda step, at, land=land: land.at[step - 1],
            )
        )
    return rings


def scatter_first(r, seconds):
    spot = place()
    rings = []
    for part in range(3):
        first, second, _ = ORDERS[part]
        total, land, line, end = r.g2[part], r.r2[part], r.f1[part], r.r1[part]
        seconds[part].wait_all()

        def pick(index, total=total, land=land, mine=spot[second]):
            return add_all([total[mine, index]] + [land[step, index] for step in range(3)]).astype(
                BF16
            )

        special = pick(8)
        for at in range(4):
            line[at, 0] = pick(2 * at)
            line[at, 1] = pick(2 * at + 1)
            line[at, 2] = special
        rings.append(
            r.links.ring(
                first,
                lambda step, line=line, first=first: line.at[shifted(spot[first], step)],
                lambda step, at, end=end: end.at[step - 1],
            )
        )
    return rings


def scatter_end(r, firsts):
    spot = place()
    for part, (row, rows) in enumerate(KV_ROWS):
        firsts[part].wait_all()
        mine = spot[ORDERS[part][0]]
        for index in range(3):
            r.kv_sum[index, row : row + rows] = add_all(
                [r.f1[part][mine, index]] + [r.r1[part][step, index] for step in range(3)]
            )


def keys_values_back(r):
    special = jnp.where(my_low(r) == 63, 1.0, 0.0)
    r.kv_sum[0] = r.kv_sum[0] + r.kv_sum[2] * special
    lanes = []
    for lane in range(4):
        pieces = [
            r.kv_sum[block, unit_rows(token, lane)] for block in range(2) for token in range(4)
        ]
        lanes.append(jnp.concatenate(pieces, axis=0))
    grad_keys = jnp.concatenate(lanes[:2], axis=1)
    grad_values = jnp.concatenate(lanes[2:], axis=1)
    back, term = norm_back(r.key_raw[...], gain(r, G_KEY), rope_back(r, grad_keys))
    note_gain(r, G_KEY, term)
    kv_low = jnp.concatenate([back, grad_values], axis=1).astype(BF16)
    terms = dot_tn(r.normed_six[...], kv_low)
    for tile in range(4):
        r.stage[pl.ds(tile, 768, stride=4)] = terms[:, 128 * tile : 128 * tile + 128]
    grad_six = dot_nt(kv_low, r.w_kv[...]).astype(BF16)
    grad_normed = dot_nt(grad_six, r.sixes[...]) + r.grad_normed[...]
    back, term = norm_back(r.x[...], gain(r, G_ATTN), grad_normed)
    note_gain(r, G_ATTN, term)
    r.tokens_grad[...] = low_first(r, (r.grad_mid[...] + back).astype(BF16))
    held = jnp.zeros((128, 128), F32)
    for number, (at, count, _, _) in enumerate(GAINS):
        lanes, owners = gain_maps(r, number)
        term = jnp.where(owners, r.gain_sums[0:1, at : at + count], 0.0).astype(BF16)
        held += dot_nt(term, lanes)
    r.stage[pl.ds(20, 128, stride=24)] = held
    r.stage[3072:3088] = jnp.zeros((16, 128), F32)

    def one(row, i0, i1):
        r.u[0][i0] = r.stage[pl.ds(row, 16)].astype(BF16)
        r.u[1][i1] = r.stage[pl.ds(row + 16, 16)].astype(BF16)

    device_loop(one)


def small_sums(r, between):
    links = r.links
    core = lax.axis_index("dp")
    spot = place()
    overs = [links.across(ref.at[1 - core], lambda at, to=to: to) for ref, to in zip(r.u, r.vh)]
    axes = ((X, Y, Z), (Y, Z, X))
    rings = []
    for unit, order in enumerate(axes):
        half, own, land = r.vh[unit], r.u[unit], r.land3[unit]
        overs[unit].wait()

        def join(number, half=half, own=own):
            at = (number // 4, number % 4)
            index = (core, *at)
            own[index] = (own[index].astype(F32) + half[at].astype(F32)).astype(BF16)

        loop(16, join)
        axis = order[0]
        rings.append(
            links.ring(
                axis,
                lambda step, own=own, axis=axis: own.at[core, shifted(spot[axis], step)],
                lambda step, at, land=land: land.at[step - 1],
            )
        )
    between[0]()
    later = []
    for unit, order in enumerate(axes):
        own, land, out, to = r.u[unit], r.land3[unit], r.sum2[unit], r.land2[unit]
        rings[unit].wait_all()
        mine = spot[order[0]]

        def add(at, own=own, land=land, out=out, mine=mine):
            out[at] = add_all([own[core, mine, at]] + [land[step, at] for step in range(3)]).astype(
                BF16
            )

        loop(4, add)
        axis = order[1]
        later.append(
            links.ring(
                axis,
                lambda step, out=out, axis=axis: out.at[shifted(spot[axis], step)],
                lambda step, at, to=to: to.at[step - 1],
            )
        )
    between[1]()
    last = []
    for unit, order in enumerate(axes):
        own, land, out, to = r.sum2[unit], r.land2[unit], r.sum1[unit], r.land1[unit]
        later[unit].wait_all()
        out[...] = add_all([own[spot[order[1]]]] + [land[step] for step in range(3)]).astype(BF16)
        axis = order[2]
        last.append(
            links.ring(
                axis,
                lambda step, out=out, axis=axis: out.at[shifted(spot[axis], step)],
                lambda step, at, to=to: to.at[step - 1],
            )
        )
    between[2]()
    for unit, order in enumerate(axes):
        last[unit].wait_all()
        r.fk[16 * unit : 16 * unit + 16] = add_all(
            [r.sum1[unit][spot[order[2]]]] + [r.land1[unit][step] for step in range(3)]
        )


def layer(r):
    greet()
    pack(r)
    greeted()
    early_rings, early_held, spreads = early(r)
    unpack_small(r)
    keys_values(r)
    firsts = gather_first(r)
    seconds = gather_second(r, firsts)
    for number in (GATE, UP):
        spreads[number] = Spread(r, number)
    for number in (QUERY, OUTPUT, DOWN):
        spreads[number].pass_on()
    thirds, specials = gather_third(r, seconds)
    spreads[QUERY].finish()
    queries(r)

    def pass_on(number):
        if number == 0:
            spreads[GATE].pass_on()
            spreads[UP].pass_on()

    attention(r, thirds, specials, pass_on)
    feed_forward(r, spreads)
    halves = feed_forward_back(r, spreads)
    rings = {}

    def between(number):
        if number == 0:
            for weight in (DOWN, GATE):
                rings[weight] = sum_halves(r, weight, halves[weight])
        if number == 1:
            for weight in (UP, OUTPUT):
                rings[weight] = sum_halves(r, weight, halves[weight])

    thirds, third_specials = attention_back(r, between)
    half = queries_back(r, spreads)
    for ring in early_rings:
        ring.sent()
    repack(r, DOWN, rings[DOWN])
    late = {2: late_second(r, 2)}
    for ring in seconds:
        ring.sent()
    seconds = scatter_second(r, thirds, third_specials)
    rings[QUERY] = sum_halves(r, QUERY, half)
    repack(r, GATE, rings[GATE])
    repack(r, OUTPUT, rings[OUTPUT])
    late[0] = late_second(r, 0)
    firsts = scatter_first(r, seconds)
    repack(r, UP, rings[UP])
    repack(r, QUERY, rings[QUERY])
    late[1] = late_second(r, 1)
    scatter_end(r, firsts)
    for copy in early_held:
        copy.sent()
    keys_values_back(r)

    def begin_last():
        for part in (2, 0, 1):
            late[part] = late_first(r, part, late[part])

    def finish_last():
        for part, out in enumerate((r.fa, r.fb, r.fc)):
            late_end(r, part, late[part], out)

    small_sums(r, (begin_last, finish_last, lambda: None))
    r.links.close()


def end(r):
    def rows(out, source, base, count, tiles):
        r.stage[base : base + count * tiles] = source
        for tile in range(tiles):
            out[:, 128 * tile : 128 * tile + 128] = columns_of(r, base, count, tiles, tile)

    rows(r.gate_grad, r.fa[0:80], 0, 5, 16)
    rows(r.output_grad, r.fa[80:120], 80, 8, 5)
    rows(r.up_grad, r.fb[0:80], 128, 5, 16)
    rows(r.query_grad, r.fb[80:120], 208, 5, 8)
    rows(r.down_grad, r.fc[...], 256, 16, 5)
    r.stage[336:368] = r.fk[...]
    for tile in range(4):
        out = (r.key_grad, r.value_grad)[tile // 2]
        half = 128 * (tile % 2)
        out[:, half : half + 128] = columns_of(r, 336, 5, 4, tile)
    line = r.fk[16:24]
    gain_grads = (r.grad_attn_norm, r.grad_post_attn, r.grad_ffn_norm, r.grad_post_ffn, r.grad_q, r.grad_k)
    for number, (_, _, held, lane) in enumerate(GAINS):
        out = gain_grads[number]
        moved = line if lane == 0 else pltpu.roll(line, 128 - lane, 1)
        out[...] = moved[4:5, :held]
    r.final_out[0] = r.block_out[...]
    r.final_grad[0] = r.tokens_grad[...]


def by_part(*dims):
    return [hold(BF16, *dims, rows, 128) for _, rows in KV_ROWS]


def by_flat(*dims):
    return [hold(BF16, *dims, rows, 128) for rows in (128, 128, 80)]


def by_unit(*dims):
    return [hold(BF16, *dims, 16, 128) for _ in range(2)]


def by_weight(lead, core):
    return [
        hold(BF16, *core, *lead, 80, 2048),
        hold(BF16, *core, *lead, 128, 640),
        hold(BF16, *core, *lead, 80, 2048),
        hold(BF16, *core, *lead, 80, 1024),
        hold(BF16, *core, *lead, 4, 4, 16, 640),
    ]


def buffers():
    return dict(
        stage=hold(F32, 3088, 128),
        x=hold(F32, 128, 640),
        cos=hold(F32, 128, 128),
        sin=hold(F32, 128, 128),
        gains=hold(F32, 8, 3072),
        gain_sums=hold(F32, 8, 3072),
        turning=hold(BF16, 640, 640),
        sixes=hold(BF16, 640, 768),
        key_base=hold(jnp.int32, 32, 16, 128),
        key_rows=hold(jnp.int32, 32, 256),
        p=by_flat(4, 4),
        second=by_flat(3, 4),
        line=by_flat(4),
        first=by_flat(3),
        u=by_unit(2, 4, 4, 4),
        vh=by_unit(4, 4, 4),
        land3=by_unit(3, 4, 4),
        sum2=by_unit(4, 4),
        land2=by_unit(3, 4),
        sum1=by_unit(4),
        land1=by_unit(3),
        w_kv=hold(BF16, 768, 512),
        w=by_weight((4,), (2,)),
        half=by_weight((4,), ()),
        landed=[
            hold(BF16, 3, 80, 2048),
            hold(BF16, 3, 128, 640),
            hold(BF16, 3, 80, 2048),
            hold(BF16, 3, 80, 1024),
            hold(BF16, 3, 4, 4, 16, 640),
        ],
        kv3=hold(BF16, 3, 256, 128),
        f1=by_part(4, 3),
        g2=by_part(4, 9),
        sel=by_part(3, 4, 4),
        sp=by_part(),
        rsp=by_part(4),
        rb=by_part(3, 4, 4),
        rs=by_part(3),
        r2=by_part(3, 9),
        r1=by_part(3, 3),
        slots=hold(BF16, 4, 4, 4, 256, 128),
        extra=hold(BF16, 3, 256, 128),
        grad_extra=hold(BF16, 3, 256, 128),
        kv_sum=hold(F32, 3, 256, 128),
        normed=hold(BF16, 128, 640),
        normed_six=hold(BF16, 128, 768),
        normed_b=hold(BF16, 128, 640),
        key_raw=hold(F32, 128, 256),
        query_raw=hold(F32, 128, 1024),
        query=hold(BF16, 512, 256),
        attn=hold(F32, 512, 256),
        total=hold(F32, 512, 128),
        dots=hold(F32, 512, 128),
        attn_low=hold(BF16, 128, 1024),
        proj=hold(F32, 128, 640),
        mid=hold(F32, 128, 640),
        ffn_in=hold(BF16, 128, 640),
        ffn_in_b=hold(BF16, 128, 640),
        gate=hold(F32, 128, 2048),
        up=hold(F32, 128, 2048),
        hidden=hold(BF16, 128, 2048),
        ffn_out=hold(F32, 128, 640),
        low_grad=hold(BF16, 128, 640),
        grad_mid=hold(F32, 128, 640),
        grad_attn=hold(BF16, 512, 256),
        grad_query=hold(F32, 512, 256),
        query_low=hold(BF16, 128, 1024),
        grad_normed=hold(F32, 128, 640),
    )


def on_device(
    tokens,
    doc_lengths,
    block_order,
    attn_norm,
    query_weight,
    key_weight,
    value_weight,
    query_gain,
    key_gain,
    output_weight,
    attn_post_norm,
    ffn_norm,
    gate_weight,
    up_weight,
    down_weight,
    ffn_post_norm,
    out_cot,
):
    gain_row = jnp.concatenate(
        [attn_norm, attn_post_norm, ffn_norm, ffn_post_norm, query_gain, key_gain]
        + [jnp.zeros((104,), BF16)]
    )[None]
    frequency = (ROPE_BASE ** (-2.0 * jnp.arange(128, dtype=F32) / 256))[None]
    made = run(
        layer,
        dict(block_order=block_order, doc_lengths=doc_lengths),
        dict(
            tokens=tokens,
            out_cot=out_cot,
            gain_row=gain_row,
            table=jnp.asarray(number_table()),
            frequency=frequency,
            gate_weight=gate_weight,
            output_weight=output_weight,
            up_weight=up_weight,
            query_weight=query_weight,
            down_weight=down_weight,
            key_weight=key_weight,
            value_weight=value_weight,
        ),
        dict(
            block_out=hold(BF16, 128, 640),
            tokens_grad=hold(BF16, 128, 640),
            fa=hold(F32, 128, 128),
            fb=hold(F32, 128, 128),
            fc=hold(F32, 80, 128),
            fk=hold(F32, 32, 128),
        ),
        buffers(),
        number=1,
        copies=260,
    )
    results = run(
        end,
        {},
        made,
        dict(
            final_out=hold(BF16, 1, 128, 640),
            final_grad=hold(BF16, 1, 128, 640),
            grad_attn_norm=hold(F32, 1, 5),
            query_grad=hold(F32, 5, 1024),
            key_grad=hold(F32, 5, 256),
            value_grad=hold(F32, 5, 256),
            grad_q=hold(F32, 1, 2),
            grad_k=hold(F32, 1, 2),
            output_grad=hold(F32, 8, 640),
            grad_post_attn=hold(F32, 1, 5),
            grad_ffn_norm=hold(F32, 1, 5),
            gate_grad=hold(F32, 5, 2048),
            up_grad=hold(F32, 5, 2048),
            down_grad=hold(F32, 16, 640),
            grad_post_ffn=hold(F32, 1, 5),
        ),
        dict(stage=hold(F32, 3088, 128)),
    )
    return tuple(
        value.reshape(-1) if value.shape[0] == 1 and value.ndim == 2 else value
        for value in results.values()
    )


def solution(mesh):
    rows = P(("dp", "ctx"), None)
    vector = P(("dp", "ctx"))
    stream = P("dp", "ctx", None)
    return jax.shard_map(
        on_device,
        mesh=mesh,
        in_specs=(
            stream,
            P("dp", None),
            P(),
            vector,
            rows,
            rows,
            rows,
            vector,
            vector,
            rows,
            vector,
            vector,
            rows,
            rows,
            rows,
            vector,
            stream,
        ),
        out_specs=(
            stream,
            stream,
            vector,
            rows,
            rows,
            rows,
            vector,
            vector,
            rows,
            vector,
            vector,
            rows,
            rows,
            rows,
            vector,
        ),
        check_vma=False,
    )
```

```python
from types import SimpleNamespace

import jax
import jax.numpy as jnp
import numpy as np
from jax import lax
from jax.experimental import pallas as pl
from jax.experimental.pallas import tpu as pltpu
from jax.sharding import PartitionSpec as P

EPSILON = 1e-06
ROPE_BASE = 1000000.0
MESH = pl.DeviceIdType.MESH
F32 = jnp.float32
BF16 = jnp.bfloat16
MIB = 2**20

X, Y, Z = 0, 1, 2
ORDERS = ((Z, Y, X), (X, Z, Y), (Y, X, Z))
UNITS = (
    ((0, 0), (0, 1), (0, 2), (0, 3), (3, 0))
    + ((1, 0), (1, 1), (1, 2), (1, 3), (3, 1))
    + ((2, 0), (2, 1), (2, 2), (2, 3), (3, 2), (3, 3))
)
KV_ROWS = ((0, 80), (80, 80), (160, 96))
HEADS = 4
HEAD = 256
SCALE = HEAD**-0.5
LOG2E = 1.4426950408889634


def place():
    chip = lax.axis_index("ctx")
    return (chip // 16, (chip // 4) % 4, chip % 4)


def shifted(value, step):
    return lax.rem(value + step + 4, 4)


def peer(axis, step):
    spot = list(place())
    spot[axis] = shifted(spot[axis], step)
    return (lax.axis_index("dp"), spot[0] * 16 + spot[1] * 4 + spot[2])


def other_core():
    return (1 - lax.axis_index("dp"), lax.axis_index("ctx"))


def greet():
    barrier = pltpu.get_barrier_semaphore()
    for axis in (X, Y, Z):
        for step in (1, 2, 3):
            pl.semaphore_signal(barrier, inc=1, device_id=peer(axis, step), device_id_type=MESH)
    pl.semaphore_signal(barrier, inc=1, device_id=other_core(), device_id_type=MESH)


def greeted():
    pl.semaphore_wait(pltpu.get_barrier_semaphore(), 10)


class Ring:
    def __init__(self, links, axis, source, landing, whole, steps, apart, sends):
        self.links, self.axis, self.source, self.landing = links, axis, source, landing
        self.whole, self.apart = whole, apart
        self.sends = links.sends(whole) if sends is None else sends
        if apart:
            self.numbers = {step: links.receive() for step in steps}
        else:
            self.numbers = dict.fromkeys(steps, links.receive())

    def copy(self, step, sender):
        return self.links.copy(
            self.sends,
            self.numbers[step],
            self.source(step),
            self.landing(step, sender),
            peer(self.axis, step),
        )

    def start(self, step):
        self.copy(step, place()[self.axis]).start()

    def wait(self, step):
        self.copy(step, shifted(place()[self.axis], -step)).wait_recv()

    def wait_all(self):
        if self.apart:
            for step in self.numbers:
                self.wait(step)
        else:
            step = next(iter(self.numbers))
            self.links.copy(
                self.sends, self.numbers[step], self.whole, self.whole, peer(self.axis, step)
            ).wait_recv()

    def sent(self):
        self.links.settle((self.sends,))


class Across:
    def __init__(self, links, whole):
        self.links, self.whole = links, whole
        self.sends, self.number = links.sends(whole), links.receive()

    def add(self, source, landing):
        there = landing(lax.axis_index("dp"))
        self.links.copy(self.sends, self.number, source, there, other_core()).start()

    def wait(self):
        self.links.copy(
            self.sends, self.number, self.whole, self.whole, other_core()
        ).wait_recv()

    def sent(self):
        self.links.settle((self.sends,))


class Links:
    def __init__(self, send, recv):
        self.send, self.recv = send, recv
        self.sending, self.receiving, self.open = 0, 0, {}

    def sends(self, whole):
        self.open[self.sending] = whole
        self.sending += 1
        return self.sending - 1

    def receive(self):
        self.receiving += 1
        return self.receiving - 1

    def copy(self, send, recv, source, landing, device):
        return pltpu.make_async_remote_copy(
            src_ref=source,
            dst_ref=landing,
            send_sem=self.send.at[send],
            recv_sem=self.recv.at[recv],
            device_id=device,
            device_id_type=MESH,
        )

    def ring(
        self, axis, source, landing, whole, begin=True, steps=(1, 2, 3), apart=False, sends=None
    ):
        ring = Ring(self, axis, source, landing, whole, steps, apart, sends)
        if begin:
            for step in steps:
                ring.start(step)
        return ring

    def across(self, source, landing, whole):
        across = Across(self, whole)
        across.add(source, landing)
        return across

    def settle(self, numbers=None):
        for number in tuple(self.open if numbers is None else numbers):
            if number in self.open:
                whole = self.open.pop(number)
                self.copy(number, 0, whole, whole, other_core()).wait_send()


VMEM = pl.BlockSpec(memory_space=pltpu.VMEM)
SMEM = pl.BlockSpec(memory_space=pltpu.SMEM)


def hold(kind, *shape):
    return pltpu.VMEM(shape, kind)


def run(stage, numbers, ins, outs, scratch, number=None, copies=()):
    flat, shape = jax.tree.flatten(scratch, is_leaf=lambda leaf: not isinstance(leaf, (dict, list)))

    def kernel(*refs):
        count = len(numbers) + len(ins) + len(outs)
        named = dict(zip((*numbers, *ins, *outs), refs))
        named.update(jax.tree.unflatten(shape, refs[count : count + len(flat)]))
        r = SimpleNamespace(**named)
        if copies:
            r.links = Links(*refs[count + len(flat) :])
        stage(r)

    remote = dict(collective_id=number, has_side_effects=True) if copies else {}
    results = pl.pallas_call(
        kernel,
        out_shape=[jax.ShapeDtypeStruct(out.shape, out.dtype) for out in outs.values()],
        in_specs=[SMEM] * len(numbers) + [VMEM] * len(ins),
        out_specs=[VMEM] * len(outs),
        scratch_shapes=flat + [pltpu.SemaphoreType.DMA((count,)) for count in copies],
        compiler_params=pltpu.CompilerParams(vmem_limit_bytes=60 * MIB, **remote),
    )(*numbers.values(), *ins.values())
    return dict(zip(outs, results))


def dot32(left, right):
    return jnp.dot(left, right, preferred_element_type=F32)


def dot_nt(left, right):
    return lax.dot_general(left, right, (((1,), (1,)), ((), ())), preferred_element_type=F32)


def dot_tn(left, right):
    return lax.dot_general(left, right, (((0,), (0,)), ((), ())), preferred_element_type=F32)


def add_all(values):
    total = values[0].astype(F32)
    for value in values[1:]:
        total += value.astype(F32)
    return total


def loop(count, body):
    def step(number, unused):
        body(number)
        return unused

    lax.fori_loop(0, count, step, 0)


def my_low(r):
    chip = lax.axis_index("ctx")
    return jnp.minimum(r.block_order[2 * chip], r.block_order[2 * chip + 1])


def low_of(r, chip):
    return jnp.minimum(r.block_order[2 * chip], r.block_order[2 * chip + 1])


def low_first(r, rows):
    chip = lax.axis_index("ctx")
    flip = r.block_order[2 * chip] > r.block_order[2 * chip + 1]
    return jnp.where(flip, jnp.concatenate([rows[64:], rows[:64]], axis=0), rows)


def document_starts(r, places):
    start = jnp.zeros_like(places)
    at = 0
    for number in range(1, 8):
        at = at + r.doc_lengths[0, number - 1]
        start = jnp.where(places >= at, at, start)
    return start


def places_of(r, within, high):
    low = my_low(r)
    return jnp.where(high, 127 - low, low) * 64 + within


def number_table():
    def turned_device(device):
        core, x, y, z = device // 64, (device // 16) % 4, (device // 4) % 4, device % 4
        return ((core * 4 + y) * 4 + z) * 4 + x

    table = np.zeros((8, 640), np.int32)
    k = np.arange(640)
    table[0], table[1] = k % 5, turned_device(k // 5)
    core, y, z, x, row = k // 320, (k // 80) % 4, (k // 20) % 4, (k // 5) % 4, k % 5
    table[2] = (((core * 4 + x) * 4 + y) * 4 + z) * 5 + row
    table[3, :512] = 5 * (k[:512] // 4) + k[:512] % 4
    device = np.arange(128)
    table[3, 512 + turned_device(device)] = 5 * device + 4
    table[4, :256], table[5, :256] = k[:256] % 2, turned_device(k[:256] // 2)
    return table


def one_hot(rows, numbers):
    shape = (rows, numbers.shape[1])
    return jnp.where(lax.broadcasted_iota(jnp.int32, shape, 0) == numbers, 1.0, 0.0).astype(BF16)


GAINS = ((0, 640, 5, 0), (640, 640, 5, 5), (1280, 640, 5, 10), (1920, 640, 5, 15))
GAINS += ((2560, 256, 2, 20), (2816, 256, 2, 22))
G_ATTN, G_POST_ATTN, G_FFN, G_POST_FFN, G_QUERY, G_KEY = range(6)


def gain_maps(r, number):
    _, columns, held, lane = GAINS[number]
    row = 0 if held == 5 else 4
    rest, owner = r.table[row : row + 1, :columns], r.table[row + 1 : row + 2, :columns]
    lanes = one_hot(128, rest + lane)
    owners = lax.broadcasted_iota(jnp.int32, (128, columns), 0) == owner
    return lanes, owners


def gain(r, number):
    at, columns, _, _ = GAINS[number]
    return r.gains[0:1, at : at + columns]


def rows_of(r, base, weight, count):
    tiles = weight.shape[1] // 128
    for tile in range(tiles):
        r.stage[pl.ds(base + tile, count, stride=tiles)] = weight[
            :, 128 * tile : 128 * tile + 128
        ].astype(F32)


def columns_of(r, base, count, tiles, tile):
    return r.stage[pl.ds(base + tile, count, stride=tiles)]


def pack(r):
    rows_of(r, 0, r.gate_weight, 5)
    rows_of(r, 80, r.output_weight, 8)
    rows_of(r, 128, r.up_weight, 5)
    rows_of(r, 208, r.query_weight, 5)
    rows_of(r, 256, r.down_weight, 16)
    for tile in range(4):
        weight = (r.key_weight, r.value_weight)[tile // 2]
        half = 128 * (tile % 2)
        r.stage[pl.ds(336 + tile, 5, stride=4)] = weight[:, half : half + 128].astype(F32)
    r.stage[356:357] = jnp.zeros((1, 128), F32)
    own = (r.attn_norm, r.attn_post_norm, r.ffn_norm, r.ffn_post_norm, r.query_gain, r.key_gain)
    for ref, (_, _, held, lane) in zip(own, GAINS):
        r.stage[356:357, lane : lane + held] = ref[...].astype(F32)
    spot = place()
    for part, ref in enumerate(r.p):
        first, second, _ = ORDERS[part]
        rows = ref.shape[2]
        ref[spot[second], spot[first]] = r.stage[128 * part : 128 * part + rows].astype(BF16)
    core = lax.axis_index("dp")
    x, y, z = spot
    r.u[0][core, x, y, z] = r.stage[336:352].astype(BF16)
    r.u[1][core, y, z, x] = r.stage[352:368].astype(BF16)


def tables(r):
    r.x[...] = low_first(r, r.tokens[0].astype(F32))
    rows = lax.broadcasted_iota(jnp.int32, (128, 1), 0)
    places = places_of(r, rows % 64, rows >= 64)
    position = (places - document_starts(r, places)).astype(F32)
    angles = position * r.frequency[...]
    r.cos[...] = jnp.cos(angles)
    r.sin[...] = jnp.sin(angles)
    r.turning[...] = one_hot(640, r.table[2:3])
    r.splitting[...] = one_hot(640, r.table[3:4])


NEVER = -(1 << 20)


def key_tables(r):
    mine = my_low(r)

    def chunk(number, token):
        plane = number % 4
        row = 4 * token + number
        for slot in range(16):
            spot = [slot // 4, slot % 4]
            spot.insert(chunk_axis(token), plane)
            low = low_of(r, spot[0] * 16 + spot[1] * 4 + spot[2])
            chosen = jnp.where(low < mine, low, 127 - low) * 64
            for_low = jnp.where(low < mine, chosen, NEVER)
            for_high = jnp.where(low == mine, NEVER, chosen)
            r.key_base[row, slot : slot + 1] = jnp.full((1, 128), for_low, jnp.int32)
            r.key_base[16 + row, slot : slot + 1] = jnp.full((1, 128), for_high, jnp.int32)

    for token in range(4):
        loop(4, lambda number, token=token: chunk(number, token))

    def turn(row):
        r.key_rows[pl.ds(row, 1)] = jnp.transpose(key_column(r, row, (row // 4) % 4))[0:1]

    loop(32, turn)


def key_column(r, row, token):
    base = jnp.broadcast_to(r.key_base[row][:, None, :], (16, 16, 128)).reshape(256, 128)
    return base + (lax.broadcasted_iota(jnp.int32, (256, 128), 0) % 16 + 16 * token)


def early(r):
    links = r.links
    core = lax.axis_index("dp")
    spot = place()
    x, y, z = spot

    def small(axis, unit, index_of):
        ref = r.u[unit]
        ring = links.ring(
            axis,
            lambda step: ref.at[index_of(spot[axis])],
            lambda step, at: ref.at[index_of(at)],
            ref.at[index_of(pl.ds(0, 3))],
        )
        held.append(ring)
        return ring

    held = []

    one = small(Z, 0, lambda at: (core, x, y, at))
    two = small(X, 1, lambda at: (core, y, z, at))
    rings = []
    for part, ref in enumerate(r.p):
        first, second, _ = ORDERS[part]
        row = spot[second]
        rings.append(
            links.ring(
                first,
                lambda step, ref=ref, row=row, first=first: ref.at[row, spot[first]],
                lambda step, at, ref=ref, row=row: ref.at[row, at],
                ref.at[row, pl.ds(0, 3)],
            )
        )
    tables(r)
    one.wait_all()
    one = small(Y, 0, lambda at: (core, x, at))
    two.wait_all()
    two = small(Z, 1, lambda at: (core, y, at))
    for part, ref in enumerate(r.p):
        rings[part].wait_all()
        second = ORDERS[part][1]
        rings.append(
            links.ring(
                second,
                lambda step, ref=ref, second=second: ref.at[spot[second]],
                lambda step, at, ref=ref: ref.at[at],
                ref.at[pl.ds(0, 3)],
            )
        )
    key_tables(r)
    one.wait_all()
    one = small(X, 0, lambda at: (core, at))
    two.wait_all()
    two = small(Y, 1, lambda at: (core, at))
    spreads = {}
    for part, weights in ((2, (DOWN,)), (0, (GATE, OUTPUT)), (1, (QUERY, UP))):
        rings[3 + part].wait_all()
        for number in weights:
            unpack(r, number)
        for piece in EARLY_PIECES[part]:
            spreads[piece] = Spread(r, piece)
    one.wait_all()
    three = links.across(r.u[0].at[core], lambda at: r.u[0].at[at], r.u[0].at[core])
    two.wait_all()
    four = links.across(r.u[1].at[core], lambda at: r.u[1].at[at], r.u[1].at[core])
    three.wait()
    four.wait()
    return rings, held + [three, four], spreads


SMALL = 2048


def unpack_small(r):
    for unit in range(2):
        for core in range(2):
            for plane in range(4):
                row = SMALL * unit + 1024 * core + 256 * plane
                r.stage[row : row + 256] = r.u[unit][core, plane].astype(F32).reshape(256, 128)
    for tile in range(4):
        lanes = slice(128 * tile, 128 * tile + 128)
        r.w_kv[:512, lanes] = columns_of(r, 0, 512, 4, tile).astype(BF16)
        r.w_kv[512:, lanes] = columns_of(r, SMALL, 128, 16, tile).astype(BF16)
    held = columns_of(r, SMALL, 128, 16, 4).astype(BF16)
    for number, (at, columns, _, _) in enumerate(GAINS):
        lanes, owners = gain_maps(r, number)
        spread = jnp.where(owners, dot32(held, lanes), 0.0)
        r.gains[0:1, at : at + columns] = jnp.sum(spread, axis=0, keepdims=True)


WEIGHTS = ((0, 0, 80, False), (0, 80, 40, False), (1, 0, 80, False), (1, 80, 40, False), (2, 0, 80, True))
GATE, OUTPUT, UP, QUERY, DOWN = range(5)


def own_plane(r, number):
    part = WEIGHTS[number][0]
    return weight_plane(r.w[number], number, lax.axis_index("dp"), place()[ORDERS[part][2]])


def weight_plane(ref, number, core, at):
    part, _, _, by_chip = WEIGHTS[number]
    if by_chip:
        return of_plane(ref.at[core], ORDERS[part][2], at)
    return ref.at[core, at]


def plane_tiles(number):
    return ((80, 16), (128, 5), (80, 16), (80, 8), (256, 5))[number]


def unpack(r, number):
    part, first, rows, by_chip = WEIGHTS[number]
    count, tiles = plane_tiles(number)
    plane = own_plane(r, number)

    def one(chip):
        r.stage[pl.ds(pl.multiple_of(chip * rows, 8), rows)] = r.p[part][
            chip // 4, chip % 4, first : first + rows
        ].astype(F32)

    loop(16, one)
    for tile in range(tiles):
        piece = columns_of(r, 0, count, tiles, tile).astype(BF16)
        lanes = slice(128 * tile, 128 * tile + 128)
        if by_chip:
            plane[:, :, :, lanes] = piece.reshape(4, 4, 16, 128)
        else:
            plane[:, lanes] = piece


def inverse_rms(values):
    return lax.rsqrt(jnp.mean(values * values, axis=-1, keepdims=True) + EPSILON)


def rms_scale(values, weights):
    return values * inverse_rms(values) * weights


def norm_back(values, weights, incoming):
    inverse = inverse_rms(values)
    normal = values * inverse
    scaled = incoming * weights
    back = (scaled - normal * jnp.mean(scaled * normal, axis=-1, keepdims=True)) * inverse
    return back, jnp.sum(incoming * normal, axis=0, keepdims=True)


def rope(r, u):
    cos, sin = r.cos[...], r.sin[...]
    one, two = u[:, :128], u[:, 128:]
    return jnp.concatenate([one * cos - two * sin, two * cos + one * sin], axis=1)


def rope_back(r, e):
    cos, sin = r.cos[...], r.sin[...]
    one, two = e[:, :128], e[:, 128:]
    return jnp.concatenate([one * cos + two * sin, two * cos - one * sin], axis=1)


def turned(r, values):
    return dot32(values, r.turning[...]).astype(BF16)


def unturned(r, values):
    return dot_nt(values.astype(BF16), r.turning[...])


def keys_values(r):
    x = r.x[...]
    normed = rms_scale(x, gain(r, G_ATTN)).astype(BF16)
    r.normed[...] = normed
    r.normed_split[...] = dot32(normed, r.splitting[...]).astype(BF16)
    raw = dot32(r.normed_split[...], r.w_kv[...])
    r.key_raw[...] = raw[:, :HEAD]
    keys = rope(r, rms_scale(raw[:, :HEAD], gain(r, G_KEY)))
    both = jnp.concatenate([keys, raw[:, HEAD:]], axis=1).astype(BF16)
    for block in range(2):
        for unit, (token, lane) in enumerate(UNITS):
            row = 64 * block + 16 * token
            r.kv3[block, 16 * unit : 16 * unit + 16] = both[
                row : row + 16, 128 * lane : 128 * lane + 128
            ]


def of_plane(ref, axis, at, *rest):
    index = [slice(None)] * 3
    index[axis] = at
    return ref.at[(*index, *rest)]


def chip_of(spot, axis, step):
    spot = list(spot)
    spot[axis] = shifted(spot[axis], step)
    return spot[0] * 16 + spot[1] * 4 + spot[2]


def plane_loop(part, body):
    first, second, last = ORDERS[part]

    def row(i2):
        for i1 in range(4):
            spot = [None] * 3
            spot[first], spot[second], spot[last] = i1, i2, place()[last]
            body(spot, i2, i1)

    loop(4, row)


PIECES = (
    (GATE, 0, 1024),
    (GATE, 1024, 1024),
    (OUTPUT, 0, 640),
    (UP, 0, 1024),
    (UP, 1024, 1024),
    (QUERY, 0, 1024),
    (DOWN, 0, 2),
    (DOWN, 2, 2),
)
GATE_ONE, GATE_TWO, OUT, UP_ONE, UP_TWO, ASK, DOWN_ONE, DOWN_TWO = range(8)
EARLY_PIECES = ((OUT, GATE_ONE), (ASK, UP_ONE), (DOWN_ONE,))
LATE_PIECES = (GATE_TWO, UP_TWO, DOWN_TWO)


def window(ref, dim, first, count):
    index = [slice(None)] * len(ref.shape)
    index[dim] = pl.ds(first, count)
    return ref.at[tuple(index)]


def piece_of(piece, ref, chips=4):
    number, first, count = PIECES[piece]
    rank = len(ref.shape)
    return window(ref, rank - 1 - chips if number == DOWN else rank - 1, first, count)


def half_of(piece, plane, half):
    number, _, count = PIECES[piece]
    if number == DOWN:
        return window(plane, len(plane.shape) - 4, half, 1)
    if number == OUTPUT:
        return window(plane, len(plane.shape) - 2, 64 * half, 64)
    return window(plane, len(plane.shape) - 1, count // 2 * half, count // 2)


def piece_plane(r, piece, core, at):
    number = PIECES[piece][0]
    return piece_of(piece, weight_plane(r.w[number], number, core, at), 3)


def piece_axis(piece):
    return ORDERS[WEIGHTS[PIECES[piece][0]][0]][2]


class Spread:
    def __init__(self, r, piece):
        self.links, axis = r.links, piece_axis(piece)
        self.core, self.mine = lax.axis_index("dp"), place()[axis]
        self.at = lambda core, at: piece_plane(r, piece, core, at)

        def half(at, which):
            return half_of(piece, self.at(self.core, at), which)

        both = piece_of(piece, r.w[PIECES[piece][0]])
        dim = 3 if PIECES[piece][0] == DOWN else 1
        planes = window(both, dim, 0, 3).at[self.core]
        sends = r.links.sends(planes)
        self.near = [
            r.links.ring(
                axis,
                lambda step, which=which: half(self.mine, which),
                lambda step, at, which=which: half(at, which),
                None,
                steps=(1, 3),
                apart=True,
                sends=sends,
            )
            for which in range(2)
        ]

        def passed(step, at):
            return half(shifted(at, -step), 0 if step == 1 else 1)

        self.far = r.links.ring(
            axis,
            lambda step: passed(step, self.mine),
            passed,
            None,
            begin=False,
            steps=(1, 3),
            apart=True,
            sends=sends,
        )
        self.across = Across(r.links, both.at[self.core])
        self.over(self.mine)

    def over(self, at):
        self.across.add(self.at(self.core, at), lambda core: self.at(core, at))

    def forward(self):
        for which, step in enumerate((1, 3)):
            self.near[which].wait(step)
            self.far.start(step)

    def pass_on(self):
        for which, step in enumerate((3, 1)):
            self.near[which].wait(step)
        self.over(shifted(self.mine, 1))
        self.over(shifted(self.mine, 3))
        self.far.wait_all()
        self.over(shifted(self.mine, 2))

    def finish(self):
        self.across.wait()

    def free(self):
        self.far.sent()
        self.across.sent()


def gather_first(r):
    rings = []
    for part, (row, rows) in enumerate(KV_ROWS):
        own = r.kv3.at[:, pl.ds(row, rows)]
        rings.append(
            r.links.ring(
                ORDERS[part][0],
                lambda step, own=own: own,
                lambda step, at, ref=r.f1[part]: ref.at[at],
                r.f1[part].at[pl.ds(0, 3)],
            )
        )
    return rings


def gather_second(r, firsts):
    spot = place()
    rings = []
    for part, (row, rows) in enumerate(KV_ROWS):
        first, second, _ = ORDERS[part]
        f1, g2, mine = r.f1[part], r.g2[part], spot[second]
        f1[spot[first]] = r.kv3[:, row : row + rows]
        firsts[part].wait_all()
        for at in range(4):
            g2[mine, 2 * at] = f1[at, 0]
            g2[mine, 2 * at + 1] = f1[at, 1]
        rings.append(
            r.links.ring(
                second,
                lambda step, g2=g2, mine=mine: g2.at[mine],
                lambda step, at, g2=g2: g2.at[at],
                g2.at[pl.ds(0, 3)],
            )
        )
    return rings


def gather_third(r, seconds):
    spot = place()
    low_me = my_low(r)
    rings, specials = [], []
    for part, (row, rows) in enumerate(KV_ROWS):
        first, second, last = ORDERS[part]
        g2, sel, sp, rsp = r.g2[part], r.sel[part], r.sp[part], r.rsp[part]
        seconds[part].wait_all()
        targets = [low_of(r, chip_of(spot, last, step)) for step in (1, 2, 3)]
        sp[...] = jnp.zeros_like(sp)

        def choose(at, i2, i1, g2=g2, sel=sel, sp=sp, row=row, rows=rows, last=last, targets=targets):
            low = g2[i2, 2 * i1]
            high = g2[i2, 2 * i1 + 1]
            source = low_of(r, chip_of(at, last, 0))
            plane = [at[axis] for axis in (X, Y, Z) if axis != last]
            r.slots[at[0], at[1], at[2], pl.ds(row, rows)] = jnp.where(source < low_me, low, high)
            for step in (1, 2, 3):
                sel[step - 1, plane[0], plane[1]] = jnp.where(
                    source < targets[step - 1], low, high
                )
            sp[...] = jnp.where(source == 63, low, sp[...])

        plane_loop(part, choose)
        rings.append(
            r.links.ring(
                last,
                lambda step, sel=sel: sel.at[step - 1],
                lambda step, at, row=row, rows=rows, last=last: of_plane(
                    r.slots, last, at, pl.ds(row, rows)
                ),
                sel,
                apart=True,
            )
        )
        specials.append(
            r.links.ring(
                last,
                lambda step, sp=sp: sp,
                lambda step, at, rsp=rsp: rsp.at[at],
                rsp.at[pl.ds(0, 3)],
            )
        )
    r.extra[0:2] = r.kv3[...]
    return rings, specials


def gather_special(r, specials):
    spot = place()
    for part, (row, rows) in enumerate(KV_ROWS):
        rsp = r.rsp[part]
        specials[part].wait_all()
        rsp[spot[ORDERS[part][2]]] = r.sp[part][...]
        r.extra[2, row : row + rows] = add_all([rsp[at] for at in range(4)]).astype(BF16)


QUARTER = 1.0 / 16
POWER = QUARTER * 1.4426950408889634


def chunk_axis(token):
    return ORDERS[token][2] if token < 3 else X


def chunk_index(token, plane):
    index = [slice(None)] * 3
    index[chunk_axis(token)] = plane
    return tuple(index)


def unit_rows(token, lane):
    return pl.ds(16 * UNITS.index((token, lane)), 16)


def chunk_kv(r, token, plane):
    index = chunk_index(token, plane)
    quarters = [
        r.slots[(*index, unit_rows(token, lane))].reshape(256, 128) for lane in range(4)
    ]
    return jnp.concatenate(quarters[:2], axis=1), jnp.concatenate(quarters[2:], axis=1)


def extra_kv(r):
    quarters = [
        jnp.concatenate(
            [r.extra[block, unit_rows(token, lane)] for block in range(3) for token in range(4)],
            axis=0,
        )
        for lane in range(4)
    ]
    return jnp.concatenate(quarters[:2], axis=1), jnp.concatenate(quarters[2:], axis=1)


def extra_places(r, numbers):
    low = my_low(r)
    block = jnp.where(numbers < 64, low, jnp.where(numbers < 128, 127 - low, 63))
    gone = (numbers >= 128) & (low == 63)
    return jnp.where(gone, 1 << 20, block * 64 + numbers % 64)


def query_places(r, numbers):
    return places_of(r, numbers % 64, numbers >= 256)


def attention(r, thirds, specials, between):
    spot = place()
    numbers = lax.broadcasted_iota(jnp.int32, (512, 1), 0)
    latest = query_places(r, numbers)
    earliest = document_starts(r, latest)
    query = r.query[...]
    r.attn[...] = jnp.zeros_like(r.attn)
    r.total[...] = jnp.zeros_like(r.total)

    def add(weights, values):
        total = weights[:, :128]
        if weights.shape[1] == 256:
            total = total + weights[:, 128:]
            r.total[...] += total
        else:
            r.total[...] += total
            r.total[:, :64] += weights[:, 128:]
        r.attn[...] += dot32(weights.astype(BF16), values)

    def chunk(token, plane):
        keys, values = chunk_kv(r, token, plane)
        scores = dot_nt(query, keys)
        row = 4 * token + plane
        allowed = jnp.concatenate(
            [
                r.key_rows[pl.ds(row, 1)] >= earliest[:256],
                r.key_rows[pl.ds(16 + row, 1)] >= earliest[256:],
            ],
            axis=0,
        )
        add(jnp.where(allowed, jnp.exp2(scores * POWER), 0.0), values)

    for token in range(3):
        chunk(token, spot[chunk_axis(token)])
    between(0)
    for number, step in enumerate((1, 3, 2)):
        for token in range(3):
            thirds[token].wait(step)
            chunk(token, shifted(spot[chunk_axis(token)], -step))
        between(number + 1)
    for plane in range(4):
        chunk(3, plane)
    gather_special(r, specials)
    keys, values = extra_kv(r)
    scores = dot_nt(query, keys)
    places = extra_places(r, lax.broadcasted_iota(jnp.int32, (1, 192), 1))
    allowed = (places >= earliest) & (places <= latest)
    add(jnp.where(allowed, jnp.exp2(scores * POWER), 0.0), values)
    total = jnp.sum(r.total[...], axis=1, keepdims=True)
    r.attn[...] = r.attn[...] / total
    r.total[...] = jnp.broadcast_to(jnp.log2(total), (512, 128))


def attention_back(r, between):
    spot = place()
    numbers = lax.broadcasted_iota(jnp.int32, (1, 512), 1)
    latest = query_places(r, numbers)
    earliest = document_starts(r, latest)
    query, grad_out = r.query[...], r.grad_attn[...]
    log_total = jnp.transpose(r.total[...])[0:1]
    row_dot = jnp.transpose(r.dots[...])[0:1]
    r.grad_query[...] = jnp.zeros_like(r.grad_query)

    def grads_of(keys, values, allowed):
        scores = dot_nt(keys, query)
        probs = jnp.where(allowed, jnp.exp2(scores * POWER - log_total), 0.0)
        grad_probs = dot_nt(values, grad_out)
        grad_scores = (probs * (grad_probs - row_dot)).astype(BF16)
        grad_values = dot32(probs.astype(BF16), grad_out)
        grad_keys = dot32(grad_scores, query) * QUARTER
        r.grad_query[...] += dot_tn(grad_scores, keys)
        return jnp.concatenate([grad_keys, grad_values], axis=1).astype(BF16)

    def chunk(token, plane):
        keys, values = chunk_kv(r, token, plane)
        row = 4 * token + plane
        low, high = key_column(r, row, token), key_column(r, 16 + row, token)
        allowed = jnp.concatenate([low, low, high, high], axis=1) >= earliest
        grads = grads_of(keys, values, allowed)
        index = chunk_index(token, plane)
        for lane in range(4):
            r.slots[(*index, unit_rows(token, lane))] = grads[
                :, 128 * lane : 128 * lane + 128
            ].reshape(4, 4, 16, 128)

    for plane in range(4):
        chunk(3, plane)
    between(0)
    rings, specials = scatter_third(r)
    for number, step in enumerate((1, 3, 2)):
        for token in range(3):
            chunk(token, shifted(spot[chunk_axis(token)], step))
            rings[token].start(step)
        between(number + 1)
    keys, values = extra_kv(r)
    places = extra_places(r, lax.broadcasted_iota(jnp.int32, (192, 1), 0))
    grads = grads_of(keys, values, (places >= earliest) & (places <= latest))
    for block in range(3):
        for unit, (token, lane) in enumerate(UNITS):
            row = 64 * block + 16 * token
            r.grad_extra[block, 16 * unit : 16 * unit + 16] = grads[
                row : row + 16, 128 * lane : 128 * lane + 128
            ]
    for ring in specials:
        for step in (1, 2, 3):
            ring.start(step)
    for token in range(3):
        chunk(token, spot[chunk_axis(token)])
    return rings, specials


GELU = 0.7978845608028654


def head_rows(block, head):
    start = 256 * block + 64 * head
    return slice(start, start + 64)


def queries(r):
    r.normed_b[...] = turned(r, r.normed[...])
    r.query_raw[...] = dot32(r.normed_b[...], r.w[QUERY][...].reshape(640, 1024))
    for head in range(HEADS):
        raw = r.query_raw[:, HEAD * head : HEAD * head + HEAD]
        rotated = rope(r, rms_scale(raw, gain(r, G_QUERY))).astype(BF16)
        for block in range(2):
            r.query[head_rows(block, head)] = rotated[64 * block : 64 * block + 64]


def gelu_parts(gate):
    inner = jnp.tanh(GELU * (gate + 0.044715 * gate * gate * gate))
    return 0.5 * gate * (1.0 + inner), inner


def columns(weight, at, width):
    rows = 8 * weight.shape[2]
    return weight[:, :, :, at : at + width].reshape(rows, width)


def down_rows(ref, number):
    return ref.at[number // 2, pl.ds(2 * (number % 2), 2)]


def feed_forward(r, spreads):
    spreads[OUT].finish()
    for block in range(2):
        for head in range(HEADS):
            r.attn_low[64 * block : 64 * block + 64, HEAD * head : HEAD * head + HEAD] = r.attn[
                head_rows(block, head)
            ].astype(BF16)
    r.proj[...] = dot32(r.attn_low[...], r.w[OUTPUT][...].reshape(1024, 640))
    r.mid[...] = r.x[...] + rms_scale(r.proj[...], gain(r, G_POST_ATTN))
    r.ffn_in[...] = rms_scale(r.mid[...], gain(r, G_FFN)).astype(BF16)
    r.ffn_in_b[...] = turned(r, r.ffn_in[...])
    for piece in (GATE_ONE, GATE_TWO, UP_ONE, UP_TWO):
        spreads[piece].finish()
    for number in range(4):
        at = slice(512 * number, 512 * number + 512)
        gate = dot32(r.ffn_in[...], columns(r.w[GATE], 512 * number, 512))
        up = dot32(r.ffn_in_b[...], columns(r.w[UP], 512 * number, 512))
        r.gate[:, at] = gate
        r.up[:, at] = up
        r.hidden[:, at] = (gelu_parts(gate)[0] * up).astype(BF16)
    spreads[DOWN_ONE].finish()
    spreads[DOWN_TWO].finish()
    r.ffn_out[...] = dot32(r.hidden[...], r.w[DOWN][...].reshape(2048, 640))
    out = r.mid[...] + rms_scale(r.ffn_out[...], gain(r, G_POST_FFN))
    r.block_out[...] = low_first(r, out.astype(BF16))


def note_gain(r, number, term):
    at, count, _, _ = GAINS[number]
    r.gain_sums[0:1, at : at + count] = term


def feed_forward_back(r, spreads):
    for piece in (GATE_ONE, GATE_TWO, OUT, UP_ONE, UP_TWO, DOWN_ONE, DOWN_TWO):
        spreads[piece].free()
    grad_out = low_first(r, r.out_cot[0].astype(F32))
    grad_ffn_out, term = norm_back(r.ffn_out[...], gain(r, G_POST_FFN), grad_out)
    note_gain(r, G_POST_FFN, term)
    low_grad = grad_ffn_out.astype(BF16)
    r.low_grad[...] = low_grad
    halves = {}
    grad_in = jnp.zeros((128, 640), F32)
    grad_in_b = jnp.zeros((128, 640), F32)
    for number in range(4):
        at = slice(512 * number, 512 * number + 512)
        down = down_rows(r.w[DOWN], number)
        grad_hidden = dot_nt(low_grad, down[...].reshape(512, 640))
        down[...] = (
            dot_tn(r.hidden[:, at], low_grad).astype(BF16).reshape(2, 4, 4, 16, 640)
        )
        gate, up = r.gate[:, at], r.up[:, at]
        activated, inner = gelu_parts(gate)
        slope = 0.5 * (1.0 + inner) + 0.5 * gate * (1.0 - inner * inner) * GELU * (
            1.0 + 3 * 0.044715 * gate * gate
        )
        grad_gate = (grad_hidden * up * slope).astype(BF16)
        grad_up = (grad_hidden * activated).astype(BF16)
        grad_in += dot_nt(grad_gate, columns(r.w[GATE], 512 * number, 512))
        grad_in_b += dot_nt(grad_up, columns(r.w[UP], 512 * number, 512))
        term = dot_tn(r.ffn_in[...], grad_gate).astype(BF16)
        r.w[GATE][:, :, :, at] = term.reshape(2, 4, 80, 512)
        term = dot_tn(r.ffn_in_b[...], grad_up).astype(BF16)
        r.w[UP][:, :, :, at] = term.reshape(2, 4, 80, 512)
        if number == 1:
            halves[GATE_ONE] = send_half(r, GATE_ONE)
            halves[UP_ONE] = send_half(r, UP_ONE)
    for piece in (DOWN_ONE, DOWN_TWO, GATE_TWO, UP_TWO):
        halves[piece] = send_half(r, piece)
    grad_in = grad_in + unturned(r, grad_in_b)
    back, term = norm_back(r.mid[...], gain(r, G_FFN), grad_in)
    note_gain(r, G_FFN, term)
    grad_mid = grad_out + back
    r.grad_mid[...] = grad_mid
    back, term = norm_back(r.proj[...], gain(r, G_POST_ATTN), grad_mid)
    note_gain(r, G_POST_ATTN, term)
    proj_low = back.astype(BF16)
    grad_attn = dot_nt(proj_low, r.w[OUTPUT][...].reshape(1024, 640)).astype(BF16)
    term = dot_tn(r.attn_low[...], proj_low).astype(BF16)
    r.w[OUTPUT][...] = term.reshape(2, 4, 128, 640)
    halves[OUT] = send_half(r, OUT)
    for block in range(2):
        for head in range(HEADS):
            r.grad_attn[head_rows(block, head)] = grad_attn[
                64 * block : 64 * block + 64, HEAD * head : HEAD * head + HEAD
            ]
    dots = jnp.sum(r.grad_attn[...].astype(F32) * r.attn[...], axis=1, keepdims=True)
    r.dots[...] = jnp.broadcast_to(dots, (512, 128))
    return halves


def queries_back(r, spreads):
    total = jnp.zeros((1, HEAD), F32)
    for head in range(HEADS):
        at = slice(HEAD * head, HEAD * head + HEAD)
        grad = jnp.concatenate([r.grad_query[head_rows(block, head)] for block in range(2)], axis=0)
        back, term = norm_back(
            r.query_raw[:, at], gain(r, G_QUERY), rope_back(r, grad * QUARTER)
        )
        total += term
        r.query_low[:, at] = back.astype(BF16)
    note_gain(r, G_QUERY, total)
    r.grad_normed[...] = unturned(r, dot_nt(r.query_low[...], r.w[QUERY][...].reshape(640, 1024)))
    spreads[ASK].free()
    term = dot_tn(r.normed_b[...], r.query_low[...]).astype(BF16)
    r.w[QUERY][...] = term.reshape(2, 4, 80, 1024)
    return send_half(r, ASK)


def send_half(r, piece):
    number = PIECES[piece][0]
    grad, half = piece_of(piece, r.w[number]), piece_of(piece, r.half[number])
    return r.links.across(grad.at[1 - lax.axis_index("dp")], lambda at: half, half)


def add_rows(count, to, value):
    def one(at):
        rows = pl.ds(pl.multiple_of(at * 16, 16), 16)
        to[rows] = (to[rows].astype(F32) + value[rows].astype(F32)).astype(BF16)

    loop(count // 16, one)


def add_into(to, value):
    lead = to.shape[:-2]
    if not lead:
        add_rows(to.shape[0], to, value)
    elif len(lead) == 1:
        for at in range(lead[0]):
            add_rows(to.shape[1], to.at[at], value.at[at])
    else:
        for at in range(lead[0]):
            add_into(to.at[at], value.at[at])


class Gather:
    def __init__(self, r, piece, over):
        self.piece, axis = piece, piece_axis(piece)
        core, mine = lax.axis_index("dp"), place()[axis]
        number = PIECES[piece][0]
        over.wait()
        add_into(piece_of(piece, r.w[number]).at[core], piece_of(piece, r.half[number]))
        self.land = piece_of(piece, r.landed[number], 3)
        self.at = lambda step: piece_plane(r, piece, core, shifted(mine, step))
        sends = r.links.sends(self.land)
        self.far = r.links.ring(
            axis,
            lambda step: half_of(piece, self.at(2), 0 if step == 1 else 1),
            lambda step, at: half_of(piece, self.land.at[2], 0 if step == 1 else 1),
            None,
            steps=(1, 3),
            apart=True,
            sends=sends,
        )
        self.near = r.links.ring(
            axis,
            self.at,
            lambda step, at: self.land.at[0 if step == 1 else 1],
            self.land.at[pl.ds(0, 2)],
            begin=False,
            steps=(1, 3),
            sends=sends,
        )

    def relay(self):
        for which, step in enumerate((1, 3)):
            self.far.wait(step)
            add_into(
                half_of(self.piece, self.at(step), which),
                half_of(self.piece, self.land.at[2], which),
            )
            self.near.start(step)


def repack(r, number, *gathers):
    part, first, rows, by_chip = WEIGHTS[number]
    count, tiles = plane_tiles(number)
    own, land = own_plane(r, number), r.landed[number]
    for gather in gathers:
        gather.near.wait_all()
    for tile in range(tiles):
        lanes = slice(128 * tile, 128 * tile + 128)
        index = (slice(None),) * (3 if by_chip else 1) + (lanes,)
        total = add_all([own[index]] + [land[(step, *index)] for step in range(2)])
        r.stage[pl.ds(tile, count, stride=tiles)] = total.reshape(count, 128)

    def one(chip):
        r.p[part][chip // 4, chip % 4, first : first + rows] = r.stage[
            pl.ds(pl.multiple_of(chip * rows, 8), rows)
        ].astype(BF16)

    loop(16, one)


def late_second(r, part):
    second = ORDERS[part][1]
    mine = place()[second]
    return r.links.ring(
        second,
        lambda step: r.p[part].at[shifted(mine, step)],
        lambda step, at: r.second[part].at[step - 1],
        r.second[part],
    )


def late_first(r, part, ring):
    first, second, _ = ORDERS[part]
    mine, own = place()[first], place()[second]
    ring.wait_all()
    for at in range(4):
        r.line[part][at] = add_all(
            [r.p[part][own, at]] + [r.second[part][step, at] for step in range(3)]
        ).astype(BF16)
    return r.links.ring(
        first,
        lambda step: r.line[part].at[shifted(mine, step)],
        lambda step, at: r.first[part].at[step - 1],
        r.first[part],
    )


def late_end(r, part, ring, out):
    mine = place()[ORDERS[part][0]]
    ring.wait_all()
    out[...] = add_all([r.line[part][mine]] + [r.first[part][step] for step in range(3)])


def scatter_third(r):
    spot = place()
    rings, specials = [], []
    for part, (row, rows) in enumerate(KV_ROWS):
        last = ORDERS[part][2]
        rings.append(
            r.links.ring(
                last,
                lambda step, row=row, rows=rows, last=last: of_plane(
                    r.slots, last, shifted(spot[last], step), pl.ds(row, rows)
                ),
                lambda step, at, rb=r.rb[part]: rb.at[step - 1],
                r.rb[part],
                begin=False,
            )
        )
        specials.append(
            r.links.ring(
                last,
                lambda step, row=row, rows=rows: r.grad_extra.at[2, pl.ds(row, rows)],
                lambda step, at, rs=r.rs[part]: rs.at[step - 1],
                r.rs[part],
                begin=False,
            )
        )
    return rings, specials


def scatter_second(r, thirds, specials):
    spot = place()
    me = lax.axis_index("ctx")
    low_me = my_low(r)
    rings = []
    for part, (row, rows) in enumerate(KV_ROWS):
        first, second, last = ORDERS[part]
        rb, rs, total, land = r.rb[part], r.rs[part], r.g2[part], r.r2[part]
        thirds[part].wait_all()
        specials[part].wait_all()
        special = add_all([r.grad_extra[2, row : row + rows]] + [rs[step] for step in range(3)])
        r.sp[part][...] = special.astype(BF16)
        senders = [low_of(r, chip_of(spot, last, -step)) for step in (1, 2, 3)]

        def collect(
            at, i2, i1, rb=rb, sp=r.sp[part], total=total, row=row, rows=rows, last=last, senders=senders
        ):
            chip = chip_of(at, last, 0)
            source = low_of(r, chip)
            plane = [at[axis] for axis in (X, Y, Z) if axis != last]
            both = r.slots[at[0], at[1], at[2], pl.ds(row, rows)].astype(F32)
            none = jnp.zeros_like(both)
            low = jnp.where(source < low_me, both, none)
            for step in (1, 2, 3):
                came = rb[step - 1, plane[0], plane[1]].astype(F32)
                low += jnp.where(source < senders[step - 1], came, none)
                both += came
            high = both - low
            low += jnp.where(chip == me, r.grad_extra[0, pl.ds(row, rows)].astype(F32), none)
            high += jnp.where(chip == me, r.grad_extra[1, pl.ds(row, rows)].astype(F32), none)
            low += jnp.where(source == 63, sp[...].astype(F32), none)
            total[i2, 2 * i1] = low.astype(BF16)
            total[i2, 2 * i1 + 1] = high.astype(BF16)

        plane_loop(part, collect)
        rings.append(
            r.links.ring(
                second,
                lambda step, total=total, second=second: total.at[shifted(spot[second], step)],
                lambda step, at, land=land: land.at[step - 1],
                land,
            )
        )
    return rings


def scatter_first(r, seconds):
    spot = place()
    rings = []
    for part in range(3):
        first, second, _ = ORDERS[part]
        total, land, line, end = r.g2[part], r.r2[part], r.f1[part], r.r1[part]
        seconds[part].wait_all()

        def pick(index, total=total, land=land, mine=spot[second]):
            return add_all([total[mine, index]] + [land[step, index] for step in range(3)]).astype(
                BF16
            )

        for at in range(4):
            line[at, 0] = pick(2 * at)
            line[at, 1] = pick(2 * at + 1)
        rings.append(
            r.links.ring(
                first,
                lambda step, line=line, first=first: line.at[shifted(spot[first], step)],
                lambda step, at, end=end: end.at[step - 1],
                end,
            )
        )
    return rings


def scatter_end(r, firsts):
    spot = place()
    for part, (row, rows) in enumerate(KV_ROWS):
        firsts[part].wait_all()
        mine = spot[ORDERS[part][0]]
        for index in range(2):
            r.kv_sum[index, row : row + rows] = add_all(
                [r.f1[part][mine, index]] + [r.r1[part][step, index] for step in range(3)]
            )


def keys_values_back(r):
    lanes = []
    for lane in range(4):
        pieces = [
            r.kv_sum[block, unit_rows(token, lane)] for block in range(2) for token in range(4)
        ]
        lanes.append(jnp.concatenate(pieces, axis=0))
    grad_keys = jnp.concatenate(lanes[:2], axis=1)
    grad_values = jnp.concatenate(lanes[2:], axis=1)
    back, term = norm_back(r.key_raw[...], gain(r, G_KEY), rope_back(r, grad_keys))
    note_gain(r, G_KEY, term)
    kv_low = jnp.concatenate([back, grad_values], axis=1).astype(BF16)
    terms = dot_tn(r.normed_split[...], kv_low)
    r.stage[SMALL : 2 * SMALL] = jnp.zeros((SMALL, 128), F32)
    for tile in range(4):
        lanes = slice(128 * tile, 128 * tile + 128)
        r.stage[pl.ds(tile, 512, stride=4)] = terms[:512, lanes]
        r.stage[pl.ds(SMALL + tile, 128, stride=16)] = terms[512:, lanes]
    grad_split = dot_nt(kv_low, r.w_kv[...]).astype(BF16)
    grad_normed = dot_nt(grad_split, r.splitting[...]) + r.grad_normed[...]
    back, term = norm_back(r.x[...], gain(r, G_ATTN), grad_normed)
    note_gain(r, G_ATTN, term)
    r.tokens_grad[...] = low_first(r, (r.grad_mid[...] + back).astype(BF16))
    held = jnp.zeros((128, 128), F32)
    for number, (at, count, _, _) in enumerate(GAINS):
        lanes, owners = gain_maps(r, number)
        term = jnp.where(owners, r.gain_sums[0:1, at : at + count], 0.0).astype(BF16)
        held += dot_nt(term, lanes)
    r.stage[pl.ds(SMALL + 4, 128, stride=16)] = held
    for unit in range(2):
        for core in range(2):
            for plane in range(4):
                row = SMALL * unit + 1024 * core + 256 * plane
                r.u[unit][core, plane] = r.stage[row : row + 256].astype(BF16).reshape(4, 4, 16, 128)


def small_sums(r, between):
    links = r.links
    core = lax.axis_index("dp")
    spot = place()
    overs = [links.across(ref.at[1 - core], lambda at, to=to: to, to) for ref, to in zip(r.u, r.vh)]
    axes = ((X, Y, Z), (Y, Z, X))
    rings = []
    for unit, order in enumerate(axes):
        half, own, land = r.vh[unit], r.u[unit], r.land3[unit]
        overs[unit].wait()

        def join(number, half=half, own=own):
            at = (number // 4, number % 4)
            index = (core, *at)
            own[index] = (own[index].astype(F32) + half[at].astype(F32)).astype(BF16)

        loop(16, join)
        axis = order[0]
        rings.append(
            links.ring(
                axis,
                lambda step, own=own, axis=axis: own.at[core, shifted(spot[axis], step)],
                lambda step, at, land=land: land.at[step - 1],
                land,
            )
        )
    between[0]()
    later = []
    for unit, order in enumerate(axes):
        own, land, out, to = r.u[unit], r.land3[unit], r.sum2[unit], r.land2[unit]
        rings[unit].wait_all()
        mine = spot[order[0]]

        def add(at, own=own, land=land, out=out, mine=mine):
            out[at] = add_all([own[core, mine, at]] + [land[step, at] for step in range(3)]).astype(
                BF16
            )

        loop(4, add)
        axis = order[1]
        later.append(
            links.ring(
                axis,
                lambda step, out=out, axis=axis: out.at[shifted(spot[axis], step)],
                lambda step, at, to=to: to.at[step - 1],
                to,
            )
        )
    between[1]()
    last = []
    for unit, order in enumerate(axes):
        own, land, out, to = r.sum2[unit], r.land2[unit], r.sum1[unit], r.land1[unit]
        later[unit].wait_all()
        out[...] = add_all([own[spot[order[1]]]] + [land[step] for step in range(3)]).astype(BF16)
        axis = order[2]
        last.append(
            links.ring(
                axis,
                lambda step, out=out, axis=axis: out.at[shifted(spot[axis], step)],
                lambda step, at, to=to: to.at[step - 1],
                to,
            )
        )
    between[2]()
    for unit, order in enumerate(axes):
        last[unit].wait_all()
        r.fk[16 * unit : 16 * unit + 16] = add_all(
            [r.sum1[unit][spot[order[2]]]] + [r.land1[unit][step] for step in range(3)]
        )


def layer(r):
    greet()
    pack(r)
    greeted()
    early_rings, early_held, spreads = early(r)
    unpack_small(r)
    keys_values(r)
    firsts = gather_first(r)
    seconds = gather_second(r, firsts)
    early_pieces = (ASK, OUT, GATE_ONE, UP_ONE, DOWN_ONE)
    for piece in early_pieces:
        spreads[piece].forward()
    before = tuple(r.links.open)
    for piece in LATE_PIECES:
        spreads[piece] = Spread(r, piece)
    thirds, specials = gather_third(r, seconds)
    for piece in early_pieces:
        spreads[piece].pass_on()
    for piece in LATE_PIECES:
        spreads[piece].forward()
    spreads[ASK].finish()
    queries(r)

    def pass_on(number):
        if number == 0:
            r.links.settle(before)
        if number == 2:
            for piece in LATE_PIECES:
                spreads[piece].pass_on()

    attention(r, thirds, specials, pass_on)
    feed_forward(r, spreads)
    before = tuple(r.links.open)
    halves = feed_forward_back(r, spreads)
    sums = {}

    def start_sums(*pieces):
        for piece in pieces:
            sums[piece] = Gather(r, piece, halves[piece])

    def relay(*pieces):
        for piece in pieces:
            sums[piece].relay()

    def between(number):
        pass

    thirds, third_specials = attention_back(r, between)
    halves[ASK] = queries_back(r, spreads)
    for ring in early_rings:
        ring.sent()
    for ring in seconds:
        ring.sent()
    r.links.settle(before)
    before = tuple(r.links.open)
    start_sums(GATE_ONE, UP_ONE, DOWN_ONE, GATE_TWO, UP_TWO, DOWN_TWO, OUT, ASK)
    seconds = scatter_second(r, thirds, third_specials)
    relay(GATE_ONE, UP_ONE, DOWN_ONE, OUT)
    firsts = scatter_first(r, seconds)
    relay(GATE_TWO, UP_TWO, DOWN_TWO, ASK)
    scatter_end(r, firsts)
    for copy in early_held:
        copy.sent()
    keys_values_back(r)
    late = {}

    def begin_late():
        r.links.settle(before)
        repack(r, DOWN, sums[DOWN_ONE], sums[DOWN_TWO])
        late[2] = late_second(r, 2)
        repack(r, GATE, sums[GATE_ONE], sums[GATE_TWO])
        repack(r, OUTPUT, sums[OUT])
        late[0] = late_second(r, 0)
        repack(r, UP, sums[UP_ONE], sums[UP_TWO])
        repack(r, QUERY, sums[ASK])
        late[1] = late_second(r, 1)

    def go_on_late():
        r.links.settle(tuple(r.links.open)[:-10])
        for part in (2, 0, 1):
            late[part] = late_first(r, part, late[part])

    def finish_late():
        for part, out in enumerate((r.fa, r.fb, r.fc)):
            late_end(r, part, late[part], out)

    small_sums(r, (begin_late, go_on_late, finish_late))
    r.links.settle()
    assert (r.links.sending, r.links.receiving) <= COPIES and r.links.receiving <= COPIES[1]


def end(r):
    def rows(out, source, base, count, tiles):
        r.stage[base : base + count * tiles] = source
        for tile in range(tiles):
            out[:, 128 * tile : 128 * tile + 128] = columns_of(r, base, count, tiles, tile)

    rows(r.gate_grad, r.fa[0:80], 0, 5, 16)
    rows(r.output_grad, r.fa[80:120], 80, 8, 5)
    rows(r.up_grad, r.fb[0:80], 128, 5, 16)
    rows(r.query_grad, r.fb[80:120], 208, 5, 8)
    rows(r.down_grad, r.fc[...], 256, 16, 5)
    r.stage[336:368] = r.fk[...]
    for tile in range(4):
        out = (r.key_grad, r.value_grad)[tile // 2]
        half = 128 * (tile % 2)
        out[:, half : half + 128] = columns_of(r, 336, 5, 4, tile)
    line = r.fk[16:24]
    gain_grads = (r.grad_attn_norm, r.grad_post_attn, r.grad_ffn_norm, r.grad_post_ffn, r.grad_q, r.grad_k)
    for number, (_, _, held, lane) in enumerate(GAINS):
        out = gain_grads[number]
        moved = line if lane == 0 else pltpu.roll(line, 128 - lane, 1)
        out[...] = moved[4:5, :held]
    r.final_out[0] = r.block_out[...]
    r.final_grad[0] = r.tokens_grad[...]


COPIES = (96, 160)


def by_part(*dims):
    return [hold(BF16, *dims, rows, 128) for _, rows in KV_ROWS]


def by_flat(*dims):
    return [hold(BF16, *dims, rows, 128) for rows in (128, 128, 80)]


def by_unit(*dims):
    return [hold(BF16, *dims, 16, 128) for _ in range(2)]


def by_weight(lead, core):
    return [
        hold(BF16, *core, *lead, 80, 2048),
        hold(BF16, *core, *lead, 128, 640),
        hold(BF16, *core, *lead, 80, 2048),
        hold(BF16, *core, *lead, 80, 1024),
        hold(BF16, *core, *lead, 4, 4, 16, 640),
    ]


def buffers():
    return dict(
        stage=hold(F32, 4096, 128),
        x=hold(F32, 128, 640),
        cos=hold(F32, 128, 128),
        sin=hold(F32, 128, 128),
        gains=hold(F32, 8, 3072),
        gain_sums=hold(F32, 8, 3072),
        turning=hold(BF16, 640, 640),
        splitting=hold(BF16, 640, 640),
        key_base=hold(jnp.int32, 32, 16, 128),
        key_rows=hold(jnp.int32, 32, 256),
        p=by_flat(4, 4),
        second=by_flat(3, 4),
        line=by_flat(4),
        first=by_flat(3),
        u=by_unit(2, 4, 4, 4),
        vh=by_unit(4, 4, 4),
        land3=by_unit(3, 4, 4),
        sum2=by_unit(4, 4),
        land2=by_unit(3, 4),
        sum1=by_unit(4),
        land1=by_unit(3),
        w_kv=hold(BF16, 640, 512),
        w=by_weight((4,), (2,)),
        half=by_weight((4,), ()),
        landed=[
            hold(BF16, 3, 80, 2048),
            hold(BF16, 3, 128, 640),
            hold(BF16, 3, 80, 2048),
            hold(BF16, 3, 80, 1024),
            hold(BF16, 3, 4, 4, 16, 640),
        ],
        kv3=hold(BF16, 2, 256, 128),
        f1=by_part(4, 2),
        g2=by_part(4, 8),
        sel=by_part(3, 4, 4),
        sp=by_part(),
        rsp=by_part(4),
        rb=by_part(3, 4, 4),
        rs=by_part(3),
        r2=by_part(3, 8),
        r1=by_part(3, 2),
        slots=hold(BF16, 4, 4, 4, 256, 128),
        extra=hold(BF16, 3, 256, 128),
        grad_extra=hold(BF16, 3, 256, 128),
        kv_sum=hold(F32, 2, 256, 128),
        normed=hold(BF16, 128, 640),
        normed_split=hold(BF16, 128, 640),
        normed_b=hold(BF16, 128, 640),
        key_raw=hold(F32, 128, 256),
        query_raw=hold(F32, 128, 1024),
        query=hold(BF16, 512, 256),
        attn=hold(F32, 512, 256),
        total=hold(F32, 512, 128),
        dots=hold(F32, 512, 128),
        attn_low=hold(BF16, 128, 1024),
        proj=hold(F32, 128, 640),
        mid=hold(F32, 128, 640),
        ffn_in=hold(BF16, 128, 640),
        ffn_in_b=hold(BF16, 128, 640),
        gate=hold(F32, 128, 2048),
        up=hold(F32, 128, 2048),
        hidden=hold(BF16, 128, 2048),
        ffn_out=hold(F32, 128, 640),
        low_grad=hold(BF16, 128, 640),
        grad_mid=hold(F32, 128, 640),
        grad_attn=hold(BF16, 512, 256),
        grad_query=hold(F32, 512, 256),
        query_low=hold(BF16, 128, 1024),
        grad_normed=hold(F32, 128, 640),
    )


def on_device(
    tokens,
    doc_lengths,
    block_order,
    attn_norm,
    query_weight,
    key_weight,
    value_weight,
    query_gain,
    key_gain,
    output_weight,
    attn_post_norm,
    ffn_norm,
    gate_weight,
    up_weight,
    down_weight,
    ffn_post_norm,
    out_cot,
):
    made = run(
        layer,
        dict(block_order=block_order, doc_lengths=doc_lengths),
        dict(
            tokens=tokens,
            out_cot=out_cot,
            attn_norm=attn_norm[None],
            attn_post_norm=attn_post_norm[None],
            ffn_norm=ffn_norm[None],
            ffn_post_norm=ffn_post_norm[None],
            query_gain=query_gain[None],
            key_gain=key_gain[None],
            table=jnp.asarray(number_table()),
            frequency=jnp.asarray(ROPE_BASE ** (-2.0 * np.arange(128) / 256), F32)[None],
            gate_weight=gate_weight,
            output_weight=output_weight,
            up_weight=up_weight,
            query_weight=query_weight,
            down_weight=down_weight,
            key_weight=key_weight,
            value_weight=value_weight,
        ),
        dict(
            block_out=hold(BF16, 128, 640),
            tokens_grad=hold(BF16, 128, 640),
            fa=hold(F32, 128, 128),
            fb=hold(F32, 128, 128),
            fc=hold(F32, 80, 128),
            fk=hold(F32, 32, 128),
        ),
        buffers(),
        number=1,
        copies=COPIES,
    )
    results = run(
        end,
        {},
        made,
        dict(
            final_out=hold(BF16, 1, 128, 640),
            final_grad=hold(BF16, 1, 128, 640),
            grad_attn_norm=hold(F32, 1, 5),
            query_grad=hold(F32, 5, 1024),
            key_grad=hold(F32, 5, 256),
            value_grad=hold(F32, 5, 256),
            grad_q=hold(F32, 1, 2),
            grad_k=hold(F32, 1, 2),
            output_grad=hold(F32, 8, 640),
            grad_post_attn=hold(F32, 1, 5),
            grad_ffn_norm=hold(F32, 1, 5),
            gate_grad=hold(F32, 5, 2048),
            up_grad=hold(F32, 5, 2048),
            down_grad=hold(F32, 16, 640),
            grad_post_ffn=hold(F32, 1, 5),
        ),
        dict(stage=hold(F32, 3088, 128)),
    )
    return tuple(
        value.reshape(-1) if value.shape[0] == 1 and value.ndim == 2 else value
        for value in results.values()
    )


def solution(mesh):
    rows = P(("dp", "ctx"), None)
    vector = P(("dp", "ctx"))
    stream = P("dp", "ctx", None)
    return jax.shard_map(
        on_device,
        mesh=mesh,
        in_specs=(
            stream,
            P("dp", None),
            P(),
            vector,
            rows,
            rows,
            rows,
            vector,
            vector,
            rows,
            vector,
            vector,
            rows,
            rows,
            rows,
            vector,
            stream,
        ),
        out_specs=(
            stream,
            stream,
            vector,
            rows,
            rows,
            rows,
            vector,
            vector,
            rows,
            vector,
            vector,
            rows,
            rows,
            rows,
            vector,
        ),
        check_vma=False,
    )
```

```python
from types import SimpleNamespace

import jax
import jax.numpy as jnp
import numpy as np
from jax import lax
from jax.experimental import pallas as pl
from jax.experimental.pallas import tpu as pltpu
from jax.sharding import PartitionSpec as P

EPSILON = 1e-06
ROPE_BASE = 1000000.0
MESH = pl.DeviceIdType.MESH
F32 = jnp.float32
BF16 = jnp.bfloat16
MIB = 2**20

X, Y, Z = 0, 1, 2
ORDERS = ((Z, Y, X), (X, Z, Y), (Y, X, Z))
UNITS = (
    ((0, 0), (0, 1), (0, 2), (0, 3), (3, 0))
    + ((1, 0), (1, 1), (1, 2), (1, 3), (3, 1))
    + ((2, 0), (2, 1), (2, 2), (2, 3), (3, 2), (3, 3))
)
KV_ROWS = ((0, 80), (80, 80), (160, 96))
HEADS = 4
HEAD = 256
SCALE = HEAD**-0.5
LOG2E = 1.4426950408889634


def place():
    chip = lax.axis_index("ctx")
    return (chip // 16, (chip // 4) % 4, chip % 4)


def shifted(value, step):
    return lax.rem(value + step + 4, 4)


def peer(axis, step):
    spot = list(place())
    spot[axis] = shifted(spot[axis], step)
    return (lax.axis_index("dp"), spot[0] * 16 + spot[1] * 4 + spot[2])


def other_core():
    return (1 - lax.axis_index("dp"), lax.axis_index("ctx"))


def greet():
    barrier = pltpu.get_barrier_semaphore()
    for axis in (X, Y, Z):
        for step in (1, 2, 3):
            pl.semaphore_signal(barrier, inc=1, device_id=peer(axis, step), device_id_type=MESH)
    pl.semaphore_signal(barrier, inc=1, device_id=other_core(), device_id_type=MESH)


def greeted():
    pl.semaphore_wait(pltpu.get_barrier_semaphore(), 10)


class Ring:
    def __init__(self, links, axis, source, landing, whole, steps, apart, sends):
        self.links, self.axis, self.source, self.landing = links, axis, source, landing
        self.whole, self.apart = whole, apart
        self.sends = links.sends(whole) if sends is None else sends
        if apart:
            self.numbers = {step: links.receive() for step in steps}
        else:
            self.numbers = dict.fromkeys(steps, links.receive())

    def copy(self, step, sender):
        return self.links.copy(
            self.sends,
            self.numbers[step],
            self.source(step),
            self.landing(step, sender),
            peer(self.axis, step),
        )

    def start(self, step, *index):
        source, landing = self.source(step), self.landing(step, place()[self.axis])
        if index:
            source, landing = source.at[index], landing.at[index]
        self.links.copy(
            self.sends, self.numbers[step], source, landing, peer(self.axis, step)
        ).start()

    def wait(self, step):
        self.copy(step, shifted(place()[self.axis], -step)).wait_recv()

    def wait_all(self):
        if self.apart:
            for step in self.numbers:
                self.wait(step)
        else:
            step = next(iter(self.numbers))
            self.links.copy(
                self.sends, self.numbers[step], self.whole, self.whole, peer(self.axis, step)
            ).wait_recv()

    def sent(self):
        self.links.settle((self.sends,))


class Across:
    def __init__(self, links, whole):
        self.links, self.whole = links, whole
        self.sends, self.number = links.sends(whole), links.receive()

    def add(self, source, landing):
        there = landing(lax.axis_index("dp"))
        self.links.copy(self.sends, self.number, source, there, other_core()).start()

    def wait(self):
        self.links.copy(
            self.sends, self.number, self.whole, self.whole, other_core()
        ).wait_recv()

    def sent(self):
        self.links.settle((self.sends,))


class Links:
    def __init__(self, send, recv):
        self.send, self.recv = send, recv
        self.sending, self.receiving, self.open = 0, 0, {}

    def sends(self, whole):
        self.open[self.sending] = whole
        self.sending += 1
        return self.sending - 1

    def receive(self):
        self.receiving += 1
        return self.receiving - 1

    def copy(self, send, recv, source, landing, device):
        return pltpu.make_async_remote_copy(
            src_ref=source,
            dst_ref=landing,
            send_sem=self.send.at[send],
            recv_sem=self.recv.at[recv],
            device_id=device,
            device_id_type=MESH,
        )

    def ring(
        self, axis, source, landing, whole, begin=True, steps=(1, 2, 3), apart=False, sends=None
    ):
        ring = Ring(self, axis, source, landing, whole, steps, apart, sends)
        if begin:
            for step in steps:
                ring.start(step)
        return ring

    def across(self, source, landing, whole):
        across = Across(self, whole)
        across.add(source, landing)
        return across

    def settle(self, numbers=None):
        for number in tuple(self.open if numbers is None else numbers):
            if number in self.open:
                whole = self.open.pop(number)
                self.copy(number, 0, whole, whole, other_core()).wait_send()


VMEM = pl.BlockSpec(memory_space=pltpu.VMEM)
SMEM = pl.BlockSpec(memory_space=pltpu.SMEM)
ANY = pl.BlockSpec(memory_space=pl.ANY)


def hold(kind, *shape):
    return pltpu.VMEM(shape, kind)


def run(stage, numbers, ins, outs, scratch, number=None, copies=(), fetched={}):
    flat, shape = jax.tree.flatten(scratch, is_leaf=lambda leaf: not isinstance(leaf, (dict, list)))

    def kernel(*refs):
        count = len(numbers) + len(fetched) + len(ins) + len(outs)
        named = dict(zip((*numbers, *fetched, *ins, *outs), refs))
        rest = refs[count + len(flat) :]
        r = SimpleNamespace(**named)
        vars(r).update(jax.tree.unflatten(shape, refs[count : count + len(flat)]))
        r.fetches = {}
        for at, name in enumerate(fetched):
            held = rest[at]
            copy = pltpu.make_async_copy(named[name], held, rest[len(fetched)].at[at])
            copy.start()
            r.fetches[name] = copy
            setattr(r, name, held)
        if copies:
            r.links = Links(*rest[-2:])
        stage(r)

    remote = dict(collective_id=number, has_side_effects=True) if copies else {}
    results = pl.pallas_call(
        kernel,
        out_shape=[jax.ShapeDtypeStruct(out.shape, out.dtype) for out in outs.values()],
        in_specs=[SMEM] * len(numbers) + [ANY] * len(fetched) + [VMEM] * len(ins),
        out_specs=[VMEM] * len(outs),
        scratch_shapes=flat
        + [pltpu.VMEM(value.shape, value.dtype) for value in fetched.values()]
        + ([pltpu.SemaphoreType.DMA((len(fetched),))] if fetched else [])
        + [pltpu.SemaphoreType.DMA((count,)) for count in copies],
        compiler_params=pltpu.CompilerParams(vmem_limit_bytes=60 * MIB, **remote),
    )(*numbers.values(), *fetched.values(), *ins.values())
    return dict(zip(outs, results))


def dot32(left, right):
    return jnp.dot(left, right, preferred_element_type=F32)


def dot_nt(left, right):
    return lax.dot_general(left, right, (((1,), (1,)), ((), ())), preferred_element_type=F32)


def dot_tn(left, right):
    return lax.dot_general(left, right, (((0,), (0,)), ((), ())), preferred_element_type=F32)


def add_all(values):
    total = values[0].astype(F32)
    for value in values[1:]:
        total += value.astype(F32)
    return total


def loop(count, body):
    def step(number, unused):
        body(number)
        return unused

    lax.fori_loop(0, count, step, 0)


def my_low(r):
    chip = lax.axis_index("ctx")
    return jnp.minimum(r.block_order[2 * chip], r.block_order[2 * chip + 1])


def low_of(r, chip):
    return jnp.minimum(r.block_order[2 * chip], r.block_order[2 * chip + 1])


def low_first(r, rows):
    chip = lax.axis_index("ctx")
    flip = r.block_order[2 * chip] > r.block_order[2 * chip + 1]
    return jnp.where(flip, jnp.concatenate([rows[64:], rows[:64]], axis=0), rows)


def document_starts(r, places):
    start = jnp.zeros_like(places)
    at = 0
    for number in range(1, 8):
        at = at + r.doc_lengths[0, number - 1]
        start = jnp.where(places >= at, at, start)
    return start


def places_of(r, within, high):
    low = my_low(r)
    return jnp.where(high, 127 - low, low) * 64 + within


def number_table():
    def turned_device(device):
        core, x, y, z = device // 64, (device // 16) % 4, (device // 4) % 4, device % 4
        return ((core * 4 + y) * 4 + z) * 4 + x

    table = np.zeros((8, 640), np.int32)
    k = np.arange(640)
    table[0], table[1] = k % 5, turned_device(k // 5)
    core, y, z, x, row = k // 320, (k // 80) % 4, (k // 20) % 4, (k // 5) % 4, k % 5
    table[2] = (((core * 4 + x) * 4 + y) * 4 + z) * 5 + row
    table[3, :512] = 5 * (k[:512] // 4) + k[:512] % 4
    device = np.arange(128)
    table[3, 512 + turned_device(device)] = 5 * device + 4
    table[4, :256], table[5, :256] = k[:256] % 2, turned_device(k[:256] // 2)
    return table


def one_hot(rows, numbers):
    shape = (rows, numbers.shape[1])
    return jnp.where(lax.broadcasted_iota(jnp.int32, shape, 0) == numbers, 1.0, 0.0).astype(BF16)


GAINS = ((0, 640, 5, 0), (640, 640, 5, 5), (1280, 640, 5, 10), (1920, 640, 5, 15))
GAINS += ((2560, 256, 2, 20), (2816, 256, 2, 22))
G_ATTN, G_POST_ATTN, G_FFN, G_POST_FFN, G_QUERY, G_KEY = range(6)


def gain_maps(r, number):
    _, columns, held, lane = GAINS[number]
    row = 0 if held == 5 else 4
    rest, owner = r.table[row : row + 1, :columns], r.table[row + 1 : row + 2, :columns]
    lanes = one_hot(128, rest + lane)
    owners = lax.broadcasted_iota(jnp.int32, (128, columns), 0) == owner
    return lanes, owners


def gain(r, number):
    at, columns, _, _ = GAINS[number]
    return r.gains[0:1, at : at + columns]


def rows_of(r, base, weight, count):
    tiles = weight.shape[1] // 128
    for tile in range(tiles):
        r.stage[pl.ds(base + tile, count, stride=tiles)] = weight[
            :, 128 * tile : 128 * tile + 128
        ].astype(F32)


def columns_of(r, base, count, tiles, tile):
    return r.stage[pl.ds(base + tile, count, stride=tiles)]


def pack(r):
    rows_of(r, 0, r.gate_weight, 5)
    rows_of(r, 80, r.output_weight, 8)
    rows_of(r, 128, r.up_weight, 5)
    rows_of(r, 208, r.query_weight, 5)
    rows_of(r, 256, r.down_weight, 16)
    for tile in range(4):
        weight = (r.key_weight, r.value_weight)[tile // 2]
        half = 128 * (tile % 2)
        r.stage[pl.ds(336 + tile, 5, stride=4)] = weight[:, half : half + 128].astype(F32)
    r.stage[356:357] = jnp.zeros((1, 128), F32)
    own = (r.attn_norm, r.attn_post_norm, r.ffn_norm, r.ffn_post_norm, r.query_gain, r.key_gain)
    for ref, (_, _, held, lane) in zip(own, GAINS):
        r.stage[356:357, lane : lane + held] = ref[...].astype(F32)
    spot = place()
    for number, ref in enumerate(r.p):
        first, second, _ = weight_order(number)
        rows = ref.shape[2]
        start = (0, 80, 128, 208, 256)[number]
        ref[spot[second], spot[first]] = r.stage[start : start + rows].astype(BF16)
    core = lax.axis_index("dp")
    x, y, z = spot
    r.u[0][core, x, y, z] = r.stage[336:352].astype(BF16)
    r.u[1][core, y, z, x] = r.stage[352:368].astype(BF16)


def tables(r):
    r.x[...] = low_first(r, r.tokens[0].astype(F32))
    rows = lax.broadcasted_iota(jnp.int32, (128, 1), 0)
    places = places_of(r, rows % 64, rows >= 64)
    position = (places - document_starts(r, places)).astype(F32)
    angles = position * r.frequency[...]
    r.cos[...] = jnp.cos(angles)
    r.sin[...] = jnp.sin(angles)
    r.turning[...] = one_hot(640, r.table[2:3])
    r.splitting[...] = one_hot(640, r.table[3:4])


NEVER = -(1 << 20)


def key_tables(r):
    mine = my_low(r)

    def chunk(number, token):
        plane = number % 4
        row = 4 * token + number
        for slot in range(16):
            spot = [slot // 4, slot % 4]
            spot.insert(chunk_axis(token), plane)
            low = low_of(r, spot[0] * 16 + spot[1] * 4 + spot[2])
            chosen = jnp.where(low < mine, low, 127 - low) * 64
            for_low = jnp.where(low < mine, chosen, NEVER)
            for_high = jnp.where(low == mine, NEVER, chosen)
            r.key_base[row, slot : slot + 1] = jnp.full((1, 128), for_low, jnp.int32)
            r.key_base[16 + row, slot : slot + 1] = jnp.full((1, 128), for_high, jnp.int32)

    for token in range(4):
        loop(4, lambda number, token=token: chunk(number, token))

    def turn(row):
        r.key_rows[pl.ds(row, 1)] = jnp.transpose(key_column(r, row, (row // 4) % 4))[0:1]

    loop(32, turn)


def key_column(r, row, token):
    base = jnp.broadcast_to(r.key_base[row][:, None, :], (16, 16, 128)).reshape(256, 128)
    return base + (lax.broadcasted_iota(jnp.int32, (256, 128), 0) % 16 + 16 * token)


def early(r):
    links = r.links
    core = lax.axis_index("dp")
    spot = place()
    x, y, z = spot

    def small(axis, unit, index_of):
        ref = r.u[unit]
        ring = links.ring(
            axis,
            lambda step: ref.at[index_of(spot[axis])],
            lambda step, at: ref.at[index_of(at)],
            ref.at[index_of(pl.ds(0, 3))],
        )
        held.append(ring)
        return ring

    held = []

    one = small(Z, 0, lambda at: (core, x, y, at))
    two = small(X, 1, lambda at: (core, y, z, at))
    rings = []
    for number, ref in enumerate(r.p):
        first, second, _ = weight_order(number)
        row = spot[second]
        rings.append(
            links.ring(
                first,
                lambda step, ref=ref, row=row, first=first: ref.at[row, spot[first]],
                lambda step, at, ref=ref, row=row: ref.at[row, at],
                ref.at[row, pl.ds(0, 3)],
            )
        )
    tables(r)
    one.wait_all()
    one = small(Y, 0, lambda at: (core, x, at))
    two.wait_all()
    two = small(Z, 1, lambda at: (core, y, at))
    for number, ref in enumerate(r.p):
        rings[number].wait_all()
        second = weight_order(number)[1]
        rings.append(
            links.ring(
                second,
                lambda step, ref=ref, second=second: ref.at[spot[second]],
                lambda step, at, ref=ref: ref.at[at],
                ref.at[pl.ds(0, 3)],
            )
        )
    key_tables(r)
    one.wait_all()
    one = small(X, 0, lambda at: (core, at))
    two.wait_all()
    two = small(Y, 1, lambda at: (core, at))
    spreads = {}

    def begin(*numbers):
        for number in numbers:
            rings[5 + number].wait_all()
            unpack(r, number)
            for piece in EARLY_PIECES[number]:
                spreads[piece] = Spread(r, piece)

    begin(DOWN, GATE, OUTPUT)
    one.wait_all()
    three = links.across(r.u[0].at[core], lambda at: r.u[0].at[at], r.u[0].at[core])
    two.wait_all()
    four = links.across(r.u[1].at[core], lambda at: r.u[1].at[at], r.u[1].at[core])
    begin(QUERY, UP)
    three.wait()
    four.wait()
    return rings, held + [three, four], spreads


SMALL = 2048


def unpack_small(r):
    for unit in range(2):
        for core in range(2):
            for plane in range(4):
                row = SMALL * unit + 1024 * core + 256 * plane
                r.stage[row : row + 256] = r.u[unit][core, plane].astype(F32).reshape(256, 128)
    for tile in range(4):
        lanes = slice(128 * tile, 128 * tile + 128)
        r.w_kv[:512, lanes] = columns_of(r, 0, 512, 4, tile).astype(BF16)
        r.w_kv[512:, lanes] = columns_of(r, SMALL, 128, 16, tile).astype(BF16)
    held = columns_of(r, SMALL, 128, 16, 4).astype(BF16)
    for number, (at, columns, _, _) in enumerate(GAINS):
        lanes, owners = gain_maps(r, number)
        spread = jnp.where(owners, dot32(held, lanes), 0.0)
        r.gains[0:1, at : at + columns] = jnp.sum(spread, axis=0, keepdims=True)


WEIGHTS = ((0, 80, False), (0, 40, False), (1, 80, False), (1, 40, False), (2, 80, True))
GATE, OUTPUT, UP, QUERY, DOWN = range(5)


def weight_order(number):
    return ORDERS[WEIGHTS[number][0]]


def own_plane(r, number):
    return weight_plane(r.w[number], number, lax.axis_index("dp"), place()[weight_order(number)[2]])


def weight_plane(ref, number, core, at):
    if WEIGHTS[number][2]:
        return of_plane(ref.at[core], weight_order(number)[2], at)
    return ref.at[core, at]


def plane_tiles(number):
    return ((80, 16), (128, 5), (80, 16), (80, 8), (256, 5))[number]


def unpack(r, number):
    _, rows, by_chip = WEIGHTS[number]
    count, tiles = plane_tiles(number)
    plane = own_plane(r, number)

    def one(chip):
        r.stage[pl.ds(pl.multiple_of(chip * rows, 8), rows)] = r.p[number][
            chip // 4, chip % 4, :rows
        ].astype(F32)

    loop(16, one)
    for tile in range(tiles):
        piece = columns_of(r, 0, count, tiles, tile).astype(BF16)
        lanes = slice(128 * tile, 128 * tile + 128)
        if by_chip:
            plane[:, :, :, lanes] = piece.reshape(4, 4, 16, 128)
        else:
            plane[:, lanes] = piece


def inverse_rms(values):
    return lax.rsqrt(jnp.mean(values * values, axis=-1, keepdims=True) + EPSILON)


def rms_scale(values, weights):
    return values * inverse_rms(values) * weights


def norm_back(values, weights, incoming):
    inverse = inverse_rms(values)
    normal = values * inverse
    scaled = incoming * weights
    back = (scaled - normal * jnp.mean(scaled * normal, axis=-1, keepdims=True)) * inverse
    return back, jnp.sum(incoming * normal, axis=0, keepdims=True)


def rope(r, u):
    cos, sin = r.cos[...], r.sin[...]
    one, two = u[:, :128], u[:, 128:]
    return jnp.concatenate([one * cos - two * sin, two * cos + one * sin], axis=1)


def rope_back(r, e):
    cos, sin = r.cos[...], r.sin[...]
    one, two = e[:, :128], e[:, 128:]
    return jnp.concatenate([one * cos + two * sin, two * cos - one * sin], axis=1)


def turned(r, values):
    return dot32(values, r.turning[...]).astype(BF16)


def unturned(r, values):
    return dot_nt(values.astype(BF16), r.turning[...])


def keys_values(r):
    x = r.x[...]
    normed = rms_scale(x, gain(r, G_ATTN)).astype(BF16)
    r.normed[...] = normed
    r.normed_split[...] = dot32(normed, r.splitting[...]).astype(BF16)
    split = r.normed_split[...].astype(F32)
    none = jnp.zeros((128, 64), F32)
    zero, one = (
        jnp.concatenate(
            [split[:, 256 * core : 256 * core + 256], split[:, 512 + 64 * core : 576 + 64 * core], none],
            axis=1,
        )
        for core in range(2)
    )
    core = lax.axis_index("dp")
    r.both_split[core] = jnp.where(core == 0, zero, one).astype(BF16)
    r.out_split[...] = jnp.where(core == 0, one, zero).astype(BF16)
    raw = dot32(r.normed_split[...], r.w_kv[...])
    r.key_raw[...] = raw[:, :HEAD]
    keys = rope(r, rms_scale(raw[:, :HEAD], gain(r, G_KEY)))
    both = jnp.concatenate([keys, raw[:, HEAD:]], axis=1).astype(BF16)
    for block in range(2):
        for unit, (token, lane) in enumerate(UNITS):
            row = 64 * block + 16 * token
            r.kv3[block, 16 * unit : 16 * unit + 16] = both[
                row : row + 16, 128 * lane : 128 * lane + 128
            ]


def of_plane(ref, axis, at, *rest):
    index = [slice(None)] * 3
    index[axis] = at
    return ref.at[(*index, *rest)]


def chip_of(spot, axis, step):
    spot = list(spot)
    spot[axis] = shifted(spot[axis], step)
    return spot[0] * 16 + spot[1] * 4 + spot[2]


def plane_loop(part, body):
    first, second, last = ORDERS[part]

    def row(i2):
        for i1 in range(4):
            spot = [None] * 3
            spot[first], spot[second], spot[last] = i1, i2, place()[last]
            body(spot, i2, i1)

    loop(4, row)


PIECES = (
    (GATE, 0, 1024),
    (GATE, 1024, 1024),
    (OUTPUT, 0, 640),
    (UP, 0, 1024),
    (UP, 1024, 1024),
    (QUERY, 0, 1024),
    (DOWN, 0, 2),
    (DOWN, 2, 2),
)
GATE_ONE, GATE_TWO, OUT, UP_ONE, UP_TWO, ASK, DOWN_ONE, DOWN_TWO = range(8)
EARLY_PIECES = ((GATE_ONE,), (OUT,), (UP_ONE,), (ASK,), (DOWN_ONE,))
LATE_PIECES = (GATE_TWO, UP_TWO, DOWN_TWO)


def window(ref, dim, first, count):
    index = [slice(None)] * len(ref.shape)
    index[dim] = pl.ds(first, count)
    return ref.at[tuple(index)]


def piece_of(piece, ref, chips=4):
    number, first, count = PIECES[piece]
    rank = len(ref.shape)
    return window(ref, rank - 1 - chips if number == DOWN else rank - 1, first, count)


def half_of(piece, plane, half):
    number, _, count = PIECES[piece]
    if number == DOWN:
        return window(plane, len(plane.shape) - 4, half, 1)
    if number == OUTPUT:
        return window(plane, len(plane.shape) - 2, 64 * half, 64)
    return window(plane, len(plane.shape) - 1, count // 2 * half, count // 2)


def piece_plane(r, piece, core, at):
    number = PIECES[piece][0]
    return piece_of(piece, weight_plane(r.w[number], number, core, at), 3)


def piece_axis(piece):
    return weight_order(PIECES[piece][0])[2]


class Spread:
    def __init__(self, r, piece):
        self.links, axis = r.links, piece_axis(piece)
        self.core, self.mine = lax.axis_index("dp"), place()[axis]
        self.at = lambda core, at: piece_plane(r, piece, core, at)

        def half(at, which):
            return half_of(piece, self.at(self.core, at), which)

        both = piece_of(piece, r.w[PIECES[piece][0]])
        dim = 3 if PIECES[piece][0] == DOWN else 1
        planes = window(both, dim, 0, 3).at[self.core]
        sends = r.links.sends(planes)
        self.near = [
            r.links.ring(
                axis,
                lambda step, which=which: half(self.mine, which),
                lambda step, at, which=which: half(at, which),
                None,
                steps=(1, 3),
                apart=True,
                sends=sends,
            )
            for which in range(2)
        ]

        def passed(step, at):
            return half(shifted(at, -step), 0 if step == 1 else 1)

        self.far = r.links.ring(
            axis,
            lambda step: passed(step, self.mine),
            passed,
            None,
            begin=False,
            steps=(1, 3),
            apart=True,
            sends=sends,
        )
        self.across = Across(r.links, both.at[self.core])
        self.over(self.mine)

    def over(self, at):
        self.across.add(self.at(self.core, at), lambda core: self.at(core, at))

    def forward(self):
        for which, step in enumerate((1, 3)):
            self.near[which].wait(step)
            self.far.start(step)

    def pass_on(self):
        for which, step in enumerate((3, 1)):
            self.near[which].wait(step)
        self.over(shifted(self.mine, 1))
        self.over(shifted(self.mine, 3))
        self.far.wait_all()
        self.over(shifted(self.mine, 2))

    def finish(self):
        self.across.wait()

    def free(self):
        self.far.sent()
        self.across.sent()


def gather_first(r):
    rings = []
    for part, (row, rows) in enumerate(KV_ROWS):
        own = r.kv3.at[:, pl.ds(row, rows)]
        rings.append(
            r.links.ring(
                ORDERS[part][0],
                lambda step, own=own: own,
                lambda step, at, ref=r.f1[part]: ref.at[at],
                r.f1[part].at[pl.ds(0, 3)],
            )
        )
    return rings


def gather_second(r, firsts):
    spot = place()
    rings = []
    for part, (row, rows) in enumerate(KV_ROWS):
        first, second, _ = ORDERS[part]
        f1, g2, mine = r.f1[part], r.g2[part], spot[second]
        f1[spot[first]] = r.kv3[:, row : row + rows]
        firsts[part].wait_all()
        for at in range(4):
            g2[mine, 2 * at] = f1[at, 0]
            g2[mine, 2 * at + 1] = f1[at, 1]
        rings.append(
            r.links.ring(
                second,
                lambda step, g2=g2, mine=mine: g2.at[mine],
                lambda step, at, g2=g2: g2.at[at],
                g2.at[pl.ds(0, 3)],
            )
        )
    return rings


def gather_third(r, seconds):
    spot = place()
    low_me = my_low(r)
    rings, specials = [], []
    for part, (row, rows) in enumerate(KV_ROWS):
        first, second, last = ORDERS[part]
        g2, sel, sp, rsp = r.g2[part], r.sel[part], r.sp[part], r.rsp[part]
        seconds[part].wait_all()
        targets = [low_of(r, chip_of(spot, last, step)) for step in (1, 2, 3)]
        sp[...] = jnp.zeros_like(sp)

        def choose(at, i2, i1, g2=g2, sel=sel, sp=sp, row=row, rows=rows, last=last, targets=targets):
            low = g2[i2, 2 * i1]
            high = g2[i2, 2 * i1 + 1]
            source = low_of(r, chip_of(at, last, 0))
            plane = [at[axis] for axis in (X, Y, Z) if axis != last]
            r.slots[at[0], at[1], at[2], pl.ds(row, rows)] = jnp.where(source < low_me, low, high)
            for step in (1, 2, 3):
                sel[step - 1, plane[0], plane[1]] = jnp.where(
                    source < targets[step - 1], low, high
                )
            sp[...] = jnp.where(source == 63, low, sp[...])

        plane_loop(part, choose)
        rings.append(
            r.links.ring(
                last,
                lambda step, sel=sel: sel.at[step - 1],
                lambda step, at, row=row, rows=rows, last=last: of_plane(
                    r.slots, last, at, pl.ds(row, rows)
                ),
                sel,
                apart=True,
            )
        )
        specials.append(
            r.links.ring(
                last,
                lambda step, sp=sp: sp,
                lambda step, at, rsp=rsp: rsp.at[at],
                rsp.at[pl.ds(0, 3)],
            )
        )
    r.extra[0:2] = r.kv3[...]
    return rings, specials


def gather_special(r, specials):
    spot = place()
    for part, (row, rows) in enumerate(KV_ROWS):
        rsp = r.rsp[part]
        specials[part].wait_all()
        rsp[spot[ORDERS[part][2]]] = r.sp[part][...]
        r.extra[2, row : row + rows] = add_all([rsp[at] for at in range(4)]).astype(BF16)


QUARTER = 1.0 / 16
POWER = QUARTER * 1.4426950408889634


def chunk_axis(token):
    return ORDERS[token][2] if token < 3 else X


def chunk_index(token, plane):
    index = [slice(None)] * 3
    index[chunk_axis(token)] = plane
    return tuple(index)


def unit_rows(token, lane):
    return pl.ds(16 * UNITS.index((token, lane)), 16)


def chunk_kv(r, token, plane):
    index = chunk_index(token, plane)
    quarters = [
        r.slots[(*index, unit_rows(token, lane))].reshape(256, 128) for lane in range(4)
    ]
    return jnp.concatenate(quarters[:2], axis=1), jnp.concatenate(quarters[2:], axis=1)


def extra_kv(r):
    quarters = [
        jnp.concatenate(
            [r.extra[block, unit_rows(token, lane)] for block in range(3) for token in range(4)],
            axis=0,
        )
        for lane in range(4)
    ]
    return jnp.concatenate(quarters[:2], axis=1), jnp.concatenate(quarters[2:], axis=1)


def extra_places(r, numbers):
    low = my_low(r)
    block = jnp.where(numbers < 64, low, jnp.where(numbers < 128, 127 - low, 63))
    gone = (numbers >= 128) & (low == 63)
    return jnp.where(gone, 1 << 20, block * 64 + numbers % 64)


def query_places(r, numbers):
    return places_of(r, numbers % 64, numbers >= 256)


def attention(r, thirds, specials, between):
    spot = place()
    numbers = lax.broadcasted_iota(jnp.int32, (512, 1), 0)
    latest = query_places(r, numbers)
    earliest = document_starts(r, latest)
    query = r.query[...]
    r.attn[...] = jnp.zeros_like(r.attn)
    r.total[...] = jnp.zeros_like(r.total)

    def add(weights, values):
        total = weights[:, :128]
        if weights.shape[1] == 256:
            total = total + weights[:, 128:]
            r.total[...] += total
        else:
            r.total[...] += total
            r.total[:, :64] += weights[:, 128:]
        r.attn[...] += dot32(weights.astype(BF16), values)

    def chunk(token, plane):
        keys, values = chunk_kv(r, token, plane)
        scores = dot_nt(query, keys)
        row = 4 * token + plane
        allowed = jnp.concatenate(
            [
                r.key_rows[pl.ds(row, 1)] >= earliest[:256],
                r.key_rows[pl.ds(16 + row, 1)] >= earliest[256:],
            ],
            axis=0,
        )
        add(jnp.where(allowed, jnp.exp2(scores * POWER), 0.0), values)

    for token in range(3):
        chunk(token, spot[chunk_axis(token)])
    between(0)
    for number, step in enumerate((1, 3, 2)):
        for token in range(3):
            thirds[token].wait(step)
            chunk(token, shifted(spot[chunk_axis(token)], -step))
        between(number + 1)
    for plane in range(4):
        chunk(3, plane)
    gather_special(r, specials)
    keys, values = extra_kv(r)
    scores = dot_nt(query, keys)
    places = extra_places(r, lax.broadcasted_iota(jnp.int32, (1, 192), 1))
    allowed = (places >= earliest) & (places <= latest)
    add(jnp.where(allowed, jnp.exp2(scores * POWER), 0.0), values)
    total = jnp.sum(r.total[...], axis=1, keepdims=True)
    r.attn[...] = r.attn[...] / total
    r.total[...] = jnp.broadcast_to(jnp.log2(total), (512, 128))


def attention_back(r, between):
    spot = place()
    numbers = lax.broadcasted_iota(jnp.int32, (1, 512), 1)
    latest = query_places(r, numbers)
    earliest = document_starts(r, latest)
    query, grad_out = r.query[...], r.grad_attn[...]
    log_total = jnp.transpose(r.total[...])[0:1]
    row_dot = jnp.transpose(r.dots[...])[0:1]
    r.grad_query[...] = jnp.zeros_like(r.grad_query)

    def grads_of(keys, values, allowed):
        scores = dot_nt(keys, query)
        probs = jnp.where(allowed, jnp.exp2(scores * POWER - log_total), 0.0)
        grad_probs = dot_nt(values, grad_out)
        grad_scores = (probs * (grad_probs - row_dot)).astype(BF16)
        grad_values = dot32(probs.astype(BF16), grad_out)
        grad_keys = dot32(grad_scores, query) * QUARTER
        r.grad_query[...] += dot_tn(grad_scores, keys)
        return jnp.concatenate([grad_keys, grad_values], axis=1).astype(BF16)

    def chunk(token, plane):
        keys, values = chunk_kv(r, token, plane)
        row = 4 * token + plane
        low, high = key_column(r, row, token), key_column(r, 16 + row, token)
        allowed = jnp.concatenate([low, low, high, high], axis=1) >= earliest
        grads = grads_of(keys, values, allowed)
        index = chunk_index(token, plane)
        for lane in range(4):
            r.slots[(*index, unit_rows(token, lane))] = grads[
                :, 128 * lane : 128 * lane + 128
            ].reshape(4, 4, 16, 128)

    every = (slice(None), slice(None))
    rings, specials = scatter_third(r)
    for number, step in enumerate((1, 3, 2)):
        for token in range(3):
            chunk(token, shifted(spot[chunk_axis(token)], step))
            rings[token].start(step, *every, pl.ds(0, 64))
        between(number)
    for plane in range(4):
        chunk(3, plane)
    for step in (1, 3, 2):
        for part, (_, rows) in enumerate(KV_ROWS):
            rings[part].start(step, *every, pl.ds(64, rows - 64))
    between(3)
    keys, values = extra_kv(r)
    places = extra_places(r, lax.broadcasted_iota(jnp.int32, (192, 1), 0))
    grads = grads_of(keys, values, (places >= earliest) & (places <= latest))
    for block in range(3):
        for unit, (token, lane) in enumerate(UNITS):
            row = 64 * block + 16 * token
            r.grad_extra[block, 16 * unit : 16 * unit + 16] = grads[
                row : row + 16, 128 * lane : 128 * lane + 128
            ]
    for ring in specials:
        for step in (1, 2, 3):
            ring.start(step)
    for token in range(3):
        chunk(token, spot[chunk_axis(token)])
    return rings, specials


GELU = 0.7978845608028654


def head_rows(block, head):
    start = 256 * block + 64 * head
    return slice(start, start + 64)


def queries(r):
    r.normed_b[...] = turned(r, r.normed[...])
    split_rows(r.both_normed, r.out_normed, r.normed_b[...])
    shared = share(r, r.both_normed, r.out_normed)
    r.query_raw[...] = dot32(r.normed_b[...], r.w[QUERY][...].reshape(640, 1024))
    for head in range(HEADS):
        raw = r.query_raw[:, HEAD * head : HEAD * head + HEAD]
        rotated = rope(r, rms_scale(raw, gain(r, G_QUERY))).astype(BF16)
        for block in range(2):
            r.query[head_rows(block, head)] = rotated[64 * block : 64 * block + 64]
    return shared


def gelu_parts(gate):
    inner = jnp.tanh(GELU * (gate + 0.044715 * gate * gate * gate))
    return 0.5 * gate * (1.0 + inner), inner


def columns(weight, at, width):
    rows = 8 * weight.shape[2]
    return weight[:, :, :, at : at + width].reshape(rows, width)


def down_rows(ref, number):
    return ref.at[number // 2, pl.ds(2 * (number % 2), 2)]


def split_rows(both, out, values):
    core = lax.axis_index("dp")
    values = values.astype(F32)
    none = jnp.zeros((128, 64), F32)
    low = jnp.concatenate([values[:, :320], none], axis=1)
    high = jnp.concatenate([values[:, 320:], none], axis=1)
    both[core] = jnp.where(core == 0, low, high).astype(BF16)
    out[...] = jnp.where(core == 0, high, low).astype(BF16)


def share(r, both, source):
    return r.links.across(source, lambda core: both.at[core], source)


def own_columns(ref, width, core):
    return ref.at[:, pl.ds(pl.multiple_of(core * width, width), width)]


def share_columns(r, both, ref):
    core = lax.axis_index("dp")
    width = ref.shape[1] // 2
    both[core] = own_columns(ref, width, core)[...]
    return share(r, both, own_columns(ref, width, 1 - core))


def pair(both):
    return both[...].reshape(256, both.shape[2])


def feed_forward(r, spreads):
    spreads[OUT].finish()
    for block in range(2):
        for head in range(HEADS):
            r.attn_low[64 * block : 64 * block + 64, HEAD * head : HEAD * head + HEAD] = r.attn[
                head_rows(block, head)
            ].astype(BF16)
    shared = {OUTPUT: share_columns(r, r.both_attn, r.attn_low)}
    r.proj[...] = dot32(r.attn_low[...], r.w[OUTPUT][...].reshape(1024, 640))
    r.mid[...] = r.x[...] + rms_scale(r.proj[...], gain(r, G_POST_ATTN))
    r.ffn_in[...] = rms_scale(r.mid[...], gain(r, G_FFN)).astype(BF16)
    r.ffn_in_b[...] = turned(r, r.ffn_in[...])
    for piece in (GATE_ONE, GATE_TWO, UP_ONE, UP_TWO):
        spreads[piece].finish()
    for number in range(4):
        at = slice(512 * number, 512 * number + 512)
        gate = dot32(r.ffn_in[...], columns(r.w[GATE], 512 * number, 512))
        up = dot32(r.ffn_in_b[...], columns(r.w[UP], 512 * number, 512))
        r.gate[:, at] = gate
        r.up[:, at] = up
        r.hidden[:, at] = (gelu_parts(gate)[0] * up).astype(BF16)
    split_rows(r.both_in, r.out_in, r.ffn_in[...])
    shared[GATE] = share(r, r.both_in, r.out_in)
    split_rows(r.both_in_b, r.out_in_b, r.ffn_in_b[...])
    shared[UP] = share(r, r.both_in_b, r.out_in_b)
    shared[DOWN] = share_columns(r, r.both_hidden, r.hidden)
    spreads[DOWN_ONE].finish()
    spreads[DOWN_TWO].finish()
    r.ffn_out[...] = dot32(r.hidden[...], r.w[DOWN][...].reshape(2048, 640))
    out = r.mid[...] + rms_scale(r.ffn_out[...], gain(r, G_POST_FFN))
    r.block_out[...] = low_first(r, out.astype(BF16))
    return shared


def note_gain(r, number, term):
    at, count, _, _ = GAINS[number]
    r.gain_sums[0:1, at : at + count] = term


def feed_forward_back(r, spreads, shared, start):
    core = lax.axis_index("dp")
    for piece in (GATE_ONE, GATE_TWO, OUT, UP_ONE, UP_TWO, DOWN_ONE, DOWN_TWO):
        spreads[piece].free()
    grad_out = low_first(r, r.out_cot[0].astype(F32))
    grad_ffn_out, term = norm_back(r.ffn_out[...], gain(r, G_POST_FFN), grad_out)
    note_gain(r, G_POST_FFN, term)
    low_grad = grad_ffn_out.astype(BF16)
    r.both_low[core] = low_grad
    low_shared = share(r, r.both_low, r.both_low.at[core])
    grad_in = jnp.zeros((128, 640), F32)
    grad_in_b = jnp.zeros((128, 640), F32)
    grads_shared = []
    for number in range(4):
        at = slice(512 * number, 512 * number + 512)
        down = down_rows(r.w[DOWN], number)
        grad_hidden = dot_nt(low_grad, down[...].reshape(512, 640))
        gate, up = r.gate[:, at], r.up[:, at]
        activated, inner = gelu_parts(gate)
        slope = 0.5 * (1.0 + inner) + 0.5 * gate * (1.0 - inner * inner) * GELU * (
            1.0 + 3 * 0.044715 * gate * gate
        )
        grad_gate = (grad_hidden * up * slope).astype(BF16)
        grad_up = (grad_hidden * activated).astype(BF16)
        r.both_gate[core, :, at] = grad_gate
        r.both_up[core, :, at] = grad_up
        grad_in += dot_nt(grad_gate, columns(r.w[GATE], 512 * number, 512))
        grad_in_b += dot_nt(grad_up, columns(r.w[UP], 512 * number, 512))
        if number % 2:
            lanes = pl.ds(512 * number - 512, 1024)
            for both in (r.both_gate, r.both_up):
                grads_shared.append(
                    r.links.across(
                        both.at[core, :, lanes],
                        lambda core, both=both, lanes=lanes: both.at[core, :, lanes],
                        both.at[core, :, lanes],
                    )
                )
    shared[DOWN].wait()
    low_shared.wait()
    term = dot_tn(pair(r.both_hidden), pair(r.both_low)).astype(BF16)
    r.w[DOWN][core] = term.reshape(4, 4, 4, 16, 640)
    start(DOWN_ONE, DOWN_TWO)
    shared[GATE].wait()
    shared[UP].wait()

    def columns_of_both(first):
        for number, ins, both, wait in (
            (GATE, r.both_in, r.both_gate, grads_shared[first // 512]),
            (UP, r.both_in_b, r.both_up, grads_shared[first // 512 + 1]),
        ):
            wait.wait()
            for at in (first, first + 512):
                lanes = slice(at, at + 512)
                term = dot_tn(pair(ins), both[:, :, lanes].reshape(256, 512))[:320].astype(BF16)
                r.w[number][core, :, :, lanes] = term.reshape(4, 80, 512)

    columns_of_both(0)
    start(GATE_ONE, UP_ONE)
    grad_in = grad_in + unturned(r, grad_in_b)
    back, term = norm_back(r.mid[...], gain(r, G_FFN), grad_in)
    note_gain(r, G_FFN, term)
    grad_mid = grad_out + back
    r.grad_mid[...] = grad_mid
    back, term = norm_back(r.proj[...], gain(r, G_POST_ATTN), grad_mid)
    note_gain(r, G_POST_ATTN, term)
    proj_low = back.astype(BF16)
    r.both_proj[core] = proj_low
    proj_shared = share(r, r.both_proj, r.both_proj.at[core])
    grad_attn = dot_nt(proj_low, r.w[OUTPUT][...].reshape(1024, 640)).astype(BF16)
    for block in range(2):
        for head in range(HEADS):
            r.grad_attn[head_rows(block, head)] = grad_attn[
                64 * block : 64 * block + 64, HEAD * head : HEAD * head + HEAD
            ]
    dots = jnp.sum(r.grad_attn[...].astype(F32) * r.attn[...], axis=1, keepdims=True)
    r.dots[...] = jnp.broadcast_to(dots, (512, 128))

    def rest_back():
        columns_of_both(1024)
        shared[OUTPUT].wait()
        proj_shared.wait()
        term = dot_tn(pair(r.both_attn), pair(r.both_proj)).astype(BF16)
        r.w[OUTPUT][core] = term.reshape(4, 128, 640)

    return rest_back


def queries_back(r, spreads, shared):
    core = lax.axis_index("dp")
    total = jnp.zeros((1, HEAD), F32)
    for head in range(HEADS):
        at = slice(HEAD * head, HEAD * head + HEAD)
        grad = jnp.concatenate([r.grad_query[head_rows(block, head)] for block in range(2)], axis=0)
        back, term = norm_back(
            r.query_raw[:, at], gain(r, G_QUERY), rope_back(r, grad * QUARTER)
        )
        total += term
        r.both_query[core, :, at] = back.astype(BF16)
    note_gain(r, G_QUERY, total)
    query_shared = share(r, r.both_query, r.both_query.at[core])
    r.grad_normed[...] = unturned(
        r, dot_nt(r.both_query[core], r.w[QUERY][...].reshape(640, 1024))
    )
    spreads[ASK].free()
    shared[QUERY].wait()
    query_shared.wait()
    term = dot_tn(pair(r.both_normed), pair(r.both_query))[:320].astype(BF16)
    r.w[QUERY][core] = term.reshape(4, 80, 1024)


def add_rows(count, to, value):
    def one(at):
        rows = pl.ds(pl.multiple_of(at * 16, 16), 16)
        to[rows] = (to[rows].astype(F32) + value[rows].astype(F32)).astype(BF16)

    loop(count // 16, one)


def add_into(to, value):
    lead = to.shape[:-2]
    if not lead:
        add_rows(to.shape[0], to, value)
    elif len(lead) == 1:
        for at in range(lead[0]):
            add_rows(to.shape[1], to.at[at], value.at[at])
    else:
        for at in range(lead[0]):
            add_into(to.at[at], value.at[at])


class Gather:
    def __init__(self, r, piece):
        self.piece, axis = piece, piece_axis(piece)
        core, mine = lax.axis_index("dp"), place()[axis]
        number = PIECES[piece][0]
        self.land = piece_of(piece, r.landed[number], 3)
        self.at = lambda step: piece_plane(r, piece, core, shifted(mine, step))
        sends = r.links.sends(self.land)
        self.far = r.links.ring(
            axis,
            lambda step: half_of(piece, self.at(2), 0 if step == 1 else 1),
            lambda step, at: half_of(piece, self.land.at[2], 0 if step == 1 else 1),
            None,
            steps=(1, 3),
            apart=True,
            sends=sends,
        )
        self.near = r.links.ring(
            axis,
            self.at,
            lambda step, at: self.land.at[0 if step == 1 else 1],
            self.land.at[pl.ds(0, 2)],
            begin=False,
            steps=(1, 3),
            sends=sends,
        )

    def relay(self):
        for which, step in enumerate((1, 3)):
            self.far.wait(step)
            add_into(
                half_of(self.piece, self.at(step), which),
                half_of(self.piece, self.land.at[2], which),
            )
            self.near.start(step)


def repack(r, number, *gathers):
    _, rows, by_chip = WEIGHTS[number]
    count, tiles = plane_tiles(number)
    own, land = own_plane(r, number), r.landed[number]
    for gather in gathers:
        gather.near.wait_all()
    for tile in range(tiles):
        lanes = slice(128 * tile, 128 * tile + 128)
        index = (slice(None),) * (3 if by_chip else 1) + (lanes,)
        total = add_all([own[index]] + [land[(step, *index)] for step in range(2)])
        r.stage[pl.ds(tile, count, stride=tiles)] = total.reshape(count, 128)

    def one(chip):
        r.p[number][chip // 4, chip % 4, :rows] = r.stage[
            pl.ds(pl.multiple_of(chip * rows, 8), rows)
        ].astype(BF16)

    loop(16, one)


def late_second(r, number):
    second = weight_order(number)[1]
    mine = place()[second]
    return r.links.ring(
        second,
        lambda step: r.p[number].at[shifted(mine, step)],
        lambda step, at: r.second[number].at[step - 1],
        r.second[number],
    )


def late_first(r, number, ring):
    first, second, _ = weight_order(number)
    mine, own = place()[first], place()[second]
    ring.wait_all()
    for at in range(4):
        r.line[number][at] = add_all(
            [r.p[number][own, at]] + [r.second[number][step, at] for step in range(3)]
        ).astype(BF16)
    return r.links.ring(
        first,
        lambda step: r.line[number].at[shifted(mine, step)],
        lambda step, at: r.first[number].at[step - 1],
        r.first[number],
    )


def late_end(r, number, ring, out):
    mine = place()[weight_order(number)[0]]
    ring.wait_all()
    out[...] = add_all([r.line[number][mine]] + [r.first[number][step] for step in range(3)])


def scatter_third(r):
    spot = place()
    rings, specials = [], []
    for part, (row, rows) in enumerate(KV_ROWS):
        last = ORDERS[part][2]
        rings.append(
            r.links.ring(
                last,
                lambda step, row=row, rows=rows, last=last: of_plane(
                    r.slots, last, shifted(spot[last], step), pl.ds(row, rows)
                ),
                lambda step, at, rb=r.rb[part]: rb.at[step - 1],
                r.rb[part],
                begin=False,
            )
        )
        specials.append(
            r.links.ring(
                last,
                lambda step, row=row, rows=rows: r.grad_extra.at[2, pl.ds(row, rows)],
                lambda step, at, rs=r.rs[part]: rs.at[step - 1],
                r.rs[part],
                begin=False,
            )
        )
    return rings, specials


def scatter_second(r, thirds, specials):
    spot = place()
    me = lax.axis_index("ctx")
    low_me = my_low(r)
    rings = []
    for part, (row, rows) in enumerate(KV_ROWS):
        first, second, last = ORDERS[part]
        rb, rs, total, land = r.rb[part], r.rs[part], r.g2[part], r.r2[part]
        thirds[part].wait_all()
        specials[part].wait_all()
        special = add_all([r.grad_extra[2, row : row + rows]] + [rs[step] for step in range(3)])
        r.sp[part][...] = special.astype(BF16)
        senders = [low_of(r, chip_of(spot, last, -step)) for step in (1, 2, 3)]

        def collect(
            at, i2, i1, rb=rb, sp=r.sp[part], total=total, row=row, rows=rows, last=last, senders=senders
        ):
            chip = chip_of(at, last, 0)
            source = low_of(r, chip)
            plane = [at[axis] for axis in (X, Y, Z) if axis != last]
            both = r.slots[at[0], at[1], at[2], pl.ds(row, rows)].astype(F32)
            none = jnp.zeros_like(both)
            low = jnp.where(source < low_me, both, none)
            for step in (1, 2, 3):
                came = rb[step - 1, plane[0], plane[1]].astype(F32)
                low += jnp.where(source < senders[step - 1], came, none)
                both += came
            high = both - low
            low += jnp.where(chip == me, r.grad_extra[0, pl.ds(row, rows)].astype(F32), none)
            high += jnp.where(chip == me, r.grad_extra[1, pl.ds(row, rows)].astype(F32), none)
            low += jnp.where(source == 63, sp[...].astype(F32), none)
            total[i2, 2 * i1] = low.astype(BF16)
            total[i2, 2 * i1 + 1] = high.astype(BF16)

        plane_loop(part, collect)
        rings.append(
            r.links.ring(
                second,
                lambda step, total=total, second=second: total.at[shifted(spot[second], step)],
                lambda step, at, land=land: land.at[step - 1],
                land,
            )
        )
    return rings


def scatter_first(r, seconds):
    spot = place()
    rings = []
    for part in range(3):
        first, second, _ = ORDERS[part]
        total, land, line, end = r.g2[part], r.r2[part], r.f1[part], r.r1[part]
        seconds[part].wait_all()

        def pick(index, total=total, land=land, mine=spot[second]):
            return add_all([total[mine, index]] + [land[step, index] for step in range(3)]).astype(
                BF16
            )

        for at in range(4):
            line[at, 0] = pick(2 * at)
            line[at, 1] = pick(2 * at + 1)
        rings.append(
            r.links.ring(
                first,
                lambda step, line=line, first=first: line.at[shifted(spot[first], step)],
                lambda step, at, end=end: end.at[step - 1],
                end,
            )
        )
    return rings


def scatter_end(r, firsts):
    spot = place()
    for part, (row, rows) in enumerate(KV_ROWS):
        firsts[part].wait_all()
        mine = spot[ORDERS[part][0]]
        for index in range(2):
            r.kv_sum[index, row : row + rows] = add_all(
                [r.f1[part][mine, index]] + [r.r1[part][step, index] for step in range(3)]
            )


def keys_values_back(r, split_shared):
    lanes = []
    for lane in range(4):
        pieces = [
            r.kv_sum[block, unit_rows(token, lane)] for block in range(2) for token in range(4)
        ]
        lanes.append(jnp.concatenate(pieces, axis=0))
    grad_keys = jnp.concatenate(lanes[:2], axis=1)
    grad_values = jnp.concatenate(lanes[2:], axis=1)
    back, term = norm_back(r.key_raw[...], gain(r, G_KEY), rope_back(r, grad_keys))
    note_gain(r, G_KEY, term)
    kv_low = jnp.concatenate([back, grad_values], axis=1).astype(BF16)
    core = lax.axis_index("dp")
    r.both_kv[core] = kv_low
    kv_shared = share(r, r.both_kv, r.both_kv.at[core])
    grad_split = dot_nt(kv_low, r.w_kv[...]).astype(BF16)
    grad_normed = dot_nt(grad_split, r.splitting[...]) + r.grad_normed[...]
    back, term = norm_back(r.x[...], gain(r, G_ATTN), grad_normed)
    note_gain(r, G_ATTN, term)
    gains_back(r, G_KEY, G_ATTN)
    low, high = r.held[:64], r.held[64:]
    r.both_held[core] = jnp.where(core == 0, low, high)
    r.out_held[...] = jnp.where(core == 0, high, low)
    held_shared = share(r, r.both_held, r.out_held)
    r.tokens_grad[...] = low_first(r, (r.grad_mid[...] + back).astype(BF16))
    r.stage[SMALL : SMALL + 1024] = jnp.zeros((1024, 128), F32)
    split_shared.wait()
    kv_shared.wait()
    terms = dot_tn(pair(r.both_split), pair(r.both_kv))
    for tile in range(4):
        lanes = slice(128 * tile, 128 * tile + 128)
        r.stage[pl.ds(tile, 256, stride=4)] = terms[:256, lanes]
        r.stage[pl.ds(SMALL + tile, 64, stride=16)] = terms[256:320, lanes]
    held_shared.wait()
    r.stage[pl.ds(SMALL + 4, 64, stride=16)] = r.both_held[0] + r.both_held[1]
    for unit in range(2):
        for plane in range(4):
            row = SMALL * unit + 256 * plane
            r.u[unit][core, plane] = r.stage[row : row + 256].astype(BF16).reshape(4, 4, 16, 128)


def gains_back(r, *numbers):
    for number in numbers:
        at, count, _, _ = GAINS[number]
        lanes, owners = gain_maps(r, number)
        term = jnp.where(owners, r.gain_sums[0:1, at : at + count], 0.0).astype(BF16)
        r.held[...] += dot_nt(term, lanes)


def small_sums(r, between):
    links = r.links
    core = lax.axis_index("dp")
    spot = place()
    axes = ((X, Y, Z), (Y, Z, X))
    rings = []
    for unit, order in enumerate(axes):
        own, land = r.u[unit], r.land3[unit]
        axis = order[0]
        rings.append(
            links.ring(
                axis,
                lambda step, own=own, axis=axis: own.at[core, shifted(spot[axis], step)],
                lambda step, at, land=land: land.at[step - 1],
                land,
            )
        )
    between[0]()
    later = []
    for unit, order in enumerate(axes):
        own, land, out, to = r.u[unit], r.land3[unit], r.sum2[unit], r.land2[unit]
        rings[unit].wait_all()
        mine = spot[order[0]]

        def add(at, own=own, land=land, out=out, mine=mine):
            out[at] = add_all([own[core, mine, at]] + [land[step, at] for step in range(3)]).astype(
                BF16
            )

        loop(4, add)
        axis = order[1]
        later.append(
            links.ring(
                axis,
                lambda step, out=out, axis=axis: out.at[shifted(spot[axis], step)],
                lambda step, at, to=to: to.at[step - 1],
                to,
            )
        )
    between[1]()
    last = []
    for unit, order in enumerate(axes):
        own, land, out, to = r.sum2[unit], r.land2[unit], r.sum1[unit], r.land1[unit]
        later[unit].wait_all()
        out[...] = add_all([own[spot[order[1]]]] + [land[step] for step in range(3)]).astype(BF16)
        axis = order[2]
        last.append(
            links.ring(
                axis,
                lambda step, out=out, axis=axis: out.at[shifted(spot[axis], step)],
                lambda step, at, to=to: to.at[step - 1],
                to,
            )
        )
    between[2]()
    for unit, order in enumerate(axes):
        last[unit].wait_all()
        r.fk[16 * unit : 16 * unit + 16] = add_all(
            [r.sum1[unit][spot[order[2]]]] + [r.land1[unit][step] for step in range(3)]
        )


def layer(r):
    greet()
    for copy in r.fetches.values():
        copy.wait()
    pack(r)
    greeted()
    early_rings, early_held, spreads = early(r)
    unpack_small(r)
    keys_values(r)
    firsts = gather_first(r)
    split_shared = share(r, r.both_split, r.out_split)
    seconds = gather_second(r, firsts)
    early_pieces = (ASK, OUT, GATE_ONE, UP_ONE, DOWN_ONE)
    for piece in early_pieces:
        spreads[piece].forward()
    before = tuple(r.links.open)
    for piece in LATE_PIECES:
        spreads[piece] = Spread(r, piece)
    thirds, specials = gather_third(r, seconds)
    for piece in early_pieces:
        spreads[piece].pass_on()
    for piece in LATE_PIECES:
        spreads[piece].forward()
    spreads[ASK].finish()
    query_shared = queries(r)

    def pass_on(number):
        if number == 0:
            r.links.settle(before)
        if number == 2:
            for piece in LATE_PIECES:
                spreads[piece].pass_on()

    attention(r, thirds, specials, pass_on)
    shared = feed_forward(r, spreads)
    shared[QUERY] = query_shared
    before = tuple(r.links.open)
    sums = {}

    def start(*pieces):
        for piece in pieces:
            sums[piece] = Gather(r, piece)

    def relay(*pieces):
        for piece in pieces:
            sums[piece].relay()

    late = {}

    def send_late(*numbers):
        pieces = {
            GATE: (GATE_ONE, GATE_TWO),
            OUTPUT: (OUT,),
            UP: (UP_ONE, UP_TWO),
            QUERY: (ASK,),
            DOWN: (DOWN_ONE, DOWN_TWO),
        }
        for number in numbers:
            repack(r, number, *(sums[piece] for piece in pieces[number]))
            late[number] = late_second(r, number)

    def go_on(*numbers):
        for number in numbers:
            late[number] = late_first(r, number, late[number])

    def finish(*numbers):
        outs = (r.fgate, r.foutput, r.fup, r.fquery, r.fdown)
        for number in numbers:
            late_end(r, number, late[number], outs[number])

    rest_back = feed_forward_back(r, spreads, shared, start)
    thirds, third_specials = attention_back(r, lambda number: None)
    queries_back(r, spreads, shared)
    rest_back()
    start(GATE_TWO, UP_TWO, OUT, ASK)
    for ring in early_rings:
        ring.sent()
    for ring in seconds:
        ring.sent()
    r.links.settle(before)
    before = tuple(r.links.open)
    r.held[...] = jnp.zeros_like(r.held)
    gains_back(r, G_POST_ATTN, G_FFN, G_POST_FFN, G_QUERY)
    seconds = scatter_second(r, thirds, third_specials)
    relay(DOWN_ONE, GATE_ONE, UP_ONE)
    firsts = scatter_first(r, seconds)
    relay(DOWN_TWO, GATE_TWO, UP_TWO)
    scatter_end(r, firsts)
    relay(OUT, ASK)
    for copy in early_held:
        copy.sent()
    keys_values_back(r, split_shared)

    def one():
        r.links.settle(before)
        send_late(DOWN, GATE, UP)

    def two():
        send_late(OUTPUT, QUERY)

    def three():
        go_on(DOWN, GATE, UP, OUTPUT, QUERY)

    small_sums(r, (one, two, three))
    finish(DOWN, GATE, UP, OUTPUT, QUERY)
    r.links.settle()
    assert r.links.sending <= COPIES[0] and r.links.receiving <= COPIES[1]


def end(r):
    def rows(out, source, base, count, tiles):
        r.stage[base : base + count * tiles] = source
        for tile in range(tiles):
            out[:, 128 * tile : 128 * tile + 128] = columns_of(r, base, count, tiles, tile)

    rows(r.gate_grad, r.fgate[...], 0, 5, 16)
    rows(r.output_grad, r.foutput[0:40], 80, 8, 5)
    rows(r.up_grad, r.fup[...], 128, 5, 16)
    rows(r.query_grad, r.fquery[0:40], 208, 5, 8)
    rows(r.down_grad, r.fdown[...], 256, 16, 5)
    r.stage[336:368] = r.fk[...]
    for tile in range(4):
        out = (r.key_grad, r.value_grad)[tile // 2]
        half = 128 * (tile % 2)
        out[:, half : half + 128] = columns_of(r, 336, 5, 4, tile)
    line = r.fk[16:24]
    gain_grads = (r.grad_attn_norm, r.grad_post_attn, r.grad_ffn_norm, r.grad_post_ffn, r.grad_q, r.grad_k)
    for number, (_, _, held, lane) in enumerate(GAINS):
        out = gain_grads[number]
        moved = line if lane == 0 else pltpu.roll(line, 128 - lane, 1)
        out[...] = moved[4:5, :held]
    r.final_out[0] = r.block_out[...]
    r.final_grad[0] = r.tokens_grad[...]


COPIES = (97, 159)


def by_part(*dims):
    return [hold(BF16, *dims, rows, 128) for _, rows in KV_ROWS]


def by_flat(*dims):
    return [hold(BF16, *dims, rows, 128) for rows in (80, 48, 80, 48, 80)]


def by_unit(*dims):
    return [hold(BF16, *dims, 16, 128) for _ in range(2)]


def by_weight(lead, core):
    return [
        hold(BF16, *core, *lead, 80, 2048),
        hold(BF16, *core, *lead, 128, 640),
        hold(BF16, *core, *lead, 80, 2048),
        hold(BF16, *core, *lead, 80, 1024),
        hold(BF16, *core, *lead, 4, 4, 16, 640),
    ]


def buffers():
    return dict(
        stage=hold(F32, 4096, 128),
        x=hold(F32, 128, 640),
        cos=hold(F32, 128, 128),
        sin=hold(F32, 128, 128),
        gains=hold(F32, 8, 3072),
        gain_sums=hold(F32, 8, 3072),
        turning=hold(BF16, 640, 640),
        splitting=hold(BF16, 640, 640),
        key_base=hold(jnp.int32, 32, 16, 128),
        key_rows=hold(jnp.int32, 32, 256),
        p=by_flat(4, 4),
        second=by_flat(3, 4),
        line=by_flat(4),
        first=by_flat(3),
        u=by_unit(2, 4, 4, 4),
        both_split=hold(BF16, 2, 128, 384),
        both_kv=hold(BF16, 2, 128, 512),
        both_held=hold(F32, 2, 64, 128),
        out_held=hold(F32, 64, 128),
        out_split=hold(BF16, 128, 384),
        held=hold(F32, 128, 128),
        land3=by_unit(3, 4, 4),
        sum2=by_unit(4, 4),
        land2=by_unit(3, 4),
        sum1=by_unit(4),
        land1=by_unit(3),
        w_kv=hold(BF16, 640, 512),
        w=by_weight((4,), (2,)),
        both_hidden=hold(BF16, 2, 128, 1024),
        both_low=hold(BF16, 2, 128, 640),
        both_gate=hold(BF16, 2, 128, 2048),
        both_up=hold(BF16, 2, 128, 2048),
        both_in=hold(BF16, 2, 128, 384),
        both_in_b=hold(BF16, 2, 128, 384),
        both_attn=hold(BF16, 2, 128, 512),
        both_proj=hold(BF16, 2, 128, 640),
        both_normed=hold(BF16, 2, 128, 384),
        both_query=hold(BF16, 2, 128, 1024),
        out_in=hold(BF16, 128, 384),
        out_in_b=hold(BF16, 128, 384),
        out_normed=hold(BF16, 128, 384),
        landed=[
            hold(BF16, 3, 80, 2048),
            hold(BF16, 3, 128, 640),
            hold(BF16, 3, 80, 2048),
            hold(BF16, 3, 80, 1024),
            hold(BF16, 3, 4, 4, 16, 640),
        ],
        kv3=hold(BF16, 2, 256, 128),
        f1=by_part(4, 2),
        g2=by_part(4, 8),
        sel=by_part(3, 4, 4),
        sp=by_part(),
        rsp=by_part(4),
        rb=by_part(3, 4, 4),
        rs=by_part(3),
        r2=by_part(3, 8),
        r1=by_part(3, 2),
        slots=hold(BF16, 4, 4, 4, 256, 128),
        extra=hold(BF16, 3, 256, 128),
        grad_extra=hold(BF16, 3, 256, 128),
        kv_sum=hold(F32, 2, 256, 128),
        normed=hold(BF16, 128, 640),
        normed_split=hold(BF16, 128, 640),
        normed_b=hold(BF16, 128, 640),
        key_raw=hold(F32, 128, 256),
        query_raw=hold(F32, 128, 1024),
        query=hold(BF16, 512, 256),
        attn=hold(F32, 512, 256),
        total=hold(F32, 512, 128),
        dots=hold(F32, 512, 128),
        attn_low=hold(BF16, 128, 1024),
        proj=hold(F32, 128, 640),
        mid=hold(F32, 128, 640),
        ffn_in=hold(BF16, 128, 640),
        ffn_in_b=hold(BF16, 128, 640),
        gate=hold(F32, 128, 2048),
        up=hold(F32, 128, 2048),
        hidden=hold(BF16, 128, 2048),
        ffn_out=hold(F32, 128, 640),
        grad_mid=hold(F32, 128, 640),
        grad_attn=hold(BF16, 512, 256),
        grad_query=hold(F32, 512, 256),
        grad_normed=hold(F32, 128, 640),
    )


def on_device(
    tokens,
    doc_lengths,
    block_order,
    attn_norm,
    query_weight,
    key_weight,
    value_weight,
    query_gain,
    key_gain,
    output_weight,
    attn_post_norm,
    ffn_norm,
    gate_weight,
    up_weight,
    down_weight,
    ffn_post_norm,
    out_cot,
):
    made = run(
        layer,
        dict(block_order=block_order, doc_lengths=doc_lengths),
        {},
        dict(
            block_out=hold(BF16, 128, 640),
            tokens_grad=hold(BF16, 128, 640),
            fgate=hold(F32, 80, 128),
            foutput=hold(F32, 48, 128),
            fup=hold(F32, 80, 128),
            fquery=hold(F32, 48, 128),
            fdown=hold(F32, 80, 128),
            fk=hold(F32, 32, 128),
        ),
        buffers(),
        number=1,
        copies=COPIES,
        fetched=dict(
            gate_weight=gate_weight,
            output_weight=output_weight,
            up_weight=up_weight,
            query_weight=query_weight,
            down_weight=down_weight,
            key_weight=key_weight,
            value_weight=value_weight,
            attn_norm=attn_norm[None],
            attn_post_norm=attn_post_norm[None],
            ffn_norm=ffn_norm[None],
            ffn_post_norm=ffn_post_norm[None],
            query_gain=query_gain[None],
            key_gain=key_gain[None],
            tokens=tokens,
            table=jnp.asarray(number_table()),
            frequency=jnp.asarray(ROPE_BASE ** (-2.0 * np.arange(128) / 256), F32)[None],
            out_cot=out_cot,
        ),
    )
    results = run(
        end,
        {},
        made,
        dict(
            final_out=hold(BF16, 1, 128, 640),
            final_grad=hold(BF16, 1, 128, 640),
            grad_attn_norm=hold(F32, 1, 5),
            query_grad=hold(F32, 5, 1024),
            key_grad=hold(F32, 5, 256),
            value_grad=hold(F32, 5, 256),
            grad_q=hold(F32, 1, 2),
            grad_k=hold(F32, 1, 2),
            output_grad=hold(F32, 8, 640),
            grad_post_attn=hold(F32, 1, 5),
            grad_ffn_norm=hold(F32, 1, 5),
            gate_grad=hold(F32, 5, 2048),
            up_grad=hold(F32, 5, 2048),
            down_grad=hold(F32, 16, 640),
            grad_post_ffn=hold(F32, 1, 5),
        ),
        dict(stage=hold(F32, 3088, 128)),
    )
    return tuple(
        value.reshape(-1) if value.shape[0] == 1 and value.ndim == 2 else value
        for value in results.values()
    )


def solution(mesh):
    rows = P(("dp", "ctx"), None)
    vector = P(("dp", "ctx"))
    stream = P("dp", "ctx", None)
    return jax.shard_map(
        on_device,
        mesh=mesh,
        in_specs=(
            stream,
            P("dp", None),
            P(),
            vector,
            rows,
            rows,
            rows,
            vector,
            vector,
            rows,
            vector,
            vector,
            rows,
            rows,
            rows,
            vector,
            stream,
        ),
        out_specs=(
            stream,
            stream,
            vector,
            rows,
            rows,
            rows,
            vector,
            vector,
            rows,
            vector,
            vector,
            rows,
            rows,
            rows,
            vector,
        ),
        check_vma=False,
    )
```

```python
from types import SimpleNamespace

import jax
import jax.numpy as jnp
import numpy as np
from jax import lax
from jax.experimental import pallas as pl
from jax.experimental.pallas import tpu as pltpu
from jax.sharding import PartitionSpec as P

EPSILON = 1e-06
ROPE_BASE = 1000000.0
MESH = pl.DeviceIdType.MESH
F32 = jnp.float32
BF16 = jnp.bfloat16
MIB = 2**20

X, Y, Z = 0, 1, 2
ORDERS = ((Z, Y, X), (X, Z, Y), (Y, X, Z))
UNITS = (
    ((0, 0), (0, 1), (0, 2), (0, 3), (3, 0))
    + ((1, 0), (1, 1), (1, 2), (1, 3), (3, 1))
    + ((2, 0), (2, 1), (2, 2), (2, 3), (3, 2), (3, 3))
)
KV_ROWS = ((0, 80), (80, 80), (160, 96))
HEADS = 4
HEAD = 256
SCALE = HEAD**-0.5
LOG2E = 1.4426950408889634


def place():
    chip = lax.axis_index("ctx")
    return (chip // 16, (chip // 4) % 4, chip % 4)


def shifted(value, step):
    return lax.rem(value + step + 4, 4)


def peer(axis, step):
    spot = list(place())
    spot[axis] = shifted(spot[axis], step)
    return (lax.axis_index("dp"), spot[0] * 16 + spot[1] * 4 + spot[2])


def other_core():
    return (1 - lax.axis_index("dp"), lax.axis_index("ctx"))


def greet():
    barrier = pltpu.get_barrier_semaphore()
    for axis in (X, Y, Z):
        for step in (1, 2, 3):
            pl.semaphore_signal(barrier, inc=1, device_id=peer(axis, step), device_id_type=MESH)
    pl.semaphore_signal(barrier, inc=1, device_id=other_core(), device_id_type=MESH)


def greeted():
    pl.semaphore_wait(pltpu.get_barrier_semaphore(), 10)


class Ring:
    def __init__(self, links, axis, source, landing, whole, steps, apart, sends):
        self.links, self.axis, self.source, self.landing = links, axis, source, landing
        self.whole, self.apart = whole, apart
        self.sends = links.sends(whole) if sends is None else sends
        if apart:
            self.numbers = {step: links.receive() for step in steps}
        else:
            self.numbers = dict.fromkeys(steps, links.receive())

    def copy(self, step, sender):
        return self.links.copy(
            self.sends,
            self.numbers[step],
            self.source(step),
            self.landing(step, sender),
            peer(self.axis, step),
        )

    def start(self, step, *index):
        source, landing = self.source(step), self.landing(step, place()[self.axis])
        if index:
            source, landing = source.at[index], landing.at[index]
        self.links.copy(
            self.sends, self.numbers[step], source, landing, peer(self.axis, step)
        ).start()

    def wait(self, step):
        self.copy(step, shifted(place()[self.axis], -step)).wait_recv()

    def wait_all(self):
        if self.apart:
            for step in self.numbers:
                self.wait(step)
        else:
            step = next(iter(self.numbers))
            self.links.copy(
                self.sends, self.numbers[step], self.whole, self.whole, peer(self.axis, step)
            ).wait_recv()

    def sent(self):
        self.links.settle((self.sends,))


class Across:
    def __init__(self, links, whole):
        self.links, self.whole = links, whole
        self.sends, self.number = links.sends(whole), links.receive()

    def add(self, source, landing):
        there = landing(lax.axis_index("dp"))
        self.links.copy(self.sends, self.number, source, there, other_core()).start()

    def wait(self):
        self.links.copy(
            self.sends, self.number, self.whole, self.whole, other_core()
        ).wait_recv()

    def sent(self):
        self.links.settle((self.sends,))


class Links:
    def __init__(self, send, recv):
        self.send, self.recv = send, recv
        self.sending, self.receiving, self.open = 0, 0, {}

    def sends(self, whole):
        self.open[self.sending] = whole
        self.sending += 1
        return self.sending - 1

    def receive(self):
        self.receiving += 1
        return self.receiving - 1

    def copy(self, send, recv, source, landing, device):
        return pltpu.make_async_remote_copy(
            src_ref=source,
            dst_ref=landing,
            send_sem=self.send.at[send],
            recv_sem=self.recv.at[recv],
            device_id=device,
            device_id_type=MESH,
        )

    def ring(
        self, axis, source, landing, whole, begin=True, steps=(1, 2, 3), apart=False, sends=None
    ):
        ring = Ring(self, axis, source, landing, whole, steps, apart, sends)
        if begin:
            for step in steps:
                ring.start(step)
        return ring

    def across(self, source, landing, whole):
        across = Across(self, whole)
        across.add(source, landing)
        return across

    def settle(self, numbers=None):
        for number in tuple(self.open if numbers is None else numbers):
            if number in self.open:
                whole = self.open.pop(number)
                self.copy(number, 0, whole, whole, other_core()).wait_send()


VMEM = pl.BlockSpec(memory_space=pltpu.VMEM)
SMEM = pl.BlockSpec(memory_space=pltpu.SMEM)
ANY = pl.BlockSpec(memory_space=pl.ANY)


def hold(kind, *shape):
    return pltpu.VMEM(shape, kind)


def run(stage, numbers, ins, outs, scratch, number=None, copies=(), fetched={}):
    flat, shape = jax.tree.flatten(scratch, is_leaf=lambda leaf: not isinstance(leaf, (dict, list)))

    def kernel(*refs):
        count = len(numbers) + len(fetched) + len(ins) + len(outs)
        named = dict(zip((*numbers, *fetched, *ins, *outs), refs))
        rest = refs[count + len(flat) :]
        r = SimpleNamespace(**named)
        vars(r).update(jax.tree.unflatten(shape, refs[count : count + len(flat)]))
        r.fetches = {}
        for at, name in enumerate(fetched):
            held = rest[at]
            copy = pltpu.make_async_copy(named[name], held, rest[len(fetched)].at[at])
            copy.start()
            r.fetches[name] = copy
            setattr(r, name, held)
        if copies:
            r.links = Links(*rest[-2:])
        stage(r)

    remote = dict(collective_id=number, has_side_effects=True) if copies else {}
    results = pl.pallas_call(
        kernel,
        out_shape=[jax.ShapeDtypeStruct(out.shape, out.dtype) for out in outs.values()],
        in_specs=[SMEM] * len(numbers) + [ANY] * len(fetched) + [VMEM] * len(ins),
        out_specs=[VMEM] * len(outs),
        scratch_shapes=flat
        + [pltpu.VMEM(value.shape, value.dtype) for value in fetched.values()]
        + ([pltpu.SemaphoreType.DMA((len(fetched),))] if fetched else [])
        + [pltpu.SemaphoreType.DMA((count,)) for count in copies],
        compiler_params=pltpu.CompilerParams(vmem_limit_bytes=60 * MIB, **remote),
    )(*numbers.values(), *fetched.values(), *ins.values())
    return dict(zip(outs, results))


def dot32(left, right):
    return jnp.dot(left, right, preferred_element_type=F32)


def dot_nt(left, right):
    return lax.dot_general(left, right, (((1,), (1,)), ((), ())), preferred_element_type=F32)


def dot_tn(left, right):
    return lax.dot_general(left, right, (((0,), (0,)), ((), ())), preferred_element_type=F32)


def add_all(values):
    total = values[0].astype(F32)
    for value in values[1:]:
        total += value.astype(F32)
    return total


def loop(count, body):
    def step(number, unused):
        body(number)
        return unused

    lax.fori_loop(0, count, step, 0)


def my_low(r):
    chip = lax.axis_index("ctx")
    return jnp.minimum(r.block_order[2 * chip], r.block_order[2 * chip + 1])


def low_of(r, chip):
    return jnp.minimum(r.block_order[2 * chip], r.block_order[2 * chip + 1])


def low_first(r, rows):
    chip = lax.axis_index("ctx")
    flip = r.block_order[2 * chip] > r.block_order[2 * chip + 1]
    return jnp.where(flip, jnp.concatenate([rows[64:], rows[:64]], axis=0), rows)


def document_starts(r, places):
    start = jnp.zeros_like(places)
    at = 0
    for number in range(1, 8):
        at = at + r.doc_lengths[0, number - 1]
        start = jnp.where(places >= at, at, start)
    return start


def places_of(r, within, high):
    low = my_low(r)
    return jnp.where(high, 127 - low, low) * 64 + within


def number_table():
    def turned_device(device):
        core, x, y, z = device // 64, (device // 16) % 4, (device // 4) % 4, device % 4
        return ((core * 4 + y) * 4 + z) * 4 + x

    table = np.zeros((8, 640), np.int32)
    k = np.arange(640)
    table[0], table[1] = k % 5, turned_device(k // 5)
    core, y, z, x, row = k // 320, (k // 80) % 4, (k // 20) % 4, (k // 5) % 4, k % 5
    table[2] = (((core * 4 + x) * 4 + y) * 4 + z) * 5 + row
    table[3, :512] = 5 * (k[:512] // 4) + k[:512] % 4
    device = np.arange(128)
    table[3, 512 + turned_device(device)] = 5 * device + 4
    table[4, :256], table[5, :256] = k[:256] % 2, turned_device(k[:256] // 2)
    return table


def one_hot(rows, numbers):
    shape = (rows, numbers.shape[1])
    return jnp.where(lax.broadcasted_iota(jnp.int32, shape, 0) == numbers, 1.0, 0.0).astype(BF16)


GAINS = ((0, 640, 5, 0), (640, 640, 5, 5), (1280, 640, 5, 10), (1920, 640, 5, 15))
GAINS += ((2560, 256, 2, 20), (2816, 256, 2, 22))
G_ATTN, G_POST_ATTN, G_FFN, G_POST_FFN, G_QUERY, G_KEY = range(6)


def gain_maps(r, number):
    _, columns, held, lane = GAINS[number]
    row = 0 if held == 5 else 4
    rest, owner = r.table[row : row + 1, :columns], r.table[row + 1 : row + 2, :columns]
    lanes = one_hot(128, rest + lane)
    owners = lax.broadcasted_iota(jnp.int32, (128, columns), 0) == owner
    return lanes, owners


def gain(r, number):
    at, columns, _, _ = GAINS[number]
    return r.gains[0:1, at : at + columns]


def rows_of(r, base, weight, count):
    tiles = weight.shape[1] // 128
    for tile in range(tiles):
        r.stage[pl.ds(base + tile, count, stride=tiles)] = weight[
            :, 128 * tile : 128 * tile + 128
        ].astype(F32)


def columns_of(r, base, count, tiles, tile):
    return r.stage[pl.ds(base + tile, count, stride=tiles)]


def pack(r):
    rows_of(r, 0, r.gate_weight, 5)
    rows_of(r, 80, r.output_weight, 8)
    rows_of(r, 128, r.up_weight, 5)
    rows_of(r, 208, r.query_weight, 5)
    rows_of(r, 256, r.down_weight, 16)
    for tile in range(4):
        weight = (r.key_weight, r.value_weight)[tile // 2]
        half = 128 * (tile % 2)
        r.stage[pl.ds(336 + tile, 5, stride=4)] = weight[:, half : half + 128].astype(F32)
    r.stage[356:357] = jnp.zeros((1, 128), F32)
    own = (r.attn_norm, r.attn_post_norm, r.ffn_norm, r.ffn_post_norm, r.query_gain, r.key_gain)
    for ref, (_, _, held, lane) in zip(own, GAINS):
        r.stage[356:357, lane : lane + held] = ref[...].astype(F32)
    spot = place()
    for number, ref in enumerate(r.p):
        first, second, _ = weight_order(number)
        rows = ref.shape[2]
        start = (0, 80, 128, 208, 256)[number]
        ref[spot[second], spot[first]] = r.stage[start : start + rows].astype(BF16)
    core = lax.axis_index("dp")
    x, y, z = spot
    r.u[0][core, x, y, z] = r.stage[336:352].astype(BF16)
    r.u[1][core, y, z, x] = r.stage[352:368].astype(BF16)


def tables(r):
    r.x[...] = low_first(r, r.tokens[0].astype(F32))
    rows = lax.broadcasted_iota(jnp.int32, (128, 1), 0)
    places = places_of(r, rows % 64, rows >= 64)
    position = (places - document_starts(r, places)).astype(F32)
    angles = position * r.frequency[...]
    r.cos[...] = jnp.cos(angles)
    r.sin[...] = jnp.sin(angles)
    r.turning[...] = one_hot(640, r.table[2:3])
    r.splitting[...] = one_hot(640, r.table[3:4])


NEVER = -(1 << 20)


def key_tables(r):
    mine = my_low(r)

    def chunk(number, token):
        plane = number % 4
        row = 4 * token + number
        for slot in range(16):
            spot = [slot // 4, slot % 4]
            spot.insert(chunk_axis(token), plane)
            low = low_of(r, spot[0] * 16 + spot[1] * 4 + spot[2])
            chosen = jnp.where(low < mine, low, 127 - low) * 64
            for_low = jnp.where(low < mine, chosen, NEVER)
            for_high = jnp.where(low == mine, NEVER, chosen)
            r.key_base[row, slot : slot + 1] = jnp.full((1, 128), for_low, jnp.int32)
            r.key_base[16 + row, slot : slot + 1] = jnp.full((1, 128), for_high, jnp.int32)

    for token in range(4):
        loop(4, lambda number, token=token: chunk(number, token))

    def turn(row):
        r.key_rows[pl.ds(row, 1)] = jnp.transpose(key_column(r, row, (row // 4) % 4))[0:1]

    loop(32, turn)


def key_column(r, row, token):
    base = jnp.broadcast_to(r.key_base[row][:, None, :], (16, 16, 128)).reshape(256, 128)
    return base + (lax.broadcasted_iota(jnp.int32, (256, 128), 0) % 16 + 16 * token)


def early(r):
    links = r.links
    core = lax.axis_index("dp")
    spot = place()
    x, y, z = spot

    def small(axis, unit, index_of):
        ref = r.u[unit]
        ring = links.ring(
            axis,
            lambda step: ref.at[index_of(spot[axis])],
            lambda step, at: ref.at[index_of(at)],
            ref.at[index_of(pl.ds(0, 3))],
        )
        held.append(ring)
        return ring

    held = []

    one = small(Z, 0, lambda at: (core, x, y, at))
    two = small(X, 1, lambda at: (core, y, z, at))
    rings = []
    for number, ref in enumerate(r.p):
        first, second, _ = weight_order(number)
        row = spot[second]
        rings.append(
            links.ring(
                first,
                lambda step, ref=ref, row=row, first=first: ref.at[row, spot[first]],
                lambda step, at, ref=ref, row=row: ref.at[row, at],
                ref.at[row, pl.ds(0, 3)],
            )
        )
    tables(r)
    one.wait_all()
    one = small(Y, 0, lambda at: (core, x, at))
    two.wait_all()
    two = small(Z, 1, lambda at: (core, y, at))
    for number, ref in enumerate(r.p):
        rings[number].wait_all()
        second = weight_order(number)[1]
        rings.append(
            links.ring(
                second,
                lambda step, ref=ref, second=second: ref.at[spot[second]],
                lambda step, at, ref=ref: ref.at[at],
                ref.at[pl.ds(0, 3)],
            )
        )
    key_tables(r)
    one.wait_all()
    one = small(X, 0, lambda at: (core, at))
    two.wait_all()
    two = small(Y, 1, lambda at: (core, at))
    spreads = {}

    def begin(*numbers):
        for number in numbers:
            rings[5 + number].wait_all()
            unpack(r, number)
            for piece in EARLY_PIECES[number]:
                spreads[piece] = Spread(r, piece)

    begin(DOWN, GATE, OUTPUT)
    one.wait_all()
    three = links.across(r.u[0].at[core], lambda at: r.u[0].at[at], r.u[0].at[core])
    two.wait_all()
    four = links.across(r.u[1].at[core], lambda at: r.u[1].at[at], r.u[1].at[core])
    begin(QUERY, UP)
    three.wait()
    four.wait()
    return rings, held + [three, four], spreads


SMALL = 2048


def unpack_small(r):
    for unit in range(2):
        for core in range(2):
            for plane in range(4):
                row = SMALL * unit + 1024 * core + 256 * plane
                r.stage[row : row + 256] = r.u[unit][core, plane].astype(F32).reshape(256, 128)
    for tile in range(4):
        lanes = slice(128 * tile, 128 * tile + 128)
        r.w_kv[:512, lanes] = columns_of(r, 0, 512, 4, tile).astype(BF16)
        r.w_kv[512:, lanes] = columns_of(r, SMALL, 128, 16, tile).astype(BF16)
    held = columns_of(r, SMALL, 128, 16, 4).astype(BF16)
    for number, (at, columns, _, _) in enumerate(GAINS):
        lanes, owners = gain_maps(r, number)
        spread = jnp.where(owners, dot32(held, lanes), 0.0)
        r.gains[0:1, at : at + columns] = jnp.sum(spread, axis=0, keepdims=True)


WEIGHTS = ((0, 80, False), (0, 40, False), (1, 80, False), (1, 40, False), (2, 80, True))
GATE, OUTPUT, UP, QUERY, DOWN = range(5)


def weight_order(number):
    return ORDERS[WEIGHTS[number][0]]


def own_plane(r, number):
    return weight_plane(r.w[number], number, lax.axis_index("dp"), place()[weight_order(number)[2]])


def weight_plane(ref, number, core, at):
    if WEIGHTS[number][2]:
        return of_plane(ref.at[core], weight_order(number)[2], at)
    return ref.at[core, at]


def plane_tiles(number):
    return ((80, 16), (128, 5), (80, 16), (80, 8), (256, 5))[number]


def unpack(r, number):
    _, rows, by_chip = WEIGHTS[number]
    count, tiles = plane_tiles(number)
    plane = own_plane(r, number)

    def one(chip):
        r.stage[pl.ds(pl.multiple_of(chip * rows, 8), rows)] = r.p[number][
            chip // 4, chip % 4, :rows
        ].astype(F32)

    loop(16, one)
    for tile in range(tiles):
        piece = columns_of(r, 0, count, tiles, tile).astype(BF16)
        lanes = slice(128 * tile, 128 * tile + 128)
        if by_chip:
            plane[:, :, :, lanes] = piece.reshape(4, 4, 16, 128)
        else:
            plane[:, lanes] = piece


def inverse_rms(values):
    return lax.rsqrt(jnp.mean(values * values, axis=-1, keepdims=True) + EPSILON)


def rms_scale(values, weights):
    return values * inverse_rms(values) * weights


def norm_back(values, weights, incoming):
    inverse = inverse_rms(values)
    normal = values * inverse
    scaled = incoming * weights
    back = (scaled - normal * jnp.mean(scaled * normal, axis=-1, keepdims=True)) * inverse
    return back, jnp.sum(incoming * normal, axis=0, keepdims=True)


def rope(r, u):
    cos, sin = r.cos[...], r.sin[...]
    one, two = u[:, :128], u[:, 128:]
    return jnp.concatenate([one * cos - two * sin, two * cos + one * sin], axis=1)


def rope_back(r, e):
    cos, sin = r.cos[...], r.sin[...]
    one, two = e[:, :128], e[:, 128:]
    return jnp.concatenate([one * cos + two * sin, two * cos - one * sin], axis=1)


def turned(r, values):
    return dot32(values, r.turning[...]).astype(BF16)


def unturned(r, values):
    return dot_nt(values.astype(BF16), r.turning[...])


def keys_values(r):
    x = r.x[...]
    normed = rms_scale(x, gain(r, G_ATTN)).astype(BF16)
    r.normed[...] = normed
    r.normed_split[...] = dot32(normed, r.splitting[...]).astype(BF16)
    split = r.normed_split[...].astype(F32)
    none = jnp.zeros((128, 64), F32)
    zero, one = (
        jnp.concatenate(
            [split[:, 256 * core : 256 * core + 256], split[:, 512 + 64 * core : 576 + 64 * core], none],
            axis=1,
        )
        for core in range(2)
    )
    core = lax.axis_index("dp")
    r.both_split[core] = jnp.where(core == 0, zero, one).astype(BF16)
    r.out_split[...] = jnp.where(core == 0, one, zero).astype(BF16)
    raw = dot32(r.normed_split[...], r.w_kv[...])
    r.key_raw[...] = raw[:, :HEAD]
    keys = rope(r, rms_scale(raw[:, :HEAD], gain(r, G_KEY)))
    both = jnp.concatenate([keys, raw[:, HEAD:]], axis=1).astype(BF16)
    for block in range(2):
        for unit, (token, lane) in enumerate(UNITS):
            row = 64 * block + 16 * token
            r.kv3[block, 16 * unit : 16 * unit + 16] = both[
                row : row + 16, 128 * lane : 128 * lane + 128
            ]


def of_plane(ref, axis, at, *rest):
    index = [slice(None)] * 3
    index[axis] = at
    return ref.at[(*index, *rest)]


def chip_of(spot, axis, step):
    spot = list(spot)
    spot[axis] = shifted(spot[axis], step)
    return spot[0] * 16 + spot[1] * 4 + spot[2]


def plane_loop(part, body):
    first, second, last = ORDERS[part]

    def row(i2):
        for i1 in range(4):
            spot = [None] * 3
            spot[first], spot[second], spot[last] = i1, i2, place()[last]
            body(spot, i2, i1)

    loop(4, row)


PIECES = (
    (GATE, 0, 1024),
    (GATE, 1024, 1024),
    (OUTPUT, 0, 640),
    (UP, 0, 1024),
    (UP, 1024, 1024),
    (QUERY, 0, 1024),
    (DOWN, 0, 2),
    (DOWN, 2, 2),
)
GATE_ONE, GATE_TWO, OUT, UP_ONE, UP_TWO, ASK, DOWN_ONE, DOWN_TWO = range(8)
EARLY_PIECES = ((GATE_ONE, GATE_TWO), (OUT,), (UP_ONE, UP_TWO), (ASK,), (DOWN_ONE, DOWN_TWO))
LATE_PIECES = (GATE_TWO, UP_TWO)


def window(ref, dim, first, count):
    index = [slice(None)] * len(ref.shape)
    index[dim] = pl.ds(first, count)
    return ref.at[tuple(index)]


def piece_of(piece, ref, chips=4):
    number, first, count = PIECES[piece]
    rank = len(ref.shape)
    return window(ref, rank - 1 - chips if number == DOWN else rank - 1, first, count)


def half_of(piece, plane, half):
    number, _, count = PIECES[piece]
    if number == DOWN:
        return window(plane, len(plane.shape) - 4, half, 1)
    if number == OUTPUT:
        return window(plane, len(plane.shape) - 2, 64 * half, 64)
    return window(plane, len(plane.shape) - 1, count // 2 * half, count // 2)


def piece_plane(r, piece, core, at):
    number = PIECES[piece][0]
    return piece_of(piece, weight_plane(r.w[number], number, core, at), 3)


def piece_axis(piece):
    return weight_order(PIECES[piece][0])[2]


class Spread:
    def __init__(self, r, piece):
        self.links, axis = r.links, piece_axis(piece)
        self.core, self.mine = lax.axis_index("dp"), place()[axis]
        self.at = lambda core, at: piece_plane(r, piece, core, at)

        def half(at, which):
            return half_of(piece, self.at(self.core, at), which)

        both = piece_of(piece, r.w[PIECES[piece][0]])
        dim = 3 if PIECES[piece][0] == DOWN else 1
        planes = window(both, dim, 0, 3).at[self.core]
        sends = r.links.sends(planes)
        self.near = [
            r.links.ring(
                axis,
                lambda step, which=which: half(self.mine, which),
                lambda step, at, which=which: half(at, which),
                None,
                steps=(1, 3),
                apart=True,
                sends=sends,
            )
            for which in range(2)
        ]

        def passed(step, at):
            return half(shifted(at, -step), 0 if step == 1 else 1)

        self.far = r.links.ring(
            axis,
            lambda step: passed(step, self.mine),
            passed,
            None,
            begin=False,
            steps=(1, 3),
            apart=True,
            sends=sends,
        )
        self.across = Across(r.links, both.at[self.core])
        self.over(self.mine)

    def over(self, at):
        self.across.add(self.at(self.core, at), lambda core: self.at(core, at))

    def forward(self):
        for which, step in enumerate((1, 3)):
            self.near[which].wait(step)
            self.far.start(step)

    def pass_on(self):
        for which, step in enumerate((3, 1)):
            self.near[which].wait(step)
        self.over(shifted(self.mine, 1))
        self.over(shifted(self.mine, 3))
        self.far.wait_all()
        self.over(shifted(self.mine, 2))

    def finish(self):
        self.across.wait()

    def free(self):
        self.far.sent()
        self.across.sent()


def gather_first(r):
    rings = []
    for part, (row, rows) in enumerate(KV_ROWS):
        own = r.kv3.at[:, pl.ds(row, rows)]
        rings.append(
            r.links.ring(
                ORDERS[part][0],
                lambda step, own=own: own,
                lambda step, at, ref=r.f1[part]: ref.at[at],
                r.f1[part].at[pl.ds(0, 3)],
            )
        )
    return rings


def gather_second(r, firsts):
    spot = place()
    rings = []
    for part, (row, rows) in enumerate(KV_ROWS):
        first, second, _ = ORDERS[part]
        f1, g2, mine = r.f1[part], r.g2[part], spot[second]
        f1[spot[first]] = r.kv3[:, row : row + rows]
        firsts[part].wait_all()
        for at in range(4):
            g2[mine, 2 * at] = f1[at, 0]
            g2[mine, 2 * at + 1] = f1[at, 1]
        rings.append(
            r.links.ring(
                second,
                lambda step, g2=g2, mine=mine: g2.at[mine],
                lambda step, at, g2=g2: g2.at[at],
                g2.at[pl.ds(0, 3)],
            )
        )
    return rings


def gather_third(r, seconds):
    spot = place()
    low_me = my_low(r)
    rings, specials = [], []
    for part, (row, rows) in enumerate(KV_ROWS):
        first, second, last = ORDERS[part]
        g2, sel, sp, rsp = r.g2[part], r.sel[part], r.sp[part], r.rsp[part]
        seconds[part].wait_all()
        targets = [low_of(r, chip_of(spot, last, step)) for step in (1, 2, 3)]
        sp[...] = jnp.zeros_like(sp)

        def choose(at, i2, i1, g2=g2, sel=sel, sp=sp, row=row, rows=rows, last=last, targets=targets):
            low = g2[i2, 2 * i1]
            high = g2[i2, 2 * i1 + 1]
            source = low_of(r, chip_of(at, last, 0))
            plane = [at[axis] for axis in (X, Y, Z) if axis != last]
            r.slots[at[0], at[1], at[2], pl.ds(row, rows)] = jnp.where(source < low_me, low, high)
            for step in (1, 2, 3):
                sel[step - 1, plane[0], plane[1]] = jnp.where(
                    source < targets[step - 1], low, high
                )
            sp[...] = jnp.where(source == 63, low, sp[...])

        plane_loop(part, choose)
        rings.append(
            r.links.ring(
                last,
                lambda step, sel=sel: sel.at[step - 1],
                lambda step, at, row=row, rows=rows, last=last: of_plane(
                    r.slots, last, at, pl.ds(row, rows)
                ),
                sel,
                apart=True,
            )
        )
        specials.append(
            r.links.ring(
                last,
                lambda step, sp=sp: sp,
                lambda step, at, rsp=rsp: rsp.at[at],
                rsp.at[pl.ds(0, 3)],
            )
        )
    r.extra[0:2] = r.kv3[...]
    return rings, specials


def gather_special(r, specials):
    spot = place()
    for part, (row, rows) in enumerate(KV_ROWS):
        rsp = r.rsp[part]
        specials[part].wait_all()
        rsp[spot[ORDERS[part][2]]] = r.sp[part][...]
        r.extra[2, row : row + rows] = add_all([rsp[at] for at in range(4)]).astype(BF16)


QUARTER = 1.0 / 16
POWER = QUARTER * 1.4426950408889634


def chunk_axis(token):
    return ORDERS[token][2] if token < 3 else X


def chunk_index(token, plane):
    index = [slice(None)] * 3
    index[chunk_axis(token)] = plane
    return tuple(index)


def unit_rows(token, lane):
    return pl.ds(16 * UNITS.index((token, lane)), 16)


def chunk_kv(r, token, plane):
    index = chunk_index(token, plane)
    quarters = [
        r.slots[(*index, unit_rows(token, lane))].reshape(256, 128) for lane in range(4)
    ]
    return jnp.concatenate(quarters[:2], axis=1), jnp.concatenate(quarters[2:], axis=1)


def extra_kv(r):
    quarters = [
        jnp.concatenate(
            [r.extra[block, unit_rows(token, lane)] for block in range(3) for token in range(4)],
            axis=0,
        )
        for lane in range(4)
    ]
    return jnp.concatenate(quarters[:2], axis=1), jnp.concatenate(quarters[2:], axis=1)


def extra_places(r, numbers):
    low = my_low(r)
    block = jnp.where(numbers < 64, low, jnp.where(numbers < 128, 127 - low, 63))
    gone = (numbers >= 128) & (low == 63)
    return jnp.where(gone, 1 << 20, block * 64 + numbers % 64)


def query_places(r, numbers):
    return places_of(r, numbers % 64, numbers >= 256)


def attention(r, thirds, specials, between):
    spot = place()
    numbers = lax.broadcasted_iota(jnp.int32, (512, 1), 0)
    latest = query_places(r, numbers)
    earliest = document_starts(r, latest)
    query = r.query[...]
    r.attn[...] = jnp.zeros_like(r.attn)
    r.total[...] = jnp.zeros_like(r.total)

    def add(weights, values):
        total = weights[:, :128]
        if weights.shape[1] == 256:
            total = total + weights[:, 128:]
            r.total[...] += total
        else:
            r.total[...] += total
            r.total[:, :64] += weights[:, 128:]
        r.attn[...] += dot32(weights.astype(BF16), values)

    def chunk(token, plane):
        keys, values = chunk_kv(r, token, plane)
        scores = dot_nt(query, keys)
        row = 4 * token + plane
        allowed = jnp.concatenate(
            [
                r.key_rows[pl.ds(row, 1)] >= earliest[:256],
                r.key_rows[pl.ds(16 + row, 1)] >= earliest[256:],
            ],
            axis=0,
        )
        add(jnp.where(allowed, jnp.exp2(scores * POWER), 0.0), values)

    for token in range(3):
        chunk(token, spot[chunk_axis(token)])
    between(0)
    for number, step in enumerate((1, 3, 2)):
        for token in range(3):
            thirds[token].wait(step)
            chunk(token, shifted(spot[chunk_axis(token)], -step))
        between(number + 1)
    for plane in range(4):
        chunk(3, plane)
    gather_special(r, specials)
    keys, values = extra_kv(r)
    scores = dot_nt(query, keys)
    places = extra_places(r, lax.broadcasted_iota(jnp.int32, (1, 192), 1))
    allowed = (places >= earliest) & (places <= latest)
    add(jnp.where(allowed, jnp.exp2(scores * POWER), 0.0), values)
    total = jnp.sum(r.total[...], axis=1, keepdims=True)
    r.attn[...] = r.attn[...] / total
    r.total[...] = jnp.broadcast_to(jnp.log2(total), (512, 128))


def attention_back(r, between):
    spot = place()
    numbers = lax.broadcasted_iota(jnp.int32, (1, 512), 1)
    latest = query_places(r, numbers)
    earliest = document_starts(r, latest)
    query, grad_out = r.query[...], r.grad_attn[...]
    log_total = jnp.transpose(r.total[...])[0:1]
    row_dot = jnp.transpose(r.dots[...])[0:1]
    r.grad_query[...] = jnp.zeros_like(r.grad_query)

    def grads_of(keys, values, allowed):
        scores = dot_nt(keys, query)
        probs = jnp.where(allowed, jnp.exp2(scores * POWER - log_total), 0.0)
        grad_probs = dot_nt(values, grad_out)
        grad_scores = (probs * (grad_probs - row_dot)).astype(BF16)
        grad_values = dot32(probs.astype(BF16), grad_out)
        grad_keys = dot32(grad_scores, query) * QUARTER
        r.grad_query[...] += dot_tn(grad_scores, keys)
        return jnp.concatenate([grad_keys, grad_values], axis=1).astype(BF16)

    def chunk(token, plane):
        keys, values = chunk_kv(r, token, plane)
        row = 4 * token + plane
        low, high = key_column(r, row, token), key_column(r, 16 + row, token)
        allowed = jnp.concatenate([low, low, high, high], axis=1) >= earliest
        grads = grads_of(keys, values, allowed)
        index = chunk_index(token, plane)
        for lane in range(4):
            r.slots[(*index, unit_rows(token, lane))] = grads[
                :, 128 * lane : 128 * lane + 128
            ].reshape(4, 4, 16, 128)

    every = (slice(None), slice(None))
    rings, specials = scatter_third(r)
    for number, step in enumerate((1, 3, 2)):
        for token in range(3):
            chunk(token, shifted(spot[chunk_axis(token)], step))
            rings[token].start(step, *every, pl.ds(0, 64))
        between(number)
    for plane in range(4):
        chunk(3, plane)
    for step in (1, 3, 2):
        for part, (_, rows) in enumerate(KV_ROWS):
            rings[part].start(step, *every, pl.ds(64, rows - 64))
    between(3)
    keys, values = extra_kv(r)
    places = extra_places(r, lax.broadcasted_iota(jnp.int32, (192, 1), 0))
    grads = grads_of(keys, values, (places >= earliest) & (places <= latest))
    for block in range(3):
        for unit, (token, lane) in enumerate(UNITS):
            row = 64 * block + 16 * token
            r.grad_extra[block, 16 * unit : 16 * unit + 16] = grads[
                row : row + 16, 128 * lane : 128 * lane + 128
            ]
    for ring in specials:
        for step in (1, 2, 3):
            ring.start(step)
    for token in range(3):
        chunk(token, spot[chunk_axis(token)])
    return rings, specials


GELU = 0.7978845608028654


def head_rows(block, head):
    start = 256 * block + 64 * head
    return slice(start, start + 64)


def queries(r):
    r.normed_b[...] = turned(r, r.normed[...])
    split_rows(r.both_normed, r.out_normed, r.normed_b[...])
    shared = share(r, r.both_normed, r.out_normed)
    r.query_raw[...] = dot32(r.normed_b[...], r.w[QUERY][...].reshape(640, 1024))
    for head in range(HEADS):
        raw = r.query_raw[:, HEAD * head : HEAD * head + HEAD]
        rotated = rope(r, rms_scale(raw, gain(r, G_QUERY))).astype(BF16)
        for block in range(2):
            r.query[head_rows(block, head)] = rotated[64 * block : 64 * block + 64]
    return shared


def gelu_parts(gate):
    inner = jnp.tanh(GELU * (gate + 0.044715 * gate * gate * gate))
    return 0.5 * gate * (1.0 + inner), inner


def columns(weight, at, width):
    rows = 8 * weight.shape[2]
    return weight[:, :, :, at : at + width].reshape(rows, width)


def down_rows(ref, number):
    return ref.at[number // 2, pl.ds(2 * (number % 2), 2)]


def split_rows(both, out, values):
    core = lax.axis_index("dp")
    values = values.astype(F32)
    none = jnp.zeros((128, 64), F32)
    low = jnp.concatenate([values[:, :320], none], axis=1)
    high = jnp.concatenate([values[:, 320:], none], axis=1)
    both[core] = jnp.where(core == 0, low, high).astype(BF16)
    out[...] = jnp.where(core == 0, high, low).astype(BF16)


def share(r, both, source):
    return r.links.across(source, lambda core: both.at[core], source)


def own_columns(ref, width, core):
    return ref.at[:, pl.ds(pl.multiple_of(core * width, width), width)]


def share_columns(r, both, ref):
    core = lax.axis_index("dp")
    width = ref.shape[1] // 2
    both[core] = own_columns(ref, width, core)[...]
    return share(r, both, own_columns(ref, width, 1 - core))


def pair(both):
    return both[...].reshape(256, both.shape[2])


def feed_forward(r, spreads):
    spreads[OUT].finish()
    for block in range(2):
        for head in range(HEADS):
            r.attn_low[64 * block : 64 * block + 64, HEAD * head : HEAD * head + HEAD] = r.attn[
                head_rows(block, head)
            ].astype(BF16)
    shared = {OUTPUT: share_columns(r, r.both_attn, r.attn_low)}
    r.proj[...] = dot32(r.attn_low[...], r.w[OUTPUT][...].reshape(1024, 640))
    r.mid[...] = r.x[...] + rms_scale(r.proj[...], gain(r, G_POST_ATTN))
    r.ffn_in[...] = rms_scale(r.mid[...], gain(r, G_FFN)).astype(BF16)
    r.ffn_in_b[...] = turned(r, r.ffn_in[...])
    for piece in (GATE_ONE, GATE_TWO, UP_ONE, UP_TWO):
        spreads[piece].finish()
    for number in range(4):
        at = slice(512 * number, 512 * number + 512)
        gate = dot32(r.ffn_in[...], columns(r.w[GATE], 512 * number, 512))
        up = dot32(r.ffn_in_b[...], columns(r.w[UP], 512 * number, 512))
        r.gate[:, at] = gate
        r.up[:, at] = up
        r.hidden[:, at] = (gelu_parts(gate)[0] * up).astype(BF16)
    split_rows(r.both_in, r.out_in, r.ffn_in[...])
    shared[GATE] = share(r, r.both_in, r.out_in)
    split_rows(r.both_in_b, r.out_in_b, r.ffn_in_b[...])
    shared[UP] = share(r, r.both_in_b, r.out_in_b)
    shared[DOWN] = share_columns(r, r.both_hidden, r.hidden)
    spreads[DOWN_ONE].finish()
    spreads[DOWN_TWO].finish()
    r.ffn_out[...] = dot32(r.hidden[...], r.w[DOWN][...].reshape(2048, 640))
    out = r.mid[...] + rms_scale(r.ffn_out[...], gain(r, G_POST_FFN))
    r.block_out[...] = low_first(r, out.astype(BF16))
    return shared


def note_gain(r, number, term):
    at, count, _, _ = GAINS[number]
    r.gain_sums[0:1, at : at + count] = term


def feed_forward_back(r, spreads, shared, start):
    core = lax.axis_index("dp")
    for piece in (GATE_ONE, GATE_TWO, OUT, UP_ONE, UP_TWO, DOWN_ONE, DOWN_TWO):
        spreads[piece].free()
    grad_out = low_first(r, r.out_cot[0].astype(F32))
    grad_ffn_out, term = norm_back(r.ffn_out[...], gain(r, G_POST_FFN), grad_out)
    note_gain(r, G_POST_FFN, term)
    low_grad = grad_ffn_out.astype(BF16)
    r.both_low[core] = low_grad
    low_shared = share(r, r.both_low, r.both_low.at[core])
    grad_in = jnp.zeros((128, 640), F32)
    grad_in_b = jnp.zeros((128, 640), F32)
    grads_shared = []
    for number in range(4):
        at = slice(512 * number, 512 * number + 512)
        down = down_rows(r.w[DOWN], number)
        grad_hidden = dot_nt(low_grad, down[...].reshape(512, 640))
        gate, up = r.gate[:, at], r.up[:, at]
        activated, inner = gelu_parts(gate)
        slope = 0.5 * (1.0 + inner) + 0.5 * gate * (1.0 - inner * inner) * GELU * (
            1.0 + 3 * 0.044715 * gate * gate
        )
        grad_gate = (grad_hidden * up * slope).astype(BF16)
        grad_up = (grad_hidden * activated).astype(BF16)
        r.both_gate[core, :, at] = grad_gate
        r.both_up[core, :, at] = grad_up
        grad_in += dot_nt(grad_gate, columns(r.w[GATE], 512 * number, 512))
        grad_in_b += dot_nt(grad_up, columns(r.w[UP], 512 * number, 512))
        if number % 2:
            lanes = pl.ds(512 * number - 512, 1024)
            for both in (r.both_gate, r.both_up):
                grads_shared.append(
                    r.links.across(
                        both.at[core, :, lanes],
                        lambda core, both=both, lanes=lanes: both.at[core, :, lanes],
                        both.at[core, :, lanes],
                    )
                )
    def columns_of_both(first):
        for number, ins, both, wait in (
            (GATE, r.both_in, r.both_gate, grads_shared[first // 512]),
            (UP, r.both_in_b, r.both_up, grads_shared[first // 512 + 1]),
        ):
            wait.wait()
            for at in (first, first + 512):
                lanes = slice(at, at + 512)
                term = dot_tn(pair(ins), both[:, :, lanes].reshape(256, 512))[:320].astype(BF16)
                r.w[number][core, :, :, lanes] = term.reshape(4, 80, 512)

    grad_in = grad_in + unturned(r, grad_in_b)
    back, term = norm_back(r.mid[...], gain(r, G_FFN), grad_in)
    note_gain(r, G_FFN, term)
    grad_mid = grad_out + back
    r.grad_mid[...] = grad_mid
    back, term = norm_back(r.proj[...], gain(r, G_POST_ATTN), grad_mid)
    note_gain(r, G_POST_ATTN, term)
    proj_low = back.astype(BF16)
    r.both_proj[core] = proj_low
    proj_shared = share(r, r.both_proj, r.both_proj.at[core])
    grad_attn = dot_nt(proj_low, r.w[OUTPUT][...].reshape(1024, 640)).astype(BF16)
    for block in range(2):
        for head in range(HEADS):
            r.grad_attn[head_rows(block, head)] = grad_attn[
                64 * block : 64 * block + 64, HEAD * head : HEAD * head + HEAD
            ]
    dots = jnp.sum(r.grad_attn[...].astype(F32) * r.attn[...], axis=1, keepdims=True)
    r.dots[...] = jnp.broadcast_to(dots, (512, 128))

    def rest_back():
        shared[DOWN].wait()
        low_shared.wait()
        term = dot_tn(pair(r.both_hidden), pair(r.both_low)).astype(BF16)
        r.w[DOWN][core] = term.reshape(4, 4, 4, 16, 640)
        start(DOWN_ONE, DOWN_TWO)
        shared[GATE].wait()
        shared[UP].wait()
        columns_of_both(0)
        start(GATE_ONE, UP_ONE)
        columns_of_both(1024)
        shared[OUTPUT].wait()
        proj_shared.wait()
        term = dot_tn(pair(r.both_attn), pair(r.both_proj)).astype(BF16)
        r.w[OUTPUT][core] = term.reshape(4, 128, 640)

    return rest_back


def queries_back(r, spreads, shared):
    core = lax.axis_index("dp")
    total = jnp.zeros((1, HEAD), F32)
    for head in range(HEADS):
        at = slice(HEAD * head, HEAD * head + HEAD)
        grad = jnp.concatenate([r.grad_query[head_rows(block, head)] for block in range(2)], axis=0)
        back, term = norm_back(
            r.query_raw[:, at], gain(r, G_QUERY), rope_back(r, grad * QUARTER)
        )
        total += term
        r.both_query[core, :, at] = back.astype(BF16)
    note_gain(r, G_QUERY, total)
    query_shared = share(r, r.both_query, r.both_query.at[core])
    r.grad_normed[...] = unturned(
        r, dot_nt(r.both_query[core], r.w[QUERY][...].reshape(640, 1024))
    )

    def rest_back():
        spreads[ASK].free()
        shared[QUERY].wait()
        query_shared.wait()
        term = dot_tn(pair(r.both_normed), pair(r.both_query))[:320].astype(BF16)
        r.w[QUERY][core] = term.reshape(4, 80, 1024)

    return rest_back


def add_rows(count, to, value):
    def one(at):
        rows = pl.ds(pl.multiple_of(at * 16, 16), 16)
        to[rows] = (to[rows].astype(F32) + value[rows].astype(F32)).astype(BF16)

    loop(count // 16, one)


def add_into(to, value):
    lead = to.shape[:-2]
    if not lead:
        add_rows(to.shape[0], to, value)
    elif len(lead) == 1:
        for at in range(lead[0]):
            add_rows(to.shape[1], to.at[at], value.at[at])
    else:
        for at in range(lead[0]):
            add_into(to.at[at], value.at[at])


class Gather:
    def __init__(self, r, piece):
        self.piece, axis = piece, piece_axis(piece)
        core, mine = lax.axis_index("dp"), place()[axis]
        number = PIECES[piece][0]
        self.land = piece_of(piece, r.landed[number], 3)
        self.at = lambda step: piece_plane(r, piece, core, shifted(mine, step))
        sends = r.links.sends(self.land)
        self.far = r.links.ring(
            axis,
            lambda step: half_of(piece, self.at(2), 0 if step == 1 else 1),
            lambda step, at: half_of(piece, self.land.at[2], 0 if step == 1 else 1),
            None,
            steps=(1, 3),
            apart=True,
            sends=sends,
        )
        self.near = r.links.ring(
            axis,
            self.at,
            lambda step, at: self.land.at[0 if step == 1 else 1],
            self.land.at[pl.ds(0, 2)],
            begin=False,
            steps=(1, 3),
            sends=sends,
        )

    def relay(self):
        for which, step in enumerate((1, 3)):
            self.far.wait(step)
            add_into(
                half_of(self.piece, self.at(step), which),
                half_of(self.piece, self.land.at[2], which),
            )
            self.near.start(step)


def repack(r, number, *gathers):
    _, rows, by_chip = WEIGHTS[number]
    count, tiles = plane_tiles(number)
    own, land = own_plane(r, number), r.landed[number]
    for gather in gathers:
        gather.near.wait_all()
    for tile in range(tiles):
        lanes = slice(128 * tile, 128 * tile + 128)
        index = (slice(None),) * (3 if by_chip else 1) + (lanes,)
        total = add_all([own[index]] + [land[(step, *index)] for step in range(2)])
        r.stage[pl.ds(tile, count, stride=tiles)] = total.reshape(count, 128)

    def one(chip):
        r.p[number][chip // 4, chip % 4, :rows] = r.stage[
            pl.ds(pl.multiple_of(chip * rows, 8), rows)
        ].astype(BF16)

    loop(16, one)


def late_second(r, number):
    second = weight_order(number)[1]
    mine = place()[second]
    return r.links.ring(
        second,
        lambda step: r.p[number].at[shifted(mine, step)],
        lambda step, at: r.second[number].at[step - 1],
        r.second[number],
        begin=False,
    )


def late_first(r, number):
    first = weight_order(number)[0]
    mine = place()[first]
    return r.links.ring(
        first,
        lambda step: r.line[number].at[shifted(mine, step)],
        lambda step, at: r.first[number].at[step - 1],
        r.first[number],
        begin=False,
    )


def late_line(r, number, ring):
    own = place()[weight_order(number)[1]]
    ring.wait_all()
    for at in range(4):
        r.line[number][at] = add_all(
            [r.p[number][own, at]] + [r.second[number][step, at] for step in range(3)]
        ).astype(BF16)


def late_end(r, number, ring, out):
    mine = place()[weight_order(number)[0]]
    ring.wait_all()
    out[...] = add_all([r.line[number][mine]] + [r.first[number][step] for step in range(3)])


def scatter_third(r):
    spot = place()
    rings, specials = [], []
    for part, (row, rows) in enumerate(KV_ROWS):
        last = ORDERS[part][2]
        rings.append(
            r.links.ring(
                last,
                lambda step, row=row, rows=rows, last=last: of_plane(
                    r.slots, last, shifted(spot[last], step), pl.ds(row, rows)
                ),
                lambda step, at, rb=r.rb[part]: rb.at[step - 1],
                r.rb[part],
                begin=False,
            )
        )
        specials.append(
            r.links.ring(
                last,
                lambda step, row=row, rows=rows: r.grad_extra.at[2, pl.ds(row, rows)],
                lambda step, at, rs=r.rs[part]: rs.at[step - 1],
                r.rs[part],
                begin=False,
            )
        )
    return rings, specials


def scatter_second(r, thirds, specials):
    spot = place()
    me = lax.axis_index("ctx")
    low_me = my_low(r)
    rings = []
    for part, (row, rows) in enumerate(KV_ROWS):
        first, second, last = ORDERS[part]
        rb, rs, total, land = r.rb[part], r.rs[part], r.g2[part], r.r2[part]
        thirds[part].wait_all()
        specials[part].wait_all()
        special = add_all([r.grad_extra[2, row : row + rows]] + [rs[step] for step in range(3)])
        r.sp[part][...] = special.astype(BF16)
        senders = [low_of(r, chip_of(spot, last, -step)) for step in (1, 2, 3)]

        def collect(
            at, i2, i1, rb=rb, sp=r.sp[part], total=total, row=row, rows=rows, last=last, senders=senders
        ):
            chip = chip_of(at, last, 0)
            source = low_of(r, chip)
            plane = [at[axis] for axis in (X, Y, Z) if axis != last]
            both = r.slots[at[0], at[1], at[2], pl.ds(row, rows)].astype(F32)
            none = jnp.zeros_like(both)
            low = jnp.where(source < low_me, both, none)
            for step in (1, 2, 3):
                came = rb[step - 1, plane[0], plane[1]].astype(F32)
                low += jnp.where(source < senders[step - 1], came, none)
                both += came
            high = both - low
            low += jnp.where(chip == me, r.grad_extra[0, pl.ds(row, rows)].astype(F32), none)
            high += jnp.where(chip == me, r.grad_extra[1, pl.ds(row, rows)].astype(F32), none)
            low += jnp.where(source == 63, sp[...].astype(F32), none)
            total[i2, 2 * i1] = low.astype(BF16)
            total[i2, 2 * i1 + 1] = high.astype(BF16)

        plane_loop(part, collect)
        rings.append(
            r.links.ring(
                second,
                lambda step, total=total, second=second: total.at[shifted(spot[second], step)],
                lambda step, at, land=land: land.at[step - 1],
                land,
            )
        )
    return rings


def scatter_first(r, seconds):
    spot = place()
    rings = []
    for part in range(3):
        first, second, _ = ORDERS[part]
        total, land, line, end = r.g2[part], r.r2[part], r.f1[part], r.r1[part]
        seconds[part].wait_all()

        def pick(index, total=total, land=land, mine=spot[second]):
            return add_all([total[mine, index]] + [land[step, index] for step in range(3)]).astype(
                BF16
            )

        for at in range(4):
            line[at, 0] = pick(2 * at)
            line[at, 1] = pick(2 * at + 1)
        rings.append(
            r.links.ring(
                first,
                lambda step, line=line, first=first: line.at[shifted(spot[first], step)],
                lambda step, at, end=end: end.at[step - 1],
                end,
            )
        )
    return rings


def scatter_end(r, firsts):
    spot = place()
    for part, (row, rows) in enumerate(KV_ROWS):
        firsts[part].wait_all()
        mine = spot[ORDERS[part][0]]
        for index in range(2):
            r.kv_sum[index, row : row + rows] = add_all(
                [r.f1[part][mine, index]] + [r.r1[part][step, index] for step in range(3)]
            )


def keys_values_back(r, split_shared, between):
    lanes = []
    for lane in range(4):
        pieces = [
            r.kv_sum[block, unit_rows(token, lane)] for block in range(2) for token in range(4)
        ]
        lanes.append(jnp.concatenate(pieces, axis=0))
    grad_keys = jnp.concatenate(lanes[:2], axis=1)
    grad_values = jnp.concatenate(lanes[2:], axis=1)
    back, term = norm_back(r.key_raw[...], gain(r, G_KEY), rope_back(r, grad_keys))
    note_gain(r, G_KEY, term)
    kv_low = jnp.concatenate([back, grad_values], axis=1).astype(BF16)
    core = lax.axis_index("dp")
    r.both_kv[core] = kv_low
    kv_shared = share(r, r.both_kv, r.both_kv.at[core])
    grad_split = dot_nt(kv_low, r.w_kv[...]).astype(BF16)
    grad_normed = dot_nt(grad_split, r.splitting[...]) + r.grad_normed[...]
    back, term = norm_back(r.x[...], gain(r, G_ATTN), grad_normed)
    note_gain(r, G_ATTN, term)
    gains_back(r, G_KEY, G_ATTN)
    low, high = r.held[:64], r.held[64:]
    r.both_held[core] = jnp.where(core == 0, low, high)
    r.out_held[...] = jnp.where(core == 0, high, low)
    held_shared = share(r, r.both_held, r.out_held)
    r.tokens_grad[...] = low_first(r, (r.grad_mid[...] + back).astype(BF16))
    between()
    r.stage[SMALL : SMALL + 1024] = jnp.zeros((1024, 128), F32)
    split_shared.wait()
    kv_shared.wait()
    terms = dot_tn(pair(r.both_split), pair(r.both_kv))
    for tile in range(4):
        lanes = slice(128 * tile, 128 * tile + 128)
        r.stage[pl.ds(tile, 256, stride=4)] = terms[:256, lanes]
        r.stage[pl.ds(SMALL + tile, 64, stride=16)] = terms[256:320, lanes]
    held_shared.wait()
    r.stage[pl.ds(SMALL + 4, 64, stride=16)] = r.both_held[0] + r.both_held[1]
    for unit in range(2):
        for plane in range(4):
            row = SMALL * unit + 256 * plane
            r.u[unit][core, plane] = r.stage[row : row + 256].astype(BF16).reshape(4, 4, 16, 128)


def gains_back(r, *numbers):
    for number in numbers:
        at, count, _, _ = GAINS[number]
        lanes, owners = gain_maps(r, number)
        term = jnp.where(owners, r.gain_sums[0:1, at : at + count], 0.0).astype(BF16)
        r.held[...] += dot_nt(term, lanes)


def small_sums(r, between):
    links = r.links
    core = lax.axis_index("dp")
    spot = place()
    axes = ((X, Y, Z), (Y, Z, X))
    rings = []
    for unit, order in enumerate(axes):
        own, land = r.u[unit], r.land3[unit]
        axis = order[0]
        rings.append(
            links.ring(
                axis,
                lambda step, own=own, axis=axis: own.at[core, shifted(spot[axis], step)],
                lambda step, at, land=land: land.at[step - 1],
                land,
            )
        )
    between[0]()
    later = []
    for unit, order in enumerate(axes):
        own, land, out, to = r.u[unit], r.land3[unit], r.sum2[unit], r.land2[unit]
        rings[unit].wait_all()
        mine = spot[order[0]]

        def add(at, own=own, land=land, out=out, mine=mine):
            out[at] = add_all([own[core, mine, at]] + [land[step, at] for step in range(3)]).astype(
                BF16
            )

        loop(4, add)
        axis = order[1]
        later.append(
            links.ring(
                axis,
                lambda step, out=out, axis=axis: out.at[shifted(spot[axis], step)],
                lambda step, at, to=to: to.at[step - 1],
                to,
            )
        )
    between[1]()
    last = []
    for unit, order in enumerate(axes):
        own, land, out, to = r.sum2[unit], r.land2[unit], r.sum1[unit], r.land1[unit]
        later[unit].wait_all()
        out[...] = add_all([own[spot[order[1]]]] + [land[step] for step in range(3)]).astype(BF16)
        axis = order[2]
        last.append(
            links.ring(
                axis,
                lambda step, out=out, axis=axis: out.at[shifted(spot[axis], step)],
                lambda step, at, to=to: to.at[step - 1],
                to,
            )
        )
    between[2]()
    for unit, order in enumerate(axes):
        last[unit].wait_all()
        r.fk[16 * unit : 16 * unit + 16] = add_all(
            [r.sum1[unit][spot[order[2]]]] + [r.land1[unit][step] for step in range(3)]
        )


def layer(r):
    greet()
    for copy in r.fetches.values():
        copy.wait()
    pack(r)
    greeted()
    early_rings, early_held, spreads = early(r)
    unpack_small(r)
    keys_values(r)
    firsts = gather_first(r)
    split_shared = share(r, r.both_split, r.out_split)
    seconds = gather_second(r, firsts)
    early_pieces = (ASK, OUT, GATE_ONE, UP_ONE, DOWN_ONE, DOWN_TWO)
    for piece in early_pieces:
        spreads[piece].forward()
    for piece in LATE_PIECES:
        spreads[piece].forward()
    before = tuple(r.links.open)
    thirds, specials = gather_third(r, seconds)
    for piece in early_pieces:
        spreads[piece].pass_on()
    for piece in LATE_PIECES:
        spreads[piece].pass_on()
    spreads[ASK].finish()
    query_shared = queries(r)

    def pass_on(number):
        if number == 0:
            r.links.settle(before)

    attention(r, thirds, specials, pass_on)
    shared = feed_forward(r, spreads)
    shared[QUERY] = query_shared
    before = tuple(r.links.open)
    sums = {}

    def start(*pieces):
        for piece in pieces:
            sums[piece] = Gather(r, piece)

    def relay(*pieces):
        for piece in pieces:
            sums[piece].relay()

    pieces = {
        GATE: (GATE_ONE, GATE_TWO),
        OUTPUT: (OUT,),
        UP: (UP_ONE, UP_TWO),
        QUERY: (ASK,),
        DOWN: (DOWN_ONE, DOWN_TWO),
    }
    second_rings, first_rings = {}, {}

    def prepare_late():
        for number in pieces:
            second_rings[number] = late_second(r, number)
            first_rings[number] = late_first(r, number)

    def send_late(*numbers):
        for number in numbers:
            repack(r, number, *(sums[piece] for piece in pieces[number]))
            for step in (1, 2, 3):
                second_rings[number].start(step)

    def go_on(*numbers):
        for number in numbers:
            late_line(r, number, second_rings[number])
            for step in (1, 2, 3):
                first_rings[number].start(step)

    def finish(*numbers):
        outs = (r.fgate, r.foutput, r.fup, r.fquery, r.fdown)
        for number in numbers:
            late_end(r, number, first_rings[number], outs[number])

    rest_back = feed_forward_back(r, spreads, shared, start)
    thirds, third_specials = attention_back(r, lambda number: None)
    query_back = queries_back(r, spreads, shared)
    rest_back()
    query_back()
    start(GATE_TWO, UP_TWO, OUT, ASK)
    for ring in early_rings:
        ring.sent()
    for ring in seconds:
        ring.sent()
    r.links.settle(before)
    before = tuple(r.links.open)
    r.held[...] = jnp.zeros_like(r.held)
    gains_back(r, G_POST_ATTN, G_FFN, G_POST_FFN, G_QUERY)
    seconds = scatter_second(r, thirds, third_specials)
    relay(DOWN_ONE, GATE_ONE, UP_ONE)
    firsts = scatter_first(r, seconds)
    relay(DOWN_TWO, GATE_TWO, UP_TWO)
    scatter_end(r, firsts)
    relay(OUT, ASK)
    for copy in early_held:
        copy.sent()
    prepare_late()
    core = lax.axis_index("dp")

    def on(which, action, *numbers):
        pl.when(core == which)(lambda: action(*numbers))

    keys_values_back(r, split_shared, lambda: on(1, send_late, DOWN, GATE, UP, OUTPUT, QUERY))

    def one():
        r.links.settle(before)
        on(0, send_late, DOWN, GATE, UP)

    def two():
        on(0, send_late, OUTPUT, QUERY)
        on(1, go_on, DOWN, GATE, UP, OUTPUT, QUERY)

    def three():
        on(0, go_on, DOWN, GATE, UP, OUTPUT, QUERY)

    small_sums(r, (one, two, three))
    finish(DOWN, GATE, UP, OUTPUT, QUERY)
    r.links.settle()
    assert r.links.sending <= COPIES[0] and r.links.receiving <= COPIES[1]


def end(r):
    def rows(out, source, base, count, tiles):
        r.stage[base : base + count * tiles] = source
        for tile in range(tiles):
            out[:, 128 * tile : 128 * tile + 128] = columns_of(r, base, count, tiles, tile)

    rows(r.gate_grad, r.fgate[...], 0, 5, 16)
    rows(r.output_grad, r.foutput[0:40], 80, 8, 5)
    rows(r.up_grad, r.fup[...], 128, 5, 16)
    rows(r.query_grad, r.fquery[0:40], 208, 5, 8)
    rows(r.down_grad, r.fdown[...], 256, 16, 5)
    r.stage[336:368] = r.fk[...]
    for tile in range(4):
        out = (r.key_grad, r.value_grad)[tile // 2]
        half = 128 * (tile % 2)
        out[:, half : half + 128] = columns_of(r, 336, 5, 4, tile)
    line = r.fk[16:24]
    gain_grads = (r.grad_attn_norm, r.grad_post_attn, r.grad_ffn_norm, r.grad_post_ffn, r.grad_q, r.grad_k)
    for number, (_, _, held, lane) in enumerate(GAINS):
        out = gain_grads[number]
        moved = line if lane == 0 else pltpu.roll(line, 128 - lane, 1)
        out[...] = moved[4:5, :held]
    r.final_out[0] = r.block_out[...]
    r.final_grad[0] = r.tokens_grad[...]


COPIES = (97, 159)


def by_part(*dims):
    return [hold(BF16, *dims, rows, 128) for _, rows in KV_ROWS]


def by_flat(*dims):
    return [hold(BF16, *dims, rows, 128) for rows in (80, 48, 80, 48, 80)]


def by_unit(*dims):
    return [hold(BF16, *dims, 16, 128) for _ in range(2)]


def by_weight(lead, core):
    return [
        hold(BF16, *core, *lead, 80, 2048),
        hold(BF16, *core, *lead, 128, 640),
        hold(BF16, *core, *lead, 80, 2048),
        hold(BF16, *core, *lead, 80, 1024),
        hold(BF16, *core, *lead, 4, 4, 16, 640),
    ]


def buffers():
    return dict(
        stage=hold(F32, 4096, 128),
        x=hold(F32, 128, 640),
        cos=hold(F32, 128, 128),
        sin=hold(F32, 128, 128),
        gains=hold(F32, 8, 3072),
        gain_sums=hold(F32, 8, 3072),
        turning=hold(BF16, 640, 640),
        splitting=hold(BF16, 640, 640),
        key_base=hold(jnp.int32, 32, 16, 128),
        key_rows=hold(jnp.int32, 32, 256),
        p=by_flat(4, 4),
        second=by_flat(3, 4),
        line=by_flat(4),
        first=by_flat(3),
        u=by_unit(2, 4, 4, 4),
        both_split=hold(BF16, 2, 128, 384),
        both_kv=hold(BF16, 2, 128, 512),
        both_held=hold(F32, 2, 64, 128),
        out_held=hold(F32, 64, 128),
        out_split=hold(BF16, 128, 384),
        held=hold(F32, 128, 128),
        land3=by_unit(3, 4, 4),
        sum2=by_unit(4, 4),
        land2=by_unit(3, 4),
        sum1=by_unit(4),
        land1=by_unit(3),
        w_kv=hold(BF16, 640, 512),
        w=by_weight((4,), (2,)),
        both_hidden=hold(BF16, 2, 128, 1024),
        both_low=hold(BF16, 2, 128, 640),
        both_gate=hold(BF16, 2, 128, 2048),
        both_up=hold(BF16, 2, 128, 2048),
        both_in=hold(BF16, 2, 128, 384),
        both_in_b=hold(BF16, 2, 128, 384),
        both_attn=hold(BF16, 2, 128, 512),
        both_proj=hold(BF16, 2, 128, 640),
        both_normed=hold(BF16, 2, 128, 384),
        both_query=hold(BF16, 2, 128, 1024),
        out_in=hold(BF16, 128, 384),
        out_in_b=hold(BF16, 128, 384),
        out_normed=hold(BF16, 128, 384),
        landed=[
            hold(BF16, 3, 80, 2048),
            hold(BF16, 3, 128, 640),
            hold(BF16, 3, 80, 2048),
            hold(BF16, 3, 80, 1024),
            hold(BF16, 3, 4, 4, 16, 640),
        ],
        kv3=hold(BF16, 2, 256, 128),
        f1=by_part(4, 2),
        g2=by_part(4, 8),
        sel=by_part(3, 4, 4),
        sp=by_part(),
        rsp=by_part(4),
        rb=by_part(3, 4, 4),
        rs=by_part(3),
        r2=by_part(3, 8),
        r1=by_part(3, 2),
        slots=hold(BF16, 4, 4, 4, 256, 128),
        extra=hold(BF16, 3, 256, 128),
        grad_extra=hold(BF16, 3, 256, 128),
        kv_sum=hold(F32, 2, 256, 128),
        normed=hold(BF16, 128, 640),
        normed_split=hold(BF16, 128, 640),
        normed_b=hold(BF16, 128, 640),
        key_raw=hold(F32, 128, 256),
        query_raw=hold(F32, 128, 1024),
        query=hold(BF16, 512, 256),
        attn=hold(F32, 512, 256),
        total=hold(F32, 512, 128),
        dots=hold(F32, 512, 128),
        attn_low=hold(BF16, 128, 1024),
        proj=hold(F32, 128, 640),
        mid=hold(F32, 128, 640),
        ffn_in=hold(BF16, 128, 640),
        ffn_in_b=hold(BF16, 128, 640),
        gate=hold(F32, 128, 2048),
        up=hold(F32, 128, 2048),
        hidden=hold(BF16, 128, 2048),
        ffn_out=hold(F32, 128, 640),
        grad_mid=hold(F32, 128, 640),
        grad_attn=hold(BF16, 512, 256),
        grad_query=hold(F32, 512, 256),
        grad_normed=hold(F32, 128, 640),
    )


def on_device(
    tokens,
    doc_lengths,
    block_order,
    attn_norm,
    query_weight,
    key_weight,
    value_weight,
    query_gain,
    key_gain,
    output_weight,
    attn_post_norm,
    ffn_norm,
    gate_weight,
    up_weight,
    down_weight,
    ffn_post_norm,
    out_cot,
):
    made = run(
        layer,
        dict(block_order=block_order, doc_lengths=doc_lengths),
        {},
        dict(
            block_out=hold(BF16, 128, 640),
            tokens_grad=hold(BF16, 128, 640),
            fgate=hold(F32, 80, 128),
            foutput=hold(F32, 48, 128),
            fup=hold(F32, 80, 128),
            fquery=hold(F32, 48, 128),
            fdown=hold(F32, 80, 128),
            fk=hold(F32, 32, 128),
        ),
        buffers(),
        number=1,
        copies=COPIES,
        fetched=dict(
            gate_weight=gate_weight,
            output_weight=output_weight,
            up_weight=up_weight,
            query_weight=query_weight,
            down_weight=down_weight,
            key_weight=key_weight,
            value_weight=value_weight,
            attn_norm=attn_norm[None],
            attn_post_norm=attn_post_norm[None],
            ffn_norm=ffn_norm[None],
            ffn_post_norm=ffn_post_norm[None],
            query_gain=query_gain[None],
            key_gain=key_gain[None],
            tokens=tokens,
            table=jnp.asarray(number_table()),
            frequency=jnp.asarray(ROPE_BASE ** (-2.0 * np.arange(128) / 256), F32)[None],
            out_cot=out_cot,
        ),
    )
    results = run(
        end,
        {},
        made,
        dict(
            final_out=hold(BF16, 1, 128, 640),
            final_grad=hold(BF16, 1, 128, 640),
            grad_attn_norm=hold(F32, 1, 5),
            query_grad=hold(F32, 5, 1024),
            key_grad=hold(F32, 5, 256),
            value_grad=hold(F32, 5, 256),
            grad_q=hold(F32, 1, 2),
            grad_k=hold(F32, 1, 2),
            output_grad=hold(F32, 8, 640),
            grad_post_attn=hold(F32, 1, 5),
            grad_ffn_norm=hold(F32, 1, 5),
            gate_grad=hold(F32, 5, 2048),
            up_grad=hold(F32, 5, 2048),
            down_grad=hold(F32, 16, 640),
            grad_post_ffn=hold(F32, 1, 5),
        ),
        dict(stage=hold(F32, 3088, 128)),
    )
    return tuple(
        value.reshape(-1) if value.shape[0] == 1 and value.ndim == 2 else value
        for value in results.values()
    )


def solution(mesh):
    rows = P(("dp", "ctx"), None)
    vector = P(("dp", "ctx"))
    stream = P("dp", "ctx", None)
    return jax.shard_map(
        on_device,
        mesh=mesh,
        in_specs=(
            stream,
            P("dp", None),
            P(),
            vector,
            rows,
            rows,
            rows,
            vector,
            vector,
            rows,
            vector,
            vector,
            rows,
            rows,
            rows,
            vector,
            stream,
        ),
        out_specs=(
            stream,
            stream,
            vector,
            rows,
            rows,
            rows,
            vector,
            vector,
            rows,
            vector,
            vector,
            rows,
            rows,
            rows,
            vector,
        ),
        check_vma=False,
    )
```

```python
from types import SimpleNamespace

import jax
import jax.numpy as jnp
import numpy as np
from jax import lax
from jax.experimental import pallas as pl
from jax.experimental.pallas import tpu as pltpu
from jax.sharding import PartitionSpec as P

EPSILON = 1e-06
ROPE_BASE = 1000000.0
MESH = pl.DeviceIdType.MESH
F32 = jnp.float32
BF16 = jnp.bfloat16
MIB = 2**20

X, Y, Z = 0, 1, 2
ORDERS = ((Z, Y, X), (X, Z, Y), (Y, X, Z))
UNITS = (
    ((0, 0), (0, 1), (0, 2), (0, 3), (3, 0))
    + ((1, 0), (1, 1), (1, 2), (1, 3), (3, 1))
    + ((2, 0), (2, 1), (2, 2), (2, 3), (3, 2), (3, 3))
)
KV_ROWS = ((0, 80), (80, 80), (160, 96))
HEADS = 4
HEAD = 256
SCALE = HEAD**-0.5
LOG2E = 1.4426950408889634


def place():
    chip = lax.axis_index("ctx")
    return (chip // 16, (chip // 4) % 4, chip % 4)


def shifted(value, step):
    return lax.rem(value + step + 4, 4)


def peer(axis, step):
    spot = list(place())
    spot[axis] = shifted(spot[axis], step)
    return (lax.axis_index("dp"), spot[0] * 16 + spot[1] * 4 + spot[2])


def other_core():
    return (1 - lax.axis_index("dp"), lax.axis_index("ctx"))


def greet():
    barrier = pltpu.get_barrier_semaphore()
    for axis in (X, Y, Z):
        for step in (1, 2, 3):
            pl.semaphore_signal(barrier, inc=1, device_id=peer(axis, step), device_id_type=MESH)
    pl.semaphore_signal(barrier, inc=1, device_id=other_core(), device_id_type=MESH)


def greeted():
    pl.semaphore_wait(pltpu.get_barrier_semaphore(), 10)


class Ring:
    def __init__(self, links, axis, source, landing, whole, steps, apart, sends):
        self.links, self.axis, self.source, self.landing = links, axis, source, landing
        self.whole, self.apart = whole, apart
        self.sends = links.sends(whole) if sends is None else sends
        if apart:
            self.numbers = {step: links.receive() for step in steps}
        else:
            self.numbers = dict.fromkeys(steps, links.receive())

    def copy(self, step, sender):
        return self.links.copy(
            self.sends,
            self.numbers[step],
            self.source(step),
            self.landing(step, sender),
            peer(self.axis, step),
        )

    def start(self, step, *index):
        source, landing = self.source(step), self.landing(step, place()[self.axis])
        if index:
            source, landing = source.at[index], landing.at[index]
        self.links.copy(
            self.sends, self.numbers[step], source, landing, peer(self.axis, step)
        ).start()

    def wait(self, step):
        self.copy(step, shifted(place()[self.axis], -step)).wait_recv()

    def wait_all(self):
        if self.apart:
            for step in self.numbers:
                self.wait(step)
        else:
            step = next(iter(self.numbers))
            self.links.copy(
                self.sends, self.numbers[step], self.whole, self.whole, peer(self.axis, step)
            ).wait_recv()

    def sent(self):
        self.links.settle((self.sends,))


class Across:
    def __init__(self, links, whole):
        self.links, self.whole = links, whole
        self.sends, self.number = links.sends(whole), links.receive()

    def add(self, source, landing):
        there = landing(lax.axis_index("dp"))
        self.links.copy(self.sends, self.number, source, there, other_core()).start()

    def wait(self):
        self.links.copy(
            self.sends, self.number, self.whole, self.whole, other_core()
        ).wait_recv()

    def sent(self):
        self.links.settle((self.sends,))


class Links:
    def __init__(self, send, recv):
        self.send, self.recv = send, recv
        self.sending, self.receiving, self.open = 0, 0, {}

    def sends(self, whole):
        self.open[self.sending] = whole
        self.sending += 1
        return self.sending - 1

    def receive(self):
        self.receiving += 1
        return self.receiving - 1

    def copy(self, send, recv, source, landing, device):
        return pltpu.make_async_remote_copy(
            src_ref=source,
            dst_ref=landing,
            send_sem=self.send.at[send],
            recv_sem=self.recv.at[recv],
            device_id=device,
            device_id_type=MESH,
        )

    def ring(
        self, axis, source, landing, whole, begin=True, steps=(1, 2, 3), apart=False, sends=None
    ):
        ring = Ring(self, axis, source, landing, whole, steps, apart, sends)
        if begin:
            for step in steps:
                ring.start(step)
        return ring

    def across(self, source, landing, whole):
        across = Across(self, whole)
        across.add(source, landing)
        return across

    def settle(self, numbers=None):
        for number in tuple(self.open if numbers is None else numbers):
            if number in self.open:
                whole = self.open.pop(number)
                self.copy(number, 0, whole, whole, other_core()).wait_send()


VMEM = pl.BlockSpec(memory_space=pltpu.VMEM)
SMEM = pl.BlockSpec(memory_space=pltpu.SMEM)
ANY = pl.BlockSpec(memory_space=pl.ANY)


def hold(kind, *shape):
    return pltpu.VMEM(shape, kind)


def run(stage, numbers, ins, outs, scratch, number=None, copies=(), fetched={}):
    flat, shape = jax.tree.flatten(scratch, is_leaf=lambda leaf: not isinstance(leaf, (dict, list)))

    def kernel(*refs):
        count = len(numbers) + len(fetched) + len(ins) + len(outs)
        named = dict(zip((*numbers, *fetched, *ins, *outs), refs))
        rest = refs[count + len(flat) :]
        r = SimpleNamespace(**named)
        vars(r).update(jax.tree.unflatten(shape, refs[count : count + len(flat)]))
        r.fetches = {}
        for at, name in enumerate(fetched):
            held = rest[at]
            copy = pltpu.make_async_copy(named[name], held, rest[len(fetched)].at[at])
            copy.start()
            r.fetches[name] = copy
            setattr(r, name, held)
        if copies:
            r.links = Links(*rest[-2:])
        stage(r)

    remote = dict(collective_id=number, has_side_effects=True) if copies else {}
    results = pl.pallas_call(
        kernel,
        out_shape=[jax.ShapeDtypeStruct(out.shape, out.dtype) for out in outs.values()],
        in_specs=[SMEM] * len(numbers) + [ANY] * len(fetched) + [VMEM] * len(ins),
        out_specs=[VMEM] * len(outs),
        scratch_shapes=flat
        + [pltpu.VMEM(value.shape, value.dtype) for value in fetched.values()]
        + ([pltpu.SemaphoreType.DMA((len(fetched),))] if fetched else [])
        + [pltpu.SemaphoreType.DMA((count,)) for count in copies],
        compiler_params=pltpu.CompilerParams(vmem_limit_bytes=60 * MIB, **remote),
    )(*numbers.values(), *fetched.values(), *ins.values())
    return dict(zip(outs, results))


def dot32(left, right):
    return jnp.dot(left, right, preferred_element_type=F32)


def dot_nt(left, right):
    return lax.dot_general(left, right, (((1,), (1,)), ((), ())), preferred_element_type=F32)


def dot_tn(left, right):
    return lax.dot_general(left, right, (((0,), (0,)), ((), ())), preferred_element_type=F32)


def add_all(values):
    total = values[0].astype(F32)
    for value in values[1:]:
        total += value.astype(F32)
    return total


def loop(count, body):
    def step(number, unused):
        body(number)
        return unused

    lax.fori_loop(0, count, step, 0)


def my_low(r):
    chip = lax.axis_index("ctx")
    return jnp.minimum(r.block_order[2 * chip], r.block_order[2 * chip + 1])


def low_of(r, chip):
    return jnp.minimum(r.block_order[2 * chip], r.block_order[2 * chip + 1])


def low_first(r, rows):
    chip = lax.axis_index("ctx")
    flip = r.block_order[2 * chip] > r.block_order[2 * chip + 1]
    return jnp.where(flip, jnp.concatenate([rows[64:], rows[:64]], axis=0), rows)


def document_starts(r, places):
    start = jnp.zeros_like(places)
    at = 0
    for number in range(1, 8):
        at = at + r.doc_lengths[0, number - 1]
        start = jnp.where(places >= at, at, start)
    return start


def places_of(r, within, high):
    low = my_low(r)
    return jnp.where(high, 127 - low, low) * 64 + within


def number_table():
    def turned_device(device):
        core, x, y, z = device // 64, (device // 16) % 4, (device // 4) % 4, device % 4
        return ((core * 4 + y) * 4 + z) * 4 + x

    table = np.zeros((8, 640), np.int32)
    k = np.arange(640)
    table[0], table[1] = k % 5, turned_device(k // 5)
    core, y, z, x, row = k // 320, (k // 80) % 4, (k // 20) % 4, (k // 5) % 4, k % 5
    table[2] = (((core * 4 + x) * 4 + y) * 4 + z) * 5 + row
    table[3, :512] = 5 * (k[:512] // 4) + k[:512] % 4
    device = np.arange(128)
    table[3, 512 + turned_device(device)] = 5 * device + 4
    table[4, :256], table[5, :256] = k[:256] % 2, turned_device(k[:256] // 2)
    return table


def one_hot(rows, numbers):
    shape = (rows, numbers.shape[1])
    return jnp.where(lax.broadcasted_iota(jnp.int32, shape, 0) == numbers, 1.0, 0.0).astype(BF16)


GAINS = ((0, 640, 5, 0), (640, 640, 5, 5), (1280, 640, 5, 10), (1920, 640, 5, 15))
GAINS += ((2560, 256, 2, 20), (2816, 256, 2, 22))
G_ATTN, G_POST_ATTN, G_FFN, G_POST_FFN, G_QUERY, G_KEY = range(6)


def gain_maps(r, number):
    _, columns, held, lane = GAINS[number]
    row = 0 if held == 5 else 4
    rest, owner = r.table[row : row + 1, :columns], r.table[row + 1 : row + 2, :columns]
    lanes = one_hot(128, rest + lane)
    owners = lax.broadcasted_iota(jnp.int32, (128, columns), 0) == owner
    return lanes, owners


def gain(r, number):
    at, columns, _, _ = GAINS[number]
    return r.gains[0:1, at : at + columns]


def rows_of(r, base, weight, count):
    tiles = weight.shape[1] // 128
    for tile in range(tiles):
        r.stage[pl.ds(base + tile, count, stride=tiles)] = weight[
            :, 128 * tile : 128 * tile + 128
        ].astype(F32)


def columns_of(r, base, count, tiles, tile):
    return r.stage[pl.ds(base + tile, count, stride=tiles)]


def pack(r):
    rows_of(r, 0, r.gate_weight, 5)
    rows_of(r, 80, r.output_weight, 8)
    rows_of(r, 128, r.up_weight, 5)
    rows_of(r, 208, r.query_weight, 5)
    rows_of(r, 256, r.down_weight, 16)
    for tile in range(4):
        weight = (r.key_weight, r.value_weight)[tile // 2]
        half = 128 * (tile % 2)
        r.stage[pl.ds(336 + tile, 5, stride=4)] = weight[:, half : half + 128].astype(F32)
    r.stage[356:357] = jnp.zeros((1, 128), F32)
    own = (r.attn_norm, r.attn_post_norm, r.ffn_norm, r.ffn_post_norm, r.query_gain, r.key_gain)
    for ref, (_, _, held, lane) in zip(own, GAINS):
        r.stage[356:357, lane : lane + held] = ref[...].astype(F32)
    spot = place()
    for number, ref in enumerate(r.p):
        first, second, _ = weight_order(number)
        rows = ref.shape[2]
        start = (0, 80, 128, 208, 256)[number]
        ref[spot[second], spot[first]] = r.stage[start : start + rows].astype(BF16)
    core = lax.axis_index("dp")
    x, y, z = spot
    r.u[0][core, x, y, z] = r.stage[336:352].astype(BF16)
    r.u[1][core, y, z, x] = r.stage[352:368].astype(BF16)


def tables(r):
    r.x[...] = low_first(r, r.tokens[0].astype(F32))
    rows = lax.broadcasted_iota(jnp.int32, (128, 1), 0)
    places = places_of(r, rows % 64, rows >= 64)
    position = (places - document_starts(r, places)).astype(F32)
    angles = position * r.frequency[...]
    r.cos[...] = jnp.cos(angles)
    r.sin[...] = jnp.sin(angles)
    r.turning[...] = one_hot(640, r.table[2:3])
    r.splitting[...] = one_hot(640, r.table[3:4])


NEVER = -(1 << 20)


def key_tables(r):
    mine = my_low(r)

    def chunk(number, token):
        plane = number % 4
        row = 4 * token + number
        for slot in range(16):
            spot = [slot // 4, slot % 4]
            spot.insert(chunk_axis(token), plane)
            low = low_of(r, spot[0] * 16 + spot[1] * 4 + spot[2])
            chosen = jnp.where(low < mine, low, 127 - low) * 64
            for_low = jnp.where(low < mine, chosen, NEVER)
            for_high = jnp.where(low == mine, NEVER, chosen)
            r.key_base[row, slot : slot + 1] = jnp.full((1, 128), for_low, jnp.int32)
            r.key_base[16 + row, slot : slot + 1] = jnp.full((1, 128), for_high, jnp.int32)

    for token in range(4):
        loop(4, lambda number, token=token: chunk(number, token))

    def turn(row):
        r.key_rows[pl.ds(row, 1)] = jnp.transpose(key_column(r, row, (row // 4) % 4))[0:1]

    loop(32, turn)


def key_column(r, row, token):
    base = jnp.broadcast_to(r.key_base[row][:, None, :], (16, 16, 128)).reshape(256, 128)
    return base + (lax.broadcasted_iota(jnp.int32, (256, 128), 0) % 16 + 16 * token)


def early(r):
    links = r.links
    core = lax.axis_index("dp")
    spot = place()
    x, y, z = spot

    def small(axis, unit, index_of):
        ref = r.u[unit]
        ring = links.ring(
            axis,
            lambda step: ref.at[index_of(spot[axis])],
            lambda step, at: ref.at[index_of(at)],
            ref.at[index_of(pl.ds(0, 3))],
        )
        held.append(ring)
        return ring

    held = []

    one = small(Z, 0, lambda at: (core, x, y, at))
    two = small(X, 1, lambda at: (core, y, z, at))
    rings = []
    for number, ref in enumerate(r.p):
        first, second, _ = weight_order(number)
        row = spot[second]
        rings.append(
            links.ring(
                first,
                lambda step, ref=ref, row=row, first=first: ref.at[row, spot[first]],
                lambda step, at, ref=ref, row=row: ref.at[row, at],
                ref.at[row, pl.ds(0, 3)],
            )
        )
    tables(r)
    one.wait_all()
    one = small(Y, 0, lambda at: (core, x, at))
    two.wait_all()
    two = small(Z, 1, lambda at: (core, y, at))
    for number, ref in enumerate(r.p):
        rings[number].wait_all()
        second = weight_order(number)[1]
        rings.append(
            links.ring(
                second,
                lambda step, ref=ref, second=second: ref.at[spot[second]],
                lambda step, at, ref=ref: ref.at[at],
                ref.at[pl.ds(0, 3)],
            )
        )
    key_tables(r)
    one.wait_all()
    one = small(X, 0, lambda at: (core, at))
    two.wait_all()
    two = small(Y, 1, lambda at: (core, at))
    spreads = {}

    def begin(*numbers):
        for number in numbers:
            rings[5 + number].wait_all()
            unpack(r, number)
            for piece in EARLY_PIECES[number]:
                spreads[piece] = Spread(r, piece)

    begin(DOWN, GATE, OUTPUT)
    one.wait_all()
    three = links.across(r.u[0].at[core], lambda at: r.u[0].at[at], r.u[0].at[core])
    two.wait_all()
    four = links.across(r.u[1].at[core], lambda at: r.u[1].at[at], r.u[1].at[core])
    begin(QUERY, UP)
    three.wait()
    four.wait()
    return rings, held + [three, four], spreads


SMALL = 2048


def unpack_small(r):
    for unit in range(2):
        for core in range(2):
            for plane in range(4):
                row = SMALL * unit + 1024 * core + 256 * plane
                r.stage[row : row + 256] = r.u[unit][core, plane].astype(F32).reshape(256, 128)
    for tile in range(4):
        lanes = slice(128 * tile, 128 * tile + 128)
        r.w_kv[:512, lanes] = columns_of(r, 0, 512, 4, tile).astype(BF16)
        r.w_kv[512:, lanes] = columns_of(r, SMALL, 128, 16, tile).astype(BF16)
    held = columns_of(r, SMALL, 128, 16, 4).astype(BF16)
    for number, (at, columns, _, _) in enumerate(GAINS):
        lanes, owners = gain_maps(r, number)
        spread = jnp.where(owners, dot32(held, lanes), 0.0)
        r.gains[0:1, at : at + columns] = jnp.sum(spread, axis=0, keepdims=True)


WEIGHTS = ((0, 80, False), (0, 40, False), (1, 80, False), (1, 40, False), (2, 80, True))
GATE, OUTPUT, UP, QUERY, DOWN = range(5)


def weight_order(number):
    return ORDERS[WEIGHTS[number][0]]


def own_plane(r, number):
    return weight_plane(r.w[number], number, lax.axis_index("dp"), place()[weight_order(number)[2]])


def weight_plane(ref, number, core, at):
    if WEIGHTS[number][2]:
        return of_plane(ref.at[core], weight_order(number)[2], at)
    return ref.at[core, at]


def plane_tiles(number):
    return ((80, 16), (128, 5), (80, 16), (80, 8), (256, 5))[number]


def unpack(r, number):
    _, rows, by_chip = WEIGHTS[number]
    count, tiles = plane_tiles(number)
    plane = own_plane(r, number)

    def one(chip):
        r.stage[pl.ds(pl.multiple_of(chip * rows, 8), rows)] = r.p[number][
            chip // 4, chip % 4, :rows
        ].astype(F32)

    loop(16, one)
    for tile in range(tiles):
        piece = columns_of(r, 0, count, tiles, tile).astype(BF16)
        lanes = slice(128 * tile, 128 * tile + 128)
        if by_chip:
            plane[:, :, :, lanes] = piece.reshape(4, 4, 16, 128)
        else:
            plane[:, lanes] = piece


def inverse_rms(values):
    return lax.rsqrt(jnp.mean(values * values, axis=-1, keepdims=True) + EPSILON)


def rms_scale(values, weights):
    return values * inverse_rms(values) * weights


def norm_back(values, weights, incoming):
    inverse = inverse_rms(values)
    normal = values * inverse
    scaled = incoming * weights
    back = (scaled - normal * jnp.mean(scaled * normal, axis=-1, keepdims=True)) * inverse
    return back, jnp.sum(incoming * normal, axis=0, keepdims=True)


def rope(r, u):
    cos, sin = r.cos[...], r.sin[...]
    one, two = u[:, :128], u[:, 128:]
    return jnp.concatenate([one * cos - two * sin, two * cos + one * sin], axis=1)


def rope_back(r, e):
    cos, sin = r.cos[...], r.sin[...]
    one, two = e[:, :128], e[:, 128:]
    return jnp.concatenate([one * cos + two * sin, two * cos - one * sin], axis=1)


def turned(r, values):
    return dot32(values, r.turning[...]).astype(BF16)


def unturned(r, values):
    return dot_nt(values.astype(BF16), r.turning[...])


def keys_values(r):
    x = r.x[...]
    normed = rms_scale(x, gain(r, G_ATTN)).astype(BF16)
    r.normed[...] = normed
    r.normed_split[...] = dot32(normed, r.splitting[...]).astype(BF16)
    split = r.normed_split[...].astype(F32)
    none = jnp.zeros((128, 64), F32)
    zero, one = (
        jnp.concatenate(
            [split[:, 256 * core : 256 * core + 256], split[:, 512 + 64 * core : 576 + 64 * core], none],
            axis=1,
        )
        for core in range(2)
    )
    core = lax.axis_index("dp")
    r.both_split[core] = jnp.where(core == 0, zero, one).astype(BF16)
    r.out_split[...] = jnp.where(core == 0, one, zero).astype(BF16)
    raw = dot32(r.normed_split[...], r.w_kv[...])
    r.key_raw[...] = raw[:, :HEAD]
    keys = rope(r, rms_scale(raw[:, :HEAD], gain(r, G_KEY)))
    both = jnp.concatenate([keys, raw[:, HEAD:]], axis=1).astype(BF16)
    for block in range(2):
        for unit, (token, lane) in enumerate(UNITS):
            row = 64 * block + 16 * token
            r.kv3[block, 16 * unit : 16 * unit + 16] = both[
                row : row + 16, 128 * lane : 128 * lane + 128
            ]


def of_plane(ref, axis, at, *rest):
    index = [slice(None)] * 3
    index[axis] = at
    return ref.at[(*index, *rest)]


def chip_of(spot, axis, step):
    spot = list(spot)
    spot[axis] = shifted(spot[axis], step)
    return spot[0] * 16 + spot[1] * 4 + spot[2]


def plane_loop(part, body):
    first, second, last = ORDERS[part]

    def row(i2):
        for i1 in range(4):
            spot = [None] * 3
            spot[first], spot[second], spot[last] = i1, i2, place()[last]
            body(spot, i2, i1)

    loop(4, row)


PIECES = (
    (GATE, 0, 1024),
    (GATE, 1024, 1024),
    (OUTPUT, 0, 640),
    (UP, 0, 1024),
    (UP, 1024, 1024),
    (QUERY, 0, 1024),
    (DOWN, 0, 2),
    (DOWN, 2, 2),
)
GATE_ONE, GATE_TWO, OUT, UP_ONE, UP_TWO, ASK, DOWN_ONE, DOWN_TWO = range(8)
EARLY_PIECES = ((GATE_ONE, GATE_TWO), (OUT,), (UP_ONE, UP_TWO), (ASK,), (DOWN_ONE, DOWN_TWO))
LATE_PIECES = (GATE_TWO, UP_TWO)


def window(ref, dim, first, count):
    index = [slice(None)] * len(ref.shape)
    index[dim] = pl.ds(first, count)
    return ref.at[tuple(index)]


def piece_of(piece, ref, chips=4):
    number, first, count = PIECES[piece]
    rank = len(ref.shape)
    return window(ref, rank - 1 - chips if number == DOWN else rank - 1, first, count)


def half_of(piece, plane, half):
    number, _, count = PIECES[piece]
    if number == DOWN:
        return window(plane, len(plane.shape) - 4, half, 1)
    if number == OUTPUT:
        return window(plane, len(plane.shape) - 2, 64 * half, 64)
    return window(plane, len(plane.shape) - 1, count // 2 * half, count // 2)


def piece_plane(r, piece, core, at):
    number = PIECES[piece][0]
    return piece_of(piece, weight_plane(r.w[number], number, core, at), 3)


def piece_axis(piece):
    return weight_order(PIECES[piece][0])[2]


class Spread:
    def __init__(self, r, piece):
        self.links, axis = r.links, piece_axis(piece)
        self.core, self.mine = lax.axis_index("dp"), place()[axis]
        self.at = lambda core, at: piece_plane(r, piece, core, at)

        def half(at, which):
            return half_of(piece, self.at(self.core, at), which)

        both = piece_of(piece, r.w[PIECES[piece][0]])
        dim = 3 if PIECES[piece][0] == DOWN else 1
        planes = window(both, dim, 0, 3).at[self.core]
        sends = r.links.sends(planes)
        self.near = [
            r.links.ring(
                axis,
                lambda step, which=which: half(self.mine, which),
                lambda step, at, which=which: half(at, which),
                None,
                steps=(1, 3),
                apart=True,
                sends=sends,
            )
            for which in range(2)
        ]

        def passed(step, at):
            return half(shifted(at, -step), 0 if step == 1 else 1)

        self.far = r.links.ring(
            axis,
            lambda step: passed(step, self.mine),
            passed,
            None,
            begin=False,
            steps=(1, 3),
            apart=True,
            sends=sends,
        )
        self.across = Across(r.links, both.at[self.core])
        self.over(self.mine)

    def over(self, at):
        self.across.add(self.at(self.core, at), lambda core: self.at(core, at))

    def forward(self):
        for which, step in enumerate((1, 3)):
            self.near[which].wait(step)
            self.far.start(step)

    def pass_on(self):
        for which, step in enumerate((3, 1)):
            self.near[which].wait(step)
        self.over(shifted(self.mine, 1))
        self.over(shifted(self.mine, 3))
        self.far.wait_all()
        self.over(shifted(self.mine, 2))

    def finish(self):
        self.across.wait()

    def free(self):
        self.far.sent()
        self.across.sent()


def gather_first(r):
    rings = []
    for part, (row, rows) in enumerate(KV_ROWS):
        own = r.kv3.at[:, pl.ds(row, rows)]
        rings.append(
            r.links.ring(
                ORDERS[part][0],
                lambda step, own=own: own,
                lambda step, at, ref=r.f1[part]: ref.at[at],
                r.f1[part].at[pl.ds(0, 3)],
            )
        )
    return rings


def gather_second(r, firsts):
    spot = place()
    rings = []
    for part, (row, rows) in enumerate(KV_ROWS):
        first, second, _ = ORDERS[part]
        f1, g2, mine = r.f1[part], r.g2[part], spot[second]
        f1[spot[first]] = r.kv3[:, row : row + rows]
        firsts[part].wait_all()
        for at in range(4):
            g2[mine, 2 * at] = f1[at, 0]
            g2[mine, 2 * at + 1] = f1[at, 1]
        rings.append(
            r.links.ring(
                second,
                lambda step, g2=g2, mine=mine: g2.at[mine],
                lambda step, at, g2=g2: g2.at[at],
                g2.at[pl.ds(0, 3)],
            )
        )
    return rings


def gather_third(r, seconds):
    spot = place()
    low_me = my_low(r)
    rings, specials = [], []
    for part, (row, rows) in enumerate(KV_ROWS):
        first, second, last = ORDERS[part]
        g2, sel, sp, rsp = r.g2[part], r.sel[part], r.sp[part], r.rsp[part]
        seconds[part].wait_all()
        targets = [low_of(r, chip_of(spot, last, step)) for step in (1, 2, 3)]
        sp[...] = jnp.zeros_like(sp)

        def choose(at, i2, i1, g2=g2, sel=sel, sp=sp, row=row, rows=rows, last=last, targets=targets):
            low = g2[i2, 2 * i1]
            high = g2[i2, 2 * i1 + 1]
            source = low_of(r, chip_of(at, last, 0))
            plane = [at[axis] for axis in (X, Y, Z) if axis != last]
            r.slots[at[0], at[1], at[2], pl.ds(row, rows)] = jnp.where(source < low_me, low, high)
            for step in (1, 2, 3):
                sel[step - 1, plane[0], plane[1]] = jnp.where(
                    source < targets[step - 1], low, high
                )
            sp[...] = jnp.where(source == 63, low, sp[...])

        plane_loop(part, choose)
        rings.append(
            r.links.ring(
                last,
                lambda step, sel=sel: sel.at[step - 1],
                lambda step, at, row=row, rows=rows, last=last: of_plane(
                    r.slots, last, at, pl.ds(row, rows)
                ),
                sel,
                apart=True,
            )
        )
        specials.append(
            r.links.ring(
                last,
                lambda step, sp=sp: sp,
                lambda step, at, rsp=rsp: rsp.at[at],
                rsp.at[pl.ds(0, 3)],
            )
        )
    r.extra[0:2] = r.kv3[...]
    return rings, specials


def gather_special(r, specials):
    spot = place()
    for part, (row, rows) in enumerate(KV_ROWS):
        rsp = r.rsp[part]
        specials[part].wait_all()
        rsp[spot[ORDERS[part][2]]] = r.sp[part][...]
        r.extra[2, row : row + rows] = add_all([rsp[at] for at in range(4)]).astype(BF16)


QUARTER = 1.0 / 16
POWER = QUARTER * 1.4426950408889634


def chunk_axis(token):
    return ORDERS[token][2] if token < 3 else X


def chunk_index(token, plane):
    index = [slice(None)] * 3
    index[chunk_axis(token)] = plane
    return tuple(index)


def unit_rows(token, lane):
    return pl.ds(16 * UNITS.index((token, lane)), 16)


def chunk_kv(r, token, plane):
    index = chunk_index(token, plane)
    quarters = [
        r.slots[(*index, unit_rows(token, lane))].reshape(256, 128) for lane in range(4)
    ]
    return jnp.concatenate(quarters[:2], axis=1), jnp.concatenate(quarters[2:], axis=1)


def extra_kv(r):
    quarters = [
        jnp.concatenate(
            [r.extra[block, unit_rows(token, lane)] for block in range(3) for token in range(4)],
            axis=0,
        )
        for lane in range(4)
    ]
    return jnp.concatenate(quarters[:2], axis=1), jnp.concatenate(quarters[2:], axis=1)


def extra_places(r, numbers):
    low = my_low(r)
    block = jnp.where(numbers < 64, low, jnp.where(numbers < 128, 127 - low, 63))
    gone = (numbers >= 128) & (low == 63)
    return jnp.where(gone, 1 << 20, block * 64 + numbers % 64)


def query_places(r, numbers):
    return places_of(r, numbers % 64, numbers >= 256)


def attention(r, thirds, specials, between):
    spot = place()
    numbers = lax.broadcasted_iota(jnp.int32, (512, 1), 0)
    latest = query_places(r, numbers)
    earliest = document_starts(r, latest)
    query = r.query[...]
    r.attn[...] = jnp.zeros_like(r.attn)
    r.total[...] = jnp.zeros_like(r.total)

    def add(weights, values):
        total = weights[:, :128]
        if weights.shape[1] == 256:
            total = total + weights[:, 128:]
            r.total[...] += total
        else:
            r.total[...] += total
            r.total[:, :64] += weights[:, 128:]
        r.attn[...] += dot32(weights.astype(BF16), values)

    def chunk(token, plane):
        keys, values = chunk_kv(r, token, plane)
        scores = dot_nt(query, keys)
        row = 4 * token + plane
        allowed = jnp.concatenate(
            [
                r.key_rows[pl.ds(row, 1)] >= earliest[:256],
                r.key_rows[pl.ds(16 + row, 1)] >= earliest[256:],
            ],
            axis=0,
        )
        add(jnp.where(allowed, jnp.exp2(scores * POWER), 0.0), values)

    for token in range(3):
        chunk(token, spot[chunk_axis(token)])
    between(0)
    for number, step in enumerate((1, 3, 2)):
        for token in range(3):
            thirds[token].wait(step)
            chunk(token, shifted(spot[chunk_axis(token)], -step))
        between(number + 1)
    for plane in range(4):
        chunk(3, plane)
    gather_special(r, specials)
    keys, values = extra_kv(r)
    scores = dot_nt(query, keys)
    places = extra_places(r, lax.broadcasted_iota(jnp.int32, (1, 192), 1))
    allowed = (places >= earliest) & (places <= latest)
    add(jnp.where(allowed, jnp.exp2(scores * POWER), 0.0), values)
    total = jnp.sum(r.total[...], axis=1, keepdims=True)
    r.attn[...] = r.attn[...] / total
    r.total[...] = jnp.broadcast_to(jnp.log2(total), (512, 128))


def attention_back(r, between):
    spot = place()
    numbers = lax.broadcasted_iota(jnp.int32, (1, 512), 1)
    latest = query_places(r, numbers)
    earliest = document_starts(r, latest)
    query, grad_out = r.query[...], r.grad_attn[...]
    log_total = jnp.transpose(r.total[...])[0:1]
    row_dot = jnp.transpose(r.dots[...])[0:1]
    r.grad_query[...] = jnp.zeros_like(r.grad_query)

    def grads_of(keys, values, allowed):
        scores = dot_nt(keys, query)
        probs = jnp.where(allowed, jnp.exp2(scores * POWER - log_total), 0.0)
        grad_probs = dot_nt(values, grad_out)
        grad_scores = (probs * (grad_probs - row_dot)).astype(BF16)
        grad_values = dot32(probs.astype(BF16), grad_out)
        grad_keys = dot32(grad_scores, query) * QUARTER
        r.grad_query[...] += dot_tn(grad_scores, keys)
        return jnp.concatenate([grad_keys, grad_values], axis=1).astype(BF16)

    def chunk(token, plane):
        keys, values = chunk_kv(r, token, plane)
        row = 4 * token + plane
        low, high = key_column(r, row, token), key_column(r, 16 + row, token)
        allowed = jnp.concatenate([low, low, high, high], axis=1) >= earliest
        grads = grads_of(keys, values, allowed)
        index = chunk_index(token, plane)
        for lane in range(4):
            r.slots[(*index, unit_rows(token, lane))] = grads[
                :, 128 * lane : 128 * lane + 128
            ].reshape(4, 4, 16, 128)

    every = (slice(None), slice(None))
    rings, specials = scatter_third(r)
    for number, step in enumerate((1, 3, 2)):
        for token in range(3):
            chunk(token, shifted(spot[chunk_axis(token)], step))
            rings[token].start(step, *every, pl.ds(0, 64))
        between(number)
    for plane in range(4):
        chunk(3, plane)
    for step in (1, 3, 2):
        for part, (_, rows) in enumerate(KV_ROWS):
            rings[part].start(step, *every, pl.ds(64, rows - 64))
    between(3)
    keys, values = extra_kv(r)
    places = extra_places(r, lax.broadcasted_iota(jnp.int32, (192, 1), 0))
    grads = grads_of(keys, values, (places >= earliest) & (places <= latest))
    for block in range(3):
        for unit, (token, lane) in enumerate(UNITS):
            row = 64 * block + 16 * token
            r.grad_extra[block, 16 * unit : 16 * unit + 16] = grads[
                row : row + 16, 128 * lane : 128 * lane + 128
            ]
    for ring in specials:
        for step in (1, 2, 3):
            ring.start(step)
    for token in range(3):
        chunk(token, spot[chunk_axis(token)])
    return rings, specials


GELU = 0.7978845608028654


def head_rows(block, head):
    start = 256 * block + 64 * head
    return slice(start, start + 64)


def queries(r):
    r.normed_b[...] = turned(r, r.normed[...])
    split_rows(r.both_normed, r.out_normed, r.normed_b[...])
    shared = share(r, r.both_normed, r.out_normed)
    r.query_raw[...] = dot32(r.normed_b[...], r.w[QUERY][...].reshape(640, 1024))
    for head in range(HEADS):
        raw = r.query_raw[:, HEAD * head : HEAD * head + HEAD]
        rotated = rope(r, rms_scale(raw, gain(r, G_QUERY))).astype(BF16)
        for block in range(2):
            r.query[head_rows(block, head)] = rotated[64 * block : 64 * block + 64]
    return shared


def gelu_parts(gate):
    inner = jnp.tanh(GELU * (gate + 0.044715 * gate * gate * gate))
    return 0.5 * gate * (1.0 + inner), inner


def columns(weight, at, width):
    rows = 8 * weight.shape[2]
    return weight[:, :, :, at : at + width].reshape(rows, width)


def down_rows(ref, number):
    return ref.at[number // 2, pl.ds(2 * (number % 2), 2)]


def split_rows(both, out, values):
    core = lax.axis_index("dp")
    values = values.astype(F32)
    none = jnp.zeros((128, 64), F32)
    low = jnp.concatenate([values[:, :320], none], axis=1)
    high = jnp.concatenate([values[:, 320:], none], axis=1)
    both[core] = jnp.where(core == 0, low, high).astype(BF16)
    out[...] = jnp.where(core == 0, high, low).astype(BF16)


def share(r, both, source):
    return r.links.across(source, lambda core: both.at[core], source)


def own_columns(ref, width, core):
    return ref.at[:, pl.ds(pl.multiple_of(core * width, width), width)]


def share_columns(r, both, ref):
    core = lax.axis_index("dp")
    width = ref.shape[1] // 2
    both[core] = own_columns(ref, width, core)[...]
    return share(r, both, own_columns(ref, width, 1 - core))


def pair(both):
    return both[...].reshape(256, both.shape[2])


def feed_forward(r, spreads):
    spreads[OUT].finish()
    for block in range(2):
        for head in range(HEADS):
            r.attn_low[64 * block : 64 * block + 64, HEAD * head : HEAD * head + HEAD] = r.attn[
                head_rows(block, head)
            ].astype(BF16)
    shared = {OUTPUT: share_columns(r, r.both_attn, r.attn_low)}
    r.proj[...] = dot32(r.attn_low[...], r.w[OUTPUT][...].reshape(1024, 640))
    r.mid[...] = r.x[...] + rms_scale(r.proj[...], gain(r, G_POST_ATTN))
    r.ffn_in[...] = rms_scale(r.mid[...], gain(r, G_FFN)).astype(BF16)
    r.ffn_in_b[...] = turned(r, r.ffn_in[...])
    for piece in (GATE_ONE, GATE_TWO, UP_ONE, UP_TWO):
        spreads[piece].finish()
    for number in range(4):
        at = slice(512 * number, 512 * number + 512)
        gate = dot32(r.ffn_in[...], columns(r.w[GATE], 512 * number, 512))
        up = dot32(r.ffn_in_b[...], columns(r.w[UP], 512 * number, 512))
        r.gate[:, at] = gate
        r.up[:, at] = up
        r.hidden[:, at] = (gelu_parts(gate)[0] * up).astype(BF16)
    split_rows(r.both_in, r.out_in, r.ffn_in[...])
    shared[GATE] = share(r, r.both_in, r.out_in)
    split_rows(r.both_in_b, r.out_in_b, r.ffn_in_b[...])
    shared[UP] = share(r, r.both_in_b, r.out_in_b)
    shared[DOWN] = share_columns(r, r.both_hidden, r.hidden)
    spreads[DOWN_ONE].finish()
    spreads[DOWN_TWO].finish()
    r.ffn_out[...] = dot32(r.hidden[...], r.w[DOWN][...].reshape(2048, 640))
    out = r.mid[...] + rms_scale(r.ffn_out[...], gain(r, G_POST_FFN))
    r.block_out[...] = low_first(r, out.astype(BF16))
    return shared


def note_gain(r, number, term):
    at, count, _, _ = GAINS[number]
    r.gain_sums[0:1, at : at + count] = term


def feed_forward_back(r, spreads, shared, start):
    core = lax.axis_index("dp")
    for piece in (GATE_ONE, GATE_TWO, OUT, UP_ONE, UP_TWO, DOWN_ONE, DOWN_TWO):
        spreads[piece].free()
    grad_out = low_first(r, r.out_cot[0].astype(F32))
    grad_ffn_out, term = norm_back(r.ffn_out[...], gain(r, G_POST_FFN), grad_out)
    note_gain(r, G_POST_FFN, term)
    low_grad = grad_ffn_out.astype(BF16)
    r.both_low[core] = low_grad
    low_shared = share(r, r.both_low, r.both_low.at[core])
    grad_in = jnp.zeros((128, 640), F32)
    grad_in_b = jnp.zeros((128, 640), F32)
    grads_shared = []
    for number in range(4):
        at = slice(512 * number, 512 * number + 512)
        down = down_rows(r.w[DOWN], number)
        grad_hidden = dot_nt(low_grad, down[...].reshape(512, 640))
        gate, up = r.gate[:, at], r.up[:, at]
        activated, inner = gelu_parts(gate)
        slope = 0.5 * (1.0 + inner) + 0.5 * gate * (1.0 - inner * inner) * GELU * (
            1.0 + 3 * 0.044715 * gate * gate
        )
        grad_gate = (grad_hidden * up * slope).astype(BF16)
        grad_up = (grad_hidden * activated).astype(BF16)
        r.both_gate[core, :, at] = grad_gate
        r.both_up[core, :, at] = grad_up
        grad_in += dot_nt(grad_gate, columns(r.w[GATE], 512 * number, 512))
        grad_in_b += dot_nt(grad_up, columns(r.w[UP], 512 * number, 512))
        if number % 2:
            lanes = pl.ds(512 * number - 512, 1024)
            for both in (r.both_gate, r.both_up):
                grads_shared.append(
                    r.links.across(
                        both.at[core, :, lanes],
                        lambda core, both=both, lanes=lanes: both.at[core, :, lanes],
                        both.at[core, :, lanes],
                    )
                )
    def columns_of_both(first):
        for number, ins, both, wait in (
            (GATE, r.both_in, r.both_gate, grads_shared[first // 512]),
            (UP, r.both_in_b, r.both_up, grads_shared[first // 512 + 1]),
        ):
            wait.wait()
            for at in (first, first + 512):
                lanes = slice(at, at + 512)
                term = dot_tn(pair(ins), both[:, :, lanes].reshape(256, 512))[:320].astype(BF16)
                r.w[number][core, :, :, lanes] = term.reshape(4, 80, 512)

    grad_in = grad_in + unturned(r, grad_in_b)
    back, term = norm_back(r.mid[...], gain(r, G_FFN), grad_in)
    note_gain(r, G_FFN, term)
    grad_mid = grad_out + back
    r.grad_mid[...] = grad_mid
    back, term = norm_back(r.proj[...], gain(r, G_POST_ATTN), grad_mid)
    note_gain(r, G_POST_ATTN, term)
    proj_low = back.astype(BF16)
    r.both_proj[core] = proj_low
    proj_shared = share(r, r.both_proj, r.both_proj.at[core])
    grad_attn = dot_nt(proj_low, r.w[OUTPUT][...].reshape(1024, 640)).astype(BF16)
    for block in range(2):
        for head in range(HEADS):
            r.grad_attn[head_rows(block, head)] = grad_attn[
                64 * block : 64 * block + 64, HEAD * head : HEAD * head + HEAD
            ]
    dots = jnp.sum(r.grad_attn[...].astype(F32) * r.attn[...], axis=1, keepdims=True)
    r.dots[...] = jnp.broadcast_to(dots, (512, 128))

    def rest_back():
        shared[DOWN].wait()
        low_shared.wait()
        term = dot_tn(pair(r.both_hidden), pair(r.both_low)).astype(BF16)
        r.w[DOWN][core] = term.reshape(4, 4, 4, 16, 640)
        start(DOWN_ONE, DOWN_TWO)
        shared[GATE].wait()
        shared[UP].wait()
        columns_of_both(0)
        start(GATE_ONE, UP_ONE)
        columns_of_both(1024)
        shared[OUTPUT].wait()
        proj_shared.wait()
        term = dot_tn(pair(r.both_attn), pair(r.both_proj)).astype(BF16)
        r.w[OUTPUT][core] = term.reshape(4, 128, 640)

    return rest_back


def queries_back(r, spreads, shared):
    core = lax.axis_index("dp")
    total = jnp.zeros((1, HEAD), F32)
    for head in range(HEADS):
        at = slice(HEAD * head, HEAD * head + HEAD)
        grad = jnp.concatenate([r.grad_query[head_rows(block, head)] for block in range(2)], axis=0)
        back, term = norm_back(
            r.query_raw[:, at], gain(r, G_QUERY), rope_back(r, grad * QUARTER)
        )
        total += term
        r.both_query[core, :, at] = back.astype(BF16)
    note_gain(r, G_QUERY, total)
    query_shared = share(r, r.both_query, r.both_query.at[core])
    r.grad_normed[...] = unturned(
        r, dot_nt(r.both_query[core], r.w[QUERY][...].reshape(640, 1024))
    )

    def rest_back():
        spreads[ASK].free()
        shared[QUERY].wait()
        query_shared.wait()
        term = dot_tn(pair(r.both_normed), pair(r.both_query))[:320].astype(BF16)
        r.w[QUERY][core] = term.reshape(4, 80, 1024)

    return rest_back


def add_rows(count, to, value):
    def one(at):
        rows = pl.ds(pl.multiple_of(at * 16, 16), 16)
        to[rows] = (to[rows].astype(F32) + value[rows].astype(F32)).astype(BF16)

    loop(count // 16, one)


def add_into(to, value):
    lead = to.shape[:-2]
    if not lead:
        add_rows(to.shape[0], to, value)
    elif len(lead) == 1:
        for at in range(lead[0]):
            add_rows(to.shape[1], to.at[at], value.at[at])
    else:
        for at in range(lead[0]):
            add_into(to.at[at], value.at[at])


class Gather:
    def __init__(self, r, piece):
        self.piece, axis = piece, piece_axis(piece)
        core, mine = lax.axis_index("dp"), place()[axis]
        number = PIECES[piece][0]
        self.land = piece_of(piece, r.landed[number], 3)
        self.at = lambda step: piece_plane(r, piece, core, shifted(mine, step))
        sends = r.links.sends(self.land)
        self.far = r.links.ring(
            axis,
            lambda step: half_of(piece, self.at(2), 0 if step == 1 else 1),
            lambda step, at: half_of(piece, self.land.at[2], 0 if step == 1 else 1),
            None,
            steps=(1, 3),
            apart=True,
            sends=sends,
        )
        self.near = r.links.ring(
            axis,
            self.at,
            lambda step, at: self.land.at[0 if step == 1 else 1],
            self.land.at[pl.ds(0, 2)],
            begin=False,
            steps=(1, 3),
            sends=sends,
        )

    def relay(self):
        for which, step in enumerate((1, 3)):
            self.far.wait(step)
            add_into(
                half_of(self.piece, self.at(step), which),
                half_of(self.piece, self.land.at[2], which),
            )
            self.near.start(step)


def repack(r, number, *gathers):
    _, rows, by_chip = WEIGHTS[number]
    count, tiles = plane_tiles(number)
    own, land = own_plane(r, number), r.landed[number]
    for gather in gathers:
        gather.near.wait_all()
    for tile in range(tiles):
        lanes = slice(128 * tile, 128 * tile + 128)
        index = (slice(None),) * (3 if by_chip else 1) + (lanes,)
        total = add_all([own[index]] + [land[(step, *index)] for step in range(2)])
        r.stage[pl.ds(tile, count, stride=tiles)] = total.reshape(count, 128)

    def one(chip):
        r.p[number][chip // 4, chip % 4, :rows] = r.stage[
            pl.ds(pl.multiple_of(chip * rows, 8), rows)
        ].astype(BF16)

    loop(16, one)


def late_second(r, number):
    second = weight_order(number)[1]
    mine = place()[second]
    return r.links.ring(
        second,
        lambda step: r.p[number].at[shifted(mine, step)],
        lambda step, at: r.second[number].at[step - 1],
        r.second[number],
        begin=False,
    )


def late_first(r, number):
    first = weight_order(number)[0]
    mine = place()[first]
    return r.links.ring(
        first,
        lambda step: r.line[number].at[shifted(mine, step)],
        lambda step, at: r.first[number].at[step - 1],
        r.first[number],
        begin=False,
    )


def late_line(r, number, ring):
    own = place()[weight_order(number)[1]]
    ring.wait_all()
    for at in range(4):
        r.line[number][at] = add_all(
            [r.p[number][own, at]] + [r.second[number][step, at] for step in range(3)]
        ).astype(BF16)


def late_end(r, number, ring, out):
    mine = place()[weight_order(number)[0]]
    ring.wait_all()
    out[...] = add_all([r.line[number][mine]] + [r.first[number][step] for step in range(3)])


def scatter_third(r):
    spot = place()
    rings, specials = [], []
    for part, (row, rows) in enumerate(KV_ROWS):
        last = ORDERS[part][2]
        rings.append(
            r.links.ring(
                last,
                lambda step, row=row, rows=rows, last=last: of_plane(
                    r.slots, last, shifted(spot[last], step), pl.ds(row, rows)
                ),
                lambda step, at, rb=r.rb[part]: rb.at[step - 1],
                r.rb[part],
                begin=False,
            )
        )
        specials.append(
            r.links.ring(
                last,
                lambda step, row=row, rows=rows: r.grad_extra.at[2, pl.ds(row, rows)],
                lambda step, at, rs=r.rs[part]: rs.at[step - 1],
                r.rs[part],
                begin=False,
            )
        )
    return rings, specials


def scatter_second(r, thirds, specials):
    spot = place()
    me = lax.axis_index("ctx")
    low_me = my_low(r)
    rings = []
    for part, (row, rows) in enumerate(KV_ROWS):
        first, second, last = ORDERS[part]
        rb, rs, total, land = r.rb[part], r.rs[part], r.g2[part], r.r2[part]
        thirds[part].wait_all()
        specials[part].wait_all()
        special = add_all([r.grad_extra[2, row : row + rows]] + [rs[step] for step in range(3)])
        r.sp[part][...] = special.astype(BF16)
        senders = [low_of(r, chip_of(spot, last, -step)) for step in (1, 2, 3)]

        def collect(
            at, i2, i1, rb=rb, sp=r.sp[part], total=total, row=row, rows=rows, last=last, senders=senders
        ):
            chip = chip_of(at, last, 0)
            source = low_of(r, chip)
            plane = [at[axis] for axis in (X, Y, Z) if axis != last]
            both = r.slots[at[0], at[1], at[2], pl.ds(row, rows)].astype(F32)
            none = jnp.zeros_like(both)
            low = jnp.where(source < low_me, both, none)
            for step in (1, 2, 3):
                came = rb[step - 1, plane[0], plane[1]].astype(F32)
                low += jnp.where(source < senders[step - 1], came, none)
                both += came
            high = both - low
            low += jnp.where(chip == me, r.grad_extra[0, pl.ds(row, rows)].astype(F32), none)
            high += jnp.where(chip == me, r.grad_extra[1, pl.ds(row, rows)].astype(F32), none)
            low += jnp.where(source == 63, sp[...].astype(F32), none)
            total[i2, 2 * i1] = low.astype(BF16)
            total[i2, 2 * i1 + 1] = high.astype(BF16)

        plane_loop(part, collect)
        rings.append(
            r.links.ring(
                second,
                lambda step, total=total, second=second: total.at[shifted(spot[second], step)],
                lambda step, at, land=land: land.at[step - 1],
                land,
            )
        )
    return rings


def scatter_first(r, seconds):
    spot = place()
    rings = []
    for part in range(3):
        first, second, _ = ORDERS[part]
        total, land, line, end = r.g2[part], r.r2[part], r.f1[part], r.r1[part]
        seconds[part].wait_all()

        def pick(index, total=total, land=land, mine=spot[second]):
            return add_all([total[mine, index]] + [land[step, index] for step in range(3)]).astype(
                BF16
            )

        for at in range(4):
            line[at, 0] = pick(2 * at)
            line[at, 1] = pick(2 * at + 1)
        rings.append(
            r.links.ring(
                first,
                lambda step, line=line, first=first: line.at[shifted(spot[first], step)],
                lambda step, at, end=end: end.at[step - 1],
                end,
            )
        )
    return rings


def scatter_end(r, firsts):
    spot = place()
    for part, (row, rows) in enumerate(KV_ROWS):
        firsts[part].wait_all()
        mine = spot[ORDERS[part][0]]
        for index in range(2):
            r.kv_sum[index, row : row + rows] = add_all(
                [r.f1[part][mine, index]] + [r.r1[part][step, index] for step in range(3)]
            )


def keys_values_back(r, split_shared, between):
    lanes = []
    for lane in range(4):
        pieces = [
            r.kv_sum[block, unit_rows(token, lane)] for block in range(2) for token in range(4)
        ]
        lanes.append(jnp.concatenate(pieces, axis=0))
    grad_keys = jnp.concatenate(lanes[:2], axis=1)
    grad_values = jnp.concatenate(lanes[2:], axis=1)
    back, term = norm_back(r.key_raw[...], gain(r, G_KEY), rope_back(r, grad_keys))
    note_gain(r, G_KEY, term)
    kv_low = jnp.concatenate([back, grad_values], axis=1).astype(BF16)
    core = lax.axis_index("dp")
    r.both_kv[core] = kv_low
    kv_shared = share(r, r.both_kv, r.both_kv.at[core])
    grad_split = dot_nt(kv_low, r.w_kv[...]).astype(BF16)
    grad_normed = dot_nt(grad_split, r.splitting[...]) + r.grad_normed[...]
    back, term = norm_back(r.x[...], gain(r, G_ATTN), grad_normed)
    note_gain(r, G_ATTN, term)
    gains_back(r, G_KEY, G_ATTN)
    low, high = r.held[:64], r.held[64:]
    r.both_held[core] = jnp.where(core == 0, low, high)
    r.out_held[...] = jnp.where(core == 0, high, low)
    held_shared = share(r, r.both_held, r.out_held)
    r.tokens_grad[...] = low_first(r, (r.grad_mid[...] + back).astype(BF16))
    between()
    r.stage[SMALL : SMALL + 1024] = jnp.zeros((1024, 128), F32)
    split_shared.wait()
    kv_shared.wait()
    terms = dot_tn(pair(r.both_split), pair(r.both_kv))
    for tile in range(4):
        lanes = slice(128 * tile, 128 * tile + 128)
        r.stage[pl.ds(tile, 256, stride=4)] = terms[:256, lanes]
        r.stage[pl.ds(SMALL + tile, 64, stride=16)] = terms[256:320, lanes]
    held_shared.wait()
    r.stage[pl.ds(SMALL + 4, 64, stride=16)] = r.both_held[0] + r.both_held[1]
    for unit in range(2):
        for plane in range(4):
            row = SMALL * unit + 256 * plane
            r.u[unit][core, plane] = r.stage[row : row + 256].astype(BF16).reshape(4, 4, 16, 128)


def gains_back(r, *numbers):
    for number in numbers:
        at, count, _, _ = GAINS[number]
        lanes, owners = gain_maps(r, number)
        term = jnp.where(owners, r.gain_sums[0:1, at : at + count], 0.0).astype(BF16)
        r.held[...] += dot_nt(term, lanes)


def small_sums(r, between):
    links = r.links
    core = lax.axis_index("dp")
    spot = place()
    axes = ((X, Y, Z), (Y, Z, X))
    rings = []
    for unit, order in enumerate(axes):
        own, land = r.u[unit], r.land3[unit]
        axis = order[0]
        rings.append(
            links.ring(
                axis,
                lambda step, own=own, axis=axis: own.at[core, shifted(spot[axis], step)],
                lambda step, at, land=land: land.at[step - 1],
                land,
            )
        )
    between[0]()
    later = []
    for unit, order in enumerate(axes):
        own, land, out, to = r.u[unit], r.land3[unit], r.sum2[unit], r.land2[unit]
        rings[unit].wait_all()
        mine = spot[order[0]]

        def add(at, own=own, land=land, out=out, mine=mine):
            out[at] = add_all([own[core, mine, at]] + [land[step, at] for step in range(3)]).astype(
                BF16
            )

        loop(4, add)
        axis = order[1]
        later.append(
            links.ring(
                axis,
                lambda step, out=out, axis=axis: out.at[shifted(spot[axis], step)],
                lambda step, at, to=to: to.at[step - 1],
                to,
            )
        )
    between[1]()
    last = []
    for unit, order in enumerate(axes):
        own, land, out, to = r.sum2[unit], r.land2[unit], r.sum1[unit], r.land1[unit]
        later[unit].wait_all()
        out[...] = add_all([own[spot[order[1]]]] + [land[step] for step in range(3)]).astype(BF16)
        axis = order[2]
        last.append(
            links.ring(
                axis,
                lambda step, out=out, axis=axis: out.at[shifted(spot[axis], step)],
                lambda step, at, to=to: to.at[step - 1],
                to,
            )
        )
    between[2]()
    for unit, order in enumerate(axes):
        last[unit].wait_all()
        r.fk[16 * unit : 16 * unit + 16] = add_all(
            [r.sum1[unit][spot[order[2]]]] + [r.land1[unit][step] for step in range(3)]
        )


def layer(r):
    greet()
    for copy in r.fetches.values():
        copy.wait()
    pack(r)
    greeted()
    early_rings, early_held, spreads = early(r)
    unpack_small(r)
    keys_values(r)
    firsts = gather_first(r)
    split_shared = share(r, r.both_split, r.out_split)
    seconds = gather_second(r, firsts)
    early_pieces = (ASK, OUT, GATE_ONE, UP_ONE, DOWN_ONE, DOWN_TWO)
    for piece in early_pieces:
        spreads[piece].forward()
    for piece in LATE_PIECES:
        spreads[piece].forward()
    before = tuple(r.links.open)
    thirds, specials = gather_third(r, seconds)
    for piece in early_pieces:
        spreads[piece].pass_on()
    for piece in LATE_PIECES:
        spreads[piece].pass_on()
    spreads[ASK].finish()
    query_shared = queries(r)

    def pass_on(number):
        if number == 0:
            r.links.settle(before)

    attention(r, thirds, specials, pass_on)
    shared = feed_forward(r, spreads)
    shared[QUERY] = query_shared
    before = tuple(r.links.open)
    sums = {}

    def start(*pieces):
        for piece in pieces:
            sums[piece] = Gather(r, piece)

    def relay(*pieces):
        for piece in pieces:
            sums[piece].relay()

    pieces = {
        GATE: (GATE_ONE, GATE_TWO),
        OUTPUT: (OUT,),
        UP: (UP_ONE, UP_TWO),
        QUERY: (ASK,),
        DOWN: (DOWN_ONE, DOWN_TWO),
    }
    second_rings, first_rings = {}, {}

    def prepare_late():
        for number in pieces:
            second_rings[number] = late_second(r, number)
            first_rings[number] = late_first(r, number)

    def send_late(*numbers):
        for number in numbers:
            repack(r, number, *(sums[piece] for piece in pieces[number]))
            for step in (1, 2, 3):
                second_rings[number].start(step)

    def go_on(*numbers):
        for number in numbers:
            late_line(r, number, second_rings[number])
            for step in (1, 2, 3):
                first_rings[number].start(step)

    def finish(*numbers):
        outs = (r.fgate, r.foutput, r.fup, r.fquery, r.fdown)
        for number in numbers:
            late_end(r, number, first_rings[number], outs[number])

    rest_back = feed_forward_back(r, spreads, shared, start)
    thirds, third_specials = attention_back(r, lambda number: None)
    query_back = queries_back(r, spreads, shared)
    rest_back()
    query_back()
    start(GATE_TWO, UP_TWO, OUT, ASK)
    for ring in early_rings:
        ring.sent()
    for ring in seconds:
        ring.sent()
    r.links.settle(before)
    before = tuple(r.links.open)
    r.held[...] = jnp.zeros_like(r.held)
    gains_back(r, G_POST_ATTN, G_FFN, G_POST_FFN, G_QUERY)
    seconds = scatter_second(r, thirds, third_specials)
    relay(DOWN_ONE, GATE_ONE, UP_ONE)
    firsts = scatter_first(r, seconds)
    relay(DOWN_TWO, GATE_TWO, UP_TWO, OUT, ASK)
    scatter_end(r, firsts)
    for copy in early_held:
        copy.sent()
    prepare_late()
    core = lax.axis_index("dp")

    def on(which, action, *numbers):
        pl.when(core == which)(lambda: action(*numbers))

    keys_values_back(r, split_shared, lambda: on(1, send_late, DOWN, GATE, UP, OUTPUT, QUERY))

    def one():
        r.links.settle(before)
        on(0, send_late, DOWN, GATE, UP, OUTPUT, QUERY)
        on(1, go_on, DOWN, GATE, UP, OUTPUT, QUERY)

    def two():
        on(0, go_on, DOWN, GATE, UP)

    def three():
        on(0, go_on, OUTPUT, QUERY)

    small_sums(r, (one, two, three))
    finish(DOWN, GATE, UP, OUTPUT, QUERY)
    r.links.settle()
    assert r.links.sending <= COPIES[0] and r.links.receiving <= COPIES[1]


def end(r):
    def rows(out, source, base, count, tiles):
        r.stage[base : base + count * tiles] = source
        for tile in range(tiles):
            out[:, 128 * tile : 128 * tile + 128] = columns_of(r, base, count, tiles, tile)

    rows(r.gate_grad, r.fgate[...], 0, 5, 16)
    rows(r.output_grad, r.foutput[0:40], 80, 8, 5)
    rows(r.up_grad, r.fup[...], 128, 5, 16)
    rows(r.query_grad, r.fquery[0:40], 208, 5, 8)
    rows(r.down_grad, r.fdown[...], 256, 16, 5)
    r.stage[336:368] = r.fk[...]
    for tile in range(4):
        out = (r.key_grad, r.value_grad)[tile // 2]
        half = 128 * (tile % 2)
        out[:, half : half + 128] = columns_of(r, 336, 5, 4, tile)
    line = r.fk[16:24]
    gain_grads = (r.grad_attn_norm, r.grad_post_attn, r.grad_ffn_norm, r.grad_post_ffn, r.grad_q, r.grad_k)
    for number, (_, _, held, lane) in enumerate(GAINS):
        out = gain_grads[number]
        moved = line if lane == 0 else pltpu.roll(line, 128 - lane, 1)
        out[...] = moved[4:5, :held]
    r.final_out[0] = r.block_out[...]
    r.final_grad[0] = r.tokens_grad[...]


COPIES = (97, 159)


def by_part(*dims):
    return [hold(BF16, *dims, rows, 128) for _, rows in KV_ROWS]


def by_flat(*dims):
    return [hold(BF16, *dims, rows, 128) for rows in (80, 48, 80, 48, 80)]


def by_unit(*dims):
    return [hold(BF16, *dims, 16, 128) for _ in range(2)]


def by_weight(lead, core):
    return [
        hold(BF16, *core, *lead, 80, 2048),
        hold(BF16, *core, *lead, 128, 640),
        hold(BF16, *core, *lead, 80, 2048),
        hold(BF16, *core, *lead, 80, 1024),
        hold(BF16, *core, *lead, 4, 4, 16, 640),
    ]


def buffers():
    return dict(
        stage=hold(F32, 4096, 128),
        x=hold(F32, 128, 640),
        cos=hold(F32, 128, 128),
        sin=hold(F32, 128, 128),
        gains=hold(F32, 8, 3072),
        gain_sums=hold(F32, 8, 3072),
        turning=hold(BF16, 640, 640),
        splitting=hold(BF16, 640, 640),
        key_base=hold(jnp.int32, 32, 16, 128),
        key_rows=hold(jnp.int32, 32, 256),
        p=by_flat(4, 4),
        second=by_flat(3, 4),
        line=by_flat(4),
        first=by_flat(3),
        u=by_unit(2, 4, 4, 4),
        both_split=hold(BF16, 2, 128, 384),
        both_kv=hold(BF16, 2, 128, 512),
        both_held=hold(F32, 2, 64, 128),
        out_held=hold(F32, 64, 128),
        out_split=hold(BF16, 128, 384),
        held=hold(F32, 128, 128),
        land3=by_unit(3, 4, 4),
        sum2=by_unit(4, 4),
        land2=by_unit(3, 4),
        sum1=by_unit(4),
        land1=by_unit(3),
        w_kv=hold(BF16, 640, 512),
        w=by_weight((4,), (2,)),
        both_hidden=hold(BF16, 2, 128, 1024),
        both_low=hold(BF16, 2, 128, 640),
        both_gate=hold(BF16, 2, 128, 2048),
        both_up=hold(BF16, 2, 128, 2048),
        both_in=hold(BF16, 2, 128, 384),
        both_in_b=hold(BF16, 2, 128, 384),
        both_attn=hold(BF16, 2, 128, 512),
        both_proj=hold(BF16, 2, 128, 640),
        both_normed=hold(BF16, 2, 128, 384),
        both_query=hold(BF16, 2, 128, 1024),
        out_in=hold(BF16, 128, 384),
        out_in_b=hold(BF16, 128, 384),
        out_normed=hold(BF16, 128, 384),
        landed=[
            hold(BF16, 3, 80, 2048),
            hold(BF16, 3, 128, 640),
            hold(BF16, 3, 80, 2048),
            hold(BF16, 3, 80, 1024),
            hold(BF16, 3, 4, 4, 16, 640),
        ],
        kv3=hold(BF16, 2, 256, 128),
        f1=by_part(4, 2),
        g2=by_part(4, 8),
        sel=by_part(3, 4, 4),
        sp=by_part(),
        rsp=by_part(4),
        rb=by_part(3, 4, 4),
        rs=by_part(3),
        r2=by_part(3, 8),
        r1=by_part(3, 2),
        slots=hold(BF16, 4, 4, 4, 256, 128),
        extra=hold(BF16, 3, 256, 128),
        grad_extra=hold(BF16, 3, 256, 128),
        kv_sum=hold(F32, 2, 256, 128),
        normed=hold(BF16, 128, 640),
        normed_split=hold(BF16, 128, 640),
        normed_b=hold(BF16, 128, 640),
        key_raw=hold(F32, 128, 256),
        query_raw=hold(F32, 128, 1024),
        query=hold(BF16, 512, 256),
        attn=hold(F32, 512, 256),
        total=hold(F32, 512, 128),
        dots=hold(F32, 512, 128),
        attn_low=hold(BF16, 128, 1024),
        proj=hold(F32, 128, 640),
        mid=hold(F32, 128, 640),
        ffn_in=hold(BF16, 128, 640),
        ffn_in_b=hold(BF16, 128, 640),
        gate=hold(F32, 128, 2048),
        up=hold(F32, 128, 2048),
        hidden=hold(BF16, 128, 2048),
        ffn_out=hold(F32, 128, 640),
        grad_mid=hold(F32, 128, 640),
        grad_attn=hold(BF16, 512, 256),
        grad_query=hold(F32, 512, 256),
        grad_normed=hold(F32, 128, 640),
    )


def on_device(
    tokens,
    doc_lengths,
    block_order,
    attn_norm,
    query_weight,
    key_weight,
    value_weight,
    query_gain,
    key_gain,
    output_weight,
    attn_post_norm,
    ffn_norm,
    gate_weight,
    up_weight,
    down_weight,
    ffn_post_norm,
    out_cot,
):
    made = run(
        layer,
        dict(block_order=block_order, doc_lengths=doc_lengths),
        {},
        dict(
            block_out=hold(BF16, 128, 640),
            tokens_grad=hold(BF16, 128, 640),
            fgate=hold(F32, 80, 128),
            foutput=hold(F32, 48, 128),
            fup=hold(F32, 80, 128),
            fquery=hold(F32, 48, 128),
            fdown=hold(F32, 80, 128),
            fk=hold(F32, 32, 128),
        ),
        buffers(),
        number=1,
        copies=COPIES,
        fetched=dict(
            gate_weight=gate_weight,
            output_weight=output_weight,
            up_weight=up_weight,
            query_weight=query_weight,
            down_weight=down_weight,
            key_weight=key_weight,
            value_weight=value_weight,
            attn_norm=attn_norm[None],
            attn_post_norm=attn_post_norm[None],
            ffn_norm=ffn_norm[None],
            ffn_post_norm=ffn_post_norm[None],
            query_gain=query_gain[None],
            key_gain=key_gain[None],
            tokens=tokens,
            table=jnp.asarray(number_table()),
            frequency=jnp.asarray(ROPE_BASE ** (-2.0 * np.arange(128) / 256), F32)[None],
            out_cot=out_cot,
        ),
    )
    results = run(
        end,
        {},
        made,
        dict(
            final_out=hold(BF16, 1, 128, 640),
            final_grad=hold(BF16, 1, 128, 640),
            grad_attn_norm=hold(F32, 1, 5),
            query_grad=hold(F32, 5, 1024),
            key_grad=hold(F32, 5, 256),
            value_grad=hold(F32, 5, 256),
            grad_q=hold(F32, 1, 2),
            grad_k=hold(F32, 1, 2),
            output_grad=hold(F32, 8, 640),
            grad_post_attn=hold(F32, 1, 5),
            grad_ffn_norm=hold(F32, 1, 5),
            gate_grad=hold(F32, 5, 2048),
            up_grad=hold(F32, 5, 2048),
            down_grad=hold(F32, 16, 640),
            grad_post_ffn=hold(F32, 1, 5),
        ),
        dict(stage=hold(F32, 3088, 128)),
    )
    return tuple(
        value.reshape(-1) if value.shape[0] == 1 and value.ndim == 2 else value
        for value in results.values()
    )


def solution(mesh):
    rows = P(("dp", "ctx"), None)
    vector = P(("dp", "ctx"))
    stream = P("dp", "ctx", None)
    return jax.shard_map(
        on_device,
        mesh=mesh,
        in_specs=(
            stream,
            P("dp", None),
            P(),
            vector,
            rows,
            rows,
            rows,
            vector,
            vector,
            rows,
            vector,
            vector,
            rows,
            rows,
            rows,
            vector,
            stream,
        ),
        out_specs=(
            stream,
            stream,
            vector,
            rows,
            rows,
            rows,
            vector,
            vector,
            rows,
            vector,
            vector,
            rows,
            rows,
            rows,
            vector,
        ),
        check_vma=False,
    )
```

```python
from types import SimpleNamespace

import jax
import jax.numpy as jnp
import numpy as np
from jax import lax
from jax.experimental import pallas as pl
from jax.experimental.pallas import tpu as pltpu
from jax.sharding import PartitionSpec as P

EPSILON = 1e-06
ROPE_BASE = 1000000.0
MESH = pl.DeviceIdType.MESH
F32 = jnp.float32
BF16 = jnp.bfloat16
MIB = 2**20

X, Y, Z = 0, 1, 2
ORDERS = ((Z, Y, X), (X, Z, Y), (Y, X, Z))
UNITS = (
    ((0, 0), (0, 1), (0, 2), (0, 3), (3, 0))
    + ((1, 0), (1, 1), (1, 2), (1, 3), (3, 1))
    + ((2, 0), (2, 1), (2, 2), (2, 3), (3, 2), (3, 3))
)
KV_ROWS = ((0, 80), (80, 80), (160, 96))
HEADS = 4
HEAD = 256
SCALE = HEAD**-0.5
LOG2E = 1.4426950408889634


def place():
    chip = lax.axis_index("ctx")
    return (chip // 16, (chip // 4) % 4, chip % 4)


def shifted(value, step):
    return lax.rem(value + step + 4, 4)


def peer(axis, step):
    spot = list(place())
    spot[axis] = shifted(spot[axis], step)
    return (lax.axis_index("dp"), spot[0] * 16 + spot[1] * 4 + spot[2])


def other_core():
    return (1 - lax.axis_index("dp"), lax.axis_index("ctx"))


def greet():
    barrier = pltpu.get_barrier_semaphore()
    for axis in (X, Y, Z):
        for step in (1, 2, 3):
            pl.semaphore_signal(barrier, inc=1, device_id=peer(axis, step), device_id_type=MESH)
    pl.semaphore_signal(barrier, inc=1, device_id=other_core(), device_id_type=MESH)


def greeted():
    pl.semaphore_wait(pltpu.get_barrier_semaphore(), 10)


class Ring:
    def __init__(self, links, axis, source, landing, whole, steps, apart, sends):
        self.links, self.axis, self.source, self.landing = links, axis, source, landing
        self.whole, self.apart = whole, apart
        self.sends = links.sends(whole) if sends is None else sends
        if apart:
            self.numbers = {step: links.receive() for step in steps}
        else:
            self.numbers = dict.fromkeys(steps, links.receive())

    def copy(self, step, sender):
        return self.links.copy(
            self.sends,
            self.numbers[step],
            self.source(step),
            self.landing(step, sender),
            peer(self.axis, step),
        )

    def start(self, step, *index):
        source, landing = self.source(step), self.landing(step, place()[self.axis])
        if index:
            source, landing = source.at[index], landing.at[index]
        self.links.copy(
            self.sends, self.numbers[step], source, landing, peer(self.axis, step)
        ).start()

    def wait(self, step):
        self.copy(step, shifted(place()[self.axis], -step)).wait_recv()

    def wait_all(self):
        if self.apart:
            for step in self.numbers:
                self.wait(step)
        else:
            step = next(iter(self.numbers))
            self.links.copy(
                self.sends, self.numbers[step], self.whole, self.whole, peer(self.axis, step)
            ).wait_recv()

    def sent(self):
        self.links.settle((self.sends,))


class Across:
    def __init__(self, links, whole):
        self.links, self.whole = links, whole
        self.sends, self.number = links.sends(whole), links.receive()

    def add(self, source, landing):
        there = landing(lax.axis_index("dp"))
        self.links.copy(self.sends, self.number, source, there, other_core()).start()

    def wait(self):
        self.links.copy(
            self.sends, self.number, self.whole, self.whole, other_core()
        ).wait_recv()

    def sent(self):
        self.links.settle((self.sends,))


class Links:
    def __init__(self, send, recv):
        self.send, self.recv = send, recv
        self.sending, self.receiving, self.open = 0, 0, {}

    def sends(self, whole):
        self.open[self.sending] = whole
        self.sending += 1
        return self.sending - 1

    def receive(self):
        self.receiving += 1
        return self.receiving - 1

    def copy(self, send, recv, source, landing, device):
        return pltpu.make_async_remote_copy(
            src_ref=source,
            dst_ref=landing,
            send_sem=self.send.at[send],
            recv_sem=self.recv.at[recv],
            device_id=device,
            device_id_type=MESH,
        )

    def ring(
        self, axis, source, landing, whole, begin=True, steps=(1, 2, 3), apart=False, sends=None
    ):
        ring = Ring(self, axis, source, landing, whole, steps, apart, sends)
        if begin:
            for step in steps:
                ring.start(step)
        return ring

    def across(self, source, landing, whole):
        across = Across(self, whole)
        across.add(source, landing)
        return across

    def settle(self, numbers=None):
        for number in tuple(self.open if numbers is None else numbers):
            if number in self.open:
                whole = self.open.pop(number)
                self.copy(number, 0, whole, whole, other_core()).wait_send()


VMEM = pl.BlockSpec(memory_space=pltpu.VMEM)
SMEM = pl.BlockSpec(memory_space=pltpu.SMEM)
ANY = pl.BlockSpec(memory_space=pl.ANY)


def hold(kind, *shape):
    return pltpu.VMEM(shape, kind)


def run(stage, numbers, ins, outs, scratch, number=None, copies=(), fetched={}):
    flat, shape = jax.tree.flatten(scratch, is_leaf=lambda leaf: not isinstance(leaf, (dict, list)))

    def kernel(*refs):
        count = len(numbers) + len(fetched) + len(ins) + len(outs)
        named = dict(zip((*numbers, *fetched, *ins, *outs), refs))
        rest = refs[count + len(flat) :]
        r = SimpleNamespace(**named)
        vars(r).update(jax.tree.unflatten(shape, refs[count : count + len(flat)]))
        r.fetches = {}
        for at, name in enumerate(fetched):
            held = rest[at]
            copy = pltpu.make_async_copy(named[name], held, rest[len(fetched)].at[at])
            copy.start()
            r.fetches[name] = copy
            setattr(r, name, held)
        if copies:
            r.links = Links(*rest[-2:])
        stage(r)

    remote = dict(collective_id=number, has_side_effects=True) if copies else {}
    results = pl.pallas_call(
        kernel,
        out_shape=[jax.ShapeDtypeStruct(out.shape, out.dtype) for out in outs.values()],
        in_specs=[SMEM] * len(numbers) + [ANY] * len(fetched) + [VMEM] * len(ins),
        out_specs=[VMEM] * len(outs),
        scratch_shapes=flat
        + [pltpu.VMEM(value.shape, value.dtype) for value in fetched.values()]
        + ([pltpu.SemaphoreType.DMA((len(fetched),))] if fetched else [])
        + [pltpu.SemaphoreType.DMA((count,)) for count in copies],
        compiler_params=pltpu.CompilerParams(vmem_limit_bytes=60 * MIB, **remote),
    )(*numbers.values(), *fetched.values(), *ins.values())
    return dict(zip(outs, results))


def dot32(left, right):
    return jnp.dot(left, right, preferred_element_type=F32)


def dot_nt(left, right):
    return lax.dot_general(left, right, (((1,), (1,)), ((), ())), preferred_element_type=F32)


def dot_tn(left, right):
    return lax.dot_general(left, right, (((0,), (0,)), ((), ())), preferred_element_type=F32)


def add_all(values):
    total = values[0].astype(F32)
    for value in values[1:]:
        total += value.astype(F32)
    return total


def loop(count, body):
    def step(number, unused):
        body(number)
        return unused

    lax.fori_loop(0, count, step, 0)


def my_low(r):
    chip = lax.axis_index("ctx")
    return jnp.minimum(r.block_order[2 * chip], r.block_order[2 * chip + 1])


def low_of(r, chip):
    return jnp.minimum(r.block_order[2 * chip], r.block_order[2 * chip + 1])


def low_first(r, rows):
    chip = lax.axis_index("ctx")
    flip = r.block_order[2 * chip] > r.block_order[2 * chip + 1]
    return jnp.where(flip, jnp.concatenate([rows[64:], rows[:64]], axis=0), rows)


def document_starts(r, places):
    start = jnp.zeros_like(places)
    at = 0
    for number in range(1, 8):
        at = at + r.doc_lengths[0, number - 1]
        start = jnp.where(places >= at, at, start)
    return start


def places_of(r, within, high):
    low = my_low(r)
    return jnp.where(high, 127 - low, low) * 64 + within


def number_table():
    def turned_device(device):
        core, x, y, z = device // 64, (device // 16) % 4, (device // 4) % 4, device % 4
        return ((core * 4 + y) * 4 + z) * 4 + x

    table = np.zeros((8, 640), np.int32)
    k = np.arange(640)
    table[0], table[1] = k % 5, turned_device(k // 5)
    core, y, z, x, row = k // 320, (k // 80) % 4, (k // 20) % 4, (k // 5) % 4, k % 5
    table[2] = (((core * 4 + x) * 4 + y) * 4 + z) * 5 + row
    table[3, :512] = 5 * (k[:512] // 4) + k[:512] % 4
    device = np.arange(128)
    table[3, 512 + turned_device(device)] = 5 * device + 4
    table[4, :256], table[5, :256] = k[:256] % 2, turned_device(k[:256] // 2)
    return table


def one_hot(rows, numbers):
    shape = (rows, numbers.shape[1])
    return jnp.where(lax.broadcasted_iota(jnp.int32, shape, 0) == numbers, 1.0, 0.0).astype(BF16)


GAINS = ((0, 640, 5, 0), (640, 640, 5, 5), (1280, 640, 5, 10), (1920, 640, 5, 15))
GAINS += ((2560, 256, 2, 20), (2816, 256, 2, 22))
G_ATTN, G_POST_ATTN, G_FFN, G_POST_FFN, G_QUERY, G_KEY = range(6)


def gain_maps(r, number):
    _, columns, held, lane = GAINS[number]
    row = 0 if held == 5 else 4
    rest, owner = r.table[row : row + 1, :columns], r.table[row + 1 : row + 2, :columns]
    lanes = one_hot(128, rest + lane)
    owners = lax.broadcasted_iota(jnp.int32, (128, columns), 0) == owner
    return lanes, owners


def gain(r, number):
    at, columns, _, _ = GAINS[number]
    return r.gains[0:1, at : at + columns]


def rows_of(r, base, weight, count):
    tiles = weight.shape[1] // 128
    for tile in range(tiles):
        r.stage[pl.ds(base + tile, count, stride=tiles)] = weight[
            :, 128 * tile : 128 * tile + 128
        ].astype(F32)


def columns_of(r, base, count, tiles, tile):
    return r.stage[pl.ds(base + tile, count, stride=tiles)]


def pack(r):
    rows_of(r, 0, r.gate_weight, 5)
    rows_of(r, 80, r.output_weight, 8)
    rows_of(r, 128, r.up_weight, 5)
    rows_of(r, 208, r.query_weight, 5)
    rows_of(r, 256, r.down_weight, 16)
    for tile in range(4):
        weight = (r.key_weight, r.value_weight)[tile // 2]
        half = 128 * (tile % 2)
        r.stage[pl.ds(336 + tile, 5, stride=4)] = weight[:, half : half + 128].astype(F32)
    r.stage[356:357] = jnp.zeros((1, 128), F32)
    own = (r.attn_norm, r.attn_post_norm, r.ffn_norm, r.ffn_post_norm, r.query_gain, r.key_gain)
    for ref, (_, _, held, lane) in zip(own, GAINS):
        r.stage[356:357, lane : lane + held] = ref[...].astype(F32)
    spot = place()
    for number, ref in enumerate(r.p):
        first, second, _ = weight_order(number)
        rows = ref.shape[2]
        start = (0, 80, 128, 208, 256)[number]
        ref[spot[second], spot[first]] = r.stage[start : start + rows].astype(BF16)
    core = lax.axis_index("dp")
    x, y, z = spot
    r.u[0][core, x, y, z] = r.stage[336:352].astype(BF16)
    r.u[1][core, y, z, x] = r.stage[352:368].astype(BF16)


def tables(r):
    r.x[...] = low_first(r, r.tokens[0].astype(F32))
    rows = lax.broadcasted_iota(jnp.int32, (128, 1), 0)
    places = places_of(r, rows % 64, rows >= 64)
    position = (places - document_starts(r, places)).astype(F32)
    angles = position * r.frequency[...]
    r.cos[...] = jnp.cos(angles)
    r.sin[...] = jnp.sin(angles)
    r.turning[...] = one_hot(640, r.table[2:3])
    r.splitting[...] = one_hot(640, r.table[3:4])


NEVER = -(1 << 20)


def key_tables(r):
    mine = my_low(r)

    def chunk(number, token):
        plane = number % 4
        row = 4 * token + number
        for slot in range(16):
            spot = [slot // 4, slot % 4]
            spot.insert(chunk_axis(token), plane)
            low = low_of(r, spot[0] * 16 + spot[1] * 4 + spot[2])
            chosen = jnp.where(low < mine, low, 127 - low) * 64
            for_low = jnp.where(low < mine, chosen, NEVER)
            for_high = jnp.where(low == mine, NEVER, chosen)
            r.key_base[row, slot : slot + 1] = jnp.full((1, 128), for_low, jnp.int32)
            r.key_base[16 + row, slot : slot + 1] = jnp.full((1, 128), for_high, jnp.int32)

    for token in range(4):
        loop(4, lambda number, token=token: chunk(number, token))

    def turn(row):
        r.key_rows[pl.ds(row, 1)] = jnp.transpose(key_column(r, row, (row // 4) % 4))[0:1]

    loop(32, turn)


def key_column(r, row, token):
    base = jnp.broadcast_to(r.key_base[row][:, None, :], (16, 16, 128)).reshape(256, 128)
    return base + (lax.broadcasted_iota(jnp.int32, (256, 128), 0) % 16 + 16 * token)


def early(r):
    links = r.links
    core = lax.axis_index("dp")
    spot = place()
    x, y, z = spot

    def small(axis, unit, index_of):
        ref = r.u[unit]
        ring = links.ring(
            axis,
            lambda step: ref.at[index_of(spot[axis])],
            lambda step, at: ref.at[index_of(at)],
            ref.at[index_of(pl.ds(0, 3))],
        )
        held.append(ring)
        return ring

    held = []

    one = small(Z, 0, lambda at: (core, x, y, at))
    two = small(X, 1, lambda at: (core, y, z, at))
    rings = []
    for number, ref in enumerate(r.p):
        first, second, _ = weight_order(number)
        row = spot[second]
        rings.append(
            links.ring(
                first,
                lambda step, ref=ref, row=row, first=first: ref.at[row, spot[first]],
                lambda step, at, ref=ref, row=row: ref.at[row, at],
                ref.at[row, pl.ds(0, 3)],
            )
        )
    tables(r)
    one.wait_all()
    one = small(Y, 0, lambda at: (core, x, at))
    two.wait_all()
    two = small(Z, 1, lambda at: (core, y, at))
    for number, ref in enumerate(r.p):
        rings[number].wait_all()
        second = weight_order(number)[1]
        rings.append(
            links.ring(
                second,
                lambda step, ref=ref, second=second: ref.at[spot[second]],
                lambda step, at, ref=ref: ref.at[at],
                ref.at[pl.ds(0, 3)],
            )
        )
    key_tables(r)
    one.wait_all()
    one = small(X, 0, lambda at: (core, at))
    two.wait_all()
    two = small(Y, 1, lambda at: (core, at))
    spreads = {}

    def begin(*numbers):
        for number in numbers:
            rings[5 + number].wait_all()
            unpack(r, number)
            for piece in EARLY_PIECES[number]:
                spreads[piece] = Spread(r, piece)

    begin(DOWN, GATE, OUTPUT)
    one.wait_all()
    three = links.across(r.u[0].at[core], lambda at: r.u[0].at[at], r.u[0].at[core])
    two.wait_all()
    four = links.across(r.u[1].at[core], lambda at: r.u[1].at[at], r.u[1].at[core])
    begin(QUERY, UP)
    three.wait()
    four.wait()
    return rings, held + [three, four], spreads


SMALL = 2048


def unpack_small(r):
    for unit in range(2):
        for core in range(2):
            for plane in range(4):
                row = SMALL * unit + 1024 * core + 256 * plane
                r.stage[row : row + 256] = r.u[unit][core, plane].astype(F32).reshape(256, 128)
    for tile in range(4):
        lanes = slice(128 * tile, 128 * tile + 128)
        r.w_kv[:512, lanes] = columns_of(r, 0, 512, 4, tile).astype(BF16)
        r.w_kv[512:, lanes] = columns_of(r, SMALL, 128, 16, tile).astype(BF16)
    held = columns_of(r, SMALL, 128, 16, 4).astype(BF16)
    for number, (at, columns, _, _) in enumerate(GAINS):
        lanes, owners = gain_maps(r, number)
        spread = jnp.where(owners, dot32(held, lanes), 0.0)
        r.gains[0:1, at : at + columns] = jnp.sum(spread, axis=0, keepdims=True)


WEIGHTS = ((0, 80, False), (0, 40, False), (1, 80, False), (1, 40, False), (2, 80, True))
GATE, OUTPUT, UP, QUERY, DOWN = range(5)


def weight_order(number):
    return ORDERS[WEIGHTS[number][0]]


def own_plane(r, number):
    return weight_plane(r.w[number], number, lax.axis_index("dp"), place()[weight_order(number)[2]])


def weight_plane(ref, number, core, at):
    if WEIGHTS[number][2]:
        return of_plane(ref.at[core], weight_order(number)[2], at)
    return ref.at[core, at]


def plane_tiles(number):
    return ((80, 16), (128, 5), (80, 16), (80, 8), (256, 5))[number]


def unpack(r, number):
    _, rows, by_chip = WEIGHTS[number]
    count, tiles = plane_tiles(number)
    plane = own_plane(r, number)

    def one(chip):
        r.stage[pl.ds(pl.multiple_of(chip * rows, 8), rows)] = r.p[number][
            chip // 4, chip % 4, :rows
        ].astype(F32)

    loop(16, one)
    for tile in range(tiles):
        piece = columns_of(r, 0, count, tiles, tile).astype(BF16)
        lanes = slice(128 * tile, 128 * tile + 128)
        if by_chip:
            plane[:, :, :, lanes] = piece.reshape(4, 4, 16, 128)
        else:
            plane[:, lanes] = piece


def inverse_rms(values):
    return lax.rsqrt(jnp.mean(values * values, axis=-1, keepdims=True) + EPSILON)


def rms_scale(values, weights):
    return values * inverse_rms(values) * weights


def norm_back(values, weights, incoming):
    inverse = inverse_rms(values)
    normal = values * inverse
    scaled = incoming * weights
    back = (scaled - normal * jnp.mean(scaled * normal, axis=-1, keepdims=True)) * inverse
    return back, jnp.sum(incoming * normal, axis=0, keepdims=True)


def rope(r, u):
    cos, sin = r.cos[...], r.sin[...]
    one, two = u[:, :128], u[:, 128:]
    return jnp.concatenate([one * cos - two * sin, two * cos + one * sin], axis=1)


def rope_back(r, e):
    cos, sin = r.cos[...], r.sin[...]
    one, two = e[:, :128], e[:, 128:]
    return jnp.concatenate([one * cos + two * sin, two * cos - one * sin], axis=1)


def turned(r, values):
    return dot32(values, r.turning[...]).astype(BF16)


def unturned(r, values):
    return dot_nt(values.astype(BF16), r.turning[...])


def keys_values(r):
    x = r.x[...]
    normed = rms_scale(x, gain(r, G_ATTN)).astype(BF16)
    r.normed[...] = normed
    r.normed_split[...] = dot32(normed, r.splitting[...]).astype(BF16)
    split = r.normed_split[...].astype(F32)
    none = jnp.zeros((128, 64), F32)
    zero, one = (
        jnp.concatenate(
            [split[:, 256 * core : 256 * core + 256], split[:, 512 + 64 * core : 576 + 64 * core], none],
            axis=1,
        )
        for core in range(2)
    )
    core = lax.axis_index("dp")
    r.both_split[core] = jnp.where(core == 0, zero, one).astype(BF16)
    r.out_split[...] = jnp.where(core == 0, one, zero).astype(BF16)
    raw = dot32(r.normed_split[...], r.w_kv[...])
    r.key_raw[...] = raw[:, :HEAD]
    keys = rope(r, rms_scale(raw[:, :HEAD], gain(r, G_KEY)))
    both = jnp.concatenate([keys, raw[:, HEAD:]], axis=1).astype(BF16)
    for block in range(2):
        for unit, (token, lane) in enumerate(UNITS):
            row = 64 * block + 16 * token
            r.kv3[block, 16 * unit : 16 * unit + 16] = both[
                row : row + 16, 128 * lane : 128 * lane + 128
            ]


def of_plane(ref, axis, at, *rest):
    index = [slice(None)] * 3
    index[axis] = at
    return ref.at[(*index, *rest)]


def chip_of(spot, axis, step):
    spot = list(spot)
    spot[axis] = shifted(spot[axis], step)
    return spot[0] * 16 + spot[1] * 4 + spot[2]


def plane_loop(part, body):
    first, second, last = ORDERS[part]

    def row(i2):
        for i1 in range(4):
            spot = [None] * 3
            spot[first], spot[second], spot[last] = i1, i2, place()[last]
            body(spot, i2, i1)

    loop(4, row)


PIECES = (
    (GATE, 0, 1024),
    (GATE, 1024, 1024),
    (OUTPUT, 0, 640),
    (UP, 0, 1024),
    (UP, 1024, 1024),
    (QUERY, 0, 1024),
    (DOWN, 0, 2),
    (DOWN, 2, 2),
)
GATE_ONE, GATE_TWO, OUT, UP_ONE, UP_TWO, ASK, DOWN_ONE, DOWN_TWO = range(8)
EARLY_PIECES = ((GATE_ONE, GATE_TWO), (OUT,), (UP_ONE, UP_TWO), (ASK,), (DOWN_ONE, DOWN_TWO))
LATE_PIECES = (GATE_TWO, UP_TWO)


def window(ref, dim, first, count):
    index = [slice(None)] * len(ref.shape)
    index[dim] = pl.ds(first, count)
    return ref.at[tuple(index)]


def piece_of(piece, ref, chips=4):
    number, first, count = PIECES[piece]
    rank = len(ref.shape)
    return window(ref, rank - 1 - chips if number == DOWN else rank - 1, first, count)


def half_of(piece, plane, half):
    number, _, count = PIECES[piece]
    if number == DOWN:
        return window(plane, len(plane.shape) - 4, half, 1)
    if number == OUTPUT:
        return window(plane, len(plane.shape) - 2, 64 * half, 64)
    return window(plane, len(plane.shape) - 1, count // 2 * half, count // 2)


def piece_plane(r, piece, core, at):
    number = PIECES[piece][0]
    return piece_of(piece, weight_plane(r.w[number], number, core, at), 3)


def piece_axis(piece):
    return weight_order(PIECES[piece][0])[2]


class Spread:
    def __init__(self, r, piece):
        self.links, axis = r.links, piece_axis(piece)
        self.core, self.mine = lax.axis_index("dp"), place()[axis]
        self.at = lambda core, at: piece_plane(r, piece, core, at)

        def half(at, which):
            return half_of(piece, self.at(self.core, at), which)

        both = piece_of(piece, r.w[PIECES[piece][0]])
        dim = 3 if PIECES[piece][0] == DOWN else 1
        planes = window(both, dim, 0, 3).at[self.core]
        sends = r.links.sends(planes)
        self.near = [
            r.links.ring(
                axis,
                lambda step, which=which: half(self.mine, which),
                lambda step, at, which=which: half(at, which),
                None,
                steps=(1, 3),
                apart=True,
                sends=sends,
            )
            for which in range(2)
        ]

        def passed(step, at):
            return half(shifted(at, -step), 0 if step == 1 else 1)

        self.far = r.links.ring(
            axis,
            lambda step: passed(step, self.mine),
            passed,
            None,
            begin=False,
            steps=(1, 3),
            apart=True,
            sends=sends,
        )
        self.across = Across(r.links, both.at[self.core])
        self.over(self.mine)

    def over(self, at):
        self.across.add(self.at(self.core, at), lambda core: self.at(core, at))

    def forward(self):
        for which, step in enumerate((1, 3)):
            self.near[which].wait(step)
            self.far.start(step)

    def pass_on(self):
        for which, step in enumerate((3, 1)):
            self.near[which].wait(step)
        self.over(shifted(self.mine, 1))
        self.over(shifted(self.mine, 3))
        self.far.wait_all()
        self.over(shifted(self.mine, 2))

    def finish(self):
        self.across.wait()

    def free(self):
        self.far.sent()
        self.across.sent()


def gather_first(r):
    rings = []
    for part, (row, rows) in enumerate(KV_ROWS):
        own = r.kv3.at[:, pl.ds(row, rows)]
        rings.append(
            r.links.ring(
                ORDERS[part][0],
                lambda step, own=own: own,
                lambda step, at, ref=r.f1[part]: ref.at[at],
                r.f1[part].at[pl.ds(0, 3)],
            )
        )
    return rings


def gather_second(r, firsts):
    spot = place()
    rings = []
    for part, (row, rows) in enumerate(KV_ROWS):
        first, second, _ = ORDERS[part]
        f1, g2, mine = r.f1[part], r.g2[part], spot[second]
        f1[spot[first]] = r.kv3[:, row : row + rows]
        firsts[part].wait_all()
        for at in range(4):
            g2[mine, 2 * at] = f1[at, 0]
            g2[mine, 2 * at + 1] = f1[at, 1]
        rings.append(
            r.links.ring(
                second,
                lambda step, g2=g2, mine=mine: g2.at[mine],
                lambda step, at, g2=g2: g2.at[at],
                g2.at[pl.ds(0, 3)],
            )
        )
    return rings


def gather_third(r, seconds):
    spot = place()
    low_me = my_low(r)
    rings, specials = [], []
    for part, (row, rows) in enumerate(KV_ROWS):
        first, second, last = ORDERS[part]
        g2, sel, sp, rsp = r.g2[part], r.sel[part], r.sp[part], r.rsp[part]
        seconds[part].wait_all()
        targets = [low_of(r, chip_of(spot, last, step)) for step in (1, 2, 3)]
        sp[...] = jnp.zeros_like(sp)

        def choose(at, i2, i1, g2=g2, sel=sel, sp=sp, row=row, rows=rows, last=last, targets=targets):
            low = g2[i2, 2 * i1]
            high = g2[i2, 2 * i1 + 1]
            source = low_of(r, chip_of(at, last, 0))
            plane = [at[axis] for axis in (X, Y, Z) if axis != last]
            r.slots[at[0], at[1], at[2], pl.ds(row, rows)] = jnp.where(source < low_me, low, high)
            for step in (1, 2, 3):
                sel[step - 1, plane[0], plane[1]] = jnp.where(
                    source < targets[step - 1], low, high
                )
            sp[...] = jnp.where(source == 63, low, sp[...])

        plane_loop(part, choose)
        rings.append(
            r.links.ring(
                last,
                lambda step, sel=sel: sel.at[step - 1],
                lambda step, at, row=row, rows=rows, last=last: of_plane(
                    r.slots, last, at, pl.ds(row, rows)
                ),
                sel,
                apart=True,
            )
        )
        specials.append(
            r.links.ring(
                last,
                lambda step, sp=sp: sp,
                lambda step, at, rsp=rsp: rsp.at[at],
                rsp.at[pl.ds(0, 3)],
            )
        )
    r.extra[0:2] = r.kv3[...]
    return rings, specials


def gather_special(r, specials):
    spot = place()
    for part, (row, rows) in enumerate(KV_ROWS):
        rsp = r.rsp[part]
        specials[part].wait_all()
        rsp[spot[ORDERS[part][2]]] = r.sp[part][...]
        r.extra[2, row : row + rows] = add_all([rsp[at] for at in range(4)]).astype(BF16)


QUARTER = 1.0 / 16
POWER = QUARTER * 1.4426950408889634


def chunk_axis(token):
    return ORDERS[token][2] if token < 3 else X


def chunk_index(token, plane):
    index = [slice(None)] * 3
    index[chunk_axis(token)] = plane
    return tuple(index)


def unit_rows(token, lane):
    return pl.ds(16 * UNITS.index((token, lane)), 16)


def chunk_kv(r, token, plane):
    index = chunk_index(token, plane)
    quarters = [
        r.slots[(*index, unit_rows(token, lane))].reshape(256, 128) for lane in range(4)
    ]
    return jnp.concatenate(quarters[:2], axis=1), jnp.concatenate(quarters[2:], axis=1)


def extra_kv(r):
    quarters = [
        jnp.concatenate(
            [r.extra[block, unit_rows(token, lane)] for block in range(3) for token in range(4)],
            axis=0,
        )
        for lane in range(4)
    ]
    return jnp.concatenate(quarters[:2], axis=1), jnp.concatenate(quarters[2:], axis=1)


def extra_places(r, numbers):
    low = my_low(r)
    block = jnp.where(numbers < 64, low, jnp.where(numbers < 128, 127 - low, 63))
    gone = (numbers >= 128) & (low == 63)
    return jnp.where(gone, 1 << 20, block * 64 + numbers % 64)


def query_places(r, numbers):
    return places_of(r, numbers % 64, numbers >= 256)


def attention(r, thirds, specials, between):
    spot = place()
    numbers = lax.broadcasted_iota(jnp.int32, (512, 1), 0)
    latest = query_places(r, numbers)
    earliest = document_starts(r, latest)
    query = r.query[...]
    r.attn[...] = jnp.zeros_like(r.attn)
    r.total[...] = jnp.zeros_like(r.total)

    def add(weights, values):
        total = weights[:, :128]
        if weights.shape[1] == 256:
            total = total + weights[:, 128:]
            r.total[...] += total
        else:
            r.total[...] += total
            r.total[:, :64] += weights[:, 128:]
        r.attn[...] += dot32(weights.astype(BF16), values)

    def chunk(token, plane):
        keys, values = chunk_kv(r, token, plane)
        scores = dot_nt(query, keys)
        row = 4 * token + plane
        allowed = jnp.concatenate(
            [
                r.key_rows[pl.ds(row, 1)] >= earliest[:256],
                r.key_rows[pl.ds(16 + row, 1)] >= earliest[256:],
            ],
            axis=0,
        )
        add(jnp.where(allowed, jnp.exp2(scores * POWER), 0.0), values)

    for token in range(3):
        chunk(token, spot[chunk_axis(token)])
    between(0)
    for number, step in enumerate((1, 3, 2)):
        for token in range(3):
            thirds[token].wait(step)
            chunk(token, shifted(spot[chunk_axis(token)], -step))
        between(number + 1)
    for plane in range(4):
        chunk(3, plane)
    gather_special(r, specials)
    keys, values = extra_kv(r)
    scores = dot_nt(query, keys)
    places = extra_places(r, lax.broadcasted_iota(jnp.int32, (1, 192), 1))
    allowed = (places >= earliest) & (places <= latest)
    add(jnp.where(allowed, jnp.exp2(scores * POWER), 0.0), values)
    total = jnp.sum(r.total[...], axis=1, keepdims=True)
    r.attn[...] = r.attn[...] / total
    r.total[...] = jnp.broadcast_to(jnp.log2(total), (512, 128))


def attention_back(r, between):
    spot = place()
    numbers = lax.broadcasted_iota(jnp.int32, (1, 512), 1)
    latest = query_places(r, numbers)
    earliest = document_starts(r, latest)
    query, grad_out = r.query[...], r.grad_attn[...]
    log_total = jnp.transpose(r.total[...])[0:1]
    row_dot = jnp.transpose(r.dots[...])[0:1]
    r.grad_query[...] = jnp.zeros_like(r.grad_query)

    def grads_of(keys, values, allowed):
        scores = dot_nt(keys, query)
        probs = jnp.where(allowed, jnp.exp2(scores * POWER - log_total), 0.0)
        grad_probs = dot_nt(values, grad_out)
        grad_scores = (probs * (grad_probs - row_dot)).astype(BF16)
        grad_values = dot32(probs.astype(BF16), grad_out)
        grad_keys = dot32(grad_scores, query) * QUARTER
        r.grad_query[...] += dot_tn(grad_scores, keys)
        return jnp.concatenate([grad_keys, grad_values], axis=1).astype(BF16)

    def chunk(token, plane):
        keys, values = chunk_kv(r, token, plane)
        row = 4 * token + plane
        low, high = key_column(r, row, token), key_column(r, 16 + row, token)
        allowed = jnp.concatenate([low, low, high, high], axis=1) >= earliest
        grads = grads_of(keys, values, allowed)
        index = chunk_index(token, plane)
        for lane in range(4):
            r.slots[(*index, unit_rows(token, lane))] = grads[
                :, 128 * lane : 128 * lane + 128
            ].reshape(4, 4, 16, 128)

    every = (slice(None), slice(None))
    rings, specials = scatter_third(r)
    for number, step in enumerate((1, 3, 2)):
        for token in range(3):
            chunk(token, shifted(spot[chunk_axis(token)], step))
            rings[token].start(step, *every, pl.ds(0, 64))
        between(number)
    for plane in range(4):
        chunk(3, plane)
    for step in (1, 3, 2):
        for part, (_, rows) in enumerate(KV_ROWS):
            rings[part].start(step, *every, pl.ds(64, rows - 64))
    between(3)
    keys, values = extra_kv(r)
    places = extra_places(r, lax.broadcasted_iota(jnp.int32, (192, 1), 0))
    grads = grads_of(keys, values, (places >= earliest) & (places <= latest))
    for block in range(3):
        for unit, (token, lane) in enumerate(UNITS):
            row = 64 * block + 16 * token
            r.grad_extra[block, 16 * unit : 16 * unit + 16] = grads[
                row : row + 16, 128 * lane : 128 * lane + 128
            ]
    for ring in specials:
        for step in (1, 2, 3):
            ring.start(step)
    for token in range(3):
        chunk(token, spot[chunk_axis(token)])
    return rings, specials


GELU = 0.7978845608028654


def head_rows(block, head):
    start = 256 * block + 64 * head
    return slice(start, start + 64)


def queries(r):
    r.normed_b[...] = turned(r, r.normed[...])
    split_rows(r.both_normed, r.out_normed, r.normed_b[...])
    shared = share(r, r.both_normed, r.out_normed)
    r.query_raw[...] = dot32(r.normed_b[...], r.w[QUERY][...].reshape(640, 1024))
    for head in range(HEADS):
        raw = r.query_raw[:, HEAD * head : HEAD * head + HEAD]
        rotated = rope(r, rms_scale(raw, gain(r, G_QUERY))).astype(BF16)
        for block in range(2):
            r.query[head_rows(block, head)] = rotated[64 * block : 64 * block + 64]
    return shared


def gelu_parts(gate):
    inner = jnp.tanh(GELU * (gate + 0.044715 * gate * gate * gate))
    return 0.5 * gate * (1.0 + inner), inner


def columns(weight, at, width):
    rows = 8 * weight.shape[2]
    return weight[:, :, :, at : at + width].reshape(rows, width)


def down_rows(ref, number):
    return ref.at[number // 2, pl.ds(2 * (number % 2), 2)]


def split_rows(both, out, values):
    core = lax.axis_index("dp")
    values = values.astype(F32)
    none = jnp.zeros((128, 64), F32)
    low = jnp.concatenate([values[:, :320], none], axis=1)
    high = jnp.concatenate([values[:, 320:], none], axis=1)
    both[core] = jnp.where(core == 0, low, high).astype(BF16)
    out[...] = jnp.where(core == 0, high, low).astype(BF16)


def share(r, both, source):
    return r.links.across(source, lambda core: both.at[core], source)


def own_columns(ref, width, core):
    return ref.at[:, pl.ds(pl.multiple_of(core * width, width), width)]


def share_columns(r, both, ref):
    core = lax.axis_index("dp")
    width = ref.shape[1] // 2
    both[core] = own_columns(ref, width, core)[...]
    return share(r, both, own_columns(ref, width, 1 - core))


def pair(both):
    return both[...].reshape(256, both.shape[2])


def feed_forward(r, spreads):
    spreads[OUT].finish()
    for block in range(2):
        for head in range(HEADS):
            r.attn_low[64 * block : 64 * block + 64, HEAD * head : HEAD * head + HEAD] = r.attn[
                head_rows(block, head)
            ].astype(BF16)
    shared = {OUTPUT: share_columns(r, r.both_attn, r.attn_low)}
    r.proj[...] = dot32(r.attn_low[...], r.w[OUTPUT][...].reshape(1024, 640))
    r.mid[...] = r.x[...] + rms_scale(r.proj[...], gain(r, G_POST_ATTN))
    r.ffn_in[...] = rms_scale(r.mid[...], gain(r, G_FFN)).astype(BF16)
    r.ffn_in_b[...] = turned(r, r.ffn_in[...])
    for piece in (GATE_ONE, GATE_TWO, UP_ONE, UP_TWO):
        spreads[piece].finish()
    for number in range(4):
        at = slice(512 * number, 512 * number + 512)
        gate = dot32(r.ffn_in[...], columns(r.w[GATE], 512 * number, 512))
        up = dot32(r.ffn_in_b[...], columns(r.w[UP], 512 * number, 512))
        r.gate[:, at] = gate
        r.up[:, at] = up
        r.hidden[:, at] = (gelu_parts(gate)[0] * up).astype(BF16)
    split_rows(r.both_in, r.out_in, r.ffn_in[...])
    shared[GATE] = share(r, r.both_in, r.out_in)
    split_rows(r.both_in_b, r.out_in_b, r.ffn_in_b[...])
    shared[UP] = share(r, r.both_in_b, r.out_in_b)
    shared[DOWN] = share_columns(r, r.both_hidden, r.hidden)
    spreads[DOWN_ONE].finish()
    spreads[DOWN_TWO].finish()
    r.ffn_out[...] = dot32(r.hidden[...], r.w[DOWN][...].reshape(2048, 640))
    out = r.mid[...] + rms_scale(r.ffn_out[...], gain(r, G_POST_FFN))
    r.block_out[...] = low_first(r, out.astype(BF16))
    return shared


def note_gain(r, number, term):
    at, count, _, _ = GAINS[number]
    r.gain_sums[0:1, at : at + count] = term


def feed_forward_back(r, spreads, shared, start):
    core = lax.axis_index("dp")
    for piece in (GATE_ONE, GATE_TWO, OUT, UP_ONE, UP_TWO, DOWN_ONE, DOWN_TWO):
        spreads[piece].free()
    grad_out = low_first(r, r.out_cot[0].astype(F32))
    grad_ffn_out, term = norm_back(r.ffn_out[...], gain(r, G_POST_FFN), grad_out)
    note_gain(r, G_POST_FFN, term)
    low_grad = grad_ffn_out.astype(BF16)
    r.both_low[core] = low_grad
    low_shared = share(r, r.both_low, r.both_low.at[core])
    grad_in = jnp.zeros((128, 640), F32)
    grad_in_b = jnp.zeros((128, 640), F32)
    grads_shared = []
    for number in range(4):
        at = slice(512 * number, 512 * number + 512)
        down = down_rows(r.w[DOWN], number)
        grad_hidden = dot_nt(low_grad, down[...].reshape(512, 640))
        gate, up = r.gate[:, at], r.up[:, at]
        activated, inner = gelu_parts(gate)
        slope = 0.5 * (1.0 + inner) + 0.5 * gate * (1.0 - inner * inner) * GELU * (
            1.0 + 3 * 0.044715 * gate * gate
        )
        grad_gate = (grad_hidden * up * slope).astype(BF16)
        grad_up = (grad_hidden * activated).astype(BF16)
        r.both_gate[core, :, at] = grad_gate
        r.both_up[core, :, at] = grad_up
        grad_in += dot_nt(grad_gate, columns(r.w[GATE], 512 * number, 512))
        grad_in_b += dot_nt(grad_up, columns(r.w[UP], 512 * number, 512))
        if number % 2:
            lanes = pl.ds(512 * number - 512, 1024)
            for both in (r.both_gate, r.both_up):
                grads_shared.append(
                    r.links.across(
                        both.at[core, :, lanes],
                        lambda core, both=both, lanes=lanes: both.at[core, :, lanes],
                        both.at[core, :, lanes],
                    )
                )
    def columns_of_both(first):
        for number, ins, both, wait in (
            (GATE, r.both_in, r.both_gate, grads_shared[first // 512]),
            (UP, r.both_in_b, r.both_up, grads_shared[first // 512 + 1]),
        ):
            wait.wait()
            for at in (first, first + 512):
                lanes = slice(at, at + 512)
                term = dot_tn(pair(ins), both[:, :, lanes].reshape(256, 512))[:320].astype(BF16)
                r.w[number][core, :, :, lanes] = term.reshape(4, 80, 512)

    grad_in = grad_in + unturned(r, grad_in_b)
    back, term = norm_back(r.mid[...], gain(r, G_FFN), grad_in)
    note_gain(r, G_FFN, term)
    grad_mid = grad_out + back
    r.grad_mid[...] = grad_mid
    back, term = norm_back(r.proj[...], gain(r, G_POST_ATTN), grad_mid)
    note_gain(r, G_POST_ATTN, term)
    proj_low = back.astype(BF16)
    r.both_proj[core] = proj_low
    proj_shared = share(r, r.both_proj, r.both_proj.at[core])
    grad_attn = dot_nt(proj_low, r.w[OUTPUT][...].reshape(1024, 640)).astype(BF16)
    for block in range(2):
        for head in range(HEADS):
            r.grad_attn[head_rows(block, head)] = grad_attn[
                64 * block : 64 * block + 64, HEAD * head : HEAD * head + HEAD
            ]
    dots = jnp.sum(r.grad_attn[...].astype(F32) * r.attn[...], axis=1, keepdims=True)
    r.dots[...] = jnp.broadcast_to(dots, (512, 128))

    def rest_back():
        shared[DOWN].wait()
        low_shared.wait()
        term = dot_tn(pair(r.both_hidden), pair(r.both_low)).astype(BF16)
        r.w[DOWN][core] = term.reshape(4, 4, 4, 16, 640)
        start(DOWN_ONE, DOWN_TWO)
        shared[GATE].wait()
        shared[UP].wait()
        columns_of_both(0)
        start(GATE_ONE, UP_ONE)
        columns_of_both(1024)
        shared[OUTPUT].wait()
        proj_shared.wait()
        term = dot_tn(pair(r.both_attn), pair(r.both_proj)).astype(BF16)
        r.w[OUTPUT][core] = term.reshape(4, 128, 640)

    return rest_back


def queries_back(r, spreads, shared):
    core = lax.axis_index("dp")
    total = jnp.zeros((1, HEAD), F32)
    for head in range(HEADS):
        at = slice(HEAD * head, HEAD * head + HEAD)
        grad = jnp.concatenate([r.grad_query[head_rows(block, head)] for block in range(2)], axis=0)
        back, term = norm_back(
            r.query_raw[:, at], gain(r, G_QUERY), rope_back(r, grad * QUARTER)
        )
        total += term
        r.both_query[core, :, at] = back.astype(BF16)
    note_gain(r, G_QUERY, total)
    query_shared = share(r, r.both_query, r.both_query.at[core])
    r.grad_normed[...] = unturned(
        r, dot_nt(r.both_query[core], r.w[QUERY][...].reshape(640, 1024))
    )

    def rest_back():
        spreads[ASK].free()
        shared[QUERY].wait()
        query_shared.wait()
        term = dot_tn(pair(r.both_normed), pair(r.both_query))[:320].astype(BF16)
        r.w[QUERY][core] = term.reshape(4, 80, 1024)

    return rest_back


def add_rows(count, to, value):
    def one(at):
        rows = pl.ds(pl.multiple_of(at * 16, 16), 16)
        to[rows] = (to[rows].astype(F32) + value[rows].astype(F32)).astype(BF16)

    loop(count // 16, one)


def add_into(to, value):
    lead = to.shape[:-2]
    if not lead:
        add_rows(to.shape[0], to, value)
    elif len(lead) == 1:
        for at in range(lead[0]):
            add_rows(to.shape[1], to.at[at], value.at[at])
    else:
        for at in range(lead[0]):
            add_into(to.at[at], value.at[at])


class Gather:
    def __init__(self, r, piece):
        self.piece, axis = piece, piece_axis(piece)
        core, mine = lax.axis_index("dp"), place()[axis]
        number = PIECES[piece][0]
        self.land = piece_of(piece, r.landed[number], 3)
        self.at = lambda step: piece_plane(r, piece, core, shifted(mine, step))
        sends = r.links.sends(self.land)
        self.far = r.links.ring(
            axis,
            lambda step: half_of(piece, self.at(2), 0 if step == 1 else 1),
            lambda step, at: half_of(piece, self.land.at[2], 0 if step == 1 else 1),
            None,
            steps=(1, 3),
            apart=True,
            sends=sends,
        )
        self.near = r.links.ring(
            axis,
            self.at,
            lambda step, at: self.land.at[0 if step == 1 else 1],
            self.land.at[pl.ds(0, 2)],
            begin=False,
            steps=(1, 3),
            sends=sends,
        )

    def relay(self):
        for which, step in enumerate((1, 3)):
            self.far.wait(step)
            add_into(
                half_of(self.piece, self.at(step), which),
                half_of(self.piece, self.land.at[2], which),
            )
            self.near.start(step)


def repack(r, number, *gathers):
    _, rows, by_chip = WEIGHTS[number]
    count, tiles = plane_tiles(number)
    own, land = own_plane(r, number), r.landed[number]
    for gather in gathers:
        gather.near.wait_all()
    for tile in range(tiles):
        lanes = slice(128 * tile, 128 * tile + 128)
        index = (slice(None),) * (3 if by_chip else 1) + (lanes,)
        total = add_all([own[index]] + [land[(step, *index)] for step in range(2)])
        r.stage[pl.ds(tile, count, stride=tiles)] = total.reshape(count, 128)

    def one(chip):
        r.p[number][chip // 4, chip % 4, :rows] = r.stage[
            pl.ds(pl.multiple_of(chip * rows, 8), rows)
        ].astype(BF16)

    loop(16, one)


def late_second(r, number):
    second = weight_order(number)[1]
    mine = place()[second]
    return r.links.ring(
        second,
        lambda step: r.p[number].at[shifted(mine, step)],
        lambda step, at: r.second[number].at[step - 1],
        r.second[number],
        begin=False,
    )


def late_first(r, number):
    first = weight_order(number)[0]
    mine = place()[first]
    return r.links.ring(
        first,
        lambda step: r.line[number].at[shifted(mine, step)],
        lambda step, at: r.first[number].at[step - 1],
        r.first[number],
        begin=False,
    )


def late_line(r, number, ring):
    own = place()[weight_order(number)[1]]
    ring.wait_all()
    for at in range(4):
        r.line[number][at] = add_all(
            [r.p[number][own, at]] + [r.second[number][step, at] for step in range(3)]
        ).astype(BF16)


def late_end(r, number, ring, out):
    mine = place()[weight_order(number)[0]]
    ring.wait_all()
    out[...] = add_all([r.line[number][mine]] + [r.first[number][step] for step in range(3)])


def scatter_third(r):
    spot = place()
    rings, specials = [], []
    for part, (row, rows) in enumerate(KV_ROWS):
        last = ORDERS[part][2]
        rings.append(
            r.links.ring(
                last,
                lambda step, row=row, rows=rows, last=last: of_plane(
                    r.slots, last, shifted(spot[last], step), pl.ds(row, rows)
                ),
                lambda step, at, rb=r.rb[part]: rb.at[step - 1],
                r.rb[part],
                begin=False,
            )
        )
        specials.append(
            r.links.ring(
                last,
                lambda step, row=row, rows=rows: r.grad_extra.at[2, pl.ds(row, rows)],
                lambda step, at, rs=r.rs[part]: rs.at[step - 1],
                r.rs[part],
                begin=False,
            )
        )
    return rings, specials


def scatter_second(r, thirds, specials):
    spot = place()
    me = lax.axis_index("ctx")
    low_me = my_low(r)
    rings = []
    for part, (row, rows) in enumerate(KV_ROWS):
        first, second, last = ORDERS[part]
        rb, rs, total, land = r.rb[part], r.rs[part], r.g2[part], r.r2[part]
        thirds[part].wait_all()
        specials[part].wait_all()
        special = add_all([r.grad_extra[2, row : row + rows]] + [rs[step] for step in range(3)])
        r.sp[part][...] = special.astype(BF16)
        senders = [low_of(r, chip_of(spot, last, -step)) for step in (1, 2, 3)]

        def collect(
            at, i2, i1, rb=rb, sp=r.sp[part], total=total, row=row, rows=rows, last=last, senders=senders
        ):
            chip = chip_of(at, last, 0)
            source = low_of(r, chip)
            plane = [at[axis] for axis in (X, Y, Z) if axis != last]
            both = r.slots[at[0], at[1], at[2], pl.ds(row, rows)].astype(F32)
            none = jnp.zeros_like(both)
            low = jnp.where(source < low_me, both, none)
            for step in (1, 2, 3):
                came = rb[step - 1, plane[0], plane[1]].astype(F32)
                low += jnp.where(source < senders[step - 1], came, none)
                both += came
            high = both - low
            low += jnp.where(chip == me, r.grad_extra[0, pl.ds(row, rows)].astype(F32), none)
            high += jnp.where(chip == me, r.grad_extra[1, pl.ds(row, rows)].astype(F32), none)
            low += jnp.where(source == 63, sp[...].astype(F32), none)
            total[i2, 2 * i1] = low.astype(BF16)
            total[i2, 2 * i1 + 1] = high.astype(BF16)

        plane_loop(part, collect)
        rings.append(
            r.links.ring(
                second,
                lambda step, total=total, second=second: total.at[shifted(spot[second], step)],
                lambda step, at, land=land: land.at[step - 1],
                land,
            )
        )
    return rings


def scatter_first(r, seconds):
    spot = place()
    rings = []
    for part in range(3):
        first, second, _ = ORDERS[part]
        total, land, line, end = r.g2[part], r.r2[part], r.f1[part], r.r1[part]
        seconds[part].wait_all()

        def pick(index, total=total, land=land, mine=spot[second]):
            return add_all([total[mine, index]] + [land[step, index] for step in range(3)]).astype(
                BF16
            )

        for at in range(4):
            line[at, 0] = pick(2 * at)
            line[at, 1] = pick(2 * at + 1)
        rings.append(
            r.links.ring(
                first,
                lambda step, line=line, first=first: line.at[shifted(spot[first], step)],
                lambda step, at, end=end: end.at[step - 1],
                end,
            )
        )
    return rings


def scatter_end(r, firsts):
    spot = place()
    for part, (row, rows) in enumerate(KV_ROWS):
        firsts[part].wait_all()
        mine = spot[ORDERS[part][0]]
        for index in range(2):
            r.kv_sum[index, row : row + rows] = add_all(
                [r.f1[part][mine, index]] + [r.r1[part][step, index] for step in range(3)]
            )


def keys_values_back(r, split_shared, between):
    lanes = []
    for lane in range(4):
        pieces = [
            r.kv_sum[block, unit_rows(token, lane)] for block in range(2) for token in range(4)
        ]
        lanes.append(jnp.concatenate(pieces, axis=0))
    grad_keys = jnp.concatenate(lanes[:2], axis=1)
    grad_values = jnp.concatenate(lanes[2:], axis=1)
    back, term = norm_back(r.key_raw[...], gain(r, G_KEY), rope_back(r, grad_keys))
    note_gain(r, G_KEY, term)
    kv_low = jnp.concatenate([back, grad_values], axis=1).astype(BF16)
    core = lax.axis_index("dp")
    r.both_kv[core] = kv_low
    kv_shared = share(r, r.both_kv, r.both_kv.at[core])
    grad_split = dot_nt(kv_low, r.w_kv[...]).astype(BF16)
    grad_normed = dot_nt(grad_split, r.splitting[...]) + r.grad_normed[...]
    back, term = norm_back(r.x[...], gain(r, G_ATTN), grad_normed)
    note_gain(r, G_ATTN, term)
    gains_back(r, G_KEY, G_ATTN)
    low, high = r.held[:64], r.held[64:]
    r.both_held[core] = jnp.where(core == 0, low, high)
    r.out_held[...] = jnp.where(core == 0, high, low)
    held_shared = share(r, r.both_held, r.out_held)
    r.tokens_grad[...] = low_first(r, (r.grad_mid[...] + back).astype(BF16))
    between()
    r.stage[SMALL : SMALL + 1024] = jnp.zeros((1024, 128), F32)
    split_shared.wait()
    kv_shared.wait()
    terms = dot_tn(pair(r.both_split), pair(r.both_kv))
    for tile in range(4):
        lanes = slice(128 * tile, 128 * tile + 128)
        r.stage[pl.ds(tile, 256, stride=4)] = terms[:256, lanes]
        r.stage[pl.ds(SMALL + tile, 64, stride=16)] = terms[256:320, lanes]
    held_shared.wait()
    r.stage[pl.ds(SMALL + 4, 64, stride=16)] = r.both_held[0] + r.both_held[1]
    for unit in range(2):
        for plane in range(4):
            row = SMALL * unit + 256 * plane
            r.u[unit][core, plane] = r.stage[row : row + 256].astype(BF16).reshape(4, 4, 16, 128)


def gains_back(r, *numbers):
    for number in numbers:
        at, count, _, _ = GAINS[number]
        lanes, owners = gain_maps(r, number)
        term = jnp.where(owners, r.gain_sums[0:1, at : at + count], 0.0).astype(BF16)
        r.held[...] += dot_nt(term, lanes)


def small_sums(r, between):
    links = r.links
    core = lax.axis_index("dp")
    spot = place()
    axes = ((X, Y, Z), (Y, Z, X))
    rings = []
    for unit, order in enumerate(axes):
        own, land = r.u[unit], r.land3[unit]
        axis = order[0]
        rings.append(
            links.ring(
                axis,
                lambda step, own=own, axis=axis: own.at[core, shifted(spot[axis], step)],
                lambda step, at, land=land: land.at[step - 1],
                land,
            )
        )
    between[0]()
    later = []
    for unit, order in enumerate(axes):
        own, land, out, to = r.u[unit], r.land3[unit], r.sum2[unit], r.land2[unit]
        rings[unit].wait_all()
        mine = spot[order[0]]

        def add(at, own=own, land=land, out=out, mine=mine):
            out[at] = add_all([own[core, mine, at]] + [land[step, at] for step in range(3)]).astype(
                BF16
            )

        loop(4, add)
        axis = order[1]
        later.append(
            links.ring(
                axis,
                lambda step, out=out, axis=axis: out.at[shifted(spot[axis], step)],
                lambda step, at, to=to: to.at[step - 1],
                to,
            )
        )
    between[1]()
    last = []
    for unit, order in enumerate(axes):
        own, land, out, to = r.sum2[unit], r.land2[unit], r.sum1[unit], r.land1[unit]
        later[unit].wait_all()
        out[...] = add_all([own[spot[order[1]]]] + [land[step] for step in range(3)]).astype(BF16)
        axis = order[2]
        last.append(
            links.ring(
                axis,
                lambda step, out=out, axis=axis: out.at[shifted(spot[axis], step)],
                lambda step, at, to=to: to.at[step - 1],
                to,
            )
        )
    between[2]()
    for unit, order in enumerate(axes):
        last[unit].wait_all()
        r.fk[16 * unit : 16 * unit + 16] = add_all(
            [r.sum1[unit][spot[order[2]]]] + [r.land1[unit][step] for step in range(3)]
        )


def layer(r):
    greet()
    for copy in r.fetches.values():
        copy.wait()
    pack(r)
    greeted()
    early_rings, early_held, spreads = early(r)
    unpack_small(r)
    keys_values(r)
    firsts = gather_first(r)
    split_shared = share(r, r.both_split, r.out_split)
    seconds = gather_second(r, firsts)
    early_pieces = (ASK, OUT, GATE_ONE, UP_ONE, DOWN_ONE, DOWN_TWO)
    for piece in early_pieces:
        spreads[piece].forward()
    for piece in LATE_PIECES:
        spreads[piece].forward()
    before = tuple(r.links.open)
    thirds, specials = gather_third(r, seconds)
    for piece in early_pieces:
        spreads[piece].pass_on()
    for piece in LATE_PIECES:
        spreads[piece].pass_on()
    spreads[ASK].finish()
    query_shared = queries(r)

    def pass_on(number):
        if number == 0:
            r.links.settle(before)

    attention(r, thirds, specials, pass_on)
    shared = feed_forward(r, spreads)
    shared[QUERY] = query_shared
    before = tuple(r.links.open)
    sums = {}

    def start(*pieces):
        for piece in pieces:
            sums[piece] = Gather(r, piece)

    def relay(*pieces):
        for piece in pieces:
            sums[piece].relay()

    pieces = {
        GATE: (GATE_ONE, GATE_TWO),
        OUTPUT: (OUT,),
        UP: (UP_ONE, UP_TWO),
        QUERY: (ASK,),
        DOWN: (DOWN_ONE, DOWN_TWO),
    }
    second_rings, first_rings = {}, {}

    def prepare_late():
        for number in pieces:
            second_rings[number] = late_second(r, number)
            first_rings[number] = late_first(r, number)

    def send_late(*numbers):
        for number in numbers:
            repack(r, number, *(sums[piece] for piece in pieces[number]))
            for step in (1, 2, 3):
                second_rings[number].start(step)

    def go_on(*numbers):
        for number in numbers:
            late_line(r, number, second_rings[number])
            for step in (1, 2, 3):
                first_rings[number].start(step)

    def finish(*numbers):
        outs = (r.fgate, r.foutput, r.fup, r.fquery, r.fdown)
        for number in numbers:
            late_end(r, number, first_rings[number], outs[number])

    rest_back = feed_forward_back(r, spreads, shared, start)
    thirds, third_specials = attention_back(r, lambda number: None)
    query_back = queries_back(r, spreads, shared)
    rest_back()
    query_back()
    start(GATE_TWO, UP_TWO, OUT, ASK)
    for ring in early_rings:
        ring.sent()
    for ring in seconds:
        ring.sent()
    r.links.settle(before)
    before = tuple(r.links.open)
    r.held[...] = jnp.zeros_like(r.held)
    gains_back(r, G_POST_ATTN, G_FFN, G_POST_FFN, G_QUERY)
    seconds = scatter_second(r, thirds, third_specials)
    relay(DOWN_ONE, GATE_ONE, UP_ONE)
    firsts = scatter_first(r, seconds)
    relay(DOWN_TWO, GATE_TWO, UP_TWO, OUT, ASK)
    scatter_end(r, firsts)
    for copy in early_held:
        copy.sent()
    prepare_late()
    core = lax.axis_index("dp")

    def on(which, action, *numbers):
        pl.when(core == which)(lambda: action(*numbers))

    keys_values_back(r, split_shared, lambda: on(1, send_late, DOWN, GATE, UP, OUTPUT, QUERY))

    def one():
        on(0, send_late, DOWN, GATE, UP, OUTPUT, QUERY)
        on(1, go_on, DOWN, GATE, UP, OUTPUT, QUERY)
        r.links.settle(before)

    def two():
        on(0, go_on, DOWN, GATE, UP)

    def three():
        on(0, go_on, OUTPUT, QUERY)

    small_sums(r, (one, two, three))
    finish(DOWN, GATE, UP, OUTPUT, QUERY)
    r.links.settle()
    assert r.links.sending <= COPIES[0] and r.links.receiving <= COPIES[1]


def end(r):
    def rows(out, source, base, count, tiles):
        r.stage[base : base + count * tiles] = source
        for tile in range(tiles):
            out[:, 128 * tile : 128 * tile + 128] = columns_of(r, base, count, tiles, tile)

    rows(r.gate_grad, r.fgate[...], 0, 5, 16)
    rows(r.output_grad, r.foutput[0:40], 80, 8, 5)
    rows(r.up_grad, r.fup[...], 128, 5, 16)
    rows(r.query_grad, r.fquery[0:40], 208, 5, 8)
    rows(r.down_grad, r.fdown[...], 256, 16, 5)
    r.stage[336:368] = r.fk[...]
    for tile in range(4):
        out = (r.key_grad, r.value_grad)[tile // 2]
        half = 128 * (tile % 2)
        out[:, half : half + 128] = columns_of(r, 336, 5, 4, tile)
    line = r.fk[16:24]
    gain_grads = (r.grad_attn_norm, r.grad_post_attn, r.grad_ffn_norm, r.grad_post_ffn, r.grad_q, r.grad_k)
    for number, (_, _, held, lane) in enumerate(GAINS):
        out = gain_grads[number]
        moved = line if lane == 0 else pltpu.roll(line, 128 - lane, 1)
        out[...] = moved[4:5, :held]
    r.final_out[0] = r.block_out[...]
    r.final_grad[0] = r.tokens_grad[...]


COPIES = (97, 159)


def by_part(*dims):
    return [hold(BF16, *dims, rows, 128) for _, rows in KV_ROWS]


def by_flat(*dims):
    return [hold(BF16, *dims, rows, 128) for rows in (80, 48, 80, 48, 80)]


def by_unit(*dims):
    return [hold(BF16, *dims, 16, 128) for _ in range(2)]


def by_weight(lead, core):
    return [
        hold(BF16, *core, *lead, 80, 2048),
        hold(BF16, *core, *lead, 128, 640),
        hold(BF16, *core, *lead, 80, 2048),
        hold(BF16, *core, *lead, 80, 1024),
        hold(BF16, *core, *lead, 4, 4, 16, 640),
    ]


def buffers():
    return dict(
        stage=hold(F32, 4096, 128),
        x=hold(F32, 128, 640),
        cos=hold(F32, 128, 128),
        sin=hold(F32, 128, 128),
        gains=hold(F32, 8, 3072),
        gain_sums=hold(F32, 8, 3072),
        turning=hold(BF16, 640, 640),
        splitting=hold(BF16, 640, 640),
        key_base=hold(jnp.int32, 32, 16, 128),
        key_rows=hold(jnp.int32, 32, 256),
        p=by_flat(4, 4),
        second=by_flat(3, 4),
        line=by_flat(4),
        first=by_flat(3),
        u=by_unit(2, 4, 4, 4),
        both_split=hold(BF16, 2, 128, 384),
        both_kv=hold(BF16, 2, 128, 512),
        both_held=hold(F32, 2, 64, 128),
        out_held=hold(F32, 64, 128),
        out_split=hold(BF16, 128, 384),
        held=hold(F32, 128, 128),
        land3=by_unit(3, 4, 4),
        sum2=by_unit(4, 4),
        land2=by_unit(3, 4),
        sum1=by_unit(4),
        land1=by_unit(3),
        w_kv=hold(BF16, 640, 512),
        w=by_weight((4,), (2,)),
        both_hidden=hold(BF16, 2, 128, 1024),
        both_low=hold(BF16, 2, 128, 640),
        both_gate=hold(BF16, 2, 128, 2048),
        both_up=hold(BF16, 2, 128, 2048),
        both_in=hold(BF16, 2, 128, 384),
        both_in_b=hold(BF16, 2, 128, 384),
        both_attn=hold(BF16, 2, 128, 512),
        both_proj=hold(BF16, 2, 128, 640),
        both_normed=hold(BF16, 2, 128, 384),
        both_query=hold(BF16, 2, 128, 1024),
        out_in=hold(BF16, 128, 384),
        out_in_b=hold(BF16, 128, 384),
        out_normed=hold(BF16, 128, 384),
        landed=[
            hold(BF16, 3, 80, 2048),
            hold(BF16, 3, 128, 640),
            hold(BF16, 3, 80, 2048),
            hold(BF16, 3, 80, 1024),
            hold(BF16, 3, 4, 4, 16, 640),
        ],
        kv3=hold(BF16, 2, 256, 128),
        f1=by_part(4, 2),
        g2=by_part(4, 8),
        sel=by_part(3, 4, 4),
        sp=by_part(),
        rsp=by_part(4),
        rb=by_part(3, 4, 4),
        rs=by_part(3),
        r2=by_part(3, 8),
        r1=by_part(3, 2),
        slots=hold(BF16, 4, 4, 4, 256, 128),
        extra=hold(BF16, 3, 256, 128),
        grad_extra=hold(BF16, 3, 256, 128),
        kv_sum=hold(F32, 2, 256, 128),
        normed=hold(BF16, 128, 640),
        normed_split=hold(BF16, 128, 640),
        normed_b=hold(BF16, 128, 640),
        key_raw=hold(F32, 128, 256),
        query_raw=hold(F32, 128, 1024),
        query=hold(BF16, 512, 256),
        attn=hold(F32, 512, 256),
        total=hold(F32, 512, 128),
        dots=hold(F32, 512, 128),
        attn_low=hold(BF16, 128, 1024),
        proj=hold(F32, 128, 640),
        mid=hold(F32, 128, 640),
        ffn_in=hold(BF16, 128, 640),
        ffn_in_b=hold(BF16, 128, 640),
        gate=hold(F32, 128, 2048),
        up=hold(F32, 128, 2048),
        hidden=hold(BF16, 128, 2048),
        ffn_out=hold(F32, 128, 640),
        grad_mid=hold(F32, 128, 640),
        grad_attn=hold(BF16, 512, 256),
        grad_query=hold(F32, 512, 256),
        grad_normed=hold(F32, 128, 640),
    )


def on_device(
    tokens,
    doc_lengths,
    block_order,
    attn_norm,
    query_weight,
    key_weight,
    value_weight,
    query_gain,
    key_gain,
    output_weight,
    attn_post_norm,
    ffn_norm,
    gate_weight,
    up_weight,
    down_weight,
    ffn_post_norm,
    out_cot,
):
    made = run(
        layer,
        dict(block_order=block_order, doc_lengths=doc_lengths),
        {},
        dict(
            block_out=hold(BF16, 128, 640),
            tokens_grad=hold(BF16, 128, 640),
            fgate=hold(F32, 80, 128),
            foutput=hold(F32, 48, 128),
            fup=hold(F32, 80, 128),
            fquery=hold(F32, 48, 128),
            fdown=hold(F32, 80, 128),
            fk=hold(F32, 32, 128),
        ),
        buffers(),
        number=1,
        copies=COPIES,
        fetched=dict(
            gate_weight=gate_weight,
            output_weight=output_weight,
            up_weight=up_weight,
            query_weight=query_weight,
            down_weight=down_weight,
            key_weight=key_weight,
            value_weight=value_weight,
            attn_norm=attn_norm[None],
            attn_post_norm=attn_post_norm[None],
            ffn_norm=ffn_norm[None],
            ffn_post_norm=ffn_post_norm[None],
            query_gain=query_gain[None],
            key_gain=key_gain[None],
            tokens=tokens,
            table=jnp.asarray(number_table()),
            frequency=jnp.asarray(ROPE_BASE ** (-2.0 * np.arange(128) / 256), F32)[None],
            out_cot=out_cot,
        ),
    )
    results = run(
        end,
        {},
        made,
        dict(
            final_out=hold(BF16, 1, 128, 640),
            final_grad=hold(BF16, 1, 128, 640),
            grad_attn_norm=hold(F32, 1, 5),
            query_grad=hold(F32, 5, 1024),
            key_grad=hold(F32, 5, 256),
            value_grad=hold(F32, 5, 256),
            grad_q=hold(F32, 1, 2),
            grad_k=hold(F32, 1, 2),
            output_grad=hold(F32, 8, 640),
            grad_post_attn=hold(F32, 1, 5),
            grad_ffn_norm=hold(F32, 1, 5),
            gate_grad=hold(F32, 5, 2048),
            up_grad=hold(F32, 5, 2048),
            down_grad=hold(F32, 16, 640),
            grad_post_ffn=hold(F32, 1, 5),
        ),
        dict(stage=hold(F32, 3088, 128)),
    )
    return tuple(
        value.reshape(-1) if value.shape[0] == 1 and value.ndim == 2 else value
        for value in results.values()
    )


def solution(mesh):
    rows = P(("dp", "ctx"), None)
    vector = P(("dp", "ctx"))
    stream = P("dp", "ctx", None)
    return jax.shard_map(
        on_device,
        mesh=mesh,
        in_specs=(
            stream,
            P("dp", None),
            P(),
            vector,
            rows,
            rows,
            rows,
            vector,
            vector,
            rows,
            vector,
            vector,
            rows,
            rows,
            rows,
            vector,
            stream,
        ),
        out_specs=(
            stream,
            stream,
            vector,
            rows,
            rows,
            rows,
            vector,
            vector,
            rows,
            vector,
            vector,
            rows,
            rows,
            rows,
            vector,
        ),
        check_vma=False,
    )
```
